32 devices in a mesh: space: 16 (over z, x, core), snap: 2 (over y).
Axes of the slice: x: 2, y: 2, z: 4, core: 2. Of those that a mesh axis runs over, the one named last changes fastest.
Arguments:
- velocity: bfloat16 [32, 3, 64, 32, 128], P('snap', None, 'space'), may hold values from -8 to 8
- metric: float32 [3, 64, 32, 128], P(None, 'space'), may hold values from 0.5 to 2
- volume: float32 [64, 32, 128], P('space'), may hold values from 0.3 to 9
- coeffs: bfloat16 [32, 32], replicated, may hold values from -1 to 1
Outputs:
- gram: float32 [32, 32], P('snap')
- modes: bfloat16 [32, 3, 64, 32, 128], P('snap', None, 'space')
The draws below stay inside these ranges and needn't reach their ends.
All inputs are finite; a program needn't handle non-finite values.
Results may differ from the reference program's by a relative error of at most 0.0004.
The reference program's roundings to bfloat16 on the way (of `vorticity` and `weighted`) count: a program that leaves them out, or rounds other values in their place, can miss the bound.
Values may be sent and summed in bfloat16 or wider, within the bound.
No kernel may reach another device: no remote copies, remote signals or barrier semaphores. Data moves between devices by JAX's collectives and lax.ppermute only.
A program may use at most 64 MiB of HBM per device.

```python
import math
import jax
import jax.numpy as jnp
from jax import lax

SNAPS = 32
NY = 32
NZ = 128
NX = 64


def draw_volume(key, part):
    place = jnp.arange(NX, dtype=jnp.float32)
    rising = 1.0 + 2.0 * place / (NX - 1)
    base = jnp.exp(jax.random.uniform(key, (NX, NY, NZ), jnp.float32, jnp.log(0.5), jnp.log(2.0)))
    return base * rising[:, None, None]


def draw_velocity(key, part):
    shared = 12
    cells = 3 * NX * NY * NZ
    key_fields = jax.random.fold_in(key, 101)
    key_amps = jax.random.fold_in(key, 202)
    key_noise = jax.random.fold_in(key, 303)
    order = jnp.arange(shared, dtype=jnp.float32)
    weights = 0.6 * jnp.power(0.85, order)
    amps = jax.random.normal(key_amps, (SNAPS, shared), jnp.float32) * weights[None, :]
    fields = jax.random.normal(key_fields, (shared, cells), jnp.float32)
    noise = jax.random.normal(key_noise, (SNAPS, cells), jnp.float32)
    mixed = jnp.dot(amps, fields) + 0.4 * noise
    mixed = jnp.clip(mixed, -8.0, 8.0)
    return mixed.reshape(SNAPS, 3, NX, NY, NZ).astype(jnp.bfloat16)


def block_scale(own_key, dims, pieces, low, top_value):
    def one(position, parts):
        draws = jax.random.uniform(jax.random.fold_in(jax.random.fold_in(own_key, 6), position), (parts,), jnp.float32, low / len(pieces), top_value / len(pieces))
        return jnp.repeat(jnp.exp(draws), dims[position] // parts).reshape((-1,) + (1,) * (len(dims) - position - 1))

    gain = one(*pieces[0])
    for cut in pieces[1:]:
        gain = gain * one(*cut)
    return gain


def scatter_about(stream_key, shape, deviation, reach, held_as=jnp.bfloat16):
    values = deviation * jax.random.normal(stream_key, shape, jnp.float32)
    return jnp.clip(values, min=-reach, max=reach).astype(held_as)


def setup_inputs(seed: int = 0) -> dict:
    arg_keys = jax.random.split(jax.random.key(seed), 5)
    velocity = draw_velocity(jax.random.fold_in(arg_keys[4], 71), 0)
    metric = jnp.clip(jnp.exp(math.log(2.0) - 1.3862944 * jax.random.uniform(arg_keys[1], (3, NX, NY, NZ), jnp.float32) ** block_scale(arg_keys[1], (3, NX, NY, NZ), ((1, 16),), -0.2, 0.2)), 0.5, 2.0)
    volume = draw_volume(jax.random.fold_in(arg_keys[4], 71), 0)
    coeffs = scatter_about(arg_keys[3], (SNAPS, SNAPS), SNAPS ** -0.5, 1.0)
    return {"velocity": velocity, "metric": metric, "volume": volume, "coeffs": coeffs}


def deriv(padded, dim):
    count = padded.shape[dim] - 4

    def cut(offset):
        return lax.slice_in_dim(padded, offset, offset + count, axis=dim)
    return (8.0 * (cut(3) - cut(1)) - (cut(4) - cut(0))) / 12.0

def curl(padded_x, metric):
    inner = padded_x[:, :, 2:-2]
    padded_y = jnp.pad(inner, ((0, 0), (0, 0), (0, 0), (2, 2), (0, 0)))
    padded_z = jnp.concatenate([inner[..., -2:], inner, inner[..., :2]], axis=4)
    along_x = deriv(padded_x, 2) * metric[0]
    along_y = deriv(padded_y, 3) * metric[1]
    along_z = deriv(padded_z, 4) * metric[2]
    omega_x = along_y[:, 2] - along_z[:, 1]
    omega_y = along_z[:, 0] - along_x[:, 2]
    omega_z = along_x[:, 1] - along_y[:, 0]
    return jnp.stack([omega_x, omega_y, omega_z], axis=1).astype(jnp.bfloat16)

def reference(velocity, metric, volume, coeffs):

    def single(snapshot):
        padded = jnp.concatenate([snapshot[:, -2:], snapshot, snapshot[:, :2]], axis=1)[None]
        return curl(padded.astype(jnp.float32), metric)[0]
    vorticity = lax.map(single, velocity)
    snaps = velocity.shape[0]
    weighted = (vorticity.astype(jnp.float32) * volume).astype(jnp.bfloat16).reshape(snaps, -1)
    flat = vorticity.reshape(snaps, -1)
    scale = 1.0 / (3.0 * volume.shape[0] * volume.shape[1] * volume.shape[2])
    gram = lax.dot_general(weighted, flat, (((1,), (1,)), ((), ())), preferred_element_type=jnp.float32) * scale
    coeff_f = coeffs.astype(jnp.float32)
    energy = lax.optimization_barrier(jnp.sum(coeff_f * jnp.dot(gram, coeff_f, precision=lax.Precision.HIGHEST), axis=0))
    raw = lax.dot_general(coeffs, flat, (((0,), (0,)), ((), ())), preferred_element_type=jnp.float32)
    modes = (raw / jnp.sqrt(energy + 1e-06)[:, None]).astype(jnp.bfloat16).reshape(vorticity.shape)
    return (gram, modes)
```

```python
import functools

import jax
import jax.numpy as jnp
from jax import lax
from jax.experimental import pallas as pl
from jax.experimental.pallas import tpu as pltpu
from jax.sharding import PartitionSpec as P

EPS = 1e-06
WIDTH = 2
ROWS = 128
LIMIT = 24 * 1024 * 1024


def with_halo(shard, sides, width):
    for axis, dim in sides:
        peers, length = (lax.axis_size(axis), shard.shape[dim])
        up = [(i, (i + 1) % peers) for i in range(peers)]
        down = [(j, i) for i, j in up]
        last = lax.slice_in_dim(shard, length - width, length, axis=dim)
        leading = lax.slice_in_dim(shard, 0, width, axis=dim)
        before = lax.ppermute(last, axis, up)
        after = lax.ppermute(leading, axis, down)
        shard = jnp.concatenate([before, shard, after], axis=dim)
    return shard


def deriv(padded, dim):
    count = padded.shape[dim] - 4

    def cut(offset):
        return lax.slice_in_dim(padded, offset, offset + count, axis=dim)

    return (8.0 * (cut(3) - cut(1)) - (cut(4) - cut(0))) / 12.0


def curl(padded_x, metric):
    inner = padded_x[:, :, 2:-2]
    padded_y = jnp.pad(inner, ((0, 0), (0, 0), (0, 0), (2, 2), (0, 0)))
    padded_z = jnp.concatenate([inner[..., -2:], inner, inner[..., :2]], axis=4)
    along_x = deriv(padded_x, 2) * metric[0]
    along_y = deriv(padded_y, 3) * metric[1]
    along_z = deriv(padded_z, 4) * metric[2]
    omega_x = along_y[:, 2] - along_z[:, 1]
    omega_y = along_z[:, 0] - along_x[:, 2]
    omega_z = along_x[:, 1] - along_y[:, 0]
    return jnp.stack([omega_x, omega_y, omega_z], axis=1).astype(jnp.bfloat16)


def many_groups(velocity, metric, volume, coeffs):
    snap_dev = velocity.shape[0]
    snaps = coeffs.shape[0]
    group = lax.axis_index("snap")
    scale = 1.0 / (
        3.0 * volume.shape[0] * lax.axis_size("space") * volume.shape[1] * volume.shape[2]
    )
    padded = with_halo(velocity, (("space", 2),), 2)
    vorticity = curl(padded.astype(jnp.float32), metric)
    coeff_f = coeffs.astype(jnp.float32)
    moved = lax.all_to_all(vorticity, "snap", split_axis=3, concat_axis=0, tiled=True)
    part_y = moved.shape[3]
    vol_part = lax.dynamic_slice_in_dim(volume, group * part_y, part_y, 1)
    weighted = (moved.astype(jnp.float32) * vol_part).astype(jnp.bfloat16).reshape(snaps, -1)
    flat = moved.reshape(snaps, -1)
    partial_value = lax.dot_general(
        weighted, flat, (((1,), (1,)), ((), ())), preferred_element_type=jnp.float32
    )
    raw = lax.dot_general(
        coeffs, flat, (((0,), (0,)), ((), ())), preferred_element_type=jnp.float32
    )
    whole = lax.psum(partial_value, ("space", "snap")) * scale
    energy = jnp.sum(coeff_f * jnp.dot(whole, coeff_f, precision=lax.Precision.HIGHEST), axis=0)
    rows = lax.dynamic_slice_in_dim(whole, group * snap_dev, snap_dev, 0)
    local_modes = (raw / jnp.sqrt(energy + EPS)[:, None]).astype(jnp.bfloat16).reshape(moved.shape)
    modes = lax.all_to_all(local_modes, "snap", split_axis=0, concat_axis=3, tiled=True)
    return (rows, modes)


def vmem():
    return pl.BlockSpec(memory_space=pltpu.VMEM)


def anywhere():
    return pl.BlockSpec(memory_space=pl.ANY)


def params():
    return pltpu.CompilerParams(vmem_limit_bytes=LIMIT)


def cost(flops, moved):
    return pl.CostEstimate(flops=flops, bytes_accessed=moved, transcendentals=0)


def z_stencil(size):
    rows = lax.broadcasted_iota(jnp.int32, (size, size), 0)
    cols = lax.broadcasted_iota(jnp.int32, (size, size), 1)
    ahead = rows - cols
    ahead = jnp.where(ahead < 0, ahead + size, ahead)
    out = jnp.where(ahead == 1, 8.0, 0.0) - jnp.where(ahead == size - 1, 8.0, 0.0)
    out = out - jnp.where(ahead == 2, 1.0, 0.0) + jnp.where(ahead == size - 2, 1.0, 0.0)
    return out.astype(jnp.bfloat16)


def spread(src, wide):
    snaps, ny, nz = src.shape
    wide[...] = src.astype(jnp.float32).reshape(snaps * ny, nz)


def row(wide, y, snaps, ny):
    return wide[pl.ds(y, snaps, ny), :]


def y_stencil(wide, y, snaps, ny):
    def at(j):
        if j < 0 or j >= ny:
            return jnp.zeros((snaps, wide.shape[1]), jnp.float32)
        return row(wide, j, snaps, ny)

    return 8.0 * (at(y + 1) - at(y - 1)) - (at(y + 2) - at(y - 2))


def z_blocks(field, matrix, ny):
    _, snaps, nz = field.shape
    block = max(1, ROWS // snaps)
    for start in range(0, ny, block):
        part = field[start : start + block].reshape(block * snaps, nz)
        along = jnp.dot(part, matrix, preferred_element_type=jnp.float32)
        along = along.reshape(block, snaps, nz)
        for k in range(block):
            yield start + k, along[k]


def factor(metric_ref, m, layer, y):
    return metric_ref[m, layer, pl.ds(y, 1), :] * (1.0 / 12.0)


def send_kernel(half, vel_ref, out_ref, buf, wide, sem):
    snaps, _, _, ny, _ = buf.shape
    base = lax.axis_index("snap") * half
    copy = pltpu.make_async_copy(vel_ref.at[:, 1:3, pl.ds(base, half)], buf, sem)
    copy.start()
    copy.wait()
    for c in range(2):
        for i in range(half):
            spread(buf[:, c, i], wide)
            for y in range(ny):
                out_ref[c, i, y] = row(wide, y, snaps, ny).astype(jnp.bfloat16)


def omega_x_theirs_kernel(half, vel_ref, metric_ref, vw_ref, ox_ref, buf, wide, sem):
    snaps, _, _, ny, nz = buf.shape
    base = (1 - lax.axis_index("snap")) * half
    copy = pltpu.make_async_copy(vel_ref.at[:, 1:3, pl.ds(base, half)], buf, sem)
    copy.start()
    matrix = z_stencil(nz)
    copy.wait()
    for i in range(half):
        for c in range(2):
            spread(buf[:, c, i], wide)
            for y in range(ny):
                vw_ref[c, i, y] = row(wide, y, snaps, ny).astype(jnp.bfloat16)
        for y, along in z_blocks(vw_ref[0, i], matrix, ny):
            value = y_stencil(wide, y, snaps, ny) * factor(metric_ref, 1, base + i, y)
            value = value - along * factor(metric_ref, 2, base + i, y)
            ox_ref[i, y] = value.astype(jnp.bfloat16)


def rest_kernel(half, vel_ref, metric_ref, vw_ref, ox_ref, zu_ref, yu_ref, buf, rows, wide, sem):
    snaps, _, ny, nz = buf.shape
    copy = pltpu.make_async_copy(vel_ref.at[:, 0], buf, sem)
    copy.start()
    matrix = z_stencil(nz)
    group = lax.axis_index("snap")
    mine = group * half
    for i in range(half):
        for y in range(ny):
            wide[pl.ds(y, snaps, ny), :] = vw_ref[1, i, y].astype(jnp.float32)
        for y, along in z_blocks(vw_ref[0, i], matrix, ny):
            value = y_stencil(wide, y, snaps, ny) * factor(metric_ref, 1, mine + i, y)
            value = value - along * factor(metric_ref, 2, mine + i, y)
            ox_ref[i, y] = value.astype(jnp.bfloat16)
    copy.wait()
    for slot in range(2):
        base = mine if slot else (1 - group) * half
        for i in range(half):
            layer = base + i
            spread(buf[:, layer], wide)
            for y in range(ny):
                rows[y] = row(wide, y, snaps, ny).astype(jnp.bfloat16)
            for y, along in z_blocks(rows[...], matrix, ny):
                zu_ref[slot, i, y] = along * factor(metric_ref, 2, layer, y)
                value = y_stencil(wide, y, snaps, ny) * factor(metric_ref, 1, layer, y)
                yu_ref[slot, i, y] = value


def curl_yz_kernel(slot, near_ref, far_ref, halo_ref, zu_ref, yu_ref, metric_ref, out_ref):
    _, half, ny, _, _ = near_ref.shape
    group = lax.axis_index("snap")
    part = group if slot else 1 - group

    def run(low_ref, high_ref):
        def plane(c, i, y):
            if i < 0:
                ref, k = low_ref, half + i
            elif i < half:
                ref, k = near_ref, i
            else:
                ref, k = high_ref, i - half
            return ref[c, k, y].astype(jnp.float32)

        def along_x(c, i, y):
            inner = plane(c, i + 1, y) - plane(c, i - 1, y)
            return 8.0 * inner - (plane(c, i + 2, y) - plane(c, i - 2, y))

        for i in range(half):
            for y in range(ny):
                scale = factor(metric_ref, 0, part * half + i, y)
                omega_y = zu_ref[slot, i, y] - along_x(1, i, y) * scale
                omega_z = along_x(0, i, y) * scale - yu_ref[slot, i, y]
                out_ref[0, i, y] = omega_y.astype(jnp.bfloat16)
                out_ref[1, i, y] = omega_z.astype(jnp.bfloat16)

    @pl.when(part == 0)
    def _():
        run(halo_ref, far_ref)

    @pl.when(part == 1)
    def _():
        run(far_ref, halo_ref)


def gram_kernel(scale, own_x, own_yz, got_x, got_yz, volume_ref, out_ref):
    half, ny, snaps, nz = own_x.shape
    base = lax.axis_index("snap") * half
    step = min(ny, 8)
    total = jnp.zeros((2 * snaps, 2 * snaps), jnp.float32)
    for c in range(3):
        own = own_x if c == 0 else own_yz.at[c - 1]
        got = got_x if c == 0 else got_yz.at[c - 1]
        for i in range(half):
            for start in range(0, ny, step):
                plain, heavy = [], []
                for y in range(start, start + step):
                    both = jnp.concatenate([own[i, y], got[i, y]], axis=0)
                    weight = volume_ref[base + i, pl.ds(y, 1), :]
                    plain.append(both)
                    heavy.append((both.astype(jnp.float32) * weight).astype(jnp.bfloat16))
                total = total + lax.dot_general(
                    jnp.concatenate(heavy, axis=1),
                    jnp.concatenate(plain, axis=1),
                    (((1,), (1,)), ((), ())),
                    preferred_element_type=jnp.float32,
                )
    out_ref[...] = total * scale


def mode_scale(gram_ref, coeff_ref, snaps, nz):
    coeff = coeff_ref[...]
    inner = jnp.dot(
        coeff, gram_ref[...], precision=lax.Precision.HIGHEST, preferred_element_type=jnp.float32
    )
    energy = jnp.sum(inner * coeff, axis=1, keepdims=True)
    return jnp.broadcast_to(1.0 / jnp.sqrt(energy + EPS), (snaps, nz))


def modes_kernel(half, gram_ref, coeff_ref, block_ref, *refs):
    (ox_mine, ox_theirs, oyz_mine, oyz_theirs, gx_mine, gx_theirs, gyz_mine, gyz_theirs) = refs[:8]
    out_ref, wide = refs[8:]
    _, ny, snaps, nz = ox_mine.shape
    group = lax.axis_index("snap")
    scale = mode_scale(gram_ref, coeff_ref, snaps, nz)
    block = block_ref.shape[0] // snaps
    for c in range(3):
        for slot in range(2):
            if c == 0:
                own, got = ((ox_theirs, gx_theirs), (ox_mine, gx_mine))[slot]
            else:
                own, got = ((oyz_theirs, gyz_theirs), (oyz_mine, gyz_mine))[slot]
                own, got = own.at[c - 1], got.at[c - 1]
            base = (group if slot else 1 - group) * half
            for i in range(half):
                for start in range(0, ny, block):
                    both = jnp.concatenate(
                        [
                            own[i, start : start + block].reshape(block * snaps, nz),
                            got[i, start : start + block].reshape(block * snaps, nz),
                        ],
                        axis=0,
                    )
                    raw = jnp.dot(block_ref[...], both, preferred_element_type=jnp.float32)
                    raw = raw.reshape(block, snaps, nz)
                    for k in range(block):
                        wide[pl.ds(start + k, snaps, ny), :] = raw[k] * scale
                value = wide[...].reshape(snaps, ny, nz).astype(jnp.bfloat16)
                out_ref[:, c, base + i] = value


def total_over_all(value, half_rows):
    other = lax.ppermute(value, "snap", [(0, 1), (1, 0)])
    value = value + jnp.roll(other, (half_rows, half_rows), axis=(0, 1))
    peers = lax.axis_size("space")
    step = 1
    while step < peers:
        value = value + lax.ppermute(value, "space", [(i, i ^ step) for i in range(peers)])
        step *= 2
    return value


def two_groups(velocity, metric, volume, coeffs):
    snaps, _, layers, ny, nz = velocity.shape
    half = layers // 2
    peers = lax.axis_size("space")
    group = lax.axis_index("snap")
    bf16, f32 = jnp.bfloat16, jnp.float32
    swap = [(0, 1), (1, 0)]
    both = ("space", "snap")

    def halo(first):
        pairs = []
        for s in range(peers):
            for g in range(2):
                down = (g == 0) == first
                pairs.append((s * 2 + g, ((s + (-1 if down else 1)) % peers) * 2 + g))
        return pairs

    field = jax.ShapeDtypeStruct((half, ny, snaps, nz), bf16)
    pair = jax.ShapeDtypeStruct((2, half, ny, snaps, nz), bf16)
    partial_sum = jax.ShapeDtypeStruct((2, half, ny, snaps, nz), f32)
    cells = half * ny * snaps * nz
    buf = pltpu.VMEM((snaps, 2, half, ny, nz), bf16)
    wide = pltpu.VMEM((snaps * ny, nz), f32)
    dma = pltpu.SemaphoreType.DMA

    vw_mine = pl.pallas_call(
        functools.partial(send_kernel, half),
        out_shape=pair,
        in_specs=[anywhere()],
        out_specs=vmem(),
        scratch_shapes=[buf, wide, dma],
        compiler_params=params(),
        cost_estimate=cost(2 * cells, 8 * cells),
        name="flip_mine",
    )(velocity)
    halo_theirs = lax.ppermute(vw_mine, both, halo(True))

    vw_theirs, ox_theirs = pl.pallas_call(
        functools.partial(omega_x_theirs_kernel, half),
        out_shape=(pair, field),
        in_specs=[anywhere(), vmem()],
        out_specs=(vmem(), vmem()),
        scratch_shapes=[buf, wide, dma],
        compiler_params=params(),
        cost_estimate=cost(20 * cells, 10 * cells),
        name="omega_x_theirs",
    )(velocity, metric)
    gx_mine = lax.ppermute(ox_theirs, "snap", swap)

    ox_mine, zu, yu = pl.pallas_call(
        functools.partial(rest_kernel, half),
        out_shape=(field, partial_sum, partial_sum),
        in_specs=[anywhere(), vmem(), vmem()],
        out_specs=(vmem(), vmem(), vmem()),
        scratch_shapes=[
            pltpu.VMEM((snaps, layers, ny, nz), bf16),
            pltpu.VMEM((ny, snaps, nz), bf16),
            wide,
            dma,
        ],
        compiler_params=params(),
        cost_estimate=cost(60 * cells, 30 * cells),
        name="omega_x_mine",
    )(velocity, metric, vw_mine)

    def curl_yz(slot, near, far, edge):
        return pl.pallas_call(
            functools.partial(curl_yz_kernel, slot),
            out_shape=pair,
            in_specs=[vmem()] * 6,
            out_specs=vmem(),
            compiler_params=params(),
            cost_estimate=cost(40 * cells, 30 * cells),
            name="omega_yz_mine" if slot else "omega_yz_theirs",
        )(near, far, edge, zu, yu, metric)

    oyz_theirs = curl_yz(0, vw_theirs, vw_mine, halo_theirs)
    gyz_mine = lax.ppermute(oyz_theirs, "snap", swap)

    late, halo_theirs = lax.optimization_barrier((vw_theirs, halo_theirs))
    halo_mine = lax.ppermute(late, both, halo(False))
    oyz_mine = curl_yz(1, vw_mine, vw_theirs, halo_mine)

    scale = 1.0 / (3.0 * layers * peers * ny * nz)
    gram = pl.pallas_call(
        functools.partial(gram_kernel, scale),
        out_shape=jax.ShapeDtypeStruct((2 * snaps, 2 * snaps), f32),
        in_specs=[vmem()] * 5,
        out_specs=vmem(),
        compiler_params=params(),
        cost_estimate=cost(100 * cells, 20 * cells),
        name="gram",
    )(ox_mine, oyz_mine, gx_mine, gyz_mine, volume)

    late_x, late_yz, _ = lax.optimization_barrier((ox_mine, oyz_mine, gyz_mine))
    gx_theirs = lax.ppermute(late_x, "snap", swap)
    gyz_theirs = lax.ppermute(late_yz, "snap", swap)

    whole = total_over_all(gram, snaps)
    ordered = jnp.where(group == 0, coeffs, jnp.roll(coeffs, (snaps, snaps), axis=(0, 1)))
    mine_t = ordered[:, :snaps].T
    block = max(1, ROWS // snaps)
    eye = jnp.eye(block, dtype=bf16)
    blocks = jnp.concatenate(
        [jnp.kron(eye, mine_t[:, :snaps]), jnp.kron(eye, mine_t[:, snaps:])], axis=1
    )
    modes = pl.pallas_call(
        functools.partial(modes_kernel, half),
        out_shape=jax.ShapeDtypeStruct(velocity.shape, bf16),
        in_specs=[vmem()] * 11,
        out_specs=vmem(),
        scratch_shapes=[wide],
        compiler_params=params(),
        cost_estimate=cost(200 * cells, 30 * cells),
        name="modes",
    )(
        whole,
        mine_t.astype(f32),
        blocks,
        ox_mine,
        ox_theirs,
        oyz_mine,
        oyz_theirs,
        gx_mine,
        gx_theirs,
        gyz_mine,
        gyz_theirs,
    )
    rows = whole[:snaps]
    rows = jnp.where(group == 0, rows, jnp.roll(rows, snaps, axis=1))
    return (rows, modes)


def per_device(velocity, metric, volume, coeffs):
    peers = lax.axis_size("space")
    paired = lax.axis_size("snap") == 2 and velocity.shape[2] == 2 * WIDTH
    if paired and velocity.shape[0] % 16 == 0 and peers & (peers - 1) == 0:
        return two_groups(velocity, metric, volume, coeffs)
    return many_groups(velocity, metric, volume, coeffs)


def solution(mesh):
    placed = (
        P("snap", None, "space", None, None),
        P(None, "space", None, None),
        P("space", None, None),
        P(),
    )
    return jax.shard_map(
        per_device,
        mesh=mesh,
        in_specs=placed,
        out_specs=(P("snap", None), P("snap", None, "space", None, None)),
        check_vma=False,
    )
```

```python
import functools

import jax
import jax.numpy as jnp
from jax import lax
from jax.experimental import pallas as pl
from jax.experimental.pallas import tpu as pltpu
from jax.sharding import PartitionSpec as P

EPS = 1e-06
WIDTH = 2
ROWS = 128
LIMIT = 24 * 1024 * 1024


def with_halo(shard, sides, width):
    for axis, dim in sides:
        peers, length = (lax.axis_size(axis), shard.shape[dim])
        up = [(i, (i + 1) % peers) for i in range(peers)]
        down = [(j, i) for i, j in up]
        last = lax.slice_in_dim(shard, length - width, length, axis=dim)
        leading = lax.slice_in_dim(shard, 0, width, axis=dim)
        before = lax.ppermute(last, axis, up)
        after = lax.ppermute(leading, axis, down)
        shard = jnp.concatenate([before, shard, after], axis=dim)
    return shard


def deriv(padded, dim):
    count = padded.shape[dim] - 4

    def cut(offset):
        return lax.slice_in_dim(padded, offset, offset + count, axis=dim)

    return (8.0 * (cut(3) - cut(1)) - (cut(4) - cut(0))) / 12.0


def curl(padded_x, metric):
    inner = padded_x[:, :, 2:-2]
    padded_y = jnp.pad(inner, ((0, 0), (0, 0), (0, 0), (2, 2), (0, 0)))
    padded_z = jnp.concatenate([inner[..., -2:], inner, inner[..., :2]], axis=4)
    along_x = deriv(padded_x, 2) * metric[0]
    along_y = deriv(padded_y, 3) * metric[1]
    along_z = deriv(padded_z, 4) * metric[2]
    omega_x = along_y[:, 2] - along_z[:, 1]
    omega_y = along_z[:, 0] - along_x[:, 2]
    omega_z = along_x[:, 1] - along_y[:, 0]
    return jnp.stack([omega_x, omega_y, omega_z], axis=1).astype(jnp.bfloat16)


def many_groups(velocity, metric, volume, coeffs):
    snap_dev = velocity.shape[0]
    snaps = coeffs.shape[0]
    group = lax.axis_index("snap")
    scale = 1.0 / (
        3.0 * volume.shape[0] * lax.axis_size("space") * volume.shape[1] * volume.shape[2]
    )
    padded = with_halo(velocity, (("space", 2),), 2)
    vorticity = curl(padded.astype(jnp.float32), metric)
    coeff_f = coeffs.astype(jnp.float32)
    moved = lax.all_to_all(vorticity, "snap", split_axis=3, concat_axis=0, tiled=True)
    part_y = moved.shape[3]
    vol_part = lax.dynamic_slice_in_dim(volume, group * part_y, part_y, 1)
    weighted = (moved.astype(jnp.float32) * vol_part).astype(jnp.bfloat16).reshape(snaps, -1)
    flat = moved.reshape(snaps, -1)
    partial_value = lax.dot_general(
        weighted, flat, (((1,), (1,)), ((), ())), preferred_element_type=jnp.float32
    )
    raw = lax.dot_general(
        coeffs, flat, (((0,), (0,)), ((), ())), preferred_element_type=jnp.float32
    )
    whole = lax.psum(partial_value, ("space", "snap")) * scale
    energy = jnp.sum(coeff_f * jnp.dot(whole, coeff_f, precision=lax.Precision.HIGHEST), axis=0)
    rows = lax.dynamic_slice_in_dim(whole, group * snap_dev, snap_dev, 0)
    local_modes = (raw / jnp.sqrt(energy + EPS)[:, None]).astype(jnp.bfloat16).reshape(moved.shape)
    modes = lax.all_to_all(local_modes, "snap", split_axis=0, concat_axis=3, tiled=True)
    return (rows, modes)


def vmem():
    return pl.BlockSpec(memory_space=pltpu.VMEM)


def hbm():
    return pl.BlockSpec(memory_space=pltpu.HBM)


def params():
    return pltpu.CompilerParams(vmem_limit_bytes=LIMIT)


def cost(flops, moved):
    return pl.CostEstimate(flops=flops, bytes_accessed=moved, transcendentals=0)


def z_stencil(size):
    rows = lax.broadcasted_iota(jnp.int32, (size, size), 0)
    cols = lax.broadcasted_iota(jnp.int32, (size, size), 1)
    ahead = rows - cols
    ahead = jnp.where(ahead < 0, ahead + size, ahead)
    out = jnp.where(ahead == 1, 8.0, 0.0) - jnp.where(ahead == size - 1, 8.0, 0.0)
    out = out - jnp.where(ahead == 2, 1.0, 0.0) + jnp.where(ahead == size - 2, 1.0, 0.0)
    return out.astype(jnp.bfloat16)


def spread(src, wide):
    snaps, ny, nz = src.shape
    wide[...] = src.astype(jnp.float32).reshape(snaps * ny, nz)


def row(wide, y, snaps, ny):
    return wide[pl.ds(y, snaps, ny), :]


def y_stencils(load, ny):
    held = {}

    def at(j):
        if j not in held:
            held[j] = load(j)
        return held[j]

    zero = jnp.zeros_like(at(0))
    for y in range(ny):
        near = (at(y + 1) if y + 1 < ny else zero) - (at(y - 1) if y >= 1 else zero)
        far = (at(y + 2) if y + 2 < ny else zero) - (at(y - 2) if y >= 2 else zero)
        held.pop(y - 2, None)
        yield y, 8.0 * near - far


def z_derivative(field, matrix, along):
    rows = field.shape[0] * field.shape[1] * field.shape[2]
    along[...] = jnp.dot(
        field.reshape(rows, field.shape[3]), matrix, preferred_element_type=jnp.float32
    ).reshape(field.shape)


def factor(metric_ref, m, layer, y):
    return metric_ref[m, layer, pl.ds(y, 1), :] * (1.0 / 12.0)


def flip_kernel(half, vel_ref, out_ref, buf, wide, sems):
    snaps, _, _, ny, _ = buf.shape
    base = lax.axis_index("snap") * half
    copies = []
    for c in range(2):
        source = vel_ref.at[:, 1 + c, pl.ds(base, half)]
        copies.append(pltpu.make_async_copy(source, buf.at[:, c], sems.at[c]))
        copies[c].start()
    for c in range(2):
        copies[c].wait()
        for i in range(half):
            spread(buf[:, c, i], wide)
            for y in range(ny):
                out_ref[c, i, y] = row(wide, y, snaps, ny).astype(jnp.bfloat16)


def omega_x_theirs_kernel(
    half, vel_ref, metric_ref, vw_ref, ox_ref, buf, wide_v, wide_w, along, sems
):
    snaps, _, _, ny, nz = buf.shape
    base = (1 - lax.axis_index("snap")) * half
    copies = []
    for c in range(2):
        source = vel_ref.at[:, 1 + c, pl.ds(base, half)]
        copies.append(pltpu.make_async_copy(source, buf.at[:, c], sems.at[c]))
        copies[c].start()
    matrix = z_stencil(nz)
    copies[0].wait()
    for i in range(half):
        spread(buf[:, 0, i], wide_v)
        for y in range(ny):
            vw_ref[0, i, y] = row(wide_v, y, snaps, ny).astype(jnp.bfloat16)
    z_derivative(vw_ref[0], matrix, along)
    copies[1].wait()
    for i in range(half):
        spread(buf[:, 1, i], wide_w)

        def load(j):
            value = row(wide_w, j, snaps, ny)
            vw_ref[1, i, j] = value.astype(jnp.bfloat16)
            return value

        for y, across in y_stencils(load, ny):
            value = across * factor(metric_ref, 1, base + i, y)
            value = value - along[i, y] * factor(metric_ref, 2, base + i, y)
            ox_ref[i, y] = value.astype(jnp.bfloat16)


def rest_kernel(
    half, vel_ref, metric_ref, vw_ref, ox_ref, zu_ref, yu_ref, buf, flat, wide, along, sem
):
    snaps, _, ny, nz = buf.shape
    copy = pltpu.make_async_copy(vel_ref.at[:, 0], buf, sem)
    copy.start()
    matrix = z_stencil(nz)
    group = lax.axis_index("snap")
    mine = group * half
    z_derivative(vw_ref[0], matrix, along)
    for i in range(half):
        for y, across in y_stencils(lambda j: vw_ref[1, i, j].astype(jnp.float32), ny):
            value = across * factor(metric_ref, 1, mine + i, y)
            value = value - along[i, y] * factor(metric_ref, 2, mine + i, y)
            ox_ref[i, y] = value.astype(jnp.bfloat16)
    copy.wait()
    for slot in range(2):
        base = mine if slot else (1 - group) * half
        for i in range(half):
            spread(buf[:, base + i], wide)

            def load(j):
                value = row(wide, j, snaps, ny)
                flat[i, j] = value.astype(jnp.bfloat16)
                return value

            for y, across in y_stencils(load, ny):
                yu_ref[slot, i, y] = across * factor(metric_ref, 1, base + i, y)
        z_derivative(flat[...], matrix, along)
        for i in range(half):
            for y in range(ny):
                zu_ref[slot, i, y] = along[i, y] * factor(metric_ref, 2, base + i, y)


def curl_yz_kernel(slot, near_ref, far_ref, halo_ref, zu_ref, yu_ref, metric_ref, out_ref):
    _, half, ny, _, _ = near_ref.shape
    group = lax.axis_index("snap")
    part = group if slot else 1 - group

    def run(low_ref, high_ref):
        def plane(c, i, y):
            if i < 0:
                ref, k = low_ref, half + i
            elif i < half:
                ref, k = near_ref, i
            else:
                ref, k = high_ref, i - half
            return ref[c, k, y].astype(jnp.float32)

        for y in range(ny):
            planes = [[plane(c, i, y) for i in range(-WIDTH, half + WIDTH)] for c in range(2)]

            def along_x(c, i):
                at = planes[c]
                return 8.0 * (at[i + 3] - at[i + 1]) - (at[i + 4] - at[i])

            for i in range(half):
                scale = factor(metric_ref, 0, part * half + i, y)
                omega_y = zu_ref[slot, i, y] - along_x(1, i) * scale
                omega_z = along_x(0, i) * scale - yu_ref[slot, i, y]
                out_ref[0, i, y] = omega_y.astype(jnp.bfloat16)
                out_ref[1, i, y] = omega_z.astype(jnp.bfloat16)

    @pl.when(part == 0)
    def _():
        run(halo_ref, far_ref)

    @pl.when(part == 1)
    def _():
        run(far_ref, halo_ref)


def gram_of(own, got, volume_ref, base):
    half, ny, _, _ = own.shape
    total = None
    for i in range(half):
        plain, heavy = [], []
        for y in range(ny):
            pair = jnp.concatenate([own[i, y], got[i, y]], axis=0)
            weight = volume_ref[base + i, pl.ds(y, 1), :]
            plain.append(pair)
            heavy.append((pair.astype(jnp.float32) * weight).astype(jnp.bfloat16))
        part = lax.dot_general(
            jnp.concatenate(heavy, axis=1),
            jnp.concatenate(plain, axis=1),
            (((1,), (1,)), ((), ())),
            preferred_element_type=jnp.float32,
        )
        total = part if total is None else total + part
    return total


def gram_x_kernel(own, got, volume_ref, out_ref):
    base = lax.axis_index("snap") * own.shape[0]
    out_ref[...] = gram_of(own, got, volume_ref, base)


def gram_yz_kernel(scale, own, got, volume_ref, first_ref, out_ref, swapped_ref):
    base = lax.axis_index("snap") * own.shape[1]
    total = first_ref[...]
    for c in range(2):
        total = total + gram_of(own.at[c], got.at[c], volume_ref, base)
    total = total * scale
    snaps = total.shape[0] // 2
    out_ref[...] = total
    turned = jnp.concatenate([total[snaps:], total[:snaps]], axis=0)
    swapped_ref[...] = jnp.concatenate([turned[:, snaps:], turned[:, :snaps]], axis=1)


def raw_blocks(own, got, block_ref, put):
    ny, snaps, nz = own.shape
    block = block_ref.shape[0] // snaps
    lanes = 2 if ny % (2 * block) == 0 else 1
    for start in range(0, ny, block * lanes):
        columns = []
        for n in range(lanes):
            at = start + n * block
            parts = [ref[at : at + block].reshape(block * snaps, nz) for ref in (own, got)]
            columns.append(jnp.concatenate(parts, axis=0))
        both = columns[0] if lanes == 1 else jnp.concatenate(columns, axis=1)
        raw = jnp.dot(block_ref[...], both, preferred_element_type=jnp.float32)
        for n in range(lanes):
            part = raw[:, n * nz : (n + 1) * nz].reshape(block, snaps, nz)
            for k in range(block):
                put(start + n * block + k, part[k])


def raw_kernel(block_ref, own_x, got_x, own_yz, got_yz, out_ref):
    half, ny, snaps, _ = own_x.shape
    stride = 3 * half * ny
    for c in range(3):
        for i in range(half):
            own = own_x.at[i] if c == 0 else own_yz.at[c - 1, i]
            got = got_x.at[i] if c == 0 else got_yz.at[c - 1, i]

            def put(y, value):
                out_ref[pl.ds((c * half + i) * ny + y, snaps, stride), :] = value

            raw_blocks(own, got, block_ref, put)


def scaled_layer(own, got, block_ref, scale, wide, stage):
    ny, snaps, _ = own.shape

    def put(y, value):
        wide[pl.ds(y, snaps, ny), :] = value * scale

    raw_blocks(own, got, block_ref, put)
    for k in range(snaps):
        stage(k, wide[k * ny : (k + 1) * ny, :].astype(jnp.bfloat16))


def finish_mine_kernel(
    gram_ref, coeff_ref, block_ref, raw_ref, own, got,
    out_ref, rows_ref, scale_ref, stage, stage_x, rows_buf, wide, sems,
):
    half, ny, snaps, nz = own.shape
    group = lax.axis_index("snap")
    total = gram_ref[...]
    coeff = coeff_ref[...]
    inner = jnp.dot(
        coeff, total, precision=lax.Precision.HIGHEST, preferred_element_type=jnp.float32
    )
    energy = jnp.sum(inner * coeff, axis=1, keepdims=True)
    scale = jnp.broadcast_to(1.0 / jnp.sqrt(energy + EPS), (snaps, nz))
    scale_ref[...] = scale
    mine = total[:snaps]
    turned = jnp.concatenate([mine[:, snaps:], mine[:, :snaps]], axis=1)
    rows_buf[...] = jnp.where(group == 0, mine, turned)
    copies = [pltpu.make_async_copy(rows_buf, rows_ref, sems.at[0])]
    copies[0].start()
    block = half * ny
    for c in range(3):
        for k in range(snaps):
            at = (k * 3 + c) * block
            value = raw_ref[at : at + block, :] * scale_ref[k : k + 1, :]
            stage[k, c] = value.astype(jnp.bfloat16).reshape(half, ny, nz)
        target = out_ref.at[:, c, pl.ds(group * half, half)]
        copies.append(pltpu.make_async_copy(stage.at[:, c], target, sems.at[1 + c]))
        copies[-1].start()
    for i in range(half):

        def put(k, value):
            stage_x[k, i] = value

        scaled_layer(own.at[i], got.at[i], block_ref, scale, wide, put)
    target = out_ref.at[:, 0, pl.ds((1 - group) * half, half)]
    copies.append(pltpu.make_async_copy(stage_x, target, sems.at[4]))
    copies[-1].start()
    for copy in copies:
        copy.wait()


def finish_theirs_kernel(block_ref, scale_ref, own, got, _, out_ref, stage, wide, sems):
    half = own.shape[1]
    base = (1 - lax.axis_index("snap")) * half
    scale = scale_ref[...]
    copies = []
    for c in range(2):
        for i in range(half):

            def put(k, value):
                stage[k, c, i] = value

            scaled_layer(own.at[c, i], got.at[c, i], block_ref, scale, wide, put)
            target = out_ref.at[:, 1 + c, base + i]
            copies.append(pltpu.make_async_copy(stage.at[:, c, i], target, sems.at[c, i]))
            copies[-1].start()
    for copy in copies:
        copy.wait()


def sum_over(value, swapped, radix):
    value = value + lax.ppermute(swapped, "snap", [(0, 1), (1, 0)])
    peers = lax.axis_size("space")
    step = 1
    while step < peers:
        count = min(radix, peers // step)
        got = [
            lax.ppermute(value, "space", [(i, i ^ (k * step)) for i in range(peers)])
            for k in range(1, count)
        ]
        value = sum(got, value)
        step *= count
    return value


def two_groups(velocity, metric, volume, coeffs):
    snaps, _, layers, ny, nz = velocity.shape
    half = layers // 2
    peers = lax.axis_size("space")
    group = lax.axis_index("snap")
    bf16, f32 = jnp.bfloat16, jnp.float32
    swap = [(0, 1), (1, 0)]

    def halo(first):
        pairs = []
        for s in range(peers):
            for g in range(2):
                down = (g == 0) == first
                pairs.append((s * 2 + g, ((s + (-1 if down else 1)) % peers) * 2 + g))
        return pairs

    field = jax.ShapeDtypeStruct((half, ny, snaps, nz), bf16)
    pair = jax.ShapeDtypeStruct((2, half, ny, snaps, nz), bf16)
    partial_sum = jax.ShapeDtypeStruct((2, half, ny, snaps, nz), f32)
    square = jax.ShapeDtypeStruct((2 * snaps, 2 * snaps), f32)
    cells = half * ny * snaps * nz
    buf = pltpu.VMEM((snaps, 2, half, ny, nz), bf16)
    wide = pltpu.VMEM((snaps * ny, nz), f32)
    along = pltpu.VMEM((half, ny, snaps, nz), f32)
    dma = pltpu.SemaphoreType.DMA

    def call(kernel, name, out_shape, in_specs, scratch=(), out_specs=None, flops=20, **more):
        if out_specs is None:
            out_specs = jax.tree.map(lambda _: vmem(), out_shape)
        return pl.pallas_call(
            kernel,
            out_shape=out_shape,
            in_specs=in_specs,
            out_specs=out_specs,
            scratch_shapes=list(scratch),
            compiler_params=params(),
            cost_estimate=cost(flops * cells, 10 * cells),
            name=name,
            **more,
        )

    velocity = pltpu.with_memory_space_constraint(velocity, pltpu.HBM)
    vw_mine = call(
        functools.partial(flip_kernel, half),
        "flip_mine",
        pair,
        [hbm()],
        [buf, wide, dma((2,))],
    )(velocity)
    halo_theirs = lax.ppermute(vw_mine, ("space", "snap"), halo(True))

    vw_theirs, ox_theirs = call(
        functools.partial(omega_x_theirs_kernel, half),
        "omega_x_theirs",
        (pair, field),
        [hbm(), vmem()],
        [buf, wide, wide, along, dma((2,))],
    )(velocity, metric)
    gx_mine = lax.ppermute(ox_theirs, "snap", swap)

    ox_mine, zu, yu = call(
        functools.partial(rest_kernel, half),
        "omega_x_mine",
        (field, partial_sum, partial_sum),
        [hbm(), vmem(), vmem()],
        [
            pltpu.VMEM((snaps, layers, ny, nz), bf16),
            pltpu.VMEM((half, ny, snaps, nz), bf16),
            wide,
            along,
            dma,
        ],
    )(velocity, metric, vw_mine)

    def curl_yz(slot, near, far, edge):
        return call(
            functools.partial(curl_yz_kernel, slot),
            "omega_yz_mine" if slot else "omega_yz_theirs",
            pair,
            [vmem()] * 6,
        )(near, far, edge, zu, yu, metric)

    halo_theirs, gx_mine = lax.optimization_barrier((halo_theirs, gx_mine))
    oyz_theirs = curl_yz(0, vw_theirs, vw_mine, halo_theirs)
    gyz_mine = lax.ppermute(oyz_theirs, "snap", swap)

    late, _ = lax.optimization_barrier((vw_theirs, oyz_theirs))
    halo_mine = lax.ppermute(late, ("space", "snap"), halo(False))
    oyz_mine = curl_yz(1, vw_mine, vw_theirs, halo_mine)

    ordered = jnp.where(group == 0, coeffs, jnp.roll(coeffs, (snaps, snaps), axis=(0, 1)))
    mine_t = ordered[:, :snaps].T
    block = max(1, ROWS // snaps)
    eye = jnp.eye(block, dtype=bf16)
    blocks = jnp.concatenate(
        [jnp.kron(eye, mine_t[:, :snaps]), jnp.kron(eye, mine_t[:, snaps:])], axis=1
    )
    gram_x = call(gram_x_kernel, "gram_x", square, [vmem()] * 3)(ox_mine, gx_mine, volume)

    late_x, late_yz, gyz_mine, gram_x, blocks = lax.optimization_barrier(
        (ox_mine, oyz_mine, gyz_mine, gram_x, blocks)
    )
    gx_theirs = lax.ppermute(late_x, "snap", swap)
    gyz_theirs = lax.ppermute(late_yz, "snap", swap)

    scale = 1.0 / (3.0 * layers * peers * ny * nz)
    gram, swapped = call(
        functools.partial(gram_yz_kernel, scale), "gram_yz", (square, square), [vmem()] * 4
    )(oyz_mine, gyz_mine, volume, gram_x)

    def total_and_raw(radix, gram, swapped, *fields):
        raw = call(
            raw_kernel,
            "raw_mine",
            jax.ShapeDtypeStruct((snaps * 3 * half * ny, nz), f32),
            [vmem()] * 5,
        )(*fields)
        return sum_over(gram, swapped, radix), raw

    whole, raw = lax.cond(
        group < 2,
        functools.partial(total_and_raw, 4),
        functools.partial(total_and_raw, 2),
        gram, swapped, blocks, ox_mine, gx_mine, oyz_mine, gyz_mine,
    )

    modes, rows, mode_scale = call(
        finish_mine_kernel,
        "finish_mine",
        (
            jax.ShapeDtypeStruct(velocity.shape, bf16),
            jax.ShapeDtypeStruct((snaps, 2 * snaps), f32),
            jax.ShapeDtypeStruct((snaps, nz), f32),
        ),
        [vmem()] * 6,
        [
            pltpu.VMEM((snaps, 3, half, ny, nz), bf16),
            pltpu.VMEM((snaps, half, ny, nz), bf16),
            pltpu.VMEM((snaps, 2 * snaps), f32),
            wide,
            dma((5,)),
        ],
        (hbm(), hbm(), vmem()),
    )(whole, mine_t.astype(f32), blocks, raw, ox_theirs, gx_theirs)
    modes = call(
        finish_theirs_kernel,
        "finish_theirs",
        jax.ShapeDtypeStruct(velocity.shape, bf16),
        [vmem()] * 4 + [hbm()],
        [pltpu.VMEM((snaps, 2, half, ny, nz), bf16), wide, dma((2, half))],
        hbm(),
        input_output_aliases={4: 0},
    )(blocks, mode_scale, oyz_theirs, gyz_theirs, modes)
    return (rows, modes)


def per_device(velocity, metric, volume, coeffs):
    peers = lax.axis_size("space")
    paired = lax.axis_size("snap") == 2 and velocity.shape[2] == 2 * WIDTH
    if paired and velocity.shape[0] % 16 == 0 and peers & (peers - 1) == 0:
        return two_groups(velocity, metric, volume, coeffs)
    return many_groups(velocity, metric, volume, coeffs)


def solution(mesh):
    placed = (
        P("snap", None, "space", None, None),
        P(None, "space", None, None),
        P("space", None, None),
        P(),
    )
    return jax.shard_map(
        per_device,
        mesh=mesh,
        in_specs=placed,
        out_specs=(P("snap", None), P("snap", None, "space", None, None)),
        check_vma=False,
    )
```

```python
import functools

import jax
import jax.numpy as jnp
from jax import lax
from jax.experimental import pallas as pl
from jax.experimental.pallas import tpu as pltpu
from jax.sharding import PartitionSpec as P

EPS = 1e-06
WIDTH = 2
ROWS = 128
LIMIT = 24 * 1024 * 1024


def with_halo(shard, sides, width):
    for axis, dim in sides:
        peers, length = (lax.axis_size(axis), shard.shape[dim])
        up = [(i, (i + 1) % peers) for i in range(peers)]
        down = [(j, i) for i, j in up]
        last = lax.slice_in_dim(shard, length - width, length, axis=dim)
        leading = lax.slice_in_dim(shard, 0, width, axis=dim)
        before = lax.ppermute(last, axis, up)
        after = lax.ppermute(leading, axis, down)
        shard = jnp.concatenate([before, shard, after], axis=dim)
    return shard


def deriv(padded, dim):
    count = padded.shape[dim] - 4

    def cut(offset):
        return lax.slice_in_dim(padded, offset, offset + count, axis=dim)

    return (8.0 * (cut(3) - cut(1)) - (cut(4) - cut(0))) / 12.0


def curl(padded_x, metric):
    inner = padded_x[:, :, 2:-2]
    padded_y = jnp.pad(inner, ((0, 0), (0, 0), (0, 0), (2, 2), (0, 0)))
    padded_z = jnp.concatenate([inner[..., -2:], inner, inner[..., :2]], axis=4)
    along_x = deriv(padded_x, 2) * metric[0]
    along_y = deriv(padded_y, 3) * metric[1]
    along_z = deriv(padded_z, 4) * metric[2]
    omega_x = along_y[:, 2] - along_z[:, 1]
    omega_y = along_z[:, 0] - along_x[:, 2]
    omega_z = along_x[:, 1] - along_y[:, 0]
    return jnp.stack([omega_x, omega_y, omega_z], axis=1).astype(jnp.bfloat16)


def many_groups(velocity, metric, volume, coeffs):
    snap_dev = velocity.shape[0]
    snaps = coeffs.shape[0]
    group = lax.axis_index("snap")
    scale = 1.0 / (
        3.0 * volume.shape[0] * lax.axis_size("space") * volume.shape[1] * volume.shape[2]
    )
    padded = with_halo(velocity, (("space", 2),), 2)
    vorticity = curl(padded.astype(jnp.float32), metric)
    coeff_f = coeffs.astype(jnp.float32)
    moved = lax.all_to_all(vorticity, "snap", split_axis=3, concat_axis=0, tiled=True)
    part_y = moved.shape[3]
    vol_part = lax.dynamic_slice_in_dim(volume, group * part_y, part_y, 1)
    weighted = (moved.astype(jnp.float32) * vol_part).astype(jnp.bfloat16).reshape(snaps, -1)
    flat = moved.reshape(snaps, -1)
    partial_value = lax.dot_general(
        weighted, flat, (((1,), (1,)), ((), ())), preferred_element_type=jnp.float32
    )
    raw = lax.dot_general(
        coeffs, flat, (((0,), (0,)), ((), ())), preferred_element_type=jnp.float32
    )
    whole = lax.psum(partial_value, ("space", "snap")) * scale
    energy = jnp.sum(coeff_f * jnp.dot(whole, coeff_f, precision=lax.Precision.HIGHEST), axis=0)
    rows = lax.dynamic_slice_in_dim(whole, group * snap_dev, snap_dev, 0)
    local_modes = (raw / jnp.sqrt(energy + EPS)[:, None]).astype(jnp.bfloat16).reshape(moved.shape)
    modes = lax.all_to_all(local_modes, "snap", split_axis=0, concat_axis=3, tiled=True)
    return (rows, modes)


def vmem():
    return pl.BlockSpec(memory_space=pltpu.VMEM)


def hbm():
    return pl.BlockSpec(memory_space=pltpu.HBM)


def params():
    return pltpu.CompilerParams(vmem_limit_bytes=LIMIT)


def cost(flops, moved):
    return pl.CostEstimate(flops=flops, bytes_accessed=moved, transcendentals=0)


def z_stencil(size):
    rows = lax.broadcasted_iota(jnp.int32, (size, size), 0)
    cols = lax.broadcasted_iota(jnp.int32, (size, size), 1)
    ahead = rows - cols
    ahead = jnp.where(ahead < 0, ahead + size, ahead)
    out = jnp.where(ahead == 1, 8.0, 0.0) - jnp.where(ahead == size - 1, 8.0, 0.0)
    out = out - jnp.where(ahead == 2, 1.0, 0.0) + jnp.where(ahead == size - 2, 1.0, 0.0)
    return out.astype(jnp.bfloat16)


def spread(src, wide):
    snaps, ny, nz = src.shape
    wide[...] = src.astype(jnp.float32).reshape(snaps * ny, nz)


def row(wide, y, snaps, ny):
    return wide[pl.ds(y, snaps, ny), :]


def y_stencils(load, ny):
    held = {}

    def at(j):
        if j not in held:
            held[j] = load(j)
        return held[j]

    zero = jnp.zeros_like(at(0))
    for y in range(ny):
        near = (at(y + 1) if y + 1 < ny else zero) - (at(y - 1) if y >= 1 else zero)
        far = (at(y + 2) if y + 2 < ny else zero) - (at(y - 2) if y >= 2 else zero)
        held.pop(y - 2, None)
        yield y, 8.0 * near - far


def z_derivative(field, matrix, along):
    rows = field.shape[0] * field.shape[1] * field.shape[2]
    along[...] = jnp.dot(
        field.reshape(rows, field.shape[3]), matrix, preferred_element_type=jnp.float32
    ).reshape(field.shape)


def factor(metric_ref, m, layer, y):
    return metric_ref[m, layer, pl.ds(y, 1), :] * (1.0 / 12.0)


def flip_kernel(half, vel_ref, out_ref, buf, wide, sems):
    snaps, _, _, ny, _ = buf.shape
    base = lax.axis_index("snap") * half
    copies = {}
    for c in range(2):
        for i in range(half):
            source = vel_ref.at[:, 1 + c, base + i]
            copies[c, i] = pltpu.make_async_copy(source, buf.at[:, c, i], sems.at[c, i])
            copies[c, i].start()
    for c in range(2):
        for i in range(half):
            copies[c, i].wait()
            spread(buf[:, c, i], wide)
            for y in range(ny):
                out_ref[c, i, y] = row(wide, y, snaps, ny).astype(jnp.bfloat16)


def omega_x_theirs_kernel(half, vel_ref, metric_ref, vw_ref, ox_ref, wide, along):
    snaps, _, _, ny, nz = vel_ref.shape
    base = (1 - lax.axis_index("snap")) * half
    matrix = z_stencil(nz)
    for i in range(half):
        spread(vel_ref[:, 1, base + i], wide)
        for y in range(ny):
            vw_ref[0, i, y] = row(wide, y, snaps, ny).astype(jnp.bfloat16)
    z_derivative(vw_ref[0], matrix, along)
    for i in range(half):
        spread(vel_ref[:, 2, base + i], wide)

        def load(j):
            value = row(wide, j, snaps, ny)
            vw_ref[1, i, j] = value.astype(jnp.bfloat16)
            return value

        for y, across in y_stencils(load, ny):
            value = across * factor(metric_ref, 1, base + i, y)
            value = value - along[i, y] * factor(metric_ref, 2, base + i, y)
            ox_ref[i, y] = value.astype(jnp.bfloat16)


def rest_kernel(half, vel_ref, metric_ref, vw_ref, ox_ref, zu_ref, yu_ref, flat, wide, along):
    snaps, _, _, ny, nz = vel_ref.shape
    matrix = z_stencil(nz)
    group = lax.axis_index("snap")
    mine = group * half
    z_derivative(vw_ref[0], matrix, along)
    for i in range(half):
        for y, across in y_stencils(lambda j: vw_ref[1, i, j].astype(jnp.float32), ny):
            value = across * factor(metric_ref, 1, mine + i, y)
            value = value - along[i, y] * factor(metric_ref, 2, mine + i, y)
            ox_ref[i, y] = value.astype(jnp.bfloat16)
    for slot in range(2):
        base = mine if slot else (1 - group) * half
        for i in range(half):
            spread(vel_ref[:, 0, base + i], wide)

            def load(j):
                value = row(wide, j, snaps, ny)
                flat[i, j] = value.astype(jnp.bfloat16)
                return value

            for y, across in y_stencils(load, ny):
                yu_ref[slot, i, y] = across * factor(metric_ref, 1, base + i, y)
        z_derivative(flat[...], matrix, along)
        for i in range(half):
            for y in range(ny):
                zu_ref[slot, i, y] = along[i, y] * factor(metric_ref, 2, base + i, y)


def curl_yz_kernel(slot, near_ref, far_ref, halo_ref, zu_ref, yu_ref, metric_ref, out_ref):
    _, half, ny, _, _ = near_ref.shape
    group = lax.axis_index("snap")
    part = group if slot else 1 - group

    def run(low_ref, high_ref):
        def plane(c, i, y):
            if i < 0:
                ref, k = low_ref, half + i
            elif i < half:
                ref, k = near_ref, i
            else:
                ref, k = high_ref, i - half
            return ref[c, k, y].astype(jnp.float32)

        for y in range(ny):
            planes = [[plane(c, i, y) for i in range(-WIDTH, half + WIDTH)] for c in range(2)]

            def along_x(c, i):
                at = planes[c]
                return 8.0 * (at[i + 3] - at[i + 1]) - (at[i + 4] - at[i])

            for i in range(half):
                scale = factor(metric_ref, 0, part * half + i, y)
                omega_y = zu_ref[slot, i, y] - along_x(1, i) * scale
                omega_z = along_x(0, i) * scale - yu_ref[slot, i, y]
                out_ref[0, i, y] = omega_y.astype(jnp.bfloat16)
                out_ref[1, i, y] = omega_z.astype(jnp.bfloat16)

    @pl.when(part == 0)
    def _():
        run(halo_ref, far_ref)

    @pl.when(part == 1)
    def _():
        run(far_ref, halo_ref)


def gram_of(own, got, volume_ref, base):
    half, ny, _, _ = own.shape
    total = None
    for i in range(half):
        plain, heavy = [], []
        for y in range(ny):
            pair = jnp.concatenate([own[i, y], got[i, y]], axis=0)
            weight = volume_ref[base + i, pl.ds(y, 1), :]
            plain.append(pair)
            heavy.append((pair.astype(jnp.float32) * weight).astype(jnp.bfloat16))
        part = lax.dot_general(
            jnp.concatenate(heavy, axis=1),
            jnp.concatenate(plain, axis=1),
            (((1,), (1,)), ((), ())),
            preferred_element_type=jnp.float32,
        )
        total = part if total is None else total + part
    return total


def gram_x_kernel(own, got, volume_ref, out_ref):
    base = lax.axis_index("snap") * own.shape[0]
    out_ref[...] = gram_of(own, got, volume_ref, base)


def gram_yz_kernel(scale, own, got, volume_ref, first_ref, out_ref):
    base = lax.axis_index("snap") * own.shape[1]
    total = first_ref[...]
    for c in range(2):
        total = total + gram_of(own.at[c], got.at[c], volume_ref, base)
    out_ref[...] = total * scale


def coeff_kernel(coeff_ref, mine_ref, block_ref):
    snaps, count = mine_ref.shape
    rows = block_ref.shape[0]
    base = lax.axis_index("snap") * snaps

    def chosen(shape, test):
        left = lax.broadcasted_iota(jnp.int32, shape, 0)
        right = lax.broadcasted_iota(jnp.int32, shape, 1)
        return jnp.where(test(left, right), 1.0, 0.0).astype(jnp.bfloat16)

    def take(a, b, dims):
        out = lax.dot_general(a, b, (dims, ((), ())), preferred_element_type=jnp.float32)
        return out.astype(jnp.bfloat16)

    mine = chosen((snaps, count), lambda k, m: m == k + base)
    mine = take(mine, coeff_ref[...], ((1,), (1,)))
    order = chosen((count, count), lambda j, m: j == lax.rem(m + base, count))
    mine = take(mine, order, ((1,), (0,)))
    mine_ref[...] = mine.astype(jnp.float32)
    down = chosen((rows, snaps), lambda r, k: lax.rem(r, snaps) == k)
    for part in range(count // snaps):
        across = chosen((count, rows), lambda j, c: j == lax.rem(c, snaps) + part * snaps)
        wide = take(take(down, mine, ((1,), (0,))), across, ((1,), (0,)))
        same = chosen((rows, rows), lambda r, c: lax.div(r, snaps) == lax.div(c, snaps))
        block_ref[:, part * rows : (part + 1) * rows] = wide * same


def raw_blocks(own, got, block_ref, put):
    ny, snaps, nz = own.shape
    block = block_ref.shape[0] // snaps
    lanes = 2 if ny % (2 * block) == 0 else 1
    for start in range(0, ny, block * lanes):
        columns = []
        for n in range(lanes):
            at = start + n * block
            parts = [ref[at : at + block].reshape(block * snaps, nz) for ref in (own, got)]
            columns.append(jnp.concatenate(parts, axis=0))
        both = columns[0] if lanes == 1 else jnp.concatenate(columns, axis=1)
        raw = jnp.dot(block_ref[...], both, preferred_element_type=jnp.float32)
        for n in range(lanes):
            part = raw[:, n * nz : (n + 1) * nz].reshape(block, snaps, nz)
            for k in range(block):
                put(start + n * block + k, part[k])


def raw_kernel(block_ref, own_x, got_x, own_yz, got_yz, out_ref):
    half, ny, snaps, _ = own_x.shape
    stride = 3 * half * ny
    for c in range(3):
        for i in range(half):
            own = own_x.at[i] if c == 0 else own_yz.at[c - 1, i]
            got = got_x.at[i] if c == 0 else got_yz.at[c - 1, i]

            def put(y, value):
                out_ref[pl.ds((c * half + i) * ny + y, snaps, stride), :] = value

            raw_blocks(own, got, block_ref, put)


def finish_kernel(
    half, part_ref, other_ref, coeff_ref, mine_ref, theirs_ref,
    out_ref, rows_ref, stage, rows_buf, wide, sems,
):
    snaps, _, _, ny, nz = stage.shape
    group = lax.axis_index("snap")
    other = other_ref[...]
    other = jnp.concatenate([other[snaps:], other[:snaps]], axis=0)
    other = jnp.concatenate([other[:, snaps:], other[:, :snaps]], axis=1)
    total = part_ref[...] + other
    coeff = coeff_ref[...]
    inner = jnp.dot(
        coeff, total, precision=lax.Precision.HIGHEST, preferred_element_type=jnp.float32
    )
    energy = jnp.sum(inner * coeff, axis=1, keepdims=True)
    wide[...] = jnp.broadcast_to(1.0 / jnp.sqrt(energy + EPS), (snaps, nz))
    mine = total[:snaps]
    turned = jnp.concatenate([mine[:, snaps:], mine[:, :snaps]], axis=1)
    rows_buf[...] = jnp.where(group == 0, mine, turned)
    copies = [pltpu.make_async_copy(rows_buf, rows_ref, sems.at[0])]
    copies[0].start()
    block = half * ny
    step = snaps // 4
    for n in range(4):
        for k in range(n * step, (n + 1) * step):
            scale = wide[k : k + 1, :]
            for c in range(3):
                at = (k * 3 + c) * block
                for raw_ref, base in ((mine_ref, group), (theirs_ref, 1 - group)):
                    value = raw_ref[at : at + block, :] * scale
                    value = value.astype(jnp.bfloat16).reshape(half, ny, nz)
                    stage[k, c, pl.ds(base * half, half)] = value
        part = pl.ds(n * step, step)
        copies.append(pltpu.make_async_copy(stage.at[part], out_ref.at[part], sems.at[1 + n]))
        copies[-1].start()
    for copy in copies:
        copy.wait()


def sum_over_space(value, radix):
    peers = lax.axis_size("space")
    step = 1
    while step < peers:
        count = min(radix, peers // step)
        got = [
            lax.ppermute(value, "space", [(i, i ^ (k * step)) for i in range(peers)])
            for k in range(1, count)
        ]
        value = sum(got, value)
        step *= count
    return value


def two_groups(velocity, metric, volume, coeffs):
    snaps, _, layers, ny, nz = velocity.shape
    half = layers // 2
    peers = lax.axis_size("space")
    bf16, f32 = jnp.bfloat16, jnp.float32
    swap = [(0, 1), (1, 0)]

    def halo(first):
        pairs = []
        for s in range(peers):
            for g in range(2):
                down = (g == 0) == first
                pairs.append((s * 2 + g, ((s + (-1 if down else 1)) % peers) * 2 + g))
        return pairs

    field = jax.ShapeDtypeStruct((half, ny, snaps, nz), bf16)
    pair = jax.ShapeDtypeStruct((2, half, ny, snaps, nz), bf16)
    partial_sum = jax.ShapeDtypeStruct((2, half, ny, snaps, nz), f32)
    square = jax.ShapeDtypeStruct((2 * snaps, 2 * snaps), f32)
    cells = half * ny * snaps * nz
    wide = pltpu.VMEM((snaps * ny, nz), f32)
    along = pltpu.VMEM((half, ny, snaps, nz), f32)
    dma = pltpu.SemaphoreType.DMA

    def call(kernel, name, out_shape, in_specs, scratch=(), out_specs=None, work=10, **more):
        if out_specs is None:
            out_specs = jax.tree.map(lambda _: vmem(), out_shape)
        return pl.pallas_call(
            kernel,
            out_shape=out_shape,
            in_specs=in_specs,
            out_specs=out_specs,
            scratch_shapes=list(scratch),
            compiler_params=params(),
            cost_estimate=cost(2 * work * cells, work * cells),
            name=name,
            **more,
        )

    vw_mine = call(
        functools.partial(flip_kernel, half),
        "flip_mine",
        pair,
        [hbm()],
        [pltpu.VMEM((snaps, 2, half, ny, nz), bf16), wide, dma((2, half))],
    )(pltpu.with_memory_space_constraint(velocity, pltpu.HBM))
    halo_theirs = lax.ppermute(vw_mine, ("space", "snap"), halo(True))

    vw_theirs, ox_theirs = call(
        functools.partial(omega_x_theirs_kernel, half),
        "omega_x_theirs",
        (pair, field),
        [vmem(), vmem()],
        [wide, along],
    )(velocity, metric)
    gx_mine = lax.ppermute(ox_theirs, "snap", swap)

    ox_mine, zu, yu = call(
        functools.partial(rest_kernel, half),
        "omega_x_mine",
        (field, partial_sum, partial_sum),
        [vmem()] * 3,
        [pltpu.VMEM((half, ny, snaps, nz), bf16), wide, along],
    )(velocity, metric, vw_mine)

    def curl_yz(slot, near, far, edge):
        return call(
            functools.partial(curl_yz_kernel, slot),
            "omega_yz_mine" if slot else "omega_yz_theirs",
            pair,
            [vmem()] * 6,
        )(near, far, edge, zu, yu, metric)

    oyz_theirs = curl_yz(0, vw_theirs, vw_mine, halo_theirs)
    gyz_mine = lax.ppermute(oyz_theirs, "snap", swap)

    late, gx_mine, _ = lax.optimization_barrier((vw_theirs, gx_mine, oyz_theirs))
    halo_mine = lax.ppermute(late, ("space", "snap"), halo(False))
    coeff_rows, blocks = call(
        coeff_kernel,
        "coeff_blocks",
        (
            jax.ShapeDtypeStruct((snaps, 2 * snaps), f32),
            jax.ShapeDtypeStruct((ROWS // snaps * snaps, ROWS // snaps * 2 * snaps), bf16),
        ),
        [vmem()],
    )(coeffs)
    gram_x = call(gram_x_kernel, "gram_x", square, [vmem()] * 3)(ox_mine, gx_mine, volume)
    halo_mine, blocks, gram_x = lax.optimization_barrier((halo_mine, blocks, gram_x))
    oyz_mine = curl_yz(1, vw_mine, vw_theirs, halo_mine)
    gx_theirs = lax.ppermute(ox_mine, "snap", swap)
    gyz_theirs = lax.ppermute(oyz_mine, "snap", swap)

    scale = 1.0 / (3.0 * layers * peers * ny * nz)
    gram = call(functools.partial(gram_yz_kernel, scale), "gram_yz", square, [vmem()] * 4)(
        oyz_mine, gyz_mine, volume, gram_x
    )

    gram = lax.cond(
        lax.axis_index("snap") < 2,
        lambda value: sum_over_space(value, 4),
        lambda value: sum_over_space(value, 2),
        gram,
    )
    other = lax.ppermute(gram, "snap", swap)

    def raw_modes(name, *fields):
        shape = jax.ShapeDtypeStruct((snaps * 3 * half * ny, nz), f32)
        return call(raw_kernel, name, shape, [vmem()] * 5)(blocks, *fields)

    raw_mine = raw_modes("raw_mine", ox_mine, gx_mine, oyz_mine, gyz_mine)
    raw_theirs = raw_modes("raw_theirs", ox_theirs, gx_theirs, oyz_theirs, gyz_theirs)
    modes, rows = call(
        functools.partial(finish_kernel, half),
        "finish",
        (
            jax.ShapeDtypeStruct(velocity.shape, bf16),
            jax.ShapeDtypeStruct((snaps, 2 * snaps), f32),
        ),
        [vmem()] * 5,
        [
            pltpu.VMEM(velocity.shape, bf16),
            pltpu.VMEM((snaps, 2 * snaps), f32),
            pltpu.VMEM((snaps, nz), f32),
            dma((5,)),
        ],
        (hbm(), hbm()),
    )(gram, other, coeff_rows, raw_mine, raw_theirs)
    return (rows, modes)


def per_device(velocity, metric, volume, coeffs):
    peers = lax.axis_size("space")
    paired = lax.axis_size("snap") == 2 and velocity.shape[2] == 2 * WIDTH
    if paired and velocity.shape[0] % 16 == 0 and peers & (peers - 1) == 0:
        return two_groups(velocity, metric, volume, coeffs)
    return many_groups(velocity, metric, volume, coeffs)


def solution(mesh):
    placed = (
        P("snap", None, "space", None, None),
        P(None, "space", None, None),
        P("space", None, None),
        P(),
    )
    return jax.shard_map(
        per_device,
        mesh=mesh,
        in_specs=placed,
        out_specs=(P("snap", None), P("snap", None, "space", None, None)),
        check_vma=False,
    )
```

```python
import functools

import jax
import jax.numpy as jnp
from jax import lax
from jax.experimental import pallas as pl
from jax.experimental.pallas import tpu as pltpu
from jax.sharding import PartitionSpec as P

EPS = 1e-06
WIDTH = 2
ROWS = 128
LIMIT = 24 * 1024 * 1024


def with_halo(shard, sides, width):
    for axis, dim in sides:
        peers, length = (lax.axis_size(axis), shard.shape[dim])
        up = [(i, (i + 1) % peers) for i in range(peers)]
        down = [(j, i) for i, j in up]
        last = lax.slice_in_dim(shard, length - width, length, axis=dim)
        leading = lax.slice_in_dim(shard, 0, width, axis=dim)
        before = lax.ppermute(last, axis, up)
        after = lax.ppermute(leading, axis, down)
        shard = jnp.concatenate([before, shard, after], axis=dim)
    return shard


def deriv(padded, dim):
    count = padded.shape[dim] - 4

    def cut(offset):
        return lax.slice_in_dim(padded, offset, offset + count, axis=dim)

    return (8.0 * (cut(3) - cut(1)) - (cut(4) - cut(0))) / 12.0


def curl(padded_x, metric):
    inner = padded_x[:, :, 2:-2]
    padded_y = jnp.pad(inner, ((0, 0), (0, 0), (0, 0), (2, 2), (0, 0)))
    padded_z = jnp.concatenate([inner[..., -2:], inner, inner[..., :2]], axis=4)
    along_x = deriv(padded_x, 2) * metric[0]
    along_y = deriv(padded_y, 3) * metric[1]
    along_z = deriv(padded_z, 4) * metric[2]
    omega_x = along_y[:, 2] - along_z[:, 1]
    omega_y = along_z[:, 0] - along_x[:, 2]
    omega_z = along_x[:, 1] - along_y[:, 0]
    return jnp.stack([omega_x, omega_y, omega_z], axis=1).astype(jnp.bfloat16)


def many_groups(velocity, metric, volume, coeffs):
    snap_dev = velocity.shape[0]
    snaps = coeffs.shape[0]
    group = lax.axis_index("snap")
    scale = 1.0 / (
        3.0 * volume.shape[0] * lax.axis_size("space") * volume.shape[1] * volume.shape[2]
    )
    padded = with_halo(velocity, (("space", 2),), 2)
    vorticity = curl(padded.astype(jnp.float32), metric)
    coeff_f = coeffs.astype(jnp.float32)
    moved = lax.all_to_all(vorticity, "snap", split_axis=3, concat_axis=0, tiled=True)
    part_y = moved.shape[3]
    vol_part = lax.dynamic_slice_in_dim(volume, group * part_y, part_y, 1)
    weighted = (moved.astype(jnp.float32) * vol_part).astype(jnp.bfloat16).reshape(snaps, -1)
    flat = moved.reshape(snaps, -1)
    partial_value = lax.dot_general(
        weighted, flat, (((1,), (1,)), ((), ())), preferred_element_type=jnp.float32
    )
    raw = lax.dot_general(
        coeffs, flat, (((0,), (0,)), ((), ())), preferred_element_type=jnp.float32
    )
    whole = lax.psum(partial_value, ("space", "snap")) * scale
    energy = jnp.sum(coeff_f * jnp.dot(whole, coeff_f, precision=lax.Precision.HIGHEST), axis=0)
    rows = lax.dynamic_slice_in_dim(whole, group * snap_dev, snap_dev, 0)
    local_modes = (raw / jnp.sqrt(energy + EPS)[:, None]).astype(jnp.bfloat16).reshape(moved.shape)
    modes = lax.all_to_all(local_modes, "snap", split_axis=0, concat_axis=3, tiled=True)
    return (rows, modes)


def vmem():
    return pl.BlockSpec(memory_space=pltpu.VMEM)


def hbm():
    return pl.BlockSpec(memory_space=pltpu.HBM)


def params():
    return pltpu.CompilerParams(vmem_limit_bytes=LIMIT)


def cost(flops, moved):
    return pl.CostEstimate(flops=flops, bytes_accessed=moved, transcendentals=0)


def z_stencil(size):
    rows = lax.broadcasted_iota(jnp.int32, (size, size), 0)
    cols = lax.broadcasted_iota(jnp.int32, (size, size), 1)
    ahead = rows - cols
    ahead = jnp.where(ahead < 0, ahead + size, ahead)
    out = jnp.where(ahead == 1, 8.0, 0.0) - jnp.where(ahead == size - 1, 8.0, 0.0)
    out = out - jnp.where(ahead == 2, 1.0, 0.0) + jnp.where(ahead == size - 2, 1.0, 0.0)
    return out.astype(jnp.bfloat16)


def spread(src, wide):
    snaps, ny, nz = src.shape
    wide[...] = src.astype(jnp.float32).reshape(snaps * ny, nz)


def row(wide, y, snaps, ny):
    return wide[pl.ds(y, snaps, ny), :]


def y_stencils(load, ny):
    held = {}

    def at(j):
        if j not in held:
            held[j] = load(j)
        return held[j]

    zero = jnp.zeros_like(at(0))
    for y in range(ny):
        near = (at(y + 1) if y + 1 < ny else zero) - (at(y - 1) if y >= 1 else zero)
        far = (at(y + 2) if y + 2 < ny else zero) - (at(y - 2) if y >= 2 else zero)
        held.pop(y - 2, None)
        yield y, 8.0 * near - far


def z_derivative(field, matrix, along):
    rows = field.shape[0] * field.shape[1] * field.shape[2]
    along[...] = jnp.dot(
        field.reshape(rows, field.shape[3]), matrix, preferred_element_type=jnp.float32
    ).reshape(field.shape)


def factor(metric_ref, m, layer, y):
    return metric_ref[m, layer, pl.ds(y, 1), :] * (1.0 / 12.0)


def flip(src, wide, out_ref, i):
    snaps, ny, _ = src.shape
    spread(src, wide)
    for y in range(ny):
        out_ref[i, y] = row(wide, y, snaps, ny).astype(jnp.bfloat16)


def flip_first_kernel(component, vel_ref, out_ref, buf, wide, sems):
    snaps, half, ny, _ = buf.shape
    base = lax.axis_index("snap") * half
    copies = []
    for i in range(half):
        source = vel_ref.at[:, component, base + i]
        copies.append(pltpu.make_async_copy(source, buf.at[:, i], sems.at[i]))
        copies[i].start()
    for i in range(half):
        copies[i].wait()
        flip(buf[:, i], wide, out_ref, i)


def flip_kernel(component, vel_ref, out_ref, wide):
    half = out_ref.shape[0]
    base = lax.axis_index("snap") * half
    for i in range(half):
        flip(vel_ref[:, component, base + i], wide, out_ref, i)


def omega_x_theirs_kernel(half, vel_ref, metric_ref, v_ref, w_ref, ox_ref, wide, along):
    snaps, _, _, ny, nz = vel_ref.shape
    base = (1 - lax.axis_index("snap")) * half
    matrix = z_stencil(nz)
    for i in range(half):
        flip(vel_ref[:, 1, base + i], wide, v_ref, i)
    z_derivative(v_ref[...], matrix, along)
    for i in range(half):
        spread(vel_ref[:, 2, base + i], wide)

        def load(j):
            value = row(wide, j, snaps, ny)
            w_ref[i, j] = value.astype(jnp.bfloat16)
            return value

        for y, across in y_stencils(load, ny):
            value = across * factor(metric_ref, 1, base + i, y)
            value = value - along[i, y] * factor(metric_ref, 2, base + i, y)
            ox_ref[i, y] = value.astype(jnp.bfloat16)


def rest_kernel(
    half, vel_ref, metric_ref, v_ref, w_ref, ox_ref, zu_ref, yu_ref, flat, wide, along
):
    snaps, _, _, ny, nz = vel_ref.shape
    matrix = z_stencil(nz)
    group = lax.axis_index("snap")
    mine = group * half
    z_derivative(v_ref[...], matrix, along)
    for i in range(half):
        for y, across in y_stencils(lambda j: w_ref[i, j].astype(jnp.float32), ny):
            value = across * factor(metric_ref, 1, mine + i, y)
            value = value - along[i, y] * factor(metric_ref, 2, mine + i, y)
            ox_ref[i, y] = value.astype(jnp.bfloat16)
    for slot in range(2):
        base = mine if slot else (1 - group) * half
        for i in range(half):
            spread(vel_ref[:, 0, base + i], wide)

            def load(j):
                value = row(wide, j, snaps, ny)
                flat[i, j] = value.astype(jnp.bfloat16)
                return value

            for y, across in y_stencils(load, ny):
                yu_ref[slot, i, y] = across * factor(metric_ref, 1, base + i, y)
        z_derivative(flat[...], matrix, along)
        for i in range(half):
            for y in range(ny):
                zu_ref[slot, i, y] = along[i, y] * factor(metric_ref, 2, base + i, y)


def finish_curl(sign, slot, near_ref, far_ref, halo_ref, known_ref, metric_ref, out_ref):
    half, ny, _, _ = near_ref.shape
    group = lax.axis_index("snap")
    part = group if slot else 1 - group

    def run(low_ref, high_ref):
        def plane(i, y):
            if i < 0:
                ref, k = low_ref, half + i
            elif i < half:
                ref, k = near_ref, i
            else:
                ref, k = high_ref, i - half
            return ref[k, y].astype(jnp.float32)

        for y in range(ny):
            at = [plane(i, y) for i in range(-WIDTH, half + WIDTH)]
            for i in range(half):
                along = 8.0 * (at[i + 3] - at[i + 1]) - (at[i + 4] - at[i])
                along = along * factor(metric_ref, 0, part * half + i, y)
                known = known_ref[slot, i, y]
                value = along - known if sign > 0 else known - along
                out_ref[i, y] = value.astype(jnp.bfloat16)

    @pl.when(part == 0)
    def _():
        run(halo_ref, far_ref)

    @pl.when(part == 1)
    def _():
        run(far_ref, halo_ref)


def omega_y_kernel(slot, *refs):
    finish_curl(-1, slot, *refs)


def omega_z_and_x_kernel(slot, near, far, halo, known, metric_ref, x_ref, out_ref):
    finish_curl(1, slot, near, far, halo, known, metric_ref, out_ref.at[0])
    out_ref[1] = x_ref[...]


def omega_yz_kernel(slot, w_refs, v_refs, metric_ref, out_ref):
    finish_curl(-1, slot, *w_refs, metric_ref, out_ref.at[0])
    finish_curl(1, slot, *v_refs, metric_ref, out_ref.at[1])


def gram_of(own, got, volume_ref, base):
    half, ny, _, _ = own.shape
    total = None
    for i in range(half):
        plain, heavy = [], []
        for y in range(ny):
            pair = jnp.concatenate([own[i, y], got[i, y]], axis=0)
            weight = volume_ref[base + i, pl.ds(y, 1), :]
            plain.append(pair)
            heavy.append((pair.astype(jnp.float32) * weight).astype(jnp.bfloat16))
        part = lax.dot_general(
            jnp.concatenate(heavy, axis=1),
            jnp.concatenate(plain, axis=1),
            (((1,), (1,)), ((), ())),
            preferred_element_type=jnp.float32,
        )
        total = part if total is None else total + part
    return total


def gram_kernel(own_slot, got_slot, own, got, volume_ref, *refs):
    own = own if own_slot is None else own.at[own_slot]
    got = got if got_slot is None else got.at[got_slot]
    total = gram_of(own, got, volume_ref, lax.axis_index("snap") * own.shape[0])
    for earlier in refs[:-1]:
        total = total + earlier[...]
    refs[-1][...] = total


def add_kernel(*refs):
    total = refs[0][...]
    for ref in refs[1:-1]:
        total = total + ref[...]
    refs[-1][...] = total


def coeff_kernel(coeff_ref, mine_ref, block_ref):
    snaps, count = mine_ref.shape
    rows = block_ref.shape[0]
    base = lax.axis_index("snap") * snaps

    def chosen(shape, test):
        left = lax.broadcasted_iota(jnp.int32, shape, 0)
        right = lax.broadcasted_iota(jnp.int32, shape, 1)
        return jnp.where(test(left, right), 1.0, 0.0).astype(jnp.bfloat16)

    def take(a, b, dims):
        out = lax.dot_general(a, b, (dims, ((), ())), preferred_element_type=jnp.float32)
        return out.astype(jnp.bfloat16)

    mine = chosen((snaps, count), lambda k, m: m == k + base)
    mine = take(mine, coeff_ref[...], ((1,), (1,)))
    order = chosen((count, count), lambda j, m: j == lax.rem(m + base, count))
    mine = take(mine, order, ((1,), (0,)))
    mine_ref[...] = mine.astype(jnp.float32)
    down = chosen((rows, snaps), lambda r, k: lax.rem(r, snaps) == k)
    for part in range(count // snaps):
        across = chosen((count, rows), lambda j, c: j == lax.rem(c, snaps) + part * snaps)
        wide = take(take(down, mine, ((1,), (0,))), across, ((1,), (0,)))
        same = chosen((rows, rows), lambda r, c: lax.div(r, snaps) == lax.div(c, snaps))
        block_ref[:, part * rows : (part + 1) * rows] = wide * same


def raw_blocks(own, got, block_ref, put):
    ny, snaps, nz = own.shape
    block = block_ref.shape[0] // snaps
    lanes = 2 if ny % (2 * block) == 0 else 1
    for start in range(0, ny, block * lanes):
        columns = []
        for n in range(lanes):
            at = start + n * block
            parts = [ref[at : at + block].reshape(block * snaps, nz) for ref in (own, got)]
            columns.append(jnp.concatenate(parts, axis=0))
        both = columns[0] if lanes == 1 else jnp.concatenate(columns, axis=1)
        raw = jnp.dot(block_ref[...], both, preferred_element_type=jnp.float32)
        for n in range(lanes):
            part = raw[:, n * nz : (n + 1) * nz].reshape(block, snaps, nz)
            for k in range(block):
                put(start + n * block + k, part[k])


def raw_kernel(picks, block_ref, *refs):
    outs = refs[-len(picks) :]

    def field(pick):
        ref, slot = pick
        return refs[ref] if slot is None else refs[ref].at[slot]

    for (own_pick, got_pick), out_ref in zip(picks, outs):
        own, got = field(own_pick), field(got_pick)
        half, ny, snaps, _ = own.shape
        for i in range(half):

            def put(y, value):
                out_ref[pl.ds(i * ny + y, snaps, half * ny), :] = value

            raw_blocks(own.at[i], got.at[i], block_ref, put)


def finish_kernel(half, scale, part_ref, other_ref, coeff_ref, *refs):
    raws, (out_ref, rows_ref, stage, rows_buf, wide, sems) = refs[:6], refs[6:]
    snaps, _, _, ny, nz = stage.shape
    group = lax.axis_index("snap")
    other = other_ref[...]
    other = jnp.concatenate([other[snaps:], other[:snaps]], axis=0)
    other = jnp.concatenate([other[:, snaps:], other[:, :snaps]], axis=1)
    total = (part_ref[...] + other) * scale
    coeff = coeff_ref[...]
    inner = jnp.dot(
        coeff, total, precision=lax.Precision.HIGHEST, preferred_element_type=jnp.float32
    )
    energy = jnp.sum(inner * coeff, axis=1, keepdims=True)
    wide[...] = jnp.broadcast_to(1.0 / jnp.sqrt(energy + EPS), (snaps, nz))
    mine = total[:snaps]
    turned = jnp.concatenate([mine[:, snaps:], mine[:, :snaps]], axis=1)
    rows_buf[...] = jnp.where(group == 0, mine, turned)
    copies = [pltpu.make_async_copy(rows_buf, rows_ref, sems.at[0])]
    copies[0].start()
    block = half * ny
    step = snaps // 4
    for n in range(4):
        for k in range(n * step, (n + 1) * step):
            factor = wide[k : k + 1, :]
            for c in range(3):
                for slot, base in ((0, 1 - group), (1, group)):
                    value = raws[3 * slot + c][k * block : (k + 1) * block, :] * factor
                    value = value.astype(jnp.bfloat16).reshape(half, ny, nz)
                    stage[k, c, pl.ds(base * half, half)] = value
        part = pl.ds(n * step, step)
        copies.append(pltpu.make_async_copy(stage.at[part], out_ref.at[part], sems.at[1 + n]))
        copies[-1].start()
    for copy in copies:
        copy.wait()


def two_groups(velocity, metric, volume, coeffs):
    snaps, _, layers, ny, nz = velocity.shape
    half = layers // 2
    peers = lax.axis_size("space")
    bf16, f32 = jnp.bfloat16, jnp.float32

    def halo(first):
        pairs = []
        for s in range(peers):
            for g in range(2):
                down = (g == 0) == first
                pairs.append((s * 2 + g, ((s + (-1 if down else 1)) % peers) * 2 + g))
        return pairs

    def swap(value):
        return lax.ppermute(value, "snap", [(0, 1), (1, 0)])

    def shift(value, first):
        return lax.ppermute(value, ("space", "snap"), halo(first))

    field = jax.ShapeDtypeStruct((half, ny, snaps, nz), bf16)
    two_fields = jax.ShapeDtypeStruct((2, half, ny, snaps, nz), bf16)
    partial_sum = jax.ShapeDtypeStruct((2, half, ny, snaps, nz), f32)
    square = jax.ShapeDtypeStruct((2 * snaps, 2 * snaps), f32)
    raw = jax.ShapeDtypeStruct((snaps * half * ny, nz), f32)
    cells = half * ny * snaps * nz
    wide = pltpu.VMEM((snaps * ny, nz), f32)
    along = pltpu.VMEM((half, ny, snaps, nz), f32)
    dma = pltpu.SemaphoreType.DMA

    def call(kernel, name, out_shape, args, scratch=(), in_specs=None, out_specs=None, work=5):
        return pl.pallas_call(
            kernel,
            out_shape=out_shape,
            in_specs=in_specs or [vmem()] * len(args),
            out_specs=out_specs or jax.tree.map(lambda _: vmem(), out_shape),
            scratch_shapes=list(scratch),
            compiler_params=params(),
            cost_estimate=cost(2 * work * cells, work * cells),
            name=name,
        )(*args)

    w_mine = call(
        functools.partial(flip_first_kernel, 2),
        "flip_w",
        field,
        [pltpu.with_memory_space_constraint(velocity, pltpu.HBM)],
        [pltpu.VMEM((snaps, half, ny, nz), bf16), wide, dma((half,))],
        [hbm()],
    )
    edge_w = shift(w_mine, True)
    v_mine = call(functools.partial(flip_kernel, 1), "flip_v", field, [velocity], [wide])
    edge_v = shift(v_mine, True)
    v_theirs, w_theirs, ox_theirs = call(
        functools.partial(omega_x_theirs_kernel, half),
        "omega_x_theirs",
        (field, field, field),
        [velocity, metric],
        [wide, along],
    )
    gx_mine = swap(ox_theirs)
    ox_mine, zu, yu = call(
        functools.partial(rest_kernel, half),
        "omega_x_mine",
        (field, partial_sum, partial_sum),
        [velocity, metric, v_mine, w_mine],
        [pltpu.VMEM((half, ny, snaps, nz), bf16), wide, along],
    )

    oy_theirs = call(
        functools.partial(omega_y_kernel, 0),
        "omega_y_theirs",
        field,
        [w_theirs, w_mine, edge_w, zu, metric],
    )
    gy_mine = swap(oy_theirs)
    late_w, late_v, _ = lax.optimization_barrier((w_theirs, v_theirs, oy_theirs))
    edge_w_mine = shift(late_w, False)
    edge_v_mine = shift(late_v, False)
    edge_v, gx_mine = lax.optimization_barrier((edge_v, gx_mine))
    oz_ox = call(
        functools.partial(omega_z_and_x_kernel, 0),
        "omega_z_theirs",
        two_fields,
        [v_theirs, v_mine, edge_v, yu, metric, ox_mine],
    )
    gz_gx = swap(oz_ox)

    def gram_part(name, own_slot, got_slot, own, got, *earlier):
        kernel = functools.partial(gram_kernel, own_slot, got_slot)
        return call(kernel, name, square, [own, got, volume, *earlier])

    coeff_rows, blocks = call(
        coeff_kernel,
        "coeff_blocks",
        (
            jax.ShapeDtypeStruct((snaps, 2 * snaps), f32),
            jax.ShapeDtypeStruct((ROWS // snaps * snaps, ROWS // snaps * 2 * snaps), bf16),
        ),
        [coeffs],
    )
    gram = gram_part("gram_x", None, None, ox_mine, gx_mine)
    edge_w_mine, blocks, gram, gy_mine, _ = lax.optimization_barrier(
        (edge_w_mine, blocks, gram, gy_mine, oz_ox)
    )
    args = ([w_mine, w_theirs, edge_w_mine, zu], [v_mine, v_theirs, edge_v_mine, yu])
    oyz_mine = pl.pallas_call(
        functools.partial(omega_yz_kernel, 1),
        out_shape=two_fields,
        in_specs=([vmem()] * 4, [vmem()] * 4, vmem()),
        out_specs=vmem(),
        compiler_params=params(),
        cost_estimate=cost(10 * cells, 5 * cells),
        name="omega_yz_mine",
    )(*args, metric)
    gyz_theirs = swap(oyz_mine)
    gram = gram_part("gram_y", 0, None, oyz_mine, gy_mine, gram)
    gram = gram_part("gram_z", 1, 0, oyz_mine, gz_gx, gram)

    def sum_over_space(radix, value):
        step = 1
        while step < peers:
            count = min(radix, peers // step)
            got = [
                lax.ppermute(value, "space", [(i, i ^ (k * step)) for i in range(peers)])
                for k in range(1, count)
            ]
            value = call(add_kernel, "add", square, [value] + got, work=1)
            step *= count
        return value

    gram = lax.cond(
        lax.axis_index("snap") < 2,
        functools.partial(sum_over_space, 4),
        functools.partial(sum_over_space, 2),
        gram,
    )
    other = swap(gram)

    def raw_modes(name, fields, *picks):
        kernel = functools.partial(raw_kernel, picks)
        return call(kernel, name, (raw,) * len(picks), [blocks, *fields])

    raws_mine = raw_modes(
        "raw_mine",
        [ox_mine, oyz_mine, gx_mine, gy_mine, gz_gx],
        ((0, None), (2, None)),
        ((1, 0), (3, None)),
        ((1, 1), (4, 0)),
    )
    raws_x = raw_modes("raw_x", [ox_theirs, gz_gx], ((0, None), (1, 1)))
    raws_yz = raw_modes(
        "raw_yz", [oy_theirs, oz_ox, gyz_theirs], ((0, None), (2, 0)), ((1, 0), (2, 1))
    )
    modes, rows = call(
        functools.partial(finish_kernel, half, 1.0 / (3.0 * layers * peers * ny * nz)),
        "finish",
        (
            jax.ShapeDtypeStruct(velocity.shape, bf16),
            jax.ShapeDtypeStruct((snaps, 2 * snaps), f32),
        ),
        [gram, other, coeff_rows, *raws_x, *raws_yz, *raws_mine],
        [
            pltpu.VMEM(velocity.shape, bf16),
            pltpu.VMEM((snaps, 2 * snaps), f32),
            pltpu.VMEM((snaps, nz), f32),
            dma((5,)),
        ],
        None,
        (hbm(), hbm()),
    )
    return (rows, modes)


def per_device(velocity, metric, volume, coeffs):
    peers = lax.axis_size("space")
    paired = lax.axis_size("snap") == 2 and velocity.shape[2] == 2 * WIDTH
    if paired and velocity.shape[0] % 16 == 0 and peers & (peers - 1) == 0:
        return two_groups(velocity, metric, volume, coeffs)
    return many_groups(velocity, metric, volume, coeffs)


def solution(mesh):
    placed = (
        P("snap", None, "space", None, None),
        P(None, "space", None, None),
        P("space", None, None),
        P(),
    )
    return jax.shard_map(
        per_device,
        mesh=mesh,
        in_specs=placed,
        out_specs=(P("snap", None), P("snap", None, "space", None, None)),
        check_vma=False,
    )
```

```python
import functools

import jax
import jax.numpy as jnp
from jax import lax
from jax.experimental import pallas as pl
from jax.experimental.pallas import tpu as pltpu
from jax.sharding import PartitionSpec as P

EPS = 1e-06
WIDTH = 2
ROWS = 128
LIMIT = 24 * 1024 * 1024


def with_halo(shard, sides, width):
    for axis, dim in sides:
        peers, length = (lax.axis_size(axis), shard.shape[dim])
        up = [(i, (i + 1) % peers) for i in range(peers)]
        down = [(j, i) for i, j in up]
        last = lax.slice_in_dim(shard, length - width, length, axis=dim)
        leading = lax.slice_in_dim(shard, 0, width, axis=dim)
        before = lax.ppermute(last, axis, up)
        after = lax.ppermute(leading, axis, down)
        shard = jnp.concatenate([before, shard, after], axis=dim)
    return shard


def deriv(padded, dim):
    count = padded.shape[dim] - 4

    def cut(offset):
        return lax.slice_in_dim(padded, offset, offset + count, axis=dim)

    return (8.0 * (cut(3) - cut(1)) - (cut(4) - cut(0))) / 12.0


def curl(padded_x, metric):
    inner = padded_x[:, :, 2:-2]
    padded_y = jnp.pad(inner, ((0, 0), (0, 0), (0, 0), (2, 2), (0, 0)))
    padded_z = jnp.concatenate([inner[..., -2:], inner, inner[..., :2]], axis=4)
    along_x = deriv(padded_x, 2) * metric[0]
    along_y = deriv(padded_y, 3) * metric[1]
    along_z = deriv(padded_z, 4) * metric[2]
    omega_x = along_y[:, 2] - along_z[:, 1]
    omega_y = along_z[:, 0] - along_x[:, 2]
    omega_z = along_x[:, 1] - along_y[:, 0]
    return jnp.stack([omega_x, omega_y, omega_z], axis=1).astype(jnp.bfloat16)


def many_groups(velocity, metric, volume, coeffs):
    snap_dev = velocity.shape[0]
    snaps = coeffs.shape[0]
    group = lax.axis_index("snap")
    scale = 1.0 / (
        3.0 * volume.shape[0] * lax.axis_size("space") * volume.shape[1] * volume.shape[2]
    )
    padded = with_halo(velocity, (("space", 2),), 2)
    vorticity = curl(padded.astype(jnp.float32), metric)
    coeff_f = coeffs.astype(jnp.float32)
    moved = lax.all_to_all(vorticity, "snap", split_axis=3, concat_axis=0, tiled=True)
    part_y = moved.shape[3]
    vol_part = lax.dynamic_slice_in_dim(volume, group * part_y, part_y, 1)
    weighted = (moved.astype(jnp.float32) * vol_part).astype(jnp.bfloat16).reshape(snaps, -1)
    flat = moved.reshape(snaps, -1)
    partial_value = lax.dot_general(
        weighted, flat, (((1,), (1,)), ((), ())), preferred_element_type=jnp.float32
    )
    raw = lax.dot_general(
        coeffs, flat, (((0,), (0,)), ((), ())), preferred_element_type=jnp.float32
    )
    whole = lax.psum(partial_value, ("space", "snap")) * scale
    energy = jnp.sum(coeff_f * jnp.dot(whole, coeff_f, precision=lax.Precision.HIGHEST), axis=0)
    rows = lax.dynamic_slice_in_dim(whole, group * snap_dev, snap_dev, 0)
    local_modes = (raw / jnp.sqrt(energy + EPS)[:, None]).astype(jnp.bfloat16).reshape(moved.shape)
    modes = lax.all_to_all(local_modes, "snap", split_axis=0, concat_axis=3, tiled=True)
    return (rows, modes)


def vmem():
    return pl.BlockSpec(memory_space=pltpu.VMEM)


def hbm():
    return pl.BlockSpec(memory_space=pltpu.HBM)


def params():
    return pltpu.CompilerParams(vmem_limit_bytes=LIMIT)


def cost(flops, moved):
    return pl.CostEstimate(flops=flops, bytes_accessed=moved, transcendentals=0)


def z_stencil(size):
    rows = lax.broadcasted_iota(jnp.int32, (size, size), 0)
    cols = lax.broadcasted_iota(jnp.int32, (size, size), 1)
    ahead = rows - cols
    ahead = jnp.where(ahead < 0, ahead + size, ahead)
    out = jnp.where(ahead == 1, 8.0, 0.0) - jnp.where(ahead == size - 1, 8.0, 0.0)
    out = out - jnp.where(ahead == 2, 1.0, 0.0) + jnp.where(ahead == size - 2, 1.0, 0.0)
    return out.astype(jnp.bfloat16)


def spread(src, wide):
    snaps, ny, nz = src.shape
    wide[...] = src.astype(jnp.float32).reshape(snaps * ny, nz)


def row(wide, y, snaps, ny):
    return wide[pl.ds(y, snaps, ny), :]


def y_stencils(load, ny):
    held = {}

    def at(j):
        if j not in held:
            held[j] = load(j)
        return held[j]

    zero = jnp.zeros_like(at(0))
    for y in range(ny):
        near = (at(y + 1) if y + 1 < ny else zero) - (at(y - 1) if y >= 1 else zero)
        far = (at(y + 2) if y + 2 < ny else zero) - (at(y - 2) if y >= 2 else zero)
        held.pop(y - 2, None)
        yield y, 8.0 * near - far


def z_derivative(field, matrix, along):
    rows = field.shape[0] * field.shape[1] * field.shape[2]
    along[...] = jnp.dot(
        field.reshape(rows, field.shape[3]), matrix, preferred_element_type=jnp.float32
    ).reshape(field.shape)


def factor(metric_ref, m, layer, y):
    return metric_ref[m, layer, pl.ds(y, 1), :] * (1.0 / 12.0)


def flip(src, wide, out_ref, i):
    snaps, ny, _ = src.shape
    spread(src, wide)
    for y in range(ny):
        out_ref[i, y] = row(wide, y, snaps, ny).astype(jnp.bfloat16)


def omega_x_kernel(vel_ref, metric_ref, theirs_ref, mine_ref, ox_ref, buf, factors, wide, along, sems):
    snaps, _, layers, ny, nz = buf.shape
    half = layers // 2
    group = lax.axis_index("snap")
    bases = ((1 - group) * half, group * half)
    copies = {}
    for slot in range(2):
        rows = pl.ds(bases[slot], half)
        inner = pl.ds(slot * half, half)
        for c in range(2):
            source, target = vel_ref.at[:, 1 + c, rows], buf.at[:, c, inner]
            copies[slot, c] = pltpu.make_async_copy(source, target, sems.at[slot, c])
            copies[slot, c].start()
        source, target = metric_ref.at[1:3, rows], factors.at[:, inner]
        copies[slot, 2] = pltpu.make_async_copy(source, target, sems.at[slot, 2])
        copies[slot, 2].start()
    matrix = z_stencil(nz)
    for slot, vw_ref in enumerate((theirs_ref, mine_ref)):
        copies[slot, 0].wait()
        for i in range(half):
            flip(buf[:, 0, slot * half + i], wide, vw_ref.at[0], i)
        z_derivative(vw_ref[0], matrix, along)
        copies[slot, 1].wait()
        copies[slot, 2].wait()
        for i in range(half):
            spread(buf[:, 1, slot * half + i], wide)

            def load(j):
                value = row(wide, j, snaps, ny)
                vw_ref[1, i, j] = value.astype(jnp.bfloat16)
                return value

            for y, across in y_stencils(load, ny):
                value = across * factor(factors, 0, slot * half + i, y)
                value = value - along[i, y] * factor(factors, 1, slot * half + i, y)
                ox_ref[slot, i, y] = value.astype(jnp.bfloat16)


def u_kernel(half, vel_ref, metric_ref, zu_ref, yu_ref, flat, wide, along):
    snaps, _, _, ny, nz = vel_ref.shape
    matrix = z_stencil(nz)
    group = lax.axis_index("snap")
    for slot in range(2):
        base = (group if slot else 1 - group) * half
        for i in range(half):
            spread(vel_ref[:, 0, base + i], wide)

            def load(j):
                value = row(wide, j, snaps, ny)
                flat[i, j] = value.astype(jnp.bfloat16)
                return value

            for y, across in y_stencils(load, ny):
                yu_ref[slot, i, y] = across * factor(metric_ref, 1, base + i, y)
        z_derivative(flat[...], matrix, along)
        for i in range(half):
            for y in range(ny):
                zu_ref[slot, i, y] = along[i, y] * factor(metric_ref, 2, base + i, y)


def finish_curl(sign, slot, near_ref, far_ref, halo_ref, known_ref, metric_ref, out_ref):
    half, ny, _, _ = near_ref.shape
    group = lax.axis_index("snap")
    part = group if slot else 1 - group

    def run(low_ref, high_ref):
        def plane(i, y):
            if i < 0:
                ref, k = low_ref, half + i
            elif i < half:
                ref, k = near_ref, i
            else:
                ref, k = high_ref, i - half
            return ref[k, y].astype(jnp.float32)

        for y in range(ny):
            at = [plane(i, y) for i in range(-WIDTH, half + WIDTH)]
            for i in range(half):
                along = 8.0 * (at[i + 3] - at[i + 1]) - (at[i + 4] - at[i])
                along = along * factor(metric_ref, 0, part * half + i, y)
                known = known_ref[slot, i, y]
                value = along - known if sign > 0 else known - along
                out_ref[i, y] = value.astype(jnp.bfloat16)

    @pl.when(part == 0)
    def _():
        run(halo_ref, far_ref)

    @pl.when(part == 1)
    def _():
        run(far_ref, halo_ref)


def omega_yz_kernel(slot, near, far, edge, zu_ref, yu_ref, metric_ref, out_ref):
    known = (yu_ref, zu_ref)
    for c, sign in ((1, -1), (0, 1)):
        fields = near.at[c], far.at[c], edge.at[c], known[c]
        finish_curl(sign, slot, *fields, metric_ref, out_ref.at[1 - c])


def gram_of(own, got, volume_ref, base):
    half, ny, _, _ = own.shape
    total = None
    for i in range(half):
        plain, heavy = [], []
        for y in range(ny):
            pair = jnp.concatenate([own[i, y], got[i, y]], axis=0)
            weight = volume_ref[base + i, pl.ds(y, 1), :]
            plain.append(pair)
            heavy.append((pair.astype(jnp.float32) * weight).astype(jnp.bfloat16))
        part = lax.dot_general(
            jnp.concatenate(heavy, axis=1),
            jnp.concatenate(plain, axis=1),
            (((1,), (1,)), ((), ())),
            preferred_element_type=jnp.float32,
        )
        total = part if total is None else total + part
    return total


def gram_kernel(own_refs, got_refs, own, got, volume_ref, *refs):
    base = lax.axis_index("snap") * own.shape[1]
    total = sum(gram_of(own.at[n], got.at[m], volume_ref, base) for n, m in zip(own_refs, got_refs))
    for earlier in refs[:-1]:
        total = total + earlier[...]
    refs[-1][...] = total


def add_kernel(*refs):
    total = refs[0][...]
    for ref in refs[1:-1]:
        total = total + ref[...]
    refs[-1][...] = total


def coeff_kernel(coeff_ref, mine_ref, block_ref):
    snaps, count = mine_ref.shape
    rows = block_ref.shape[0]
    base = lax.axis_index("snap") * snaps

    def chosen(shape, test):
        left = lax.broadcasted_iota(jnp.int32, shape, 0)
        right = lax.broadcasted_iota(jnp.int32, shape, 1)
        return jnp.where(test(left, right), 1.0, 0.0).astype(jnp.bfloat16)

    def take(a, b, dims):
        out = lax.dot_general(a, b, (dims, ((), ())), preferred_element_type=jnp.float32)
        return out.astype(jnp.bfloat16)

    mine = chosen((snaps, count), lambda k, m: m == k + base)
    mine = take(mine, coeff_ref[...], ((1,), (1,)))
    order = chosen((count, count), lambda j, m: j == lax.rem(m + base, count))
    mine = take(mine, order, ((1,), (0,)))
    mine_ref[...] = mine.astype(jnp.float32)
    down = chosen((rows, snaps), lambda r, k: lax.rem(r, snaps) == k)
    for part in range(count // snaps):
        across = chosen((count, rows), lambda j, c: j == lax.rem(c, snaps) + part * snaps)
        wide = take(take(down, mine, ((1,), (0,))), across, ((1,), (0,)))
        same = chosen((rows, rows), lambda r, c: lax.div(r, snaps) == lax.div(c, snaps))
        block_ref[:, part * rows : (part + 1) * rows] = wide * same


def raw_blocks(own, got, block_ref, put):
    ny, snaps, nz = own.shape
    block = block_ref.shape[0] // snaps
    lanes = 2 if ny % (2 * block) == 0 else 1
    for start in range(0, ny, block * lanes):
        columns = []
        for n in range(lanes):
            at = start + n * block
            parts = [ref[at : at + block].reshape(block * snaps, nz) for ref in (own, got)]
            columns.append(jnp.concatenate(parts, axis=0))
        both = columns[0] if lanes == 1 else jnp.concatenate(columns, axis=1)
        raw = jnp.dot(block_ref[...], both, preferred_element_type=jnp.float32)
        for n in range(lanes):
            part = raw[:, n * nz : (n + 1) * nz].reshape(block, snaps, nz)
            for k in range(block):
                put(start + n * block + k, part[k])


def raw_kernel(picks, block_ref, *refs):
    outs = refs[-len(picks) :]

    def field(pick):
        ref, slot = pick
        return refs[ref] if slot is None else refs[ref].at[slot]

    for (own_pick, got_pick), out_ref in zip(picks, outs):
        own, got = field(own_pick), field(got_pick)
        half, ny, snaps, _ = own.shape
        for i in range(half):

            def put(y, value):
                out_ref[pl.ds(i * ny + y, snaps, half * ny), :] = value

            raw_blocks(own.at[i], got.at[i], block_ref, put)


def finish_kernel(half, scale, part_ref, other_ref, coeff_ref, *refs):
    raws, (out_ref, rows_ref, stage, rows_buf, wide, sems) = refs[:6], refs[6:]
    snaps, _, _, ny, nz = stage.shape
    group = lax.axis_index("snap")
    other = other_ref[...]
    other = jnp.concatenate([other[snaps:], other[:snaps]], axis=0)
    other = jnp.concatenate([other[:, snaps:], other[:, :snaps]], axis=1)
    total = (part_ref[...] + other) * scale
    coeff = coeff_ref[...]
    inner = jnp.dot(
        coeff, total, precision=lax.Precision.HIGHEST, preferred_element_type=jnp.float32
    )
    energy = jnp.sum(inner * coeff, axis=1, keepdims=True)
    wide[...] = jnp.broadcast_to(1.0 / jnp.sqrt(energy + EPS), (snaps, nz))
    mine = total[:snaps]
    turned = jnp.concatenate([mine[:, snaps:], mine[:, :snaps]], axis=1)
    rows_buf[...] = jnp.where(group == 0, mine, turned)
    copies = [pltpu.make_async_copy(rows_buf, rows_ref, sems.at[0])]
    copies[0].start()
    block = half * ny
    step = snaps // 4
    for n in range(4):
        for k in range(n * step, (n + 1) * step):
            factor = wide[k : k + 1, :]
            for c in range(3):
                for slot, base in ((0, 1 - group), (1, group)):
                    value = raws[3 * slot + c][k * block : (k + 1) * block, :] * factor
                    value = value.astype(jnp.bfloat16).reshape(half, ny, nz)
                    stage[k, c, pl.ds(base * half, half)] = value
        part = pl.ds(n * step, step)
        copies.append(pltpu.make_async_copy(stage.at[part], out_ref.at[part], sems.at[1 + n]))
        copies[-1].start()
    for copy in copies:
        copy.wait()


def two_groups(velocity, metric, volume, coeffs):
    snaps, _, layers, ny, nz = velocity.shape
    half = layers // 2
    peers = lax.axis_size("space")
    bf16, f32 = jnp.bfloat16, jnp.float32

    def halo(first):
        pairs = []
        for s in range(peers):
            for g in range(2):
                down = (g == 0) == first
                pairs.append((s * 2 + g, ((s + (-1 if down else 1)) % peers) * 2 + g))
        return pairs

    def swap(value):
        return lax.ppermute(value, "snap", [(0, 1), (1, 0)])

    def shift(value, first):
        return lax.ppermute(value, ("space", "snap"), halo(first))

    pair = jax.ShapeDtypeStruct((2, half, ny, snaps, nz), bf16)
    partial_sum = jax.ShapeDtypeStruct((2, half, ny, snaps, nz), f32)
    square = jax.ShapeDtypeStruct((2 * snaps, 2 * snaps), f32)
    raw = jax.ShapeDtypeStruct((snaps * half * ny, nz), f32)
    cells = half * ny * snaps * nz
    wide = pltpu.VMEM((snaps * ny, nz), f32)
    along = pltpu.VMEM((half, ny, snaps, nz), f32)
    dma = pltpu.SemaphoreType.DMA

    def call(kernel, name, out_shape, args, scratch=(), in_specs=None, out_specs=None, work=5):
        return pl.pallas_call(
            kernel,
            out_shape=out_shape,
            in_specs=in_specs or [vmem()] * len(args),
            out_specs=out_specs or jax.tree.map(lambda _: vmem(), out_shape),
            scratch_shapes=list(scratch),
            compiler_params=params(),
            cost_estimate=cost(2 * work * cells, work * cells),
            name=name,
        )(*args)

    theirs, mine, ox = call(
        omega_x_kernel,
        "omega_x",
        (pair, pair, pair),
        [pltpu.with_memory_space_constraint(a, pltpu.HBM) for a in (velocity, metric)],
        [
            pltpu.VMEM((snaps, 2, layers, ny, nz), bf16),
            pltpu.VMEM((2, layers, ny, nz), f32),
            wide,
            along,
            dma((2, 3)),
        ],
        [hbm()] * 2,
    )
    got_x = swap(ox)
    edge_theirs = shift(mine, True)
    zu, yu = call(
        functools.partial(u_kernel, half),
        "u_terms",
        (partial_sum, partial_sum),
        [velocity, metric],
        [pltpu.VMEM((half, ny, snaps, nz), bf16), wide, along],
    )

    def omega_yz(slot, near, far, edge):
        name = "omega_yz_mine" if slot else "omega_yz_theirs"
        args = [near, far, edge, zu, yu, metric]
        return call(functools.partial(omega_yz_kernel, slot), name, pair, args)

    yz_theirs = omega_yz(0, theirs, mine, edge_theirs)
    got_yz = swap(yz_theirs)
    late, _ = lax.optimization_barrier((theirs, yz_theirs))
    edge_mine = shift(late, False)

    coeff_rows, blocks = call(
        coeff_kernel,
        "coeff_blocks",
        (
            jax.ShapeDtypeStruct((snaps, 2 * snaps), f32),
            jax.ShapeDtypeStruct((ROWS // snaps * snaps, ROWS // snaps * 2 * snaps), bf16),
        ),
        [coeffs],
    )
    gram = call(functools.partial(gram_kernel, (1,), (0,)), "gram_x", square, [ox, got_x, volume])
    edge_mine, blocks, gram = lax.optimization_barrier((edge_mine, blocks, gram))
    yz_mine = omega_yz(1, mine, theirs, edge_mine)
    got_yz_theirs = swap(yz_mine)
    gram = call(
        functools.partial(gram_kernel, (0, 1), (0, 1)),
        "gram_yz",
        square,
        [yz_mine, got_yz, volume, gram],
    )

    def sum_over_space(radix, value):
        step = 1
        while step < peers:
            count = min(radix, peers // step)
            got = [
                lax.ppermute(value, "space", [(i, i ^ (k * step)) for i in range(peers)])
                for k in range(1, count)
            ]
            value = call(add_kernel, "add", square, [value] + got, work=1)
            step *= count
        return value

    gram = lax.cond(
        lax.axis_index("snap") < 2,
        functools.partial(sum_over_space, 2),
        functools.partial(sum_over_space, 4),
        gram,
    )
    other = swap(gram)

    def raw_modes(name, fields, *picks):
        kernel = functools.partial(raw_kernel, picks)
        return call(kernel, name, (raw,) * len(picks), [blocks, *fields])

    mine_x, theirs_x = raw_modes("raw_x", [ox, got_x], ((0, 1), (1, 0)), ((0, 0), (1, 1)))
    mine_yz = raw_modes("raw_yz", [yz_mine, got_yz], ((0, 0), (1, 0)), ((0, 1), (1, 1)))
    theirs_yz = raw_modes(
        "raw_yz_theirs", [yz_theirs, got_yz_theirs], ((0, 0), (1, 0)), ((0, 1), (1, 1))
    )
    modes, rows = call(
        functools.partial(finish_kernel, half, 1.0 / (3.0 * layers * peers * ny * nz)),
        "finish",
        (
            jax.ShapeDtypeStruct(velocity.shape, bf16),
            jax.ShapeDtypeStruct((snaps, 2 * snaps), f32),
        ),
        [gram, other, coeff_rows, theirs_x, *theirs_yz, mine_x, *mine_yz],
        [
            pltpu.VMEM(velocity.shape, bf16),
            pltpu.VMEM((snaps, 2 * snaps), f32),
            pltpu.VMEM((snaps, nz), f32),
            dma((5,)),
        ],
        None,
        (hbm(), hbm()),
    )
    return (rows, modes)


def per_device(velocity, metric, volume, coeffs):
    peers = lax.axis_size("space")
    paired = lax.axis_size("snap") == 2 and velocity.shape[2] == 2 * WIDTH
    if paired and velocity.shape[0] % 16 == 0 and peers & (peers - 1) == 0:
        return two_groups(velocity, metric, volume, coeffs)
    return many_groups(velocity, metric, volume, coeffs)


def solution(mesh):
    placed = (
        P("snap", None, "space", None, None),
        P(None, "space", None, None),
        P("space", None, None),
        P(),
    )
    return jax.shard_map(
        per_device,
        mesh=mesh,
        in_specs=placed,
        out_specs=(P("snap", None), P("snap", None, "space", None, None)),
        check_vma=False,
    )
```

```python
import functools

import jax
import jax.numpy as jnp
from jax import lax
from jax.experimental import pallas as pl
from jax.experimental.pallas import tpu as pltpu
from jax.sharding import PartitionSpec as P

EPS = 1e-06
WIDTH = 2
ROWS = 128
LIMIT = 24 * 1024 * 1024


def with_halo(shard, sides, width):
    for axis, dim in sides:
        peers, length = (lax.axis_size(axis), shard.shape[dim])
        up = [(i, (i + 1) % peers) for i in range(peers)]
        down = [(j, i) for i, j in up]
        last = lax.slice_in_dim(shard, length - width, length, axis=dim)
        leading = lax.slice_in_dim(shard, 0, width, axis=dim)
        before = lax.ppermute(last, axis, up)
        after = lax.ppermute(leading, axis, down)
        shard = jnp.concatenate([before, shard, after], axis=dim)
    return shard


def deriv(padded, dim):
    count = padded.shape[dim] - 4

    def cut(offset):
        return lax.slice_in_dim(padded, offset, offset + count, axis=dim)

    return (8.0 * (cut(3) - cut(1)) - (cut(4) - cut(0))) / 12.0


def curl(padded_x, metric):
    inner = padded_x[:, :, 2:-2]
    padded_y = jnp.pad(inner, ((0, 0), (0, 0), (0, 0), (2, 2), (0, 0)))
    padded_z = jnp.concatenate([inner[..., -2:], inner, inner[..., :2]], axis=4)
    along_x = deriv(padded_x, 2) * metric[0]
    along_y = deriv(padded_y, 3) * metric[1]
    along_z = deriv(padded_z, 4) * metric[2]
    omega_x = along_y[:, 2] - along_z[:, 1]
    omega_y = along_z[:, 0] - along_x[:, 2]
    omega_z = along_x[:, 1] - along_y[:, 0]
    return jnp.stack([omega_x, omega_y, omega_z], axis=1).astype(jnp.bfloat16)


def many_groups(velocity, metric, volume, coeffs):
    snap_dev = velocity.shape[0]
    snaps = coeffs.shape[0]
    group = lax.axis_index("snap")
    scale = 1.0 / (
        3.0 * volume.shape[0] * lax.axis_size("space") * volume.shape[1] * volume.shape[2]
    )
    padded = with_halo(velocity, (("space", 2),), 2)
    vorticity = curl(padded.astype(jnp.float32), metric)
    coeff_f = coeffs.astype(jnp.float32)
    moved = lax.all_to_all(vorticity, "snap", split_axis=3, concat_axis=0, tiled=True)
    part_y = moved.shape[3]
    vol_part = lax.dynamic_slice_in_dim(volume, group * part_y, part_y, 1)
    weighted = (moved.astype(jnp.float32) * vol_part).astype(jnp.bfloat16).reshape(snaps, -1)
    flat = moved.reshape(snaps, -1)
    partial_value = lax.dot_general(
        weighted, flat, (((1,), (1,)), ((), ())), preferred_element_type=jnp.float32
    )
    raw = lax.dot_general(
        coeffs, flat, (((0,), (0,)), ((), ())), preferred_element_type=jnp.float32
    )
    whole = lax.psum(partial_value, ("space", "snap")) * scale
    energy = jnp.sum(coeff_f * jnp.dot(whole, coeff_f, precision=lax.Precision.HIGHEST), axis=0)
    rows = lax.dynamic_slice_in_dim(whole, group * snap_dev, snap_dev, 0)
    local_modes = (raw / jnp.sqrt(energy + EPS)[:, None]).astype(jnp.bfloat16).reshape(moved.shape)
    modes = lax.all_to_all(local_modes, "snap", split_axis=0, concat_axis=3, tiled=True)
    return (rows, modes)


def vmem():
    return pl.BlockSpec(memory_space=pltpu.VMEM)


def hbm():
    return pl.BlockSpec(memory_space=pltpu.HBM)


def params():
    return pltpu.CompilerParams(vmem_limit_bytes=LIMIT)


def cost(flops, moved):
    return pl.CostEstimate(flops=flops, bytes_accessed=moved, transcendentals=0)


def z_stencil(size):
    rows = lax.broadcasted_iota(jnp.int32, (size, size), 0)
    cols = lax.broadcasted_iota(jnp.int32, (size, size), 1)
    ahead = rows - cols
    ahead = jnp.where(ahead < 0, ahead + size, ahead)
    out = jnp.where(ahead == 1, 8.0, 0.0) - jnp.where(ahead == size - 1, 8.0, 0.0)
    out = out - jnp.where(ahead == 2, 1.0, 0.0) + jnp.where(ahead == size - 2, 1.0, 0.0)
    return out.astype(jnp.bfloat16)


def spread(src, wide):
    snaps, ny, nz = src.shape
    wide[...] = src.astype(jnp.float32).reshape(snaps * ny, nz)


def row(wide, y, snaps, ny):
    return wide[pl.ds(y, snaps, ny), :]


def y_stencils(load, ny):
    held = {}

    def at(j):
        if j not in held:
            held[j] = load(j)
        return held[j]

    zero = jnp.zeros_like(at(0))
    for y in range(ny):
        near = (at(y + 1) if y + 1 < ny else zero) - (at(y - 1) if y >= 1 else zero)
        far = (at(y + 2) if y + 2 < ny else zero) - (at(y - 2) if y >= 2 else zero)
        held.pop(y - 2, None)
        yield y, 8.0 * near - far


def z_derivative(field, matrix, along):
    rows = field.shape[0] * field.shape[1] * field.shape[2]
    along[...] = jnp.dot(
        field.reshape(rows, field.shape[3]), matrix, preferred_element_type=jnp.float32
    ).reshape(field.shape)


def factor(metric_ref, m, layer, y):
    return metric_ref[m, layer, pl.ds(y, 1), :] * (1.0 / 12.0)


def flip(src, wide, out_ref, i):
    snaps, ny, _ = src.shape
    spread(src, wide)
    for y in range(ny):
        out_ref[i, y] = row(wide, y, snaps, ny).astype(jnp.bfloat16)


def omega_x_kernel(vel_ref, metric_ref, theirs_ref, mine_ref, ox_ref, buf, factors, wide, along, sems):
    snaps, _, layers, ny, nz = buf.shape
    half = layers // 2
    group = lax.axis_index("snap")
    bases = ((1 - group) * half, group * half)
    copies = {}
    for slot in range(2):
        rows = pl.ds(bases[slot], half)
        inner = pl.ds(slot * half, half)
        for c in range(2):
            source, target = vel_ref.at[:, 1 + c, rows], buf.at[:, c, inner]
            copies[slot, c] = pltpu.make_async_copy(source, target, sems.at[slot, c])
            copies[slot, c].start()
        source, target = metric_ref.at[1:3, rows], factors.at[:, inner]
        copies[slot, 2] = pltpu.make_async_copy(source, target, sems.at[slot, 2])
        copies[slot, 2].start()
    matrix = z_stencil(nz)
    for slot, vw_ref in enumerate((theirs_ref, mine_ref)):
        copies[slot, 0].wait()
        for i in range(half):
            flip(buf[:, 0, slot * half + i], wide, vw_ref.at[0], i)
        z_derivative(vw_ref[0], matrix, along)
        copies[slot, 1].wait()
        copies[slot, 2].wait()
        for i in range(half):
            spread(buf[:, 1, slot * half + i], wide)

            def load(j):
                value = row(wide, j, snaps, ny)
                vw_ref[1, i, j] = value.astype(jnp.bfloat16)
                return value

            for y, across in y_stencils(load, ny):
                value = across * factor(factors, 0, slot * half + i, y)
                value = value - along[i, y] * factor(factors, 1, slot * half + i, y)
                ox_ref[slot, i, y] = value.astype(jnp.bfloat16)


def u_kernel(half, vel_ref, metric_ref, zu_ref, yu_ref, flat, wide, along):
    snaps, _, _, ny, nz = vel_ref.shape
    matrix = z_stencil(nz)
    group = lax.axis_index("snap")
    for slot in range(2):
        base = (group if slot else 1 - group) * half
        for i in range(half):
            spread(vel_ref[:, 0, base + i], wide)

            def load(j):
                value = row(wide, j, snaps, ny)
                flat[i, j] = value.astype(jnp.bfloat16)
                return value

            for y, across in y_stencils(load, ny):
                yu_ref[slot, i, y] = across * factor(metric_ref, 1, base + i, y)
        z_derivative(flat[...], matrix, along)
        for i in range(half):
            for y in range(ny):
                zu_ref[slot, i, y] = along[i, y] * factor(metric_ref, 2, base + i, y)


def finish_curl(sign, slot, near_ref, far_ref, halo_ref, known_ref, metric_ref, out_ref):
    half, ny, _, _ = near_ref.shape
    group = lax.axis_index("snap")
    part = group if slot else 1 - group

    def run(low_ref, high_ref):
        def plane(i, y):
            if i < 0:
                ref, k = low_ref, half + i
            elif i < half:
                ref, k = near_ref, i
            else:
                ref, k = high_ref, i - half
            return ref[k, y].astype(jnp.float32)

        for y in range(ny):
            at = [plane(i, y) for i in range(-WIDTH, half + WIDTH)]
            for i in range(half):
                along = 8.0 * (at[i + 3] - at[i + 1]) - (at[i + 4] - at[i])
                along = along * factor(metric_ref, 0, part * half + i, y)
                known = known_ref[slot, i, y]
                value = along - known if sign > 0 else known - along
                out_ref[i, y] = value.astype(jnp.bfloat16)

    @pl.when(part == 0)
    def _():
        run(halo_ref, far_ref)

    @pl.when(part == 1)
    def _():
        run(far_ref, halo_ref)


def omega_yz_kernel(slot, near, far, edge, zu_ref, yu_ref, metric_ref, out_ref):
    known = (yu_ref, zu_ref)
    for c, sign in ((1, -1), (0, 1)):
        fields = near.at[c], far.at[c], edge.at[c], known[c]
        finish_curl(sign, slot, *fields, metric_ref, out_ref.at[1 - c])


def gram_of(own, got, volume_ref, base):
    half, ny, _, _ = own.shape
    total = None
    for i in range(half):
        plain, heavy = [], []
        for y in range(ny):
            pair = jnp.concatenate([own[i, y], got[i, y]], axis=0)
            weight = volume_ref[base + i, pl.ds(y, 1), :]
            plain.append(pair)
            heavy.append((pair.astype(jnp.float32) * weight).astype(jnp.bfloat16))
        part = lax.dot_general(
            jnp.concatenate(heavy, axis=1),
            jnp.concatenate(plain, axis=1),
            (((1,), (1,)), ((), ())),
            preferred_element_type=jnp.float32,
        )
        total = part if total is None else total + part
    return total


def gram_kernel(own_refs, got_refs, own, got, volume_ref, *refs):
    base = lax.axis_index("snap") * own.shape[1]
    total = sum(gram_of(own.at[n], got.at[m], volume_ref, base) for n, m in zip(own_refs, got_refs))
    for earlier in refs[:-1]:
        total = total + earlier[...]
    if len(refs[-1].shape) == 3:
        count, rows, _ = refs[-1].shape
        total = jnp.concatenate(
            [total[n : n + rows] for n in range(0, total.shape[0], rows)], axis=1
        )
        for peer in range(count):
            refs[-1][peer] = total
    else:
        refs[-1][...] = total


def add_kernel(parts_ref, out_ref):
    parts = [parts_ref[n] for n in range(parts_ref.shape[0])]
    while len(parts) > 1:
        parts = [sum(parts[n : n + 2]) for n in range(0, len(parts), 2)]
    rows, side = parts_ref.shape[1], out_ref.shape[0]
    for n in range(side // rows):
        out_ref[n * rows : (n + 1) * rows] = parts[0][:, n * side : (n + 1) * side]


def coeff_kernel(coeff_ref, mine_ref, block_ref):
    snaps, count = mine_ref.shape
    rows = block_ref.shape[0]
    base = lax.axis_index("snap") * snaps

    def chosen(shape, test):
        left = lax.broadcasted_iota(jnp.int32, shape, 0)
        right = lax.broadcasted_iota(jnp.int32, shape, 1)
        return jnp.where(test(left, right), 1.0, 0.0).astype(jnp.bfloat16)

    def take(a, b, dims):
        out = lax.dot_general(a, b, (dims, ((), ())), preferred_element_type=jnp.float32)
        return out.astype(jnp.bfloat16)

    mine = chosen((snaps, count), lambda k, m: m == k + base)
    mine = take(mine, coeff_ref[...], ((1,), (1,)))
    order = chosen((count, count), lambda j, m: j == lax.rem(m + base, count))
    mine = take(mine, order, ((1,), (0,)))
    mine_ref[...] = mine.astype(jnp.float32)
    down = chosen((rows, snaps), lambda r, k: lax.rem(r, snaps) == k)
    for part in range(count // snaps):
        across = chosen((count, rows), lambda j, c: j == lax.rem(c, snaps) + part * snaps)
        wide = take(take(down, mine, ((1,), (0,))), across, ((1,), (0,)))
        same = chosen((rows, rows), lambda r, c: lax.div(r, snaps) == lax.div(c, snaps))
        block_ref[:, part * rows : (part + 1) * rows] = wide * same


def raw_blocks(own, got, block_ref, put):
    ny, snaps, nz = own.shape
    block = block_ref.shape[0] // snaps
    lanes = 2 if ny % (2 * block) == 0 else 1
    for start in range(0, ny, block * lanes):
        columns = []
        for n in range(lanes):
            at = start + n * block
            parts = [ref[at : at + block].reshape(block * snaps, nz) for ref in (own, got)]
            columns.append(jnp.concatenate(parts, axis=0))
        both = columns[0] if lanes == 1 else jnp.concatenate(columns, axis=1)
        raw = jnp.dot(block_ref[...], both, preferred_element_type=jnp.float32)
        for n in range(lanes):
            part = raw[:, n * nz : (n + 1) * nz].reshape(block, snaps, nz)
            for k in range(block):
                put(start + n * block + k, part[k])


def raw_kernel(picks, block_ref, *refs):
    outs = refs[-len(picks) :]

    def field(pick):
        ref, slot = pick
        return refs[ref] if slot is None else refs[ref].at[slot]

    for (own_pick, got_pick), out_ref in zip(picks, outs):
        own, got = field(own_pick), field(got_pick)
        half, ny, snaps, _ = own.shape
        for i in range(half):

            def put(y, value):
                out_ref[pl.ds(i * ny + y, snaps, half * ny), :] = value

            raw_blocks(own.at[i], got.at[i], block_ref, put)


def finish_kernel(half, scale, part_ref, other_ref, coeff_ref, *refs):
    raws, (out_ref, rows_ref, stage, rows_buf, wide, sems) = refs[:6], refs[6:]
    snaps, _, _, ny, nz = stage.shape
    group = lax.axis_index("snap")
    other = other_ref[...]
    other = jnp.concatenate([other[snaps:], other[:snaps]], axis=0)
    other = jnp.concatenate([other[:, snaps:], other[:, :snaps]], axis=1)
    total = (part_ref[...] + other) * scale
    coeff = coeff_ref[...]
    inner = jnp.dot(
        coeff, total, precision=lax.Precision.HIGHEST, preferred_element_type=jnp.float32
    )
    energy = jnp.sum(inner * coeff, axis=1, keepdims=True)
    wide[...] = jnp.broadcast_to(1.0 / jnp.sqrt(energy + EPS), (snaps, nz))
    mine = total[:snaps]
    turned = jnp.concatenate([mine[:, snaps:], mine[:, :snaps]], axis=1)
    rows_buf[...] = jnp.where(group == 0, mine, turned)
    copies = [pltpu.make_async_copy(rows_buf, rows_ref, sems.at[0])]
    copies[0].start()
    block = half * ny
    step = snaps // 4
    for n in range(4):
        for k in range(n * step, (n + 1) * step):
            factor = wide[k : k + 1, :]
            for c in range(3):
                for slot, base in ((0, 1 - group), (1, group)):
                    value = raws[3 * slot + c][k * block : (k + 1) * block, :] * factor
                    value = value.astype(jnp.bfloat16).reshape(half, ny, nz)
                    stage[k, c, pl.ds(base * half, half)] = value
        part = pl.ds(n * step, step)
        copies.append(pltpu.make_async_copy(stage.at[part], out_ref.at[part], sems.at[1 + n]))
        copies[-1].start()
    for copy in copies:
        copy.wait()


def two_groups(velocity, metric, volume, coeffs):
    snaps, _, layers, ny, nz = velocity.shape
    half = layers // 2
    peers = lax.axis_size("space")
    bf16, f32 = jnp.bfloat16, jnp.float32

    def halo(first):
        pairs = []
        for s in range(peers):
            for g in range(2):
                down = (g == 0) == first
                pairs.append((s * 2 + g, ((s + (-1 if down else 1)) % peers) * 2 + g))
        return pairs

    def swap(value):
        return lax.ppermute(value, "snap", [(0, 1), (1, 0)])

    def shift(value, first):
        return lax.ppermute(value, ("space", "snap"), halo(first))

    pair = jax.ShapeDtypeStruct((2, half, ny, snaps, nz), bf16)
    partial_sum = jax.ShapeDtypeStruct((2, half, ny, snaps, nz), f32)
    square = jax.ShapeDtypeStruct((2 * snaps, 2 * snaps), f32)
    raw = jax.ShapeDtypeStruct((snaps * half * ny, nz), f32)
    cells = half * ny * snaps * nz
    wide = pltpu.VMEM((snaps * ny, nz), f32)
    along = pltpu.VMEM((half, ny, snaps, nz), f32)
    dma = pltpu.SemaphoreType.DMA

    def call(kernel, name, out_shape, args, scratch=(), in_specs=None, out_specs=None, work=5):
        return pl.pallas_call(
            kernel,
            out_shape=out_shape,
            in_specs=in_specs or [vmem()] * len(args),
            out_specs=out_specs or jax.tree.map(lambda _: vmem(), out_shape),
            scratch_shapes=list(scratch),
            compiler_params=params(),
            cost_estimate=cost(2 * work * cells, work * cells),
            name=name,
        )(*args)

    theirs, mine, ox = call(
        omega_x_kernel,
        "omega_x",
        (pair, pair, pair),
        [pltpu.with_memory_space_constraint(a, pltpu.HBM) for a in (velocity, metric)],
        [
            pltpu.VMEM((snaps, 2, layers, ny, nz), bf16),
            pltpu.VMEM((2, layers, ny, nz), f32),
            wide,
            along,
            dma((2, 3)),
        ],
        [hbm()] * 2,
    )
    got_x = swap(ox)
    edge_theirs = shift(mine, True)
    zu, yu = call(
        functools.partial(u_kernel, half),
        "u_terms",
        (partial_sum, partial_sum),
        [velocity, metric],
        [pltpu.VMEM((half, ny, snaps, nz), bf16), wide, along],
    )

    def omega_yz(slot, near, far, edge):
        name = "omega_yz_mine" if slot else "omega_yz_theirs"
        args = [near, far, edge, zu, yu, metric]
        return call(functools.partial(omega_yz_kernel, slot), name, pair, args)

    yz_theirs = omega_yz(0, theirs, mine, edge_theirs)
    got_yz = swap(yz_theirs)
    late, _ = lax.optimization_barrier((theirs, yz_theirs))
    edge_mine = shift(late, False)

    coeff_rows, blocks = call(
        coeff_kernel,
        "coeff_blocks",
        (
            jax.ShapeDtypeStruct((snaps, 2 * snaps), f32),
            jax.ShapeDtypeStruct((ROWS // snaps * snaps, ROWS // snaps * 2 * snaps), bf16),
        ),
        [coeffs],
    )
    gram = call(functools.partial(gram_kernel, (1,), (0,)), "gram_x", square, [ox, got_x, volume])
    edge_mine, blocks, gram = lax.optimization_barrier((edge_mine, blocks, gram))
    yz_mine = omega_yz(1, mine, theirs, edge_mine)
    got_yz_theirs = swap(yz_mine)
    copies = jax.ShapeDtypeStruct((peers, 4 * snaps**2 // nz, nz), f32)
    grams = call(
        functools.partial(gram_kernel, (0, 1), (0, 1)),
        "gram_yz",
        copies,
        [yz_mine, got_yz, volume, gram],
    )

    grams = lax.all_to_all(grams, "space", 0, 0, tiled=True)
    gram = call(add_kernel, "add", square, [grams])
    other = swap(gram)

    def raw_modes(name, fields, *picks):
        kernel = functools.partial(raw_kernel, picks)
        return call(kernel, name, (raw,) * len(picks), [blocks, *fields])

    mine_x, theirs_x = raw_modes("raw_x", [ox, got_x], ((0, 1), (1, 0)), ((0, 0), (1, 1)))
    mine_yz = raw_modes("raw_yz", [yz_mine, got_yz], ((0, 0), (1, 0)), ((0, 1), (1, 1)))
    theirs_yz = raw_modes(
        "raw_yz_theirs", [yz_theirs, got_yz_theirs], ((0, 0), (1, 0)), ((0, 1), (1, 1))
    )
    modes, rows = call(
        functools.partial(finish_kernel, half, 1.0 / (3.0 * layers * peers * ny * nz)),
        "finish",
        (
            jax.ShapeDtypeStruct(velocity.shape, bf16),
            jax.ShapeDtypeStruct((snaps, 2 * snaps), f32),
        ),
        [gram, other, coeff_rows, theirs_x, *theirs_yz, mine_x, *mine_yz],
        [
            pltpu.VMEM(velocity.shape, bf16),
            pltpu.VMEM((snaps, 2 * snaps), f32),
            pltpu.VMEM((snaps, nz), f32),
            dma((5,)),
        ],
        None,
        (hbm(), hbm()),
    )
    return (rows, modes)


def per_device(velocity, metric, volume, coeffs):
    peers = lax.axis_size("space")
    paired = lax.axis_size("snap") == 2 and velocity.shape[2] == 2 * WIDTH
    if paired and velocity.shape[0] % 16 == 0 and peers & (peers - 1) == 0:
        return two_groups(velocity, metric, volume, coeffs)
    return many_groups(velocity, metric, volume, coeffs)


def solution(mesh):
    placed = (
        P("snap", None, "space", None, None),
        P(None, "space", None, None),
        P("space", None, None),
        P(),
    )
    return jax.shard_map(
        per_device,
        mesh=mesh,
        in_specs=placed,
        out_specs=(P("snap", None), P("snap", None, "space", None, None)),
        check_vma=False,
    )
```

```python
import functools

import jax
import jax.numpy as jnp
from jax import lax
from jax.experimental import pallas as pl
from jax.experimental.pallas import tpu as pltpu
from jax.sharding import PartitionSpec as P

EPS = 1e-06
WIDTH = 2
ROWS = 128
LIMIT = 24 * 1024 * 1024


def with_halo(shard, sides, width):
    for axis, dim in sides:
        peers, length = (lax.axis_size(axis), shard.shape[dim])
        up = [(i, (i + 1) % peers) for i in range(peers)]
        down = [(j, i) for i, j in up]
        last = lax.slice_in_dim(shard, length - width, length, axis=dim)
        leading = lax.slice_in_dim(shard, 0, width, axis=dim)
        before = lax.ppermute(last, axis, up)
        after = lax.ppermute(leading, axis, down)
        shard = jnp.concatenate([before, shard, after], axis=dim)
    return shard


def deriv(padded, dim):
    count = padded.shape[dim] - 4

    def cut(offset):
        return lax.slice_in_dim(padded, offset, offset + count, axis=dim)

    return (8.0 * (cut(3) - cut(1)) - (cut(4) - cut(0))) / 12.0


def curl(padded_x, metric):
    inner = padded_x[:, :, 2:-2]
    padded_y = jnp.pad(inner, ((0, 0), (0, 0), (0, 0), (2, 2), (0, 0)))
    padded_z = jnp.concatenate([inner[..., -2:], inner, inner[..., :2]], axis=4)
    along_x = deriv(padded_x, 2) * metric[0]
    along_y = deriv(padded_y, 3) * metric[1]
    along_z = deriv(padded_z, 4) * metric[2]
    omega_x = along_y[:, 2] - along_z[:, 1]
    omega_y = along_z[:, 0] - along_x[:, 2]
    omega_z = along_x[:, 1] - along_y[:, 0]
    return jnp.stack([omega_x, omega_y, omega_z], axis=1).astype(jnp.bfloat16)


def many_groups(velocity, metric, volume, coeffs):
    snap_dev = velocity.shape[0]
    snaps = coeffs.shape[0]
    group = lax.axis_index("snap")
    scale = 1.0 / (
        3.0 * volume.shape[0] * lax.axis_size("space") * volume.shape[1] * volume.shape[2]
    )
    padded = with_halo(velocity, (("space", 2),), 2)
    vorticity = curl(padded.astype(jnp.float32), metric)
    coeff_f = coeffs.astype(jnp.float32)
    moved = lax.all_to_all(vorticity, "snap", split_axis=3, concat_axis=0, tiled=True)
    part_y = moved.shape[3]
    vol_part = lax.dynamic_slice_in_dim(volume, group * part_y, part_y, 1)
    weighted = (moved.astype(jnp.float32) * vol_part).astype(jnp.bfloat16).reshape(snaps, -1)
    flat = moved.reshape(snaps, -1)
    partial_value = lax.dot_general(
        weighted, flat, (((1,), (1,)), ((), ())), preferred_element_type=jnp.float32
    )
    raw = lax.dot_general(
        coeffs, flat, (((0,), (0,)), ((), ())), preferred_element_type=jnp.float32
    )
    whole = lax.psum(partial_value, ("space", "snap")) * scale
    energy = jnp.sum(coeff_f * jnp.dot(whole, coeff_f, precision=lax.Precision.HIGHEST), axis=0)
    rows = lax.dynamic_slice_in_dim(whole, group * snap_dev, snap_dev, 0)
    local_modes = (raw / jnp.sqrt(energy + EPS)[:, None]).astype(jnp.bfloat16).reshape(moved.shape)
    modes = lax.all_to_all(local_modes, "snap", split_axis=0, concat_axis=3, tiled=True)
    return (rows, modes)


def vmem():
    return pl.BlockSpec(memory_space=pltpu.VMEM)


def hbm():
    return pl.BlockSpec(memory_space=pltpu.HBM)


def params():
    return pltpu.CompilerParams(vmem_limit_bytes=LIMIT)


def cost(flops, moved):
    return pl.CostEstimate(flops=flops, bytes_accessed=moved, transcendentals=0)


def z_stencil(size):
    rows = lax.broadcasted_iota(jnp.int32, (size, size), 0)
    cols = lax.broadcasted_iota(jnp.int32, (size, size), 1)
    ahead = rows - cols
    ahead = jnp.where(ahead < 0, ahead + size, ahead)
    out = jnp.where(ahead == 1, 8.0, 0.0) - jnp.where(ahead == size - 1, 8.0, 0.0)
    out = out - jnp.where(ahead == 2, 1.0, 0.0) + jnp.where(ahead == size - 2, 1.0, 0.0)
    return out.astype(jnp.bfloat16)


def spread(src, wide):
    snaps, ny, nz = src.shape
    wide[...] = src.astype(jnp.float32).reshape(snaps * ny, nz)


def row(wide, y, snaps, ny):
    return wide[pl.ds(y, snaps, ny), :]


def y_stencils(load, ny):
    held = {}

    def at(j):
        if j not in held:
            held[j] = load(j)
        return held[j]

    zero = jnp.zeros_like(at(0))
    for y in range(ny):
        near = (at(y + 1) if y + 1 < ny else zero) - (at(y - 1) if y >= 1 else zero)
        far = (at(y + 2) if y + 2 < ny else zero) - (at(y - 2) if y >= 2 else zero)
        held.pop(y - 2, None)
        yield y, 8.0 * near - far


def z_derivative(field, matrix, along):
    rows = field.shape[0] * field.shape[1] * field.shape[2]
    along[...] = jnp.dot(
        field.reshape(rows, field.shape[3]), matrix, preferred_element_type=jnp.float32
    ).reshape(field.shape)


def factor(metric_ref, m, layer, y):
    return metric_ref[m, layer, pl.ds(y, 1), :] * (1.0 / 12.0)


def flip(src, wide, out_ref, i):
    snaps, ny, _ = src.shape
    spread(src, wide)
    for y in range(ny):
        out_ref[i, y] = row(wide, y, snaps, ny).astype(jnp.bfloat16)


def omega_x_of(source, factors, offset, v_ref, w_ref, ox_ref, wide, along, ready):
    half, ny, snaps, nz = ox_ref.shape
    matrix = z_stencil(nz)
    ready(0)
    for i in range(half):
        flip(source(0, i), wide, v_ref, i)
    z_derivative(v_ref[...], matrix, along)
    ready(1)
    for i in range(half):
        spread(source(1, i), wide)

        def load(j):
            value = row(wide, j, snaps, ny)
            w_ref[i, j] = value.astype(jnp.bfloat16)
            return value

        for y, across in y_stencils(load, ny):
            value = across * factor(factors, 1, offset + i, y)
            value = value - along[i, y] * factor(factors, 2, offset + i, y)
            ox_ref[i, y] = value.astype(jnp.bfloat16)


def omega_x_theirs_kernel(
    vel_ref, metric_ref, v_ref, w_ref, ox_ref, buf, factors, wide, along, sems
):
    half = ox_ref.shape[0]
    base = (1 - lax.axis_index("snap")) * half
    copies = []
    for c in range(2):
        source = vel_ref.at[:, 1 + c, pl.ds(base, half)]
        copies.append(pltpu.make_async_copy(source, buf.at[:, c], sems.at[c]))
        copies[c].start()
    source = metric_ref.at[:, pl.ds(base, half)]
    copies.append(pltpu.make_async_copy(source, factors, sems.at[2]))
    copies[2].start()

    def ready(step):
        copies[step].wait()
        if step == 1:
            copies[2].wait()

    omega_x_of(lambda c, i: buf[:, c, i], factors, 0, v_ref, w_ref, ox_ref, wide, along, ready)


def omega_x_mine_kernel(vel_ref, metric_ref, v_ref, w_ref, ox_ref, wide, along):
    base = lax.axis_index("snap") * ox_ref.shape[0]

    def source(c, i):
        return vel_ref[:, 1 + c, base + i]

    refs = v_ref, w_ref, ox_ref, wide, along
    omega_x_of(source, metric_ref, base, *refs, lambda step: None)


def u_kernel(half, vel_ref, metric_ref, zu_ref, yu_ref, flat, wide, along):
    snaps, _, _, ny, nz = vel_ref.shape
    matrix = z_stencil(nz)
    group = lax.axis_index("snap")
    for slot in range(2):
        base = (group if slot else 1 - group) * half
        for i in range(half):
            spread(vel_ref[:, 0, base + i], wide)

            def load(j):
                value = row(wide, j, snaps, ny)
                flat[i, j] = value.astype(jnp.bfloat16)
                return value

            for y, across in y_stencils(load, ny):
                yu_ref[slot, i, y] = across * factor(metric_ref, 1, base + i, y)
        z_derivative(flat[...], matrix, along)
        for i in range(half):
            for y in range(ny):
                zu_ref[slot, i, y] = along[i, y] * factor(metric_ref, 2, base + i, y)


def finish_curl(sign, slot, near_ref, far_ref, halo_ref, known_ref, metric_ref, out_ref):
    half, ny, _, _ = near_ref.shape
    group = lax.axis_index("snap")
    part = group if slot else 1 - group

    def run(low_ref, high_ref):
        def plane(i, y):
            if i < 0:
                ref, k = low_ref, half + i
            elif i < half:
                ref, k = near_ref, i
            else:
                ref, k = high_ref, i - half
            return ref[k, y].astype(jnp.float32)

        for y in range(ny):
            at = [plane(i, y) for i in range(-WIDTH, half + WIDTH)]
            for i in range(half):
                along = 8.0 * (at[i + 3] - at[i + 1]) - (at[i + 4] - at[i])
                along = along * factor(metric_ref, 0, part * half + i, y)
                known = known_ref[slot, i, y]
                value = along - known if sign > 0 else known - along
                out_ref[i, y] = value.astype(jnp.bfloat16)

    @pl.when(part == 0)
    def _():
        run(halo_ref, far_ref)

    @pl.when(part == 1)
    def _():
        run(far_ref, halo_ref)


def omega_yz_kernel(slot, *refs):
    near, far, edge = refs[:2], refs[2:4], refs[4:6]
    zu_ref, yu_ref, metric_ref, out_ref = refs[6:]
    known = (yu_ref, zu_ref)
    for c, sign in ((1, -1), (0, 1)):
        fields = near[c], far[c], edge[c], known[c]
        finish_curl(sign, slot, *fields, metric_ref, out_ref.at[1 - c])


def gram_of(own, got, volume_ref, base):
    half, ny, _, _ = own.shape
    total = None
    for i in range(half):
        plain, heavy = [], []
        for y in range(ny):
            pair = jnp.concatenate([own[i, y], got[i, y]], axis=0)
            weight = volume_ref[base + i, pl.ds(y, 1), :]
            plain.append(pair)
            heavy.append((pair.astype(jnp.float32) * weight).astype(jnp.bfloat16))
        part = lax.dot_general(
            jnp.concatenate(heavy, axis=1),
            jnp.concatenate(plain, axis=1),
            (((1,), (1,)), ((), ())),
            preferred_element_type=jnp.float32,
        )
        total = part if total is None else total + part
    return total


def gram_kernel(slots, own, got, volume_ref, *refs):
    base = lax.axis_index("snap") * volume_ref.shape[0] // 2
    total = sum(gram_of(ref_slot(own, n), ref_slot(got, n), volume_ref, base) for n in slots)
    for earlier in refs[:-1]:
        total = total + earlier[...]
    if len(refs[-1].shape) == 3:
        count, rows, _ = refs[-1].shape
        total = jnp.concatenate(
            [total[n : n + rows] for n in range(0, total.shape[0], rows)], axis=1
        )
        for peer in range(count):
            refs[-1][peer] = total
    else:
        refs[-1][...] = total


def ref_slot(ref, slot):
    return ref if slot is None else ref.at[slot]


def add_kernel(parts_ref, out_ref):
    parts = [parts_ref[n] for n in range(parts_ref.shape[0])]
    while len(parts) > 1:
        parts = [sum(parts[n : n + 2]) for n in range(0, len(parts), 2)]
    rows, side = parts_ref.shape[1], out_ref.shape[0]
    for n in range(side // rows):
        out_ref[n * rows : (n + 1) * rows] = parts[0][:, n * side : (n + 1) * side]


def coeff_kernel(coeff_ref, mine_ref, block_ref):
    snaps, count = mine_ref.shape
    rows = block_ref.shape[0]
    base = lax.axis_index("snap") * snaps

    def chosen(shape, test):
        left = lax.broadcasted_iota(jnp.int32, shape, 0)
        right = lax.broadcasted_iota(jnp.int32, shape, 1)
        return jnp.where(test(left, right), 1.0, 0.0).astype(jnp.bfloat16)

    def take(a, b, dims):
        out = lax.dot_general(a, b, (dims, ((), ())), preferred_element_type=jnp.float32)
        return out.astype(jnp.bfloat16)

    mine = chosen((snaps, count), lambda k, m: m == k + base)
    mine = take(mine, coeff_ref[...], ((1,), (1,)))
    order = chosen((count, count), lambda j, m: j == lax.rem(m + base, count))
    mine = take(mine, order, ((1,), (0,)))
    mine_ref[...] = mine.astype(jnp.float32)
    down = chosen((rows, snaps), lambda r, k: lax.rem(r, snaps) == k)
    for part in range(count // snaps):
        across = chosen((count, rows), lambda j, c: j == lax.rem(c, snaps) + part * snaps)
        wide = take(take(down, mine, ((1,), (0,))), across, ((1,), (0,)))
        same = chosen((rows, rows), lambda r, c: lax.div(r, snaps) == lax.div(c, snaps))
        block_ref[:, part * rows : (part + 1) * rows] = wide * same


def raw_blocks(own, got, block_ref, put):
    ny, snaps, nz = own.shape
    block = block_ref.shape[0] // snaps
    lanes = 2 if ny % (2 * block) == 0 else 1
    for start in range(0, ny, block * lanes):
        columns = []
        for n in range(lanes):
            at = start + n * block
            parts = [ref[at : at + block].reshape(block * snaps, nz) for ref in (own, got)]
            columns.append(jnp.concatenate(parts, axis=0))
        both = columns[0] if lanes == 1 else jnp.concatenate(columns, axis=1)
        raw = jnp.dot(block_ref[...], both, preferred_element_type=jnp.float32)
        for n in range(lanes):
            part = raw[:, n * nz : (n + 1) * nz].reshape(block, snaps, nz)
            for k in range(block):
                put(start + n * block + k, part[k])


def raw_kernel(slots, own_ref, got_ref, block_ref, *outs):
    for slot, out_ref in zip(slots, outs):
        own, got = ref_slot(own_ref, slot), ref_slot(got_ref, slot)
        half, ny, snaps, _ = own.shape
        for i in range(half):

            def put(y, value):
                out_ref[pl.ds(i * ny + y, snaps, half * ny), :] = value

            raw_blocks(own.at[i], got.at[i], block_ref, put)


def finish_kernel(half, scale, part_ref, other_ref, coeff_ref, *refs):
    raws, (out_ref, rows_ref, stage, rows_buf, wide, sems) = refs[:6], refs[6:]
    snaps, _, _, ny, nz = stage.shape
    group = lax.axis_index("snap")
    other = other_ref[...]
    other = jnp.concatenate([other[snaps:], other[:snaps]], axis=0)
    other = jnp.concatenate([other[:, snaps:], other[:, :snaps]], axis=1)
    total = (part_ref[...] + other) * scale
    coeff = coeff_ref[...]
    inner = jnp.dot(
        coeff, total, precision=lax.Precision.HIGHEST, preferred_element_type=jnp.float32
    )
    energy = jnp.sum(inner * coeff, axis=1, keepdims=True)
    wide[...] = jnp.broadcast_to(1.0 / jnp.sqrt(energy + EPS), (snaps, nz))
    mine = total[:snaps]
    turned = jnp.concatenate([mine[:, snaps:], mine[:, :snaps]], axis=1)
    rows_buf[...] = jnp.where(group == 0, mine, turned)
    copies = [pltpu.make_async_copy(rows_buf, rows_ref, sems.at[0])]
    copies[0].start()
    block = half * ny
    step = snaps // 4
    for n in range(4):
        for k in range(n * step, (n + 1) * step):
            factor = wide[k : k + 1, :]
            for c in range(3):
                for slot, base in ((0, 1 - group), (1, group)):
                    value = raws[3 * slot + c][k * block : (k + 1) * block, :] * factor
                    value = value.astype(jnp.bfloat16).reshape(half, ny, nz)
                    stage[k, c, pl.ds(base * half, half)] = value
        part = pl.ds(n * step, step)
        copies.append(pltpu.make_async_copy(stage.at[part], out_ref.at[part], sems.at[1 + n]))
        copies[-1].start()
    for copy in copies:
        copy.wait()


def two_groups(velocity, metric, volume, coeffs):
    snaps, _, layers, ny, nz = velocity.shape
    half = layers // 2
    peers = lax.axis_size("space")
    bf16, f32 = jnp.bfloat16, jnp.float32

    def halo(first):
        pairs = []
        for s in range(peers):
            for g in range(2):
                down = (g == 0) == first
                pairs.append((s * 2 + g, ((s + (-1 if down else 1)) % peers) * 2 + g))
        return pairs

    def swap(value):
        return lax.ppermute(value, "snap", [(0, 1), (1, 0)])

    def shift(value, first):
        axes, pairs = ("space", "snap"), halo(first)
        return [lax.ppermute(part, axes, pairs) for part in value]

    field = jax.ShapeDtypeStruct((half, ny, snaps, nz), bf16)
    pair = jax.ShapeDtypeStruct((2, half, ny, snaps, nz), bf16)
    partial_sum = jax.ShapeDtypeStruct((2, half, ny, snaps, nz), f32)
    square = jax.ShapeDtypeStruct((2 * snaps, 2 * snaps), f32)
    raw = jax.ShapeDtypeStruct((snaps * half * ny, nz), f32)
    cells = half * ny * snaps * nz
    wide = pltpu.VMEM((snaps * ny, nz), f32)
    along = pltpu.VMEM((half, ny, snaps, nz), f32)
    dma = pltpu.SemaphoreType.DMA

    def call(kernel, name, out_shape, args, scratch=(), in_specs=None, out_specs=None, work=5):
        return pl.pallas_call(
            kernel,
            out_shape=out_shape,
            in_specs=in_specs or [vmem()] * len(args),
            out_specs=out_specs or jax.tree.map(lambda _: vmem(), out_shape),
            scratch_shapes=list(scratch),
            compiler_params=params(),
            cost_estimate=cost(2 * work * cells, work * cells),
            name=name,
        )(*args)

    *theirs, x_theirs = call(
        omega_x_theirs_kernel,
        "omega_x_theirs",
        (field, field, field),
        [pltpu.with_memory_space_constraint(a, pltpu.HBM) for a in (velocity, metric)],
        [
            pltpu.VMEM((snaps, 2, half, ny, nz), bf16),
            pltpu.VMEM((3, half, ny, nz), f32),
            wide,
            along,
            dma((3,)),
        ],
        [hbm()] * 2,
    )
    got_x_mine = swap(x_theirs)
    velocity, _ = lax.optimization_barrier((velocity, x_theirs))
    *mine, x_mine = call(
        omega_x_mine_kernel,
        "omega_x_mine",
        (field, field, field),
        [velocity, metric],
        [wide, along],
    )
    edge_theirs = shift(mine, True)
    got_x_theirs = swap(x_mine)
    edge_mine = shift(theirs, False)
    zu, yu = call(
        functools.partial(u_kernel, half),
        "u_terms",
        (partial_sum, partial_sum),
        [velocity, metric],
        [pltpu.VMEM((half, ny, snaps, nz), bf16), wide, along],
    )

    def omega_yz(slot, near, far, edge):
        name = "omega_yz_mine" if slot else "omega_yz_theirs"
        args = [*near, *far, *edge, zu, yu, metric]
        return call(functools.partial(omega_yz_kernel, slot), name, pair, args)

    def gram_part(name, slots, shape, *args):
        return call(functools.partial(gram_kernel, slots), name, shape, args)

    def raw_modes(name, slots, own, got):
        kernel = functools.partial(raw_kernel, slots)
        return call(kernel, name, (raw,) * len(slots), [own, got, blocks])

    gram = gram_part("gram_x", (None,), square, x_mine, got_x_mine, volume)
    edge_theirs, gram = lax.optimization_barrier((edge_theirs, gram))
    yz_theirs = omega_yz(0, theirs, mine, edge_theirs)
    got_yz_mine = swap(yz_theirs)
    coeff_rows, blocks = call(
        coeff_kernel,
        "coeff_blocks",
        (
            jax.ShapeDtypeStruct((snaps, 2 * snaps), f32),
            jax.ShapeDtypeStruct((ROWS // snaps * snaps, ROWS // snaps * 2 * snaps), bf16),
        ),
        [coeffs],
    )
    (theirs_x,) = raw_modes("raw_x_theirs", (None,), x_theirs, got_x_theirs)
    (mine_x,) = raw_modes("raw_x_mine", (None,), x_mine, got_x_mine)
    edge_mine, theirs_x, mine_x, _ = lax.optimization_barrier(
        (edge_mine, theirs_x, mine_x, yz_theirs)
    )
    yz_mine = omega_yz(1, mine, theirs, edge_mine)
    got_yz_theirs = swap(yz_mine)
    copies = jax.ShapeDtypeStruct((peers, 4 * snaps**2 // nz, nz), f32)
    grams = gram_part("gram_yz", (0, 1), copies, yz_mine, got_yz_mine, volume, gram)
    grams = lax.all_to_all(grams, "space", 0, 0, tiled=True)
    gram = call(add_kernel, "add", square, [grams])
    other = swap(gram)
    mine_yz = raw_modes("raw_yz_mine", (0, 1), yz_mine, got_yz_mine)
    theirs_yz = raw_modes("raw_yz_theirs", (0, 1), yz_theirs, got_yz_theirs)
    modes, rows = call(
        functools.partial(finish_kernel, half, 1.0 / (3.0 * layers * peers * ny * nz)),
        "finish",
        (
            jax.ShapeDtypeStruct(velocity.shape, bf16),
            jax.ShapeDtypeStruct((snaps, 2 * snaps), f32),
        ),
        [gram, other, coeff_rows, theirs_x, *theirs_yz, mine_x, *mine_yz],
        [
            pltpu.VMEM(velocity.shape, bf16),
            pltpu.VMEM((snaps, 2 * snaps), f32),
            pltpu.VMEM((snaps, nz), f32),
            dma((5,)),
        ],
        None,
        (hbm(), hbm()),
    )
    return (rows, modes)


def per_device(velocity, metric, volume, coeffs):
    peers = lax.axis_size("space")
    paired = lax.axis_size("snap") == 2 and velocity.shape[2] == 2 * WIDTH
    if paired and velocity.shape[0] % 16 == 0 and peers & (peers - 1) == 0:
        return two_groups(velocity, metric, volume, coeffs)
    return many_groups(velocity, metric, volume, coeffs)


def solution(mesh):
    placed = (
        P("snap", None, "space", None, None),
        P(None, "space", None, None),
        P("space", None, None),
        P(),
    )
    return jax.shard_map(
        per_device,
        mesh=mesh,
        in_specs=placed,
        out_specs=(P("snap", None), P("snap", None, "space", None, None)),
        check_vma=False,
    )
```

```python
import functools

import jax
import jax.numpy as jnp
from jax import lax
from jax.experimental import pallas as pl
from jax.experimental.pallas import tpu as pltpu
from jax.sharding import PartitionSpec as P

EPS = 1e-06
WIDTH = 2
ROWS = 128
LIMIT = 24 * 1024 * 1024


def with_halo(shard, sides, width):
    for axis, dim in sides:
        peers, length = (lax.axis_size(axis), shard.shape[dim])
        up = [(i, (i + 1) % peers) for i in range(peers)]
        down = [(j, i) for i, j in up]
        last = lax.slice_in_dim(shard, length - width, length, axis=dim)
        leading = lax.slice_in_dim(shard, 0, width, axis=dim)
        before = lax.ppermute(last, axis, up)
        after = lax.ppermute(leading, axis, down)
        shard = jnp.concatenate([before, shard, after], axis=dim)
    return shard


def deriv(padded, dim):
    count = padded.shape[dim] - 4

    def cut(offset):
        return lax.slice_in_dim(padded, offset, offset + count, axis=dim)

    return (8.0 * (cut(3) - cut(1)) - (cut(4) - cut(0))) / 12.0


def curl(padded_x, metric):
    inner = padded_x[:, :, 2:-2]
    padded_y = jnp.pad(inner, ((0, 0), (0, 0), (0, 0), (2, 2), (0, 0)))
    padded_z = jnp.concatenate([inner[..., -2:], inner, inner[..., :2]], axis=4)
    along_x = deriv(padded_x, 2) * metric[0]
    along_y = deriv(padded_y, 3) * metric[1]
    along_z = deriv(padded_z, 4) * metric[2]
    omega_x = along_y[:, 2] - along_z[:, 1]
    omega_y = along_z[:, 0] - along_x[:, 2]
    omega_z = along_x[:, 1] - along_y[:, 0]
    return jnp.stack([omega_x, omega_y, omega_z], axis=1).astype(jnp.bfloat16)


def many_groups(velocity, metric, volume, coeffs):
    snap_dev = velocity.shape[0]
    snaps = coeffs.shape[0]
    group = lax.axis_index("snap")
    scale = 1.0 / (
        3.0 * volume.shape[0] * lax.axis_size("space") * volume.shape[1] * volume.shape[2]
    )
    padded = with_halo(velocity, (("space", 2),), 2)
    vorticity = curl(padded.astype(jnp.float32), metric)
    coeff_f = coeffs.astype(jnp.float32)
    moved = lax.all_to_all(vorticity, "snap", split_axis=3, concat_axis=0, tiled=True)
    part_y = moved.shape[3]
    vol_part = lax.dynamic_slice_in_dim(volume, group * part_y, part_y, 1)
    weighted = (moved.astype(jnp.float32) * vol_part).astype(jnp.bfloat16).reshape(snaps, -1)
    flat = moved.reshape(snaps, -1)
    partial_value = lax.dot_general(
        weighted, flat, (((1,), (1,)), ((), ())), preferred_element_type=jnp.float32
    )
    raw = lax.dot_general(
        coeffs, flat, (((0,), (0,)), ((), ())), preferred_element_type=jnp.float32
    )
    whole = lax.psum(partial_value, ("space", "snap")) * scale
    energy = jnp.sum(coeff_f * jnp.dot(whole, coeff_f, precision=lax.Precision.HIGHEST), axis=0)
    rows = lax.dynamic_slice_in_dim(whole, group * snap_dev, snap_dev, 0)
    local_modes = (raw / jnp.sqrt(energy + EPS)[:, None]).astype(jnp.bfloat16).reshape(moved.shape)
    modes = lax.all_to_all(local_modes, "snap", split_axis=0, concat_axis=3, tiled=True)
    return (rows, modes)


def vmem():
    return pl.BlockSpec(memory_space=pltpu.VMEM)


def hbm():
    return pl.BlockSpec(memory_space=pltpu.HBM)


def params():
    return pltpu.CompilerParams(vmem_limit_bytes=LIMIT)


def cost(flops, moved):
    return pl.CostEstimate(flops=flops, bytes_accessed=moved, transcendentals=0)


def z_stencil(size):
    rows = lax.broadcasted_iota(jnp.int32, (size, size), 0)
    cols = lax.broadcasted_iota(jnp.int32, (size, size), 1)
    ahead = rows - cols
    ahead = jnp.where(ahead < 0, ahead + size, ahead)
    out = jnp.where(ahead == 1, 8.0, 0.0) - jnp.where(ahead == size - 1, 8.0, 0.0)
    out = out - jnp.where(ahead == 2, 1.0, 0.0) + jnp.where(ahead == size - 2, 1.0, 0.0)
    return out.astype(jnp.bfloat16)


def spread(src, wide):
    snaps, ny, nz = src.shape
    wide[...] = src.astype(jnp.float32).reshape(snaps * ny, nz)


def row(wide, y, snaps, ny):
    return wide[pl.ds(y, snaps, ny), :]


def y_stencils(load, ny):
    held = {}

    def at(j):
        if j not in held:
            held[j] = load(j)
        return held[j]

    zero = jnp.zeros_like(at(0))
    for y in range(ny):
        near = (at(y + 1) if y + 1 < ny else zero) - (at(y - 1) if y >= 1 else zero)
        far = (at(y + 2) if y + 2 < ny else zero) - (at(y - 2) if y >= 2 else zero)
        held.pop(y - 2, None)
        yield y, 8.0 * near - far


def z_derivative(field, matrix, along):
    rows = field.shape[0] * field.shape[1] * field.shape[2]
    along[...] = jnp.dot(
        field.reshape(rows, field.shape[3]), matrix, preferred_element_type=jnp.float32
    ).reshape(field.shape)


def factor(metric_ref, m, layer, y):
    return metric_ref[m, layer, pl.ds(y, 1), :] * (1.0 / 12.0)


def flip(src, wide, out_ref, i):
    snaps, ny, _ = src.shape
    spread(src, wide)
    for y in range(ny):
        out_ref[i, y] = row(wide, y, snaps, ny).astype(jnp.bfloat16)


def omega_x_of(source, factors, offset, v_ref, w_ref, ox_ref, wide, along, ready):
    half, ny, snaps, nz = ox_ref.shape
    matrix = z_stencil(nz)
    ready(0)
    for i in range(half):
        flip(source(0, i), wide, v_ref, i)
    z_derivative(v_ref[...], matrix, along)
    ready(1)
    for i in range(half):
        spread(source(1, i), wide)

        def load(j):
            value = row(wide, j, snaps, ny)
            w_ref[i, j] = value.astype(jnp.bfloat16)
            return value

        for y, across in y_stencils(load, ny):
            value = across * factor(factors, 1, offset + i, y)
            value = value - along[i, y] * factor(factors, 2, offset + i, y)
            ox_ref[i, y] = value.astype(jnp.bfloat16)


def omega_x_theirs_kernel(
    vel_ref, metric_ref, v_ref, w_ref, ox_ref, buf, factors, wide, along, sems
):
    half = ox_ref.shape[0]
    base = (1 - lax.axis_index("snap")) * half
    copies = []
    for c in range(2):
        source = vel_ref.at[:, 1 + c, pl.ds(base, half)]
        copies.append(pltpu.make_async_copy(source, buf.at[:, c], sems.at[c]))
        copies[c].start()
    source = metric_ref.at[:, pl.ds(base, half)]
    copies.append(pltpu.make_async_copy(source, factors, sems.at[2]))
    copies[2].start()

    def ready(step):
        copies[step].wait()
        if step == 1:
            copies[2].wait()

    omega_x_of(lambda c, i: buf[:, c, i], factors, 0, v_ref, w_ref, ox_ref, wide, along, ready)


def omega_x_mine_kernel(vel_ref, metric_ref, v_ref, w_ref, ox_ref, wide, along):
    base = lax.axis_index("snap") * ox_ref.shape[0]

    def source(c, i):
        return vel_ref[:, 1 + c, base + i]

    refs = v_ref, w_ref, ox_ref, wide, along
    omega_x_of(source, metric_ref, base, *refs, lambda step: None)


def u_kernel(half, vel_ref, metric_ref, zu_ref, yu_ref, flat, wide, along):
    snaps, _, _, ny, nz = vel_ref.shape
    matrix = z_stencil(nz)
    group = lax.axis_index("snap")
    for slot in range(2):
        base = (group if slot else 1 - group) * half
        for i in range(half):
            spread(vel_ref[:, 0, base + i], wide)

            def load(j):
                value = row(wide, j, snaps, ny)
                flat[i, j] = value.astype(jnp.bfloat16)
                return value

            for y, across in y_stencils(load, ny):
                yu_ref[slot, i, y] = across * factor(metric_ref, 1, base + i, y)
        z_derivative(flat[...], matrix, along)
        for i in range(half):
            for y in range(ny):
                zu_ref[slot, i, y] = along[i, y] * factor(metric_ref, 2, base + i, y)


def finish_curl(sign, slot, near_ref, far_ref, halo_ref, known_ref, metric_ref, out_ref):
    half, ny, _, _ = near_ref.shape
    group = lax.axis_index("snap")
    part = group if slot else 1 - group

    def run(low_ref, high_ref):
        def plane(i, y):
            if i < 0:
                ref, k = low_ref, half + i
            elif i < half:
                ref, k = near_ref, i
            else:
                ref, k = high_ref, i - half
            return ref[k, y].astype(jnp.float32)

        for y in range(ny):
            at = [plane(i, y) for i in range(-WIDTH, half + WIDTH)]
            for i in range(half):
                along = 8.0 * (at[i + 3] - at[i + 1]) - (at[i + 4] - at[i])
                along = along * factor(metric_ref, 0, part * half + i, y)
                known = known_ref[slot, i, y]
                value = along - known if sign > 0 else known - along
                out_ref[i, y] = value.astype(jnp.bfloat16)

    @pl.when(part == 0)
    def _():
        run(halo_ref, far_ref)

    @pl.when(part == 1)
    def _():
        run(far_ref, halo_ref)


def omega_yz_kernel(slot, *refs):
    near, far, edge = refs[:2], refs[2:4], refs[4:6]
    zu_ref, yu_ref, metric_ref, out_ref = refs[6:]
    known = (yu_ref, zu_ref)
    for c, sign in ((1, -1), (0, 1)):
        fields = near[c], far[c], edge[c], known[c]
        finish_curl(sign, slot, *fields, metric_ref, out_ref.at[1 - c])


def gram_of(own, got, volume_ref, base):
    half, ny, _, _ = own.shape
    total = None
    for i in range(half):
        plain, heavy = [], []
        for y in range(ny):
            pair = jnp.concatenate([own[i, y], got[i, y]], axis=0)
            weight = volume_ref[base + i, pl.ds(y, 1), :]
            plain.append(pair)
            heavy.append((pair.astype(jnp.float32) * weight).astype(jnp.bfloat16))
        part = lax.dot_general(
            jnp.concatenate(heavy, axis=1),
            jnp.concatenate(plain, axis=1),
            (((1,), (1,)), ((), ())),
            preferred_element_type=jnp.float32,
        )
        total = part if total is None else total + part
    return total


def gram_kernel(slots, own, got, volume_ref, *refs):
    base = lax.axis_index("snap") * volume_ref.shape[0] // 2
    total = sum(gram_of(ref_slot(own, n), ref_slot(got, n), volume_ref, base) for n in slots)
    for earlier in refs[:-1]:
        total = total + earlier[...]
    if len(refs[-1].shape) == 3:
        count, rows, _ = refs[-1].shape
        total = jnp.concatenate(
            [total[n : n + rows] for n in range(0, total.shape[0], rows)], axis=1
        )
        for peer in range(count):
            refs[-1][peer] = total
    else:
        refs[-1][...] = total


def ref_slot(ref, slot):
    return ref if slot is None else ref.at[slot]


def add_kernel(parts_ref, out_ref):
    parts = [parts_ref[n] for n in range(parts_ref.shape[0])]
    while len(parts) > 1:
        parts = [sum(parts[n : n + 2]) for n in range(0, len(parts), 2)]
    rows, side = parts_ref.shape[1], out_ref.shape[0]
    for n in range(side // rows):
        out_ref[n * rows : (n + 1) * rows] = parts[0][:, n * side : (n + 1) * side]


def coeff_kernel(coeff_ref, mine_ref, block_ref):
    snaps, count = mine_ref.shape
    rows = block_ref.shape[0]
    base = lax.axis_index("snap") * snaps

    def chosen(shape, test):
        left = lax.broadcasted_iota(jnp.int32, shape, 0)
        right = lax.broadcasted_iota(jnp.int32, shape, 1)
        return jnp.where(test(left, right), 1.0, 0.0).astype(jnp.bfloat16)

    def take(a, b, dims):
        out = lax.dot_general(a, b, (dims, ((), ())), preferred_element_type=jnp.float32)
        return out.astype(jnp.bfloat16)

    mine = chosen((snaps, count), lambda k, m: m == k + base)
    mine = take(mine, coeff_ref[...], ((1,), (1,)))
    order = chosen((count, count), lambda j, m: j == lax.rem(m + base, count))
    mine = take(mine, order, ((1,), (0,)))
    mine_ref[...] = mine.astype(jnp.float32)
    down = chosen((rows, snaps), lambda r, k: lax.rem(r, snaps) == k)
    for part in range(count // snaps):
        across = chosen((count, rows), lambda j, c: j == lax.rem(c, snaps) + part * snaps)
        wide = take(take(down, mine, ((1,), (0,))), across, ((1,), (0,)))
        same = chosen((rows, rows), lambda r, c: lax.div(r, snaps) == lax.div(c, snaps))
        block_ref[:, part * rows : (part + 1) * rows] = wide * same


def raw_blocks(own, got, block_ref, put):
    ny, snaps, nz = own.shape
    block = block_ref.shape[0] // snaps
    lanes = 2 if ny % (2 * block) == 0 else 1
    for start in range(0, ny, block * lanes):
        columns = []
        for n in range(lanes):
            at = start + n * block
            parts = [ref[at : at + block].reshape(block * snaps, nz) for ref in (own, got)]
            columns.append(jnp.concatenate(parts, axis=0))
        both = columns[0] if lanes == 1 else jnp.concatenate(columns, axis=1)
        raw = jnp.dot(block_ref[...], both, preferred_element_type=jnp.float32)
        for n in range(lanes):
            part = raw[:, n * nz : (n + 1) * nz].reshape(block, snaps, nz)
            for k in range(block):
                put(start + n * block + k, part[k])


def raw_kernel(slots, own_ref, got_ref, block_ref, *outs):
    for slot, out_ref in zip(slots, outs):
        own, got = ref_slot(own_ref, slot), ref_slot(got_ref, slot)
        half, ny, snaps, _ = own.shape
        for i in range(half):

            def put(y, value):
                out_ref[pl.ds(i * ny + y, snaps, half * ny), :] = value

            raw_blocks(own.at[i], got.at[i], block_ref, put)


def finish_kernel(half, scale, part_ref, other_ref, coeff_ref, *refs):
    raws, (out_ref, rows_ref, stage, rows_buf, wide, sems) = refs[:6], refs[6:]
    snaps, _, _, ny, nz = stage.shape
    group = lax.axis_index("snap")
    other = other_ref[...]
    other = jnp.concatenate([other[snaps:], other[:snaps]], axis=0)
    other = jnp.concatenate([other[:, snaps:], other[:, :snaps]], axis=1)
    total = (part_ref[...] + other) * scale
    coeff = coeff_ref[...]
    inner = jnp.dot(
        coeff, total, precision=lax.Precision.HIGHEST, preferred_element_type=jnp.float32
    )
    energy = jnp.sum(inner * coeff, axis=1, keepdims=True)
    wide[...] = jnp.broadcast_to(1.0 / jnp.sqrt(energy + EPS), (snaps, nz))
    mine = total[:snaps]
    turned = jnp.concatenate([mine[:, snaps:], mine[:, :snaps]], axis=1)
    rows_buf[...] = jnp.where(group == 0, mine, turned)
    copies = [pltpu.make_async_copy(rows_buf, rows_ref, sems.at[0])]
    copies[0].start()
    block = half * ny
    step = snaps // 4
    for n in range(4):
        for k in range(n * step, (n + 1) * step):
            factor = wide[k : k + 1, :]
            for c in range(3):
                for slot, base in ((0, 1 - group), (1, group)):
                    value = raws[3 * slot + c][k * block : (k + 1) * block, :] * factor
                    value = value.astype(jnp.bfloat16).reshape(half, ny, nz)
                    stage[k, c, pl.ds(base * half, half)] = value
        part = pl.ds(n * step, step)
        copies.append(pltpu.make_async_copy(stage.at[part], out_ref.at[part], sems.at[1 + n]))
        copies[-1].start()
    for copy in copies:
        copy.wait()


def two_groups(velocity, metric, volume, coeffs):
    snaps, _, layers, ny, nz = velocity.shape
    half = layers // 2
    peers = lax.axis_size("space")
    bf16, f32 = jnp.bfloat16, jnp.float32

    def halo(first):
        pairs = []
        for s in range(peers):
            for g in range(2):
                down = (g == 0) == first
                pairs.append((s * 2 + g, ((s + (-1 if down else 1)) % peers) * 2 + g))
        return pairs

    def swap(value):
        return lax.ppermute(value, "snap", [(0, 1), (1, 0)])

    def shift(value, first):
        axes, pairs = ("space", "snap"), halo(first)
        return [lax.ppermute(part, axes, pairs) for part in value]

    field = jax.ShapeDtypeStruct((half, ny, snaps, nz), bf16)
    pair = jax.ShapeDtypeStruct((2, half, ny, snaps, nz), bf16)
    partial_sum = jax.ShapeDtypeStruct((2, half, ny, snaps, nz), f32)
    square = jax.ShapeDtypeStruct((2 * snaps, 2 * snaps), f32)
    raw = jax.ShapeDtypeStruct((snaps * half * ny, nz), f32)
    cells = half * ny * snaps * nz
    wide = pltpu.VMEM((snaps * ny, nz), f32)
    along = pltpu.VMEM((half, ny, snaps, nz), f32)
    dma = pltpu.SemaphoreType.DMA

    def call(kernel, name, out_shape, args, scratch=(), in_specs=None, out_specs=None, work=5):
        return pl.pallas_call(
            kernel,
            out_shape=out_shape,
            in_specs=in_specs or [vmem()] * len(args),
            out_specs=out_specs or jax.tree.map(lambda _: vmem(), out_shape),
            scratch_shapes=list(scratch),
            compiler_params=params(),
            cost_estimate=cost(2 * work * cells, work * cells),
            name=name,
        )(*args)

    *theirs, x_theirs = call(
        omega_x_theirs_kernel,
        "omega_x_theirs",
        (field, field, field),
        [pltpu.with_memory_space_constraint(a, pltpu.HBM) for a in (velocity, metric)],
        [
            pltpu.VMEM((snaps, 2, half, ny, nz), bf16),
            pltpu.VMEM((3, half, ny, nz), f32),
            wide,
            along,
            dma((3,)),
        ],
        [hbm()] * 2,
    )
    got_x_mine = swap(x_theirs)
    velocity, _ = lax.optimization_barrier((velocity, x_theirs))
    *mine, x_mine = call(
        omega_x_mine_kernel,
        "omega_x_mine",
        (field, field, field),
        [velocity, metric],
        [wide, along],
    )
    edge_theirs = shift(mine, True)
    got_x_theirs = swap(x_mine)
    zu, yu = call(
        functools.partial(u_kernel, half),
        "u_terms",
        (partial_sum, partial_sum),
        [velocity, metric],
        [pltpu.VMEM((half, ny, snaps, nz), bf16), wide, along],
    )

    def omega_yz(slot, near, far, edge):
        name = "omega_yz_mine" if slot else "omega_yz_theirs"
        args = [*near, *far, *edge, zu, yu, metric]
        return call(functools.partial(omega_yz_kernel, slot), name, pair, args)

    def gram_part(name, slots, shape, *args):
        return call(functools.partial(gram_kernel, slots), name, shape, args)

    def raw_modes(name, slots, own, got):
        kernel = functools.partial(raw_kernel, slots)
        return call(kernel, name, (raw,) * len(slots), [own, got, blocks])

    gram = gram_part("gram_x", (None,), square, x_mine, got_x_mine, volume)
    edge_theirs, gram = lax.optimization_barrier((edge_theirs, gram))
    yz_theirs = omega_yz(0, theirs, mine, edge_theirs)
    got_yz_mine = swap(yz_theirs)
    *late, _ = lax.optimization_barrier((*theirs, yz_theirs))
    edge_mine = shift(late, False)
    coeff_rows, blocks = call(
        coeff_kernel,
        "coeff_blocks",
        (
            jax.ShapeDtypeStruct((snaps, 2 * snaps), f32),
            jax.ShapeDtypeStruct((ROWS // snaps * snaps, ROWS // snaps * 2 * snaps), bf16),
        ),
        [coeffs],
    )
    (theirs_x,) = raw_modes("raw_x_theirs", (None,), x_theirs, got_x_theirs)
    (mine_x,) = raw_modes("raw_x_mine", (None,), x_mine, got_x_mine)
    edge_mine, theirs_x, mine_x = lax.optimization_barrier((edge_mine, theirs_x, mine_x))
    yz_mine = omega_yz(1, mine, theirs, edge_mine)
    got_yz_theirs = swap(yz_mine)
    copies = jax.ShapeDtypeStruct((peers, 4 * snaps**2 // nz, nz), f32)
    grams = gram_part("gram_yz", (0, 1), copies, yz_mine, got_yz_mine, volume, gram)
    grams = lax.all_to_all(grams, "space", 0, 0, tiled=True)
    gram = call(add_kernel, "add", square, [grams])
    other = swap(gram)
    mine_yz = raw_modes("raw_yz_mine", (0, 1), yz_mine, got_yz_mine)
    theirs_yz = raw_modes("raw_yz_theirs", (0, 1), yz_theirs, got_yz_theirs)
    modes, rows = call(
        functools.partial(finish_kernel, half, 1.0 / (3.0 * layers * peers * ny * nz)),
        "finish",
        (
            jax.ShapeDtypeStruct(velocity.shape, bf16),
            jax.ShapeDtypeStruct((snaps, 2 * snaps), f32),
        ),
        [gram, other, coeff_rows, theirs_x, *theirs_yz, mine_x, *mine_yz],
        [
            pltpu.VMEM(velocity.shape, bf16),
            pltpu.VMEM((snaps, 2 * snaps), f32),
            pltpu.VMEM((snaps, nz), f32),
            dma((5,)),
        ],
        None,
        (hbm(), hbm()),
    )
    return (rows, modes)


def per_device(velocity, metric, volume, coeffs):
    peers = lax.axis_size("space")
    paired = lax.axis_size("snap") == 2 and velocity.shape[2] == 2 * WIDTH
    if paired and velocity.shape[0] % 16 == 0 and peers & (peers - 1) == 0:
        return two_groups(velocity, metric, volume, coeffs)
    return many_groups(velocity, metric, volume, coeffs)


def solution(mesh):
    placed = (
        P("snap", None, "space", None, None),
        P(None, "space", None, None),
        P("space", None, None),
        P(),
    )
    return jax.shard_map(
        per_device,
        mesh=mesh,
        in_specs=placed,
        out_specs=(P("snap", None), P("snap", None, "space", None, None)),
        check_vma=False,
    )
```

```python
import functools

import jax
import jax.numpy as jnp
from jax import lax
from jax.experimental import pallas as pl
from jax.experimental.pallas import tpu as pltpu
from jax.sharding import PartitionSpec as P

EPS = 1e-06
WIDTH = 2
ROWS = 128
LIMIT = 24 * 1024 * 1024


def with_halo(shard, sides, width):
    for axis, dim in sides:
        peers, length = (lax.axis_size(axis), shard.shape[dim])
        up = [(i, (i + 1) % peers) for i in range(peers)]
        down = [(j, i) for i, j in up]
        last = lax.slice_in_dim(shard, length - width, length, axis=dim)
        leading = lax.slice_in_dim(shard, 0, width, axis=dim)
        before = lax.ppermute(last, axis, up)
        after = lax.ppermute(leading, axis, down)
        shard = jnp.concatenate([before, shard, after], axis=dim)
    return shard


def deriv(padded, dim):
    count = padded.shape[dim] - 4

    def cut(offset):
        return lax.slice_in_dim(padded, offset, offset + count, axis=dim)

    return (8.0 * (cut(3) - cut(1)) - (cut(4) - cut(0))) / 12.0


def curl(padded_x, metric):
    inner = padded_x[:, :, 2:-2]
    padded_y = jnp.pad(inner, ((0, 0), (0, 0), (0, 0), (2, 2), (0, 0)))
    padded_z = jnp.concatenate([inner[..., -2:], inner, inner[..., :2]], axis=4)
    along_x = deriv(padded_x, 2) * metric[0]
    along_y = deriv(padded_y, 3) * metric[1]
    along_z = deriv(padded_z, 4) * metric[2]
    omega_x = along_y[:, 2] - along_z[:, 1]
    omega_y = along_z[:, 0] - along_x[:, 2]
    omega_z = along_x[:, 1] - along_y[:, 0]
    return jnp.stack([omega_x, omega_y, omega_z], axis=1).astype(jnp.bfloat16)


def many_groups(velocity, metric, volume, coeffs):
    snap_dev = velocity.shape[0]
    snaps = coeffs.shape[0]
    group = lax.axis_index("snap")
    scale = 1.0 / (
        3.0 * volume.shape[0] * lax.axis_size("space") * volume.shape[1] * volume.shape[2]
    )
    padded = with_halo(velocity, (("space", 2),), 2)
    vorticity = curl(padded.astype(jnp.float32), metric)
    coeff_f = coeffs.astype(jnp.float32)
    moved = lax.all_to_all(vorticity, "snap", split_axis=3, concat_axis=0, tiled=True)
    part_y = moved.shape[3]
    vol_part = lax.dynamic_slice_in_dim(volume, group * part_y, part_y, 1)
    weighted = (moved.astype(jnp.float32) * vol_part).astype(jnp.bfloat16).reshape(snaps, -1)
    flat = moved.reshape(snaps, -1)
    partial_value = lax.dot_general(
        weighted, flat, (((1,), (1,)), ((), ())), preferred_element_type=jnp.float32
    )
    raw = lax.dot_general(
        coeffs, flat, (((0,), (0,)), ((), ())), preferred_element_type=jnp.float32
    )
    whole = lax.psum(partial_value, ("space", "snap")) * scale
    energy = jnp.sum(coeff_f * jnp.dot(whole, coeff_f, precision=lax.Precision.HIGHEST), axis=0)
    rows = lax.dynamic_slice_in_dim(whole, group * snap_dev, snap_dev, 0)
    local_modes = (raw / jnp.sqrt(energy + EPS)[:, None]).astype(jnp.bfloat16).reshape(moved.shape)
    modes = lax.all_to_all(local_modes, "snap", split_axis=0, concat_axis=3, tiled=True)
    return (rows, modes)


def vmem():
    return pl.BlockSpec(memory_space=pltpu.VMEM)


def hbm():
    return pl.BlockSpec(memory_space=pltpu.HBM)


def params():
    return pltpu.CompilerParams(vmem_limit_bytes=LIMIT)


def cost(flops, moved):
    return pl.CostEstimate(flops=flops, bytes_accessed=moved, transcendentals=0)


def z_stencil(size):
    rows = lax.broadcasted_iota(jnp.int32, (size, size), 0)
    cols = lax.broadcasted_iota(jnp.int32, (size, size), 1)
    ahead = rows - cols
    ahead = jnp.where(ahead < 0, ahead + size, ahead)
    out = jnp.where(ahead == 1, 8.0, 0.0) - jnp.where(ahead == size - 1, 8.0, 0.0)
    out = out - jnp.where(ahead == 2, 1.0, 0.0) + jnp.where(ahead == size - 2, 1.0, 0.0)
    return out.astype(jnp.bfloat16)


def spread(src, wide):
    snaps, ny, nz = src.shape
    wide[...] = src.astype(jnp.float32).reshape(snaps * ny, nz)


def row(wide, y, snaps, ny):
    return wide[pl.ds(y, snaps, ny), :]


def y_stencils(load, ny):
    held = {}

    def at(j):
        if j not in held:
            held[j] = load(j)
        return held[j]

    zero = jnp.zeros_like(at(0))
    for y in range(ny):
        near = (at(y + 1) if y + 1 < ny else zero) - (at(y - 1) if y >= 1 else zero)
        far = (at(y + 2) if y + 2 < ny else zero) - (at(y - 2) if y >= 2 else zero)
        held.pop(y - 2, None)
        yield y, 8.0 * near - far


def z_derivative(field, matrix, along):
    rows = field.shape[0] * field.shape[1] * field.shape[2]
    along[...] = jnp.dot(
        field.reshape(rows, field.shape[3]), matrix, preferred_element_type=jnp.float32
    ).reshape(field.shape)


def factor(metric_ref, m, layer, y):
    return metric_ref[m, layer, pl.ds(y, 1), :] * (1.0 / 12.0)


def flip(src, wide, out_ref, i):
    snaps, ny, _ = src.shape
    spread(src, wide)
    for y in range(ny):
        out_ref[i, y] = row(wide, y, snaps, ny).astype(jnp.bfloat16)


def omega_x_kernel(vel_ref, metric_ref, theirs_ref, mine_ref, ox_ref, buf, factors, wide, along, sems):
    snaps, _, layers, ny, nz = buf.shape
    half = layers // 2
    group = lax.axis_index("snap")
    bases = ((1 - group) * half, group * half)
    copies = {}
    for slot in range(2):
        rows = pl.ds(bases[slot], half)
        inner = pl.ds(slot * half, half)
        for c in range(2):
            source, target = vel_ref.at[:, 1 + c, rows], buf.at[:, c, inner]
            copies[slot, c] = pltpu.make_async_copy(source, target, sems.at[slot, c])
            copies[slot, c].start()
        source, target = metric_ref.at[1:3, rows], factors.at[:, inner]
        copies[slot, 2] = pltpu.make_async_copy(source, target, sems.at[slot, 2])
        copies[slot, 2].start()
    matrix = z_stencil(nz)
    for slot, vw_ref in enumerate((theirs_ref, mine_ref)):
        copies[slot, 0].wait()
        for i in range(half):
            flip(buf[:, 0, slot * half + i], wide, vw_ref.at[0], i)
        z_derivative(vw_ref[0], matrix, along)
        copies[slot, 1].wait()
        copies[slot, 2].wait()
        for i in range(half):
            spread(buf[:, 1, slot * half + i], wide)

            def load(j):
                value = row(wide, j, snaps, ny)
                vw_ref[1, i, j] = value.astype(jnp.bfloat16)
                return value

            for y, across in y_stencils(load, ny):
                value = across * factor(factors, 0, slot * half + i, y)
                value = value - along[i, y] * factor(factors, 1, slot * half + i, y)
                ox_ref[slot, i, y] = value.astype(jnp.bfloat16)


def u_kernel(half, vel_ref, metric_ref, zu_ref, yu_ref, flat, wide, along):
    snaps, _, _, ny, nz = vel_ref.shape
    matrix = z_stencil(nz)
    group = lax.axis_index("snap")
    for slot in range(2):
        base = (group if slot else 1 - group) * half
        for i in range(half):
            spread(vel_ref[:, 0, base + i], wide)

            def load(j):
                value = row(wide, j, snaps, ny)
                flat[i, j] = value.astype(jnp.bfloat16)
                return value

            for y, across in y_stencils(load, ny):
                yu_ref[slot, i, y] = across * factor(metric_ref, 1, base + i, y)
        z_derivative(flat[...], matrix, along)
        for i in range(half):
            for y in range(ny):
                zu_ref[slot, i, y] = along[i, y] * factor(metric_ref, 2, base + i, y)


def finish_curl(sign, slot, near_ref, far_ref, halo_ref, known_ref, metric_ref, out_ref):
    half, ny, _, _ = near_ref.shape
    group = lax.axis_index("snap")
    part = group if slot else 1 - group

    def run(low_ref, high_ref):
        def plane(i, y):
            if i < 0:
                ref, k = low_ref, half + i
            elif i < half:
                ref, k = near_ref, i
            else:
                ref, k = high_ref, i - half
            return ref[k, y].astype(jnp.float32)

        for y in range(ny):
            at = [plane(i, y) for i in range(-WIDTH, half + WIDTH)]
            for i in range(half):
                along = 8.0 * (at[i + 3] - at[i + 1]) - (at[i + 4] - at[i])
                along = along * factor(metric_ref, 0, part * half + i, y)
                known = known_ref[slot, i, y]
                value = along - known if sign > 0 else known - along
                out_ref[i, y] = value.astype(jnp.bfloat16)

    @pl.when(part == 0)
    def _():
        run(halo_ref, far_ref)

    @pl.when(part == 1)
    def _():
        run(far_ref, halo_ref)


def omega_yz_kernel(slot, near, far, edge, zu_ref, yu_ref, metric_ref, out_ref):
    known = (yu_ref, zu_ref)
    for c, sign in ((1, -1), (0, 1)):
        fields = near.at[c], far.at[c], edge.at[c], known[c]
        finish_curl(sign, slot, *fields, metric_ref, out_ref.at[1 - c])


def gram_of(own, got, volume_ref, base):
    half, ny, _, _ = own.shape
    total = None
    for i in range(half):
        plain, heavy = [], []
        for y in range(ny):
            pair = jnp.concatenate([own[i, y], got[i, y]], axis=0)
            weight = volume_ref[base + i, pl.ds(y, 1), :]
            plain.append(pair)
            heavy.append((pair.astype(jnp.float32) * weight).astype(jnp.bfloat16))
        part = lax.dot_general(
            jnp.concatenate(heavy, axis=1),
            jnp.concatenate(plain, axis=1),
            (((1,), (1,)), ((), ())),
            preferred_element_type=jnp.float32,
        )
        total = part if total is None else total + part
    return total


def gram_kernel(own_refs, got_refs, own, got, volume_ref, *refs):
    base = lax.axis_index("snap") * own.shape[1]
    total = sum(gram_of(own.at[n], got.at[m], volume_ref, base) for n, m in zip(own_refs, got_refs))
    for earlier in refs[:-1]:
        total = total + earlier[...]
    if len(refs[-1].shape) == 3:
        count, rows, _ = refs[-1].shape
        total = jnp.concatenate(
            [total[n : n + rows] for n in range(0, total.shape[0], rows)], axis=1
        )
        for peer in range(count):
            refs[-1][peer] = total
    else:
        refs[-1][...] = total


def add_kernel(parts_ref, own_ref, other_ref):
    peers, rows, _ = parts_ref.shape
    group = lax.axis_index("snap")
    side = own_ref.shape[0]
    for out_ref, first in ((own_ref, group), (other_ref, 1 - group)):
        parts = [parts_ref[n + first] for n in range(0, peers, 2)]
        while len(parts) > 1:
            parts = [sum(parts[n : n + 2]) for n in range(0, len(parts), 2)]
        for n in range(side // rows):
            out_ref[n * rows : (n + 1) * rows] = parts[0][:, n * side : (n + 1) * side]


def coeff_kernel(coeff_ref, mine_ref, block_ref):
    snaps, count = mine_ref.shape
    rows = block_ref.shape[0]
    base = lax.axis_index("snap") * snaps

    def chosen(shape, test):
        left = lax.broadcasted_iota(jnp.int32, shape, 0)
        right = lax.broadcasted_iota(jnp.int32, shape, 1)
        return jnp.where(test(left, right), 1.0, 0.0).astype(jnp.bfloat16)

    def take(a, b, dims):
        out = lax.dot_general(a, b, (dims, ((), ())), preferred_element_type=jnp.float32)
        return out.astype(jnp.bfloat16)

    mine = chosen((snaps, count), lambda k, m: m == k + base)
    mine = take(mine, coeff_ref[...], ((1,), (1,)))
    order = chosen((count, count), lambda j, m: j == lax.rem(m + base, count))
    mine = take(mine, order, ((1,), (0,)))
    mine_ref[...] = mine.astype(jnp.float32)
    down = chosen((rows, snaps), lambda r, k: lax.rem(r, snaps) == k)
    for part in range(count // snaps):
        across = chosen((count, rows), lambda j, c: j == lax.rem(c, snaps) + part * snaps)
        wide = take(take(down, mine, ((1,), (0,))), across, ((1,), (0,)))
        same = chosen((rows, rows), lambda r, c: lax.div(r, snaps) == lax.div(c, snaps))
        block_ref[:, part * rows : (part + 1) * rows] = wide * same


def raw_blocks(own, got, block_ref, put):
    ny, snaps, nz = own.shape
    block = block_ref.shape[0] // snaps
    lanes = 2 if ny % (2 * block) == 0 else 1
    for start in range(0, ny, block * lanes):
        columns = []
        for n in range(lanes):
            at = start + n * block
            parts = [ref[at : at + block].reshape(block * snaps, nz) for ref in (own, got)]
            columns.append(jnp.concatenate(parts, axis=0))
        both = columns[0] if lanes == 1 else jnp.concatenate(columns, axis=1)
        raw = jnp.dot(block_ref[...], both, preferred_element_type=jnp.float32)
        for n in range(lanes):
            part = raw[:, n * nz : (n + 1) * nz].reshape(block, snaps, nz)
            for k in range(block):
                put(start + n * block + k, part[k])


def raw_kernel(picks, block_ref, *refs):
    outs = refs[-len(picks) :]

    def field(pick):
        ref, slot = pick
        return refs[ref] if slot is None else refs[ref].at[slot]

    for (own_pick, got_pick), out_ref in zip(picks, outs):
        own, got = field(own_pick), field(got_pick)
        half, ny, snaps, _ = own.shape
        for i in range(half):

            def put(y, value):
                out_ref[pl.ds(i * ny + y, snaps, half * ny), :] = value

            raw_blocks(own.at[i], got.at[i], block_ref, put)


def finish_kernel(
    half, scale, part_ref, other_ref, coeff_ref, block_ref,
    x_theirs, x_mine, own_theirs, own_mine, got_theirs, got_mine,
    out_ref, rows_ref, stage, rows_buf, factors, wide, sems,
):
    _, snaps, _, ny, nz = stage.shape
    group = lax.axis_index("snap")
    other = other_ref[...]
    other = jnp.concatenate([other[snaps:], other[:snaps]], axis=0)
    other = jnp.concatenate([other[:, snaps:], other[:, :snaps]], axis=1)
    total = (part_ref[...] + other) * scale
    coeff = coeff_ref[...]
    inner = jnp.dot(
        coeff, total, precision=lax.Precision.HIGHEST, preferred_element_type=jnp.float32
    )
    energy = jnp.sum(inner * coeff, axis=1, keepdims=True)
    factor = jnp.broadcast_to(1.0 / jnp.sqrt(energy + EPS), (snaps, nz))
    factors[...] = factor
    mine = total[:snaps]
    turned = jnp.concatenate([mine[:, snaps:], mine[:, :snaps]], axis=1)
    rows_buf[...] = jnp.where(group == 0, mine, turned)
    copies = [pltpu.make_async_copy(rows_buf, rows_ref, sems.at[6])]
    copies[0].start()
    bases = (1 - group) * half, group * half

    def send(c, slot):
        n = 2 * c + slot
        target = out_ref.at[:, c, pl.ds(bases[slot], half)]
        copies.append(pltpu.make_async_copy(stage.at[n], target, sems.at[n]))
        copies[-1].start()

    for slot, raw_ref in ((0, x_theirs), (1, x_mine)):
        for k in range(snaps):
            value = raw_ref[k * half * ny : (k + 1) * half * ny, :] * factors[k : k + 1, :]
            stage[slot, k] = value.astype(jnp.bfloat16).reshape(half, ny, nz)
        send(0, slot)
    for slot, own, got in ((1, own_mine, got_mine), (0, own_theirs, got_theirs)):
        for c in range(2):
            for i in range(half):

                def put(y, value):
                    wide[i, pl.ds(y, snaps, ny), :] = value * factor

                raw_blocks(own.at[c, i], got.at[c, i], block_ref, put)
                for k in range(snaps):
                    value = wide[i, k * ny : (k + 1) * ny, :]
                    stage[2 * (c + 1) + slot, k, i] = value.astype(jnp.bfloat16)
            send(c + 1, slot)
    for copy in copies:
        copy.wait()


def two_groups(velocity, metric, volume, coeffs):
    snaps, _, layers, ny, nz = velocity.shape
    half = layers // 2
    peers = lax.axis_size("space")
    bf16, f32 = jnp.bfloat16, jnp.float32

    def halo(first):
        pairs = []
        for s in range(peers):
            for g in range(2):
                down = (g == 0) == first
                pairs.append((s * 2 + g, ((s + (-1 if down else 1)) % peers) * 2 + g))
        return pairs

    def swap(value):
        return lax.ppermute(value, "snap", [(0, 1), (1, 0)])

    def shift(value, first):
        return lax.ppermute(value, ("space", "snap"), halo(first))

    pair = jax.ShapeDtypeStruct((2, half, ny, snaps, nz), bf16)
    partial_sum = jax.ShapeDtypeStruct((2, half, ny, snaps, nz), f32)
    square = jax.ShapeDtypeStruct((2 * snaps, 2 * snaps), f32)
    raw = jax.ShapeDtypeStruct((snaps * half * ny, nz), f32)
    cells = half * ny * snaps * nz
    wide = pltpu.VMEM((snaps * ny, nz), f32)
    along = pltpu.VMEM((half, ny, snaps, nz), f32)
    dma = pltpu.SemaphoreType.DMA

    def call(kernel, name, out_shape, args, scratch=(), in_specs=None, out_specs=None, work=5):
        return pl.pallas_call(
            kernel,
            out_shape=out_shape,
            in_specs=in_specs or [vmem()] * len(args),
            out_specs=out_specs or jax.tree.map(lambda _: vmem(), out_shape),
            scratch_shapes=list(scratch),
            compiler_params=params(),
            cost_estimate=cost(2 * work * cells, work * cells),
            name=name,
        )(*args)

    theirs, mine, ox = call(
        omega_x_kernel,
        "omega_x",
        (pair, pair, pair),
        [pltpu.with_memory_space_constraint(a, pltpu.HBM) for a in (velocity, metric)],
        [
            pltpu.VMEM((snaps, 2, layers, ny, nz), bf16),
            pltpu.VMEM((2, layers, ny, nz), f32),
            wide,
            along,
            dma((2, 3)),
        ],
        [hbm()] * 2,
    )
    got_x = swap(ox)
    edge_theirs = shift(mine, True)
    zu, yu = call(
        functools.partial(u_kernel, half),
        "u_terms",
        (partial_sum, partial_sum),
        [velocity, metric],
        [pltpu.VMEM((half, ny, snaps, nz), bf16), wide, along],
    )

    def omega_yz(slot, near, far, edge):
        name = "omega_yz_mine" if slot else "omega_yz_theirs"
        args = [near, far, edge, zu, yu, metric]
        return call(functools.partial(omega_yz_kernel, slot), name, pair, args)

    yz_theirs = omega_yz(0, theirs, mine, edge_theirs)
    got_yz = swap(yz_theirs)
    late, _ = lax.optimization_barrier((theirs, yz_theirs))
    edge_mine = shift(late, False)

    coeff_rows, blocks = call(
        coeff_kernel,
        "coeff_blocks",
        (
            jax.ShapeDtypeStruct((snaps, 2 * snaps), f32),
            jax.ShapeDtypeStruct((ROWS // snaps * snaps, ROWS // snaps * 2 * snaps), bf16),
        ),
        [coeffs],
    )
    gram = call(functools.partial(gram_kernel, (1,), (0,)), "gram_x", square, [ox, got_x, volume])
    kernel = functools.partial(raw_kernel, (((0, 1), (1, 0)), ((0, 0), (1, 1))))
    mine_x, theirs_x = call(kernel, "raw_x", (raw, raw), [blocks, ox, got_x])
    edge_mine, mine_x, gram = lax.optimization_barrier((edge_mine, mine_x, gram))
    yz_mine = omega_yz(1, mine, theirs, edge_mine)
    got_yz_theirs = swap(yz_mine)
    copies = jax.ShapeDtypeStruct((2 * peers, 4 * snaps**2 // nz, nz), f32)
    grams = call(
        functools.partial(gram_kernel, (0, 1), (0, 1)),
        "gram_yz",
        copies,
        [yz_mine, got_yz, volume, gram],
    )

    grams = lax.all_to_all(grams, ("space", "snap"), 0, 0, tiled=True)
    gram, other = call(add_kernel, "add", (square, square), [grams])

    modes, rows = call(
        functools.partial(finish_kernel, half, 1.0 / (3.0 * layers * peers * ny * nz)),
        "finish",
        (
            jax.ShapeDtypeStruct(velocity.shape, bf16),
            jax.ShapeDtypeStruct((snaps, 2 * snaps), f32),
        ),
        [
            gram, other, coeff_rows, blocks, theirs_x, mine_x,
            yz_theirs, yz_mine, got_yz_theirs, got_yz,
        ],
        [
            pltpu.VMEM((6, snaps, half, ny, nz), bf16),
            pltpu.VMEM((snaps, 2 * snaps), f32),
            pltpu.VMEM((snaps, nz), f32),
            pltpu.VMEM((half, snaps * ny, nz), f32),
            dma((7,)),
        ],
        None,
        (hbm(), hbm()),
    )
    return (rows, modes)


def per_device(velocity, metric, volume, coeffs):
    peers = lax.axis_size("space")
    paired = lax.axis_size("snap") == 2 and velocity.shape[2] == 2 * WIDTH
    if paired and velocity.shape[0] % 16 == 0 and peers & (peers - 1) == 0:
        return two_groups(velocity, metric, volume, coeffs)
    return many_groups(velocity, metric, volume, coeffs)


def solution(mesh):
    placed = (
        P("snap", None, "space", None, None),
        P(None, "space", None, None),
        P("space", None, None),
        P(),
    )
    return jax.shard_map(
        per_device,
        mesh=mesh,
        in_specs=placed,
        out_specs=(P("snap", None), P("snap", None, "space", None, None)),
        check_vma=False,
    )
```

```python
import functools

import jax
import jax.numpy as jnp
from jax import lax
from jax.experimental import pallas as pl
from jax.experimental.pallas import tpu as pltpu
from jax.sharding import PartitionSpec as P

EPS = 1e-06
WIDTH = 2
ROWS = 128
LIMIT = 24 * 1024 * 1024


def with_halo(shard, sides, width):
    for axis, dim in sides:
        peers, length = (lax.axis_size(axis), shard.shape[dim])
        up = [(i, (i + 1) % peers) for i in range(peers)]
        down = [(j, i) for i, j in up]
        last = lax.slice_in_dim(shard, length - width, length, axis=dim)
        leading = lax.slice_in_dim(shard, 0, width, axis=dim)
        before = lax.ppermute(last, axis, up)
        after = lax.ppermute(leading, axis, down)
        shard = jnp.concatenate([before, shard, after], axis=dim)
    return shard


def deriv(padded, dim):
    count = padded.shape[dim] - 4

    def cut(offset):
        return lax.slice_in_dim(padded, offset, offset + count, axis=dim)

    return (8.0 * (cut(3) - cut(1)) - (cut(4) - cut(0))) / 12.0


def curl(padded_x, metric):
    inner = padded_x[:, :, 2:-2]
    padded_y = jnp.pad(inner, ((0, 0), (0, 0), (0, 0), (2, 2), (0, 0)))
    padded_z = jnp.concatenate([inner[..., -2:], inner, inner[..., :2]], axis=4)
    along_x = deriv(padded_x, 2) * metric[0]
    along_y = deriv(padded_y, 3) * metric[1]
    along_z = deriv(padded_z, 4) * metric[2]
    omega_x = along_y[:, 2] - along_z[:, 1]
    omega_y = along_z[:, 0] - along_x[:, 2]
    omega_z = along_x[:, 1] - along_y[:, 0]
    return jnp.stack([omega_x, omega_y, omega_z], axis=1).astype(jnp.bfloat16)


def many_groups(velocity, metric, volume, coeffs):
    snap_dev = velocity.shape[0]
    snaps = coeffs.shape[0]
    group = lax.axis_index("snap")
    scale = 1.0 / (
        3.0 * volume.shape[0] * lax.axis_size("space") * volume.shape[1] * volume.shape[2]
    )
    padded = with_halo(velocity, (("space", 2),), 2)
    vorticity = curl(padded.astype(jnp.float32), metric)
    coeff_f = coeffs.astype(jnp.float32)
    moved = lax.all_to_all(vorticity, "snap", split_axis=3, concat_axis=0, tiled=True)
    part_y = moved.shape[3]
    vol_part = lax.dynamic_slice_in_dim(volume, group * part_y, part_y, 1)
    weighted = (moved.astype(jnp.float32) * vol_part).astype(jnp.bfloat16).reshape(snaps, -1)
    flat = moved.reshape(snaps, -1)
    partial_value = lax.dot_general(
        weighted, flat, (((1,), (1,)), ((), ())), preferred_element_type=jnp.float32
    )
    raw = lax.dot_general(
        coeffs, flat, (((0,), (0,)), ((), ())), preferred_element_type=jnp.float32
    )
    whole = lax.psum(partial_value, ("space", "snap")) * scale
    energy = jnp.sum(coeff_f * jnp.dot(whole, coeff_f, precision=lax.Precision.HIGHEST), axis=0)
    rows = lax.dynamic_slice_in_dim(whole, group * snap_dev, snap_dev, 0)
    local_modes = (raw / jnp.sqrt(energy + EPS)[:, None]).astype(jnp.bfloat16).reshape(moved.shape)
    modes = lax.all_to_all(local_modes, "snap", split_axis=0, concat_axis=3, tiled=True)
    return (rows, modes)


def vmem():
    return pl.BlockSpec(memory_space=pltpu.VMEM)


def hbm():
    return pl.BlockSpec(memory_space=pltpu.HBM)


def params():
    return pltpu.CompilerParams(vmem_limit_bytes=LIMIT)


def cost(flops, moved):
    return pl.CostEstimate(flops=flops, bytes_accessed=moved, transcendentals=0)


def z_stencil(size):
    rows = lax.broadcasted_iota(jnp.int32, (size, size), 0)
    cols = lax.broadcasted_iota(jnp.int32, (size, size), 1)
    ahead = rows - cols
    ahead = jnp.where(ahead < 0, ahead + size, ahead)
    out = jnp.where(ahead == 1, 8.0, 0.0) - jnp.where(ahead == size - 1, 8.0, 0.0)
    out = out - jnp.where(ahead == 2, 1.0, 0.0) + jnp.where(ahead == size - 2, 1.0, 0.0)
    return out.astype(jnp.bfloat16)


def spread(src, wide):
    snaps, ny, nz = src.shape
    wide[...] = src.astype(jnp.float32).reshape(snaps * ny, nz)


def row(wide, y, snaps, ny):
    return wide[pl.ds(y, snaps, ny), :]


def y_stencils(load, ny):
    held = {}

    def at(j):
        if j not in held:
            held[j] = load(j)
        return held[j]

    zero = jnp.zeros_like(at(0))
    for y in range(ny):
        near = (at(y + 1) if y + 1 < ny else zero) - (at(y - 1) if y >= 1 else zero)
        far = (at(y + 2) if y + 2 < ny else zero) - (at(y - 2) if y >= 2 else zero)
        held.pop(y - 2, None)
        yield y, 8.0 * near - far


def z_derivative(field, matrix, along):
    rows = field.shape[0] * field.shape[1] * field.shape[2]
    along[...] = jnp.dot(
        field.reshape(rows, field.shape[3]), matrix, preferred_element_type=jnp.float32
    ).reshape(field.shape)


def factor(metric_ref, m, layer, y):
    return metric_ref[m, layer, pl.ds(y, 1), :] * (1.0 / 12.0)


def flip(src, wide, out_ref, i):
    snaps, ny, _ = src.shape
    spread(src, wide)
    for y in range(ny):
        out_ref[i, y] = row(wide, y, snaps, ny).astype(jnp.bfloat16)


def flip_kernel(vel_ref, out_ref, buf, wide, sems):
    half = out_ref.shape[1]
    base = lax.axis_index("snap") * half
    copies = {}
    for c in range(2):
        for i in range(half):
            source = vel_ref.at[:, 1 + c, base + i]
            copies[c, i] = pltpu.make_async_copy(source, buf.at[:, c, i], sems.at[c, i])
            copies[c, i].start()
    for c in range(2):
        for i in range(half):
            copies[c, i].wait()
            flip(buf[:, c, i], wide, out_ref.at[c], i)


def omega_x_kernel(vel_ref, metric_ref, mine_ref, vw_ref, ox_ref, wide, along):
    _, half, ny, snaps, nz = ox_ref.shape
    group = lax.axis_index("snap")
    matrix = z_stencil(nz)
    for slot, base in ((0, (1 - group) * half), (1, group * half)):
        fields = mine_ref if slot else vw_ref
        if slot == 0:
            for i in range(half):
                flip(vel_ref[:, 1, base + i], wide, vw_ref.at[0], i)
        z_derivative(fields[0], matrix, along)
        for i in range(half):
            if slot == 0:
                spread(vel_ref[:, 2, base + i], wide)

            def load(j):
                if slot:
                    return mine_ref[1, i, j].astype(jnp.float32)
                value = row(wide, j, snaps, ny)
                vw_ref[1, i, j] = value.astype(jnp.bfloat16)
                return value

            for y, across in y_stencils(load, ny):
                value = across * factor(metric_ref, 1, base + i, y)
                value = value - along[i, y] * factor(metric_ref, 2, base + i, y)
                ox_ref[slot, i, y] = value.astype(jnp.bfloat16)


def u_kernel(half, vel_ref, metric_ref, zu_ref, yu_ref, flat, wide, along):
    snaps, _, _, ny, nz = vel_ref.shape
    matrix = z_stencil(nz)
    group = lax.axis_index("snap")
    for slot in range(2):
        base = (group if slot else 1 - group) * half
        for i in range(half):
            spread(vel_ref[:, 0, base + i], wide)

            def load(j):
                value = row(wide, j, snaps, ny)
                flat[i, j] = value.astype(jnp.bfloat16)
                return value

            for y, across in y_stencils(load, ny):
                yu_ref[slot, i, y] = across * factor(metric_ref, 1, base + i, y)
        z_derivative(flat[...], matrix, along)
        for i in range(half):
            for y in range(ny):
                zu_ref[slot, i, y] = along[i, y] * factor(metric_ref, 2, base + i, y)


def finish_curl(sign, slot, near_ref, far_ref, halo_ref, known_ref, metric_ref, out_ref):
    half, ny, _, _ = near_ref.shape
    group = lax.axis_index("snap")
    part = group if slot else 1 - group

    def run(low_ref, high_ref):
        def plane(i, y):
            if i < 0:
                ref, k = low_ref, half + i
            elif i < half:
                ref, k = near_ref, i
            else:
                ref, k = high_ref, i - half
            return ref[k, y].astype(jnp.float32)

        for y in range(ny):
            at = [plane(i, y) for i in range(-WIDTH, half + WIDTH)]
            for i in range(half):
                along = 8.0 * (at[i + 3] - at[i + 1]) - (at[i + 4] - at[i])
                along = along * factor(metric_ref, 0, part * half + i, y)
                known = known_ref[slot, i, y]
                value = along - known if sign > 0 else known - along
                out_ref[i, y] = value.astype(jnp.bfloat16)

    @pl.when(part == 0)
    def _():
        run(halo_ref, far_ref)

    @pl.when(part == 1)
    def _():
        run(far_ref, halo_ref)


def omega_yz_kernel(slot, near, far, edge, zu_ref, yu_ref, metric_ref, out_ref):
    known = (yu_ref, zu_ref)
    for c, sign in ((1, -1), (0, 1)):
        fields = near.at[c], far.at[c], edge.at[c], known[c]
        finish_curl(sign, slot, *fields, metric_ref, out_ref.at[1 - c])


def gram_of(own, got, volume_ref, base):
    half, ny, _, _ = own.shape
    total = None
    for i in range(half):
        plain, heavy = [], []
        for y in range(ny):
            pair = jnp.concatenate([own[i, y], got[i, y]], axis=0)
            weight = volume_ref[base + i, pl.ds(y, 1), :]
            plain.append(pair)
            heavy.append((pair.astype(jnp.float32) * weight).astype(jnp.bfloat16))
        part = lax.dot_general(
            jnp.concatenate(heavy, axis=1),
            jnp.concatenate(plain, axis=1),
            (((1,), (1,)), ((), ())),
            preferred_element_type=jnp.float32,
        )
        total = part if total is None else total + part
    return total


def gram_kernel(slots, own, got, volume_ref, *refs):
    base = lax.axis_index("snap") * volume_ref.shape[0] // 2
    total = sum(gram_of(own.at[n], got.at[m], volume_ref, base) for n, m in slots)
    for earlier in refs[:-1]:
        total = total + earlier[...]
    if len(refs[-1].shape) == 3:
        count, rows, _ = refs[-1].shape
        total = jnp.concatenate(
            [total[n : n + rows] for n in range(0, total.shape[0], rows)], axis=1
        )
        for peer in range(count):
            refs[-1][peer] = total
    else:
        refs[-1][...] = total


def add_kernel(parts_ref, own_ref, other_ref):
    peers, rows, _ = parts_ref.shape
    group = lax.axis_index("snap")
    side = own_ref.shape[0]
    for out_ref, first in ((own_ref, group), (other_ref, 1 - group)):
        parts = [parts_ref[n + first] for n in range(0, peers, 2)]
        while len(parts) > 1:
            parts = [sum(parts[n : n + 2]) for n in range(0, len(parts), 2)]
        for n in range(side // rows):
            out_ref[n * rows : (n + 1) * rows] = parts[0][:, n * side : (n + 1) * side]


def coeff_kernel(coeff_ref, mine_ref, block_ref):
    snaps, count = mine_ref.shape
    rows = block_ref.shape[0]
    base = lax.axis_index("snap") * snaps

    def chosen(shape, test):
        left = lax.broadcasted_iota(jnp.int32, shape, 0)
        right = lax.broadcasted_iota(jnp.int32, shape, 1)
        return jnp.where(test(left, right), 1.0, 0.0).astype(jnp.bfloat16)

    def take(a, b, dims):
        out = lax.dot_general(a, b, (dims, ((), ())), preferred_element_type=jnp.float32)
        return out.astype(jnp.bfloat16)

    mine = chosen((snaps, count), lambda k, m: m == k + base)
    mine = take(mine, coeff_ref[...], ((1,), (1,)))
    order = chosen((count, count), lambda j, m: j == lax.rem(m + base, count))
    mine = take(mine, order, ((1,), (0,)))
    mine_ref[...] = mine.astype(jnp.float32)
    down = chosen((rows, snaps), lambda r, k: lax.rem(r, snaps) == k)
    for part in range(count // snaps):
        across = chosen((count, rows), lambda j, c: j == lax.rem(c, snaps) + part * snaps)
        wide = take(take(down, mine, ((1,), (0,))), across, ((1,), (0,)))
        same = chosen((rows, rows), lambda r, c: lax.div(r, snaps) == lax.div(c, snaps))
        block_ref[:, part * rows : (part + 1) * rows] = wide * same


def raw_blocks(own, got, block_ref, put):
    ny, snaps, nz = own.shape
    block = block_ref.shape[0] // snaps
    lanes = 2 if ny % (2 * block) == 0 else 1
    for start in range(0, ny, block * lanes):
        columns = []
        for n in range(lanes):
            at = start + n * block
            parts = [ref[at : at + block].reshape(block * snaps, nz) for ref in (own, got)]
            columns.append(jnp.concatenate(parts, axis=0))
        both = columns[0] if lanes == 1 else jnp.concatenate(columns, axis=1)
        raw = jnp.dot(block_ref[...], both, preferred_element_type=jnp.float32)
        for n in range(lanes):
            part = raw[:, n * nz : (n + 1) * nz].reshape(block, snaps, nz)
            for k in range(block):
                put(start + n * block + k, part[k])


def raw_kernel(slots, own_ref, got_ref, block_ref, *outs):
    for (n, m), out_ref in zip(slots, outs):
        own, got = own_ref.at[n], got_ref.at[m]
        half, ny, snaps, _ = own.shape
        for i in range(half):

            def put(y, value):
                out_ref[pl.ds(i * ny + y, snaps, half * ny), :] = value

            raw_blocks(own.at[i], got.at[i], block_ref, put)


def finish_kernel(
    half, scale, part_ref, other_ref, coeff_ref, block_ref,
    x_theirs, x_mine, y_mine, z_mine, own_theirs, got_theirs,
    out_ref, rows_ref, stage, rows_buf, factors, wide, sems,
):
    _, snaps, _, ny, nz = stage.shape
    group = lax.axis_index("snap")
    other = other_ref[...]
    other = jnp.concatenate([other[snaps:], other[:snaps]], axis=0)
    other = jnp.concatenate([other[:, snaps:], other[:, :snaps]], axis=1)
    total = (part_ref[...] + other) * scale
    coeff = coeff_ref[...]
    inner = jnp.dot(
        coeff, total, precision=lax.Precision.HIGHEST, preferred_element_type=jnp.float32
    )
    energy = jnp.sum(inner * coeff, axis=1, keepdims=True)
    factor = jnp.broadcast_to(1.0 / jnp.sqrt(energy + EPS), (snaps, nz))
    factors[...] = factor
    mine = total[:snaps]
    turned = jnp.concatenate([mine[:, snaps:], mine[:, :snaps]], axis=1)
    rows_buf[...] = jnp.where(group == 0, mine, turned)
    copies = [pltpu.make_async_copy(rows_buf, rows_ref, sems.at[6])]
    copies[0].start()
    bases = (1 - group) * half, group * half

    def send(c, slot):
        n = 2 * c + slot
        target = out_ref.at[:, c, pl.ds(bases[slot], half)]
        copies.append(pltpu.make_async_copy(stage.at[n], target, sems.at[n]))
        copies[-1].start()

    for c, slot, raw_ref in ((0, 0, x_theirs), (0, 1, x_mine), (1, 1, y_mine), (2, 1, z_mine)):
        for k in range(snaps):
            value = raw_ref[k * half * ny : (k + 1) * half * ny, :] * factors[k : k + 1, :]
            stage[2 * c + slot, k] = value.astype(jnp.bfloat16).reshape(half, ny, nz)
        send(c, slot)
    for c in range(2):
        for i in range(half):

            def put(y, value):
                wide[i, pl.ds(y, snaps, ny), :] = value * factor

            raw_blocks(own_theirs.at[c, i], got_theirs.at[c, i], block_ref, put)
            for k in range(snaps):
                value = wide[i, k * ny : (k + 1) * ny, :]
                stage[2 * (c + 1), k, i] = value.astype(jnp.bfloat16)
        send(c + 1, 0)
    for copy in copies:
        copy.wait()


def two_groups(velocity, metric, volume, coeffs):
    snaps, _, layers, ny, nz = velocity.shape
    half = layers // 2
    peers = lax.axis_size("space")
    bf16, f32 = jnp.bfloat16, jnp.float32

    def halo(first):
        pairs = []
        for s in range(peers):
            for g in range(2):
                down = (g == 0) == first
                pairs.append((s * 2 + g, ((s + (-1 if down else 1)) % peers) * 2 + g))
        return pairs

    def swap(value):
        return lax.ppermute(value, "snap", [(0, 1), (1, 0)])

    def shift(value, first):
        return lax.ppermute(value, ("space", "snap"), halo(first))

    field = jax.ShapeDtypeStruct((half, ny, snaps, nz), bf16)
    pair = jax.ShapeDtypeStruct((2, half, ny, snaps, nz), bf16)
    partial_sum = jax.ShapeDtypeStruct((2, half, ny, snaps, nz), f32)
    square = jax.ShapeDtypeStruct((2 * snaps, 2 * snaps), f32)
    raw = jax.ShapeDtypeStruct((snaps * half * ny, nz), f32)
    cells = half * ny * snaps * nz
    wide = pltpu.VMEM((snaps * ny, nz), f32)
    along = pltpu.VMEM((half, ny, snaps, nz), f32)
    dma = pltpu.SemaphoreType.DMA

    def call(kernel, name, out_shape, args, scratch=(), in_specs=None, out_specs=None, work=5):
        return pl.pallas_call(
            kernel,
            out_shape=out_shape,
            in_specs=in_specs or [vmem()] * len(args),
            out_specs=out_specs or jax.tree.map(lambda _: vmem(), out_shape),
            scratch_shapes=list(scratch),
            compiler_params=params(),
            cost_estimate=cost(2 * work * cells, work * cells),
            name=name,
        )(*args)

    mine = call(
        flip_kernel,
        "flip_mine",
        pair,
        [pltpu.with_memory_space_constraint(velocity, pltpu.HBM)],
        [pltpu.VMEM((snaps, 2, half, ny, nz), bf16), wide, dma((2, half))],
        [hbm()],
    )
    edge_theirs = shift(mine, True)
    theirs, ox = call(
        omega_x_kernel, "omega_x", (pair, pair), [velocity, metric, mine], [wide, along]
    )
    got_x = swap(ox)
    zu, yu = call(
        functools.partial(u_kernel, half),
        "u_terms",
        (partial_sum, partial_sum),
        [velocity, metric],
        [pltpu.VMEM((half, ny, snaps, nz), bf16), wide, along],
    )

    def omega_yz(slot, near, far, edge):
        name = "omega_yz_mine" if slot else "omega_yz_theirs"
        args = [near, far, edge, zu, yu, metric]
        return call(functools.partial(omega_yz_kernel, slot), name, pair, args)

    def gram_part(name, slots, shape, *args):
        return call(functools.partial(gram_kernel, slots), name, shape, args)

    def raw_modes(name, slots, own, got):
        kernel = functools.partial(raw_kernel, slots)
        return call(kernel, name, (raw,) * len(slots), [own, got, blocks])

    gram = gram_part("gram_x", ((1, 0),), square, ox, got_x, volume)
    yz_theirs = omega_yz(0, theirs, mine, edge_theirs)
    got_yz_mine = swap(yz_theirs)
    late, _ = lax.optimization_barrier((theirs, yz_theirs))
    edge_mine = shift(late, False)
    coeff_rows, blocks = call(
        coeff_kernel,
        "coeff_blocks",
        (
            jax.ShapeDtypeStruct((snaps, 2 * snaps), f32),
            jax.ShapeDtypeStruct((ROWS // snaps * snaps, ROWS // snaps * 2 * snaps), bf16),
        ),
        [coeffs],
    )
    theirs_x, mine_x = raw_modes("raw_x", ((0, 1), (1, 0)), ox, got_x)
    edge_mine, gram, mine_x = lax.optimization_barrier((edge_mine, gram, mine_x))
    yz_mine = omega_yz(1, mine, theirs, edge_mine)
    got_yz_theirs = swap(yz_mine)
    copies = jax.ShapeDtypeStruct((2 * peers, 4 * snaps**2 // nz, nz), f32)
    grams = gram_part("gram_yz", ((0, 0), (1, 1)), copies, yz_mine, got_yz_mine, volume, gram)
    mine_yz = raw_modes("raw_yz_mine", ((0, 0), (1, 1)), yz_mine, got_yz_mine)
    grams, *mine_yz = lax.optimization_barrier((grams, *mine_yz))
    grams = lax.all_to_all(grams, ("space", "snap"), 0, 0, tiled=True)
    gram, other = call(add_kernel, "add", (square, square), [grams])
    modes, rows = call(
        functools.partial(finish_kernel, half, 1.0 / (3.0 * layers * peers * ny * nz)),
        "finish",
        (
            jax.ShapeDtypeStruct(velocity.shape, bf16),
            jax.ShapeDtypeStruct((snaps, 2 * snaps), f32),
        ),
        [
            gram, other, coeff_rows, blocks, theirs_x, mine_x, *mine_yz, yz_theirs, got_yz_theirs,
        ],
        [
            pltpu.VMEM((6, snaps, half, ny, nz), bf16),
            pltpu.VMEM((snaps, 2 * snaps), f32),
            pltpu.VMEM((snaps, nz), f32),
            pltpu.VMEM((half, snaps * ny, nz), f32),
            dma((7,)),
        ],
        None,
        (hbm(), hbm()),
    )
    return (rows, modes)


def per_device(velocity, metric, volume, coeffs):
    peers = lax.axis_size("space")
    paired = lax.axis_size("snap") == 2 and velocity.shape[2] == 2 * WIDTH
    if paired and velocity.shape[0] % 16 == 0 and peers & (peers - 1) == 0:
        return two_groups(velocity, metric, volume, coeffs)
    return many_groups(velocity, metric, volume, coeffs)


def solution(mesh):
    placed = (
        P("snap", None, "space", None, None),
        P(None, "space", None, None),
        P("space", None, None),
        P(),
    )
    return jax.shard_map(
        per_device,
        mesh=mesh,
        in_specs=placed,
        out_specs=(P("snap", None), P("snap", None, "space", None, None)),
        check_vma=False,
    )
```

```python
import functools

import jax
import jax.numpy as jnp
from jax import lax
from jax.experimental import pallas as pl
from jax.experimental.pallas import tpu as pltpu
from jax.sharding import PartitionSpec as P

EPS = 1e-06
WIDTH = 2
ROWS = 128
LIMIT = 24 * 1024 * 1024


def with_halo(shard, sides, width):
    for axis, dim in sides:
        peers, length = (lax.axis_size(axis), shard.shape[dim])
        up = [(i, (i + 1) % peers) for i in range(peers)]
        down = [(j, i) for i, j in up]
        last = lax.slice_in_dim(shard, length - width, length, axis=dim)
        leading = lax.slice_in_dim(shard, 0, width, axis=dim)
        before = lax.ppermute(last, axis, up)
        after = lax.ppermute(leading, axis, down)
        shard = jnp.concatenate([before, shard, after], axis=dim)
    return shard


def deriv(padded, dim):
    count = padded.shape[dim] - 4

    def cut(offset):
        return lax.slice_in_dim(padded, offset, offset + count, axis=dim)

    return (8.0 * (cut(3) - cut(1)) - (cut(4) - cut(0))) / 12.0


def curl(padded_x, metric):
    inner = padded_x[:, :, 2:-2]
    padded_y = jnp.pad(inner, ((0, 0), (0, 0), (0, 0), (2, 2), (0, 0)))
    padded_z = jnp.concatenate([inner[..., -2:], inner, inner[..., :2]], axis=4)
    along_x = deriv(padded_x, 2) * metric[0]
    along_y = deriv(padded_y, 3) * metric[1]
    along_z = deriv(padded_z, 4) * metric[2]
    omega_x = along_y[:, 2] - along_z[:, 1]
    omega_y = along_z[:, 0] - along_x[:, 2]
    omega_z = along_x[:, 1] - along_y[:, 0]
    return jnp.stack([omega_x, omega_y, omega_z], axis=1).astype(jnp.bfloat16)


def many_groups(velocity, metric, volume, coeffs):
    snap_dev = velocity.shape[0]
    snaps = coeffs.shape[0]
    group = lax.axis_index("snap")
    scale = 1.0 / (
        3.0 * volume.shape[0] * lax.axis_size("space") * volume.shape[1] * volume.shape[2]
    )
    padded = with_halo(velocity, (("space", 2),), 2)
    vorticity = curl(padded.astype(jnp.float32), metric)
    coeff_f = coeffs.astype(jnp.float32)
    moved = lax.all_to_all(vorticity, "snap", split_axis=3, concat_axis=0, tiled=True)
    part_y = moved.shape[3]
    vol_part = lax.dynamic_slice_in_dim(volume, group * part_y, part_y, 1)
    weighted = (moved.astype(jnp.float32) * vol_part).astype(jnp.bfloat16).reshape(snaps, -1)
    flat = moved.reshape(snaps, -1)
    partial_value = lax.dot_general(
        weighted, flat, (((1,), (1,)), ((), ())), preferred_element_type=jnp.float32
    )
    raw = lax.dot_general(
        coeffs, flat, (((0,), (0,)), ((), ())), preferred_element_type=jnp.float32
    )
    whole = lax.psum(partial_value, ("space", "snap")) * scale
    energy = jnp.sum(coeff_f * jnp.dot(whole, coeff_f, precision=lax.Precision.HIGHEST), axis=0)
    rows = lax.dynamic_slice_in_dim(whole, group * snap_dev, snap_dev, 0)
    local_modes = (raw / jnp.sqrt(energy + EPS)[:, None]).astype(jnp.bfloat16).reshape(moved.shape)
    modes = lax.all_to_all(local_modes, "snap", split_axis=0, concat_axis=3, tiled=True)
    return (rows, modes)


def vmem():
    return pl.BlockSpec(memory_space=pltpu.VMEM)


def hbm():
    return pl.BlockSpec(memory_space=pltpu.HBM)


def params():
    return pltpu.CompilerParams(vmem_limit_bytes=LIMIT)


def cost(flops, moved):
    return pl.CostEstimate(flops=flops, bytes_accessed=moved, transcendentals=0)


def z_stencil(size):
    rows = lax.broadcasted_iota(jnp.int32, (size, size), 0)
    cols = lax.broadcasted_iota(jnp.int32, (size, size), 1)
    ahead = rows - cols
    ahead = jnp.where(ahead < 0, ahead + size, ahead)
    out = jnp.where(ahead == 1, 8.0, 0.0) - jnp.where(ahead == size - 1, 8.0, 0.0)
    out = out - jnp.where(ahead == 2, 1.0, 0.0) + jnp.where(ahead == size - 2, 1.0, 0.0)
    return out.astype(jnp.bfloat16)


def spread(src, wide):
    snaps, ny, nz = src.shape
    wide[...] = src.astype(jnp.float32).reshape(snaps * ny, nz)


def row(wide, y, snaps, ny):
    return wide[pl.ds(y, snaps, ny), :]


def y_stencils(load, ny):
    held = {}

    def at(j):
        if j not in held:
            held[j] = load(j)
        return held[j]

    zero = jnp.zeros_like(at(0))
    for y in range(ny):
        near = (at(y + 1) if y + 1 < ny else zero) - (at(y - 1) if y >= 1 else zero)
        far = (at(y + 2) if y + 2 < ny else zero) - (at(y - 2) if y >= 2 else zero)
        held.pop(y - 2, None)
        yield y, 8.0 * near - far


def z_derivative(field, matrix, along):
    rows = field.shape[0] * field.shape[1] * field.shape[2]
    along[...] = jnp.dot(
        field.reshape(rows, field.shape[3]), matrix, preferred_element_type=jnp.float32
    ).reshape(field.shape)


def factor(metric_ref, m, layer, y):
    return metric_ref[m, layer, pl.ds(y, 1), :] * (1.0 / 12.0)


def flip(src, wide, out_ref, i):
    snaps, ny, _ = src.shape
    spread(src, wide)
    for y in range(ny):
        out_ref[i, y] = row(wide, y, snaps, ny).astype(jnp.bfloat16)


def omega_x_kernel(vel_ref, metric_ref, theirs_ref, mine_ref, ox_ref, buf, factors, wide, along, sems):
    snaps, _, layers, ny, nz = buf.shape
    half = layers // 2
    group = lax.axis_index("snap")
    bases = ((1 - group) * half, group * half)
    copies = {}
    for slot in range(2):
        rows = pl.ds(bases[slot], half)
        inner = pl.ds(slot * half, half)
        for c in range(2):
            source, target = vel_ref.at[:, 1 + c, rows], buf.at[:, c, inner]
            copies[slot, c] = pltpu.make_async_copy(source, target, sems.at[slot, c])
            copies[slot, c].start()
        source, target = metric_ref.at[1:3, rows], factors.at[:, inner]
        copies[slot, 2] = pltpu.make_async_copy(source, target, sems.at[slot, 2])
        copies[slot, 2].start()
    matrix = z_stencil(nz)
    for slot, vw_ref in enumerate((theirs_ref, mine_ref)):
        copies[slot, 0].wait()
        for i in range(half):
            flip(buf[:, 0, slot * half + i], wide, vw_ref.at[0], i)
        z_derivative(vw_ref[0], matrix, along)
        copies[slot, 1].wait()
        copies[slot, 2].wait()
        for i in range(half):
            spread(buf[:, 1, slot * half + i], wide)

            def load(j):
                value = row(wide, j, snaps, ny)
                vw_ref[1, i, j] = value.astype(jnp.bfloat16)
                return value

            for y, across in y_stencils(load, ny):
                value = across * factor(factors, 0, slot * half + i, y)
                value = value - along[i, y] * factor(factors, 1, slot * half + i, y)
                ox_ref[slot, i, y] = value.astype(jnp.bfloat16)


def u_kernel(slot, vel_ref, metric_ref, zu_ref, yu_ref, flat, wide, along):
    half, ny, snaps, nz = zu_ref.shape
    group = lax.axis_index("snap")
    base = (group if slot else 1 - group) * half
    for i in range(half):
        spread(vel_ref[:, 0, base + i], wide)

        def load(j):
            value = row(wide, j, snaps, ny)
            flat[i, j] = value.astype(jnp.bfloat16)
            return value

        for y, across in y_stencils(load, ny):
            yu_ref[i, y] = across * factor(metric_ref, 1, base + i, y)
    z_derivative(flat[...], z_stencil(nz), along)
    for i in range(half):
        for y in range(ny):
            zu_ref[i, y] = along[i, y] * factor(metric_ref, 2, base + i, y)


def finish_curl(sign, slot, near_ref, far_ref, halo_ref, known_ref, metric_ref, out_ref):
    half, ny, _, _ = near_ref.shape
    group = lax.axis_index("snap")
    part = group if slot else 1 - group

    def run(low_ref, high_ref):
        def plane(i, y):
            if i < 0:
                ref, k = low_ref, half + i
            elif i < half:
                ref, k = near_ref, i
            else:
                ref, k = high_ref, i - half
            return ref[k, y].astype(jnp.float32)

        for y in range(ny):
            at = [plane(i, y) for i in range(-WIDTH, half + WIDTH)]
            for i in range(half):
                along = 8.0 * (at[i + 3] - at[i + 1]) - (at[i + 4] - at[i])
                along = along * factor(metric_ref, 0, part * half + i, y)
                known = known_ref[i, y]
                value = along - known if sign > 0 else known - along
                out_ref[i, y] = value.astype(jnp.bfloat16)

    @pl.when(part == 0)
    def _():
        run(halo_ref, far_ref)

    @pl.when(part == 1)
    def _():
        run(far_ref, halo_ref)


def omega_yz_kernel(slot, near, far, edge, zu_ref, yu_ref, metric_ref, out_ref):
    known = (yu_ref, zu_ref)
    for c, sign in ((1, -1), (0, 1)):
        fields = near.at[c], far.at[c], edge.at[c], known[c]
        finish_curl(sign, slot, *fields, metric_ref, out_ref.at[1 - c])


def gram_of(own, got, volume_ref, base):
    half, ny, _, _ = own.shape
    total = None
    for i in range(half):
        plain, heavy = [], []
        for y in range(ny):
            pair = jnp.concatenate([own[i, y], got[i, y]], axis=0)
            weight = volume_ref[base + i, pl.ds(y, 1), :]
            plain.append(pair)
            heavy.append((pair.astype(jnp.float32) * weight).astype(jnp.bfloat16))
        part = lax.dot_general(
            jnp.concatenate(heavy, axis=1),
            jnp.concatenate(plain, axis=1),
            (((1,), (1,)), ((), ())),
            preferred_element_type=jnp.float32,
        )
        total = part if total is None else total + part
    return total


def gram_kernel(slots, own, got, volume_ref, *refs):
    base = lax.axis_index("snap") * volume_ref.shape[0] // 2
    total = sum(gram_of(own.at[n], got.at[m], volume_ref, base) for n, m in slots)
    for earlier in refs[:-1]:
        total = total + earlier[...]
    if len(refs[-1].shape) == 3:
        count, rows, _ = refs[-1].shape
        total = jnp.concatenate(
            [total[n : n + rows] for n in range(0, total.shape[0], rows)], axis=1
        )
        for peer in range(count):
            refs[-1][peer] = total
    else:
        refs[-1][...] = total


def add_kernel(parts_ref, out_ref):
    parts = [parts_ref[n] for n in range(parts_ref.shape[0])]
    while len(parts) > 1:
        parts = [sum(parts[n : n + 2]) for n in range(0, len(parts), 2)]
    rows, side = parts_ref.shape[1], out_ref.shape[0]
    for n in range(side // rows):
        out_ref[n * rows : (n + 1) * rows] = parts[0][:, n * side : (n + 1) * side]


def coeff_kernel(coeff_ref, mine_ref, block_ref):
    snaps, count = mine_ref.shape
    rows = block_ref.shape[0]
    base = lax.axis_index("snap") * snaps

    def chosen(shape, test):
        left = lax.broadcasted_iota(jnp.int32, shape, 0)
        right = lax.broadcasted_iota(jnp.int32, shape, 1)
        return jnp.where(test(left, right), 1.0, 0.0).astype(jnp.bfloat16)

    def take(a, b, dims):
        out = lax.dot_general(a, b, (dims, ((), ())), preferred_element_type=jnp.float32)
        return out.astype(jnp.bfloat16)

    mine = chosen((snaps, count), lambda k, m: m == k + base)
    mine = take(mine, coeff_ref[...], ((1,), (1,)))
    order = chosen((count, count), lambda j, m: j == lax.rem(m + base, count))
    mine = take(mine, order, ((1,), (0,)))
    mine_ref[...] = mine.astype(jnp.float32)
    down = chosen((rows, snaps), lambda r, k: lax.rem(r, snaps) == k)
    for part in range(count // snaps):
        across = chosen((count, rows), lambda j, c: j == lax.rem(c, snaps) + part * snaps)
        wide = take(take(down, mine, ((1,), (0,))), across, ((1,), (0,)))
        same = chosen((rows, rows), lambda r, c: lax.div(r, snaps) == lax.div(c, snaps))
        block_ref[:, part * rows : (part + 1) * rows] = wide * same


def raw_blocks(own, got, block_ref, put):
    ny, snaps, nz = own.shape
    block = block_ref.shape[0] // snaps
    lanes = 2 if ny % (2 * block) == 0 else 1
    for start in range(0, ny, block * lanes):
        columns = []
        for n in range(lanes):
            at = start + n * block
            parts = [ref[at : at + block].reshape(block * snaps, nz) for ref in (own, got)]
            columns.append(jnp.concatenate(parts, axis=0))
        both = columns[0] if lanes == 1 else jnp.concatenate(columns, axis=1)
        raw = jnp.dot(block_ref[...], both, preferred_element_type=jnp.float32)
        for n in range(lanes):
            part = raw[:, n * nz : (n + 1) * nz].reshape(block, snaps, nz)
            for k in range(block):
                put(start + n * block + k, part[k])


def raw_kernel(slots, own_ref, got_ref, block_ref, *outs):
    for (n, m), out_ref in zip(slots, outs):
        own, got = own_ref.at[n], got_ref.at[m]
        half, ny, snaps, _ = own.shape
        for i in range(half):

            def put(y, value):
                out_ref[pl.ds(i * ny + y, snaps, half * ny), :] = value

            raw_blocks(own.at[i], got.at[i], block_ref, put)


def finish_kernel(half, scale, part_ref, other_ref, coeff_ref, *refs):
    raws, (out_ref, rows_ref, stage, rows_buf, wide, sems) = refs[:6], refs[6:]
    snaps, _, _, ny, nz = stage.shape
    group = lax.axis_index("snap")
    other = other_ref[...]
    other = jnp.concatenate([other[snaps:], other[:snaps]], axis=0)
    other = jnp.concatenate([other[:, snaps:], other[:, :snaps]], axis=1)
    total = (part_ref[...] + other) * scale
    coeff = coeff_ref[...]
    inner = jnp.dot(
        coeff, total, precision=lax.Precision.HIGHEST, preferred_element_type=jnp.float32
    )
    energy = jnp.sum(inner * coeff, axis=1, keepdims=True)
    wide[...] = jnp.broadcast_to(1.0 / jnp.sqrt(energy + EPS), (snaps, nz))
    mine = total[:snaps]
    turned = jnp.concatenate([mine[:, snaps:], mine[:, :snaps]], axis=1)
    rows_buf[...] = jnp.where(group == 0, mine, turned)
    copies = [pltpu.make_async_copy(rows_buf, rows_ref, sems.at[0])]
    copies[0].start()
    block = half * ny
    step = 2
    for n in range(snaps // step):
        for k in range(n * step, (n + 1) * step):
            factor = wide[k : k + 1, :]
            for c in range(3):
                for slot, base in ((0, 1 - group), (1, group)):
                    value = raws[3 * slot + c][k * block : (k + 1) * block, :] * factor
                    value = value.astype(jnp.bfloat16).reshape(half, ny, nz)
                    stage[k, c, pl.ds(base * half, half)] = value
        part = pl.ds(n * step, step)
        copies.append(pltpu.make_async_copy(stage.at[part], out_ref.at[part], sems.at[1 + n]))
        copies[-1].start()
    for copy in copies:
        copy.wait()


def two_groups(velocity, metric, volume, coeffs):
    snaps, _, layers, ny, nz = velocity.shape
    half = layers // 2
    peers = lax.axis_size("space")
    bf16, f32 = jnp.bfloat16, jnp.float32

    def halo(first):
        pairs = []
        for s in range(peers):
            for g in range(2):
                down = (g == 0) == first
                pairs.append((s * 2 + g, ((s + (-1 if down else 1)) % peers) * 2 + g))
        return pairs

    def swap(value):
        return lax.ppermute(value, "snap", [(0, 1), (1, 0)])

    def shift(value, first, pieces):
        parts = jnp.split(value, pieces)
        parts = [lax.ppermute(part, ("space", "snap"), halo(first)) for part in parts]
        return parts[0] if pieces == 1 else jnp.concatenate(parts)

    field = jax.ShapeDtypeStruct((half, ny, snaps, nz), bf16)
    pair = jax.ShapeDtypeStruct((2, half, ny, snaps, nz), bf16)
    partial_sum = jax.ShapeDtypeStruct((half, ny, snaps, nz), f32)
    square = jax.ShapeDtypeStruct((2 * snaps, 2 * snaps), f32)
    raw = jax.ShapeDtypeStruct((snaps * half * ny, nz), f32)
    cells = half * ny * snaps * nz
    wide = pltpu.VMEM((snaps * ny, nz), f32)
    along = pltpu.VMEM((half, ny, snaps, nz), f32)
    dma = pltpu.SemaphoreType.DMA

    def call(kernel, name, out_shape, args, scratch=(), in_specs=None, out_specs=None, work=5):
        return pl.pallas_call(
            kernel,
            out_shape=out_shape,
            in_specs=in_specs or [vmem()] * len(args),
            out_specs=out_specs or jax.tree.map(lambda _: vmem(), out_shape),
            scratch_shapes=list(scratch),
            compiler_params=params(),
            cost_estimate=cost(2 * work * cells, work * cells),
            name=name,
        )(*args)

    theirs, mine, ox = call(
        omega_x_kernel,
        "omega_x",
        (pair, pair, pair),
        [pltpu.with_memory_space_constraint(a, pltpu.HBM) for a in (velocity, metric)],
        [
            pltpu.VMEM((snaps, 2, layers, ny, nz), bf16),
            pltpu.VMEM((2, layers, ny, nz), f32),
            wide,
            along,
            dma((2, 3)),
        ],
        [hbm()] * 2,
    )
    got_x = swap(ox)

    def omega_yz(slot, near, far, edge, velocity, metric):
        zu, yu = call(
            functools.partial(u_kernel, slot),
            "u_mine" if slot else "u_theirs",
            (partial_sum, partial_sum),
            [velocity, metric],
            [pltpu.VMEM((half, ny, snaps, nz), bf16), wide, along],
        )
        name = "omega_yz_mine" if slot else "omega_yz_theirs"
        args = [near, far, edge, zu, yu, metric]
        return call(functools.partial(omega_yz_kernel, slot), name, pair, args)

    def one_unit(work, *args):
        first = lax.axis_index("snap") < 2
        return lax.cond(first, functools.partial(work, 1), functools.partial(work, 2), *args)

    def first_halo(pieces, mine, theirs, velocity, metric):
        return omega_yz(0, theirs, mine, shift(mine, True, pieces), velocity, metric)

    def second_halo(pieces, mine, theirs, velocity, metric):
        return omega_yz(1, mine, theirs, shift(theirs, False, pieces), velocity, metric)

    yz_theirs = one_unit(first_halo, mine, theirs, velocity, metric)
    got_yz = swap(yz_theirs)
    late, got_x, _ = lax.optimization_barrier((theirs, got_x, yz_theirs))
    yz_mine = one_unit(second_halo, mine, late, velocity, metric)
    got_yz_theirs = swap(yz_mine)
    coeff_rows, blocks = call(
        coeff_kernel,
        "coeff_blocks",
        (
            jax.ShapeDtypeStruct((snaps, 2 * snaps), f32),
            jax.ShapeDtypeStruct((ROWS // snaps * snaps, ROWS // snaps * 2 * snaps), bf16),
        ),
        [coeffs],
    )

    def gram_part(name, slots, shape, *args):
        return call(functools.partial(gram_kernel, slots), name, shape, args)

    def raw_modes(name, slots, own, got):
        kernel = functools.partial(raw_kernel, slots)
        return call(kernel, name, (raw,) * len(slots), [own, got, blocks])

    gram = gram_part("gram_x", ((1, 0),), square, ox, got_x, volume)
    theirs_x, mine_x = raw_modes("raw_x", ((0, 1), (1, 0)), ox, got_x)
    got_yz, gram, mine_x = lax.optimization_barrier((got_yz, gram, mine_x))
    copies = jax.ShapeDtypeStruct((peers, 4 * snaps**2 // nz, nz), f32)
    grams = gram_part("gram_yz", ((0, 0), (1, 1)), copies, yz_mine, got_yz, volume, gram)
    grams = lax.all_to_all(grams, "space", 0, 0, tiled=True)
    gram = call(add_kernel, "add", square, [grams])
    other = swap(gram)
    mine_yz = raw_modes("raw_yz_mine", ((0, 0), (1, 1)), yz_mine, got_yz)
    theirs_yz = raw_modes("raw_yz_theirs", ((0, 0), (1, 1)), yz_theirs, got_yz_theirs)
    modes, rows = call(
        functools.partial(finish_kernel, half, 1.0 / (3.0 * layers * peers * ny * nz)),
        "finish",
        (
            jax.ShapeDtypeStruct(velocity.shape, bf16),
            jax.ShapeDtypeStruct((snaps, 2 * snaps), f32),
        ),
        [gram, other, coeff_rows, theirs_x, *theirs_yz, mine_x, *mine_yz],
        [
            pltpu.VMEM(velocity.shape, bf16),
            pltpu.VMEM((snaps, 2 * snaps), f32),
            pltpu.VMEM((snaps, nz), f32),
            dma((1 + snaps // 2,)),
        ],
        None,
        (hbm(), hbm()),
    )
    return (rows, modes)


def per_device(velocity, metric, volume, coeffs):
    peers = lax.axis_size("space")
    paired = lax.axis_size("snap") == 2 and velocity.shape[2] == 2 * WIDTH
    if paired and velocity.shape[0] % 16 == 0 and peers & (peers - 1) == 0:
        return two_groups(velocity, metric, volume, coeffs)
    return many_groups(velocity, metric, volume, coeffs)


def solution(mesh):
    placed = (
        P("snap", None, "space", None, None),
        P(None, "space", None, None),
        P("space", None, None),
        P(),
    )
    return jax.shard_map(
        per_device,
        mesh=mesh,
        in_specs=placed,
        out_specs=(P("snap", None), P("snap", None, "space", None, None)),
        check_vma=False,
    )
```

```python
import functools

import jax
import jax.numpy as jnp
from jax import lax
from jax.experimental import pallas as pl
from jax.experimental.pallas import tpu as pltpu
from jax.sharding import PartitionSpec as P

EPS = 1e-06
WIDTH = 2
ROWS = 128
LIMIT = 24 * 1024 * 1024


def with_halo(shard, sides, width):
    for axis, dim in sides:
        peers, length = (lax.axis_size(axis), shard.shape[dim])
        up = [(i, (i + 1) % peers) for i in range(peers)]
        down = [(j, i) for i, j in up]
        last = lax.slice_in_dim(shard, length - width, length, axis=dim)
        leading = lax.slice_in_dim(shard, 0, width, axis=dim)
        before = lax.ppermute(last, axis, up)
        after = lax.ppermute(leading, axis, down)
        shard = jnp.concatenate([before, shard, after], axis=dim)
    return shard


def deriv(padded, dim):
    count = padded.shape[dim] - 4

    def cut(offset):
        return lax.slice_in_dim(padded, offset, offset + count, axis=dim)

    return (8.0 * (cut(3) - cut(1)) - (cut(4) - cut(0))) / 12.0


def curl(padded_x, metric):
    inner = padded_x[:, :, 2:-2]
    padded_y = jnp.pad(inner, ((0, 0), (0, 0), (0, 0), (2, 2), (0, 0)))
    padded_z = jnp.concatenate([inner[..., -2:], inner, inner[..., :2]], axis=4)
    along_x = deriv(padded_x, 2) * metric[0]
    along_y = deriv(padded_y, 3) * metric[1]
    along_z = deriv(padded_z, 4) * metric[2]
    omega_x = along_y[:, 2] - along_z[:, 1]
    omega_y = along_z[:, 0] - along_x[:, 2]
    omega_z = along_x[:, 1] - along_y[:, 0]
    return jnp.stack([omega_x, omega_y, omega_z], axis=1).astype(jnp.bfloat16)


def many_groups(velocity, metric, volume, coeffs):
    snap_dev = velocity.shape[0]
    snaps = coeffs.shape[0]
    group = lax.axis_index("snap")
    scale = 1.0 / (
        3.0 * volume.shape[0] * lax.axis_size("space") * volume.shape[1] * volume.shape[2]
    )
    padded = with_halo(velocity, (("space", 2),), 2)
    vorticity = curl(padded.astype(jnp.float32), metric)
    coeff_f = coeffs.astype(jnp.float32)
    moved = lax.all_to_all(vorticity, "snap", split_axis=3, concat_axis=0, tiled=True)
    part_y = moved.shape[3]
    vol_part = lax.dynamic_slice_in_dim(volume, group * part_y, part_y, 1)
    weighted = (moved.astype(jnp.float32) * vol_part).astype(jnp.bfloat16).reshape(snaps, -1)
    flat = moved.reshape(snaps, -1)
    partial_value = lax.dot_general(
        weighted, flat, (((1,), (1,)), ((), ())), preferred_element_type=jnp.float32
    )
    raw = lax.dot_general(
        coeffs, flat, (((0,), (0,)), ((), ())), preferred_element_type=jnp.float32
    )
    whole = lax.psum(partial_value, ("space", "snap")) * scale
    energy = jnp.sum(coeff_f * jnp.dot(whole, coeff_f, precision=lax.Precision.HIGHEST), axis=0)
    rows = lax.dynamic_slice_in_dim(whole, group * snap_dev, snap_dev, 0)
    local_modes = (raw / jnp.sqrt(energy + EPS)[:, None]).astype(jnp.bfloat16).reshape(moved.shape)
    modes = lax.all_to_all(local_modes, "snap", split_axis=0, concat_axis=3, tiled=True)
    return (rows, modes)


def vmem():
    return pl.BlockSpec(memory_space=pltpu.VMEM)


def hbm():
    return pl.BlockSpec(memory_space=pltpu.HBM)


def params():
    return pltpu.CompilerParams(vmem_limit_bytes=LIMIT)


def cost(flops, moved):
    return pl.CostEstimate(flops=flops, bytes_accessed=moved, transcendentals=0)


def z_stencil(size):
    rows = lax.broadcasted_iota(jnp.int32, (size, size), 0)
    cols = lax.broadcasted_iota(jnp.int32, (size, size), 1)
    ahead = rows - cols
    ahead = jnp.where(ahead < 0, ahead + size, ahead)
    out = jnp.where(ahead == 1, 8.0, 0.0) - jnp.where(ahead == size - 1, 8.0, 0.0)
    out = out - jnp.where(ahead == 2, 1.0, 0.0) + jnp.where(ahead == size - 2, 1.0, 0.0)
    return out.astype(jnp.bfloat16)


def spread(src, wide):
    snaps, ny, nz = src.shape
    wide[...] = src.astype(jnp.float32).reshape(snaps * ny, nz)


def row(wide, y, snaps, ny):
    return wide[pl.ds(y, snaps, ny), :]


def y_stencils(load, ny):
    held = {}

    def at(j):
        if j not in held:
            held[j] = load(j)
        return held[j]

    zero = jnp.zeros_like(at(0))
    for y in range(ny):
        near = (at(y + 1) if y + 1 < ny else zero) - (at(y - 1) if y >= 1 else zero)
        far = (at(y + 2) if y + 2 < ny else zero) - (at(y - 2) if y >= 2 else zero)
        held.pop(y - 2, None)
        yield y, 8.0 * near - far


def z_derivative(field, matrix, along):
    rows = field.shape[0] * field.shape[1] * field.shape[2]
    along[...] = jnp.dot(
        field.reshape(rows, field.shape[3]), matrix, preferred_element_type=jnp.float32
    ).reshape(field.shape)


def factor(metric_ref, m, layer, y):
    return metric_ref[m, layer, pl.ds(y, 1), :] * (1.0 / 12.0)


def flip(src, wide, out_ref, i):
    snaps, ny, _ = src.shape
    spread(src, wide)
    for y in range(ny):
        out_ref[i, y] = row(wide, y, snaps, ny).astype(jnp.bfloat16)


def flip_kernel(vel_ref, out_ref, buf, wide, sems):
    half = out_ref.shape[1]
    base = lax.axis_index("snap") * half
    copies = {}
    for c in range(2):
        for i in range(half):
            source = vel_ref.at[:, 1 + c, base + i]
            copies[c, i] = pltpu.make_async_copy(source, buf.at[:, c, i], sems.at[c, i])
            copies[c, i].start()
    for c in range(2):
        for i in range(half):
            copies[c, i].wait()
            flip(buf[:, c, i], wide, out_ref.at[c], i)


def omega_x_kernel(vel_ref, metric_ref, mine_ref, vw_ref, ox_ref, wide, along):
    _, half, ny, snaps, nz = ox_ref.shape
    group = lax.axis_index("snap")
    matrix = z_stencil(nz)
    for slot, base in ((0, (1 - group) * half), (1, group * half)):
        fields = mine_ref if slot else vw_ref
        if slot == 0:
            for i in range(half):
                flip(vel_ref[:, 1, base + i], wide, vw_ref.at[0], i)
        z_derivative(fields[0], matrix, along)
        for i in range(half):
            if slot == 0:
                spread(vel_ref[:, 2, base + i], wide)

            def load(j):
                if slot:
                    return mine_ref[1, i, j].astype(jnp.float32)
                value = row(wide, j, snaps, ny)
                vw_ref[1, i, j] = value.astype(jnp.bfloat16)
                return value

            for y, across in y_stencils(load, ny):
                value = across * factor(metric_ref, 1, base + i, y)
                value = value - along[i, y] * factor(metric_ref, 2, base + i, y)
                ox_ref[slot, i, y] = value.astype(jnp.bfloat16)


def u_kernel(half, vel_ref, metric_ref, zu_ref, yu_ref, flat, wide, along):
    snaps, _, _, ny, nz = vel_ref.shape
    matrix = z_stencil(nz)
    group = lax.axis_index("snap")
    for slot in range(2):
        base = (group if slot else 1 - group) * half
        for i in range(half):
            spread(vel_ref[:, 0, base + i], wide)

            def load(j):
                value = row(wide, j, snaps, ny)
                flat[i, j] = value.astype(jnp.bfloat16)
                return value

            for y, across in y_stencils(load, ny):
                yu_ref[slot, i, y] = across * factor(metric_ref, 1, base + i, y)
        z_derivative(flat[...], matrix, along)
        for i in range(half):
            for y in range(ny):
                zu_ref[slot, i, y] = along[i, y] * factor(metric_ref, 2, base + i, y)


def finish_curl(sign, slot, near_ref, far_ref, halo_ref, known_ref, metric_ref, out_ref):
    half, ny, _, _ = near_ref.shape
    group = lax.axis_index("snap")
    part = group if slot else 1 - group

    def run(low_ref, high_ref):
        def plane(i, y):
            if i < 0:
                ref, k = low_ref, half + i
            elif i < half:
                ref, k = near_ref, i
            else:
                ref, k = high_ref, i - half
            return ref[k, y].astype(jnp.float32)

        for y in range(ny):
            at = [plane(i, y) for i in range(-WIDTH, half + WIDTH)]
            for i in range(half):
                along = 8.0 * (at[i + 3] - at[i + 1]) - (at[i + 4] - at[i])
                along = along * factor(metric_ref, 0, part * half + i, y)
                known = known_ref[slot, i, y]
                value = along - known if sign > 0 else known - along
                out_ref[i, y] = value.astype(jnp.bfloat16)

    @pl.when(part == 0)
    def _():
        run(halo_ref, far_ref)

    @pl.when(part == 1)
    def _():
        run(far_ref, halo_ref)


def omega_yz_kernel(slot, near, far, edge, zu_ref, yu_ref, metric_ref, out_ref):
    known = (yu_ref, zu_ref)
    for c, sign in ((1, -1), (0, 1)):
        fields = near.at[c], far.at[c], edge.at[c], known[c]
        finish_curl(sign, slot, *fields, metric_ref, out_ref.at[1 - c])


def gram_of(own, got, volume_ref, base):
    half, ny, _, _ = own.shape
    total = None
    for i in range(half):
        plain, heavy = [], []
        for y in range(ny):
            pair = jnp.concatenate([own[i, y], got[i, y]], axis=0)
            weight = volume_ref[base + i, pl.ds(y, 1), :]
            plain.append(pair)
            heavy.append((pair.astype(jnp.float32) * weight).astype(jnp.bfloat16))
        part = lax.dot_general(
            jnp.concatenate(heavy, axis=1),
            jnp.concatenate(plain, axis=1),
            (((1,), (1,)), ((), ())),
            preferred_element_type=jnp.float32,
        )
        total = part if total is None else total + part
    return total


def gram_kernel(slots, own, got, volume_ref, *refs):
    base = lax.axis_index("snap") * volume_ref.shape[0] // 2
    total = sum(gram_of(own.at[n], got.at[m], volume_ref, base) for n, m in slots)
    for earlier in refs[:-1]:
        total = total + earlier[...]
    if len(refs[-1].shape) == 3:
        count, rows, _ = refs[-1].shape
        total = jnp.concatenate(
            [total[n : n + rows] for n in range(0, total.shape[0], rows)], axis=1
        )
        for peer in range(count):
            refs[-1][peer] = total
    else:
        refs[-1][...] = total


def add_kernel(parts_ref, out_ref):
    parts = [parts_ref[n] for n in range(parts_ref.shape[0])]
    while len(parts) > 1:
        parts = [sum(parts[n : n + 2]) for n in range(0, len(parts), 2)]
    rows, side = parts_ref.shape[1], out_ref.shape[0]
    for n in range(side // rows):
        out_ref[n * rows : (n + 1) * rows] = parts[0][:, n * side : (n + 1) * side]


def coeff_kernel(coeff_ref, mine_ref, block_ref):
    snaps, count = mine_ref.shape
    rows = block_ref.shape[0]
    base = lax.axis_index("snap") * snaps

    def chosen(shape, test):
        left = lax.broadcasted_iota(jnp.int32, shape, 0)
        right = lax.broadcasted_iota(jnp.int32, shape, 1)
        return jnp.where(test(left, right), 1.0, 0.0).astype(jnp.bfloat16)

    def take(a, b, dims):
        out = lax.dot_general(a, b, (dims, ((), ())), preferred_element_type=jnp.float32)
        return out.astype(jnp.bfloat16)

    mine = chosen((snaps, count), lambda k, m: m == k + base)
    mine = take(mine, coeff_ref[...], ((1,), (1,)))
    order = chosen((count, count), lambda j, m: j == lax.rem(m + base, count))
    mine = take(mine, order, ((1,), (0,)))
    mine_ref[...] = mine.astype(jnp.float32)
    down = chosen((rows, snaps), lambda r, k: lax.rem(r, snaps) == k)
    for part in range(count // snaps):
        across = chosen((count, rows), lambda j, c: j == lax.rem(c, snaps) + part * snaps)
        wide = take(take(down, mine, ((1,), (0,))), across, ((1,), (0,)))
        same = chosen((rows, rows), lambda r, c: lax.div(r, snaps) == lax.div(c, snaps))
        block_ref[:, part * rows : (part + 1) * rows] = wide * same


def raw_blocks(own, got, block_ref, put):
    ny, snaps, nz = own.shape
    block = block_ref.shape[0] // snaps
    lanes = 2 if ny % (2 * block) == 0 else 1
    for start in range(0, ny, block * lanes):
        columns = []
        for n in range(lanes):
            at = start + n * block
            parts = [ref[at : at + block].reshape(block * snaps, nz) for ref in (own, got)]
            columns.append(jnp.concatenate(parts, axis=0))
        both = columns[0] if lanes == 1 else jnp.concatenate(columns, axis=1)
        raw = jnp.dot(block_ref[...], both, preferred_element_type=jnp.float32)
        for n in range(lanes):
            part = raw[:, n * nz : (n + 1) * nz].reshape(block, snaps, nz)
            for k in range(block):
                put(start + n * block + k, part[k])


def raw_kernel(slots, own_ref, got_ref, block_ref, *outs):
    for (n, m), out_ref in zip(slots, outs):
        own, got = own_ref.at[n], got_ref.at[m]
        half, ny, snaps, _ = own.shape
        for i in range(half):

            def put(y, value):
                out_ref[pl.ds(i * ny + y, snaps, half * ny), :] = value

            raw_blocks(own.at[i], got.at[i], block_ref, put)


def finish_kernel(half, scale, part_ref, other_ref, coeff_ref, *refs):
    raws, (out_ref, rows_ref, stage, rows_buf, wide, sems) = refs[:6], refs[6:]
    snaps, _, _, ny, nz = stage.shape
    group = lax.axis_index("snap")
    other = other_ref[...]
    other = jnp.concatenate([other[snaps:], other[:snaps]], axis=0)
    other = jnp.concatenate([other[:, snaps:], other[:, :snaps]], axis=1)
    total = (part_ref[...] + other) * scale
    coeff = coeff_ref[...]
    inner = jnp.dot(
        coeff, total, precision=lax.Precision.HIGHEST, preferred_element_type=jnp.float32
    )
    energy = jnp.sum(inner * coeff, axis=1, keepdims=True)
    wide[...] = jnp.broadcast_to(1.0 / jnp.sqrt(energy + EPS), (snaps, nz))
    mine = total[:snaps]
    turned = jnp.concatenate([mine[:, snaps:], mine[:, :snaps]], axis=1)
    rows_buf[...] = jnp.where(group == 0, mine, turned)
    copies = [pltpu.make_async_copy(rows_buf, rows_ref, sems.at[0])]
    copies[0].start()
    block = half * ny
    step = 2
    for n in range(snaps // step):
        for k in range(n * step, (n + 1) * step):
            factor = wide[k : k + 1, :]
            for c in range(3):
                for slot, base in ((0, 1 - group), (1, group)):
                    value = raws[3 * slot + c][k * block : (k + 1) * block, :] * factor
                    value = value.astype(jnp.bfloat16).reshape(half, ny, nz)
                    stage[k, c, pl.ds(base * half, half)] = value
        part = pl.ds(n * step, step)
        copies.append(pltpu.make_async_copy(stage.at[part], out_ref.at[part], sems.at[1 + n]))
        copies[-1].start()
    for copy in copies:
        copy.wait()


def two_groups(velocity, metric, volume, coeffs):
    snaps, _, layers, ny, nz = velocity.shape
    half = layers // 2
    peers = lax.axis_size("space")
    bf16, f32 = jnp.bfloat16, jnp.float32

    def halo(first):
        pairs = []
        for s in range(peers):
            for g in range(2):
                down = (g == 0) == first
                pairs.append((s * 2 + g, ((s + (-1 if down else 1)) % peers) * 2 + g))
        return pairs

    def swap(value):
        return lax.ppermute(value, "snap", [(0, 1), (1, 0)])

    def shift(value, first):
        return lax.ppermute(value, ("space", "snap"), halo(first))

    field = jax.ShapeDtypeStruct((half, ny, snaps, nz), bf16)
    pair = jax.ShapeDtypeStruct((2, half, ny, snaps, nz), bf16)
    partial_sum = jax.ShapeDtypeStruct((2, half, ny, snaps, nz), f32)
    square = jax.ShapeDtypeStruct((2 * snaps, 2 * snaps), f32)
    raw = jax.ShapeDtypeStruct((snaps * half * ny, nz), f32)
    cells = half * ny * snaps * nz
    wide = pltpu.VMEM((snaps * ny, nz), f32)
    along = pltpu.VMEM((half, ny, snaps, nz), f32)
    dma = pltpu.SemaphoreType.DMA

    def call(kernel, name, out_shape, args, scratch=(), in_specs=None, out_specs=None, work=5):
        return pl.pallas_call(
            kernel,
            out_shape=out_shape,
            in_specs=in_specs or [vmem()] * len(args),
            out_specs=out_specs or jax.tree.map(lambda _: vmem(), out_shape),
            scratch_shapes=list(scratch),
            compiler_params=params(),
            cost_estimate=cost(2 * work * cells, work * cells),
            name=name,
        )(*args)

    mine = call(
        flip_kernel,
        "flip_mine",
        pair,
        [pltpu.with_memory_space_constraint(velocity, pltpu.HBM)],
        [pltpu.VMEM((snaps, 2, half, ny, nz), bf16), wide, dma((2, half))],
        [hbm()],
    )
    edge_theirs = shift(mine, True)
    theirs, ox = call(
        omega_x_kernel, "omega_x", (pair, pair), [velocity, metric, mine], [wide, along]
    )
    got_x = swap(ox)
    zu, yu = call(
        functools.partial(u_kernel, half),
        "u_terms",
        (partial_sum, partial_sum),
        [velocity, metric],
        [pltpu.VMEM((half, ny, snaps, nz), bf16), wide, along],
    )

    def omega_yz(slot, near, far, edge):
        name = "omega_yz_mine" if slot else "omega_yz_theirs"
        args = [near, far, edge, zu, yu, metric]
        return call(functools.partial(omega_yz_kernel, slot), name, pair, args)

    def gram_part(name, slots, shape, *args):
        return call(functools.partial(gram_kernel, slots), name, shape, args)

    def raw_modes(name, slots, own, got):
        kernel = functools.partial(raw_kernel, slots)
        return call(kernel, name, (raw,) * len(slots), [own, got, blocks])

    gram = gram_part("gram_x", ((1, 0),), square, ox, got_x, volume)
    yz_theirs = omega_yz(0, theirs, mine, edge_theirs)
    got_yz_mine = swap(yz_theirs)
    late, _ = lax.optimization_barrier((theirs, yz_theirs))
    edge_mine = shift(late, False)
    coeff_rows, blocks = call(
        coeff_kernel,
        "coeff_blocks",
        (
            jax.ShapeDtypeStruct((snaps, 2 * snaps), f32),
            jax.ShapeDtypeStruct((ROWS // snaps * snaps, ROWS // snaps * 2 * snaps), bf16),
        ),
        [coeffs],
    )
    theirs_x, mine_x = raw_modes("raw_x", ((0, 1), (1, 0)), ox, got_x)
    edge_mine, gram, mine_x = lax.optimization_barrier((edge_mine, gram, mine_x))
    yz_mine = omega_yz(1, mine, theirs, edge_mine)
    got_yz_theirs = swap(yz_mine)
    copies = jax.ShapeDtypeStruct((peers, 4 * snaps**2 // nz, nz), f32)
    grams = gram_part("gram_yz", ((0, 0), (1, 1)), copies, yz_mine, got_yz_mine, volume, gram)
    grams = lax.all_to_all(grams, "space", 0, 0, tiled=True)
    gram = call(add_kernel, "add", square, [grams])
    other = swap(gram)
    mine_yz = raw_modes("raw_yz_mine", ((0, 0), (1, 1)), yz_mine, got_yz_mine)
    theirs_yz = raw_modes("raw_yz_theirs", ((0, 0), (1, 1)), yz_theirs, got_yz_theirs)
    modes, rows = call(
        functools.partial(finish_kernel, half, 1.0 / (3.0 * layers * peers * ny * nz)),
        "finish",
        (
            jax.ShapeDtypeStruct(velocity.shape, bf16),
            jax.ShapeDtypeStruct((snaps, 2 * snaps), f32),
        ),
        [gram, other, coeff_rows, theirs_x, *theirs_yz, mine_x, *mine_yz],
        [
            pltpu.VMEM(velocity.shape, bf16),
            pltpu.VMEM((snaps, 2 * snaps), f32),
            pltpu.VMEM((snaps, nz), f32),
            dma((1 + snaps // 2,)),
        ],
        None,
        (hbm(), hbm()),
    )
    return (rows, modes)


def per_device(velocity, metric, volume, coeffs):
    peers = lax.axis_size("space")
    paired = lax.axis_size("snap") == 2 and velocity.shape[2] == 2 * WIDTH
    if paired and velocity.shape[0] % 16 == 0 and peers & (peers - 1) == 0:
        return two_groups(velocity, metric, volume, coeffs)
    return many_groups(velocity, metric, volume, coeffs)


def solution(mesh):
    placed = (
        P("snap", None, "space", None, None),
        P(None, "space", None, None),
        P("space", None, None),
        P(),
    )
    return jax.shard_map(
        per_device,
        mesh=mesh,
        in_specs=placed,
        out_specs=(P("snap", None), P("snap", None, "space", None, None)),
        check_vma=False,
    )
```

```python
import functools

import jax
import jax.numpy as jnp
from jax import lax
from jax.experimental import pallas as pl
from jax.experimental.pallas import tpu as pltpu
from jax.sharding import PartitionSpec as P

EPS = 1e-06
WIDTH = 2
ROWS = 128
LIMIT = 24 * 1024 * 1024


def with_halo(shard, sides, width):
    for axis, dim in sides:
        peers, length = (lax.axis_size(axis), shard.shape[dim])
        up = [(i, (i + 1) % peers) for i in range(peers)]
        down = [(j, i) for i, j in up]
        last = lax.slice_in_dim(shard, length - width, length, axis=dim)
        leading = lax.slice_in_dim(shard, 0, width, axis=dim)
        before = lax.ppermute(last, axis, up)
        after = lax.ppermute(leading, axis, down)
        shard = jnp.concatenate([before, shard, after], axis=dim)
    return shard


def deriv(padded, dim):
    count = padded.shape[dim] - 4

    def cut(offset):
        return lax.slice_in_dim(padded, offset, offset + count, axis=dim)

    return (8.0 * (cut(3) - cut(1)) - (cut(4) - cut(0))) / 12.0


def curl(padded_x, metric):
    inner = padded_x[:, :, 2:-2]
    padded_y = jnp.pad(inner, ((0, 0), (0, 0), (0, 0), (2, 2), (0, 0)))
    padded_z = jnp.concatenate([inner[..., -2:], inner, inner[..., :2]], axis=4)
    along_x = deriv(padded_x, 2) * metric[0]
    along_y = deriv(padded_y, 3) * metric[1]
    along_z = deriv(padded_z, 4) * metric[2]
    omega_x = along_y[:, 2] - along_z[:, 1]
    omega_y = along_z[:, 0] - along_x[:, 2]
    omega_z = along_x[:, 1] - along_y[:, 0]
    return jnp.stack([omega_x, omega_y, omega_z], axis=1).astype(jnp.bfloat16)


def many_groups(velocity, metric, volume, coeffs):
    snap_dev = velocity.shape[0]
    snaps = coeffs.shape[0]
    group = lax.axis_index("snap")
    scale = 1.0 / (
        3.0 * volume.shape[0] * lax.axis_size("space") * volume.shape[1] * volume.shape[2]
    )
    padded = with_halo(velocity, (("space", 2),), 2)
    vorticity = curl(padded.astype(jnp.float32), metric)
    coeff_f = coeffs.astype(jnp.float32)
    moved = lax.all_to_all(vorticity, "snap", split_axis=3, concat_axis=0, tiled=True)
    part_y = moved.shape[3]
    vol_part = lax.dynamic_slice_in_dim(volume, group * part_y, part_y, 1)
    weighted = (moved.astype(jnp.float32) * vol_part).astype(jnp.bfloat16).reshape(snaps, -1)
    flat = moved.reshape(snaps, -1)
    partial_value = lax.dot_general(
        weighted, flat, (((1,), (1,)), ((), ())), preferred_element_type=jnp.float32
    )
    raw = lax.dot_general(
        coeffs, flat, (((0,), (0,)), ((), ())), preferred_element_type=jnp.float32
    )
    whole = lax.psum(partial_value, ("space", "snap")) * scale
    energy = jnp.sum(coeff_f * jnp.dot(whole, coeff_f, precision=lax.Precision.HIGHEST), axis=0)
    rows = lax.dynamic_slice_in_dim(whole, group * snap_dev, snap_dev, 0)
    local_modes = (raw / jnp.sqrt(energy + EPS)[:, None]).astype(jnp.bfloat16).reshape(moved.shape)
    modes = lax.all_to_all(local_modes, "snap", split_axis=0, concat_axis=3, tiled=True)
    return (rows, modes)


def vmem():
    return pl.BlockSpec(memory_space=pltpu.VMEM)


def hbm():
    return pl.BlockSpec(memory_space=pltpu.HBM)


def params():
    return pltpu.CompilerParams(vmem_limit_bytes=LIMIT)


def cost(flops, moved):
    return pl.CostEstimate(flops=flops, bytes_accessed=moved, transcendentals=0)


def z_stencil(size):
    rows = lax.broadcasted_iota(jnp.int32, (size, size), 0)
    cols = lax.broadcasted_iota(jnp.int32, (size, size), 1)
    ahead = rows - cols
    ahead = jnp.where(ahead < 0, ahead + size, ahead)
    out = jnp.where(ahead == 1, 8.0, 0.0) - jnp.where(ahead == size - 1, 8.0, 0.0)
    out = out - jnp.where(ahead == 2, 1.0, 0.0) + jnp.where(ahead == size - 2, 1.0, 0.0)
    return out.astype(jnp.bfloat16)


def spread(src, wide):
    snaps, ny, nz = src.shape
    wide[...] = src.astype(jnp.float32).reshape(snaps * ny, nz)


def row(wide, y, snaps, ny):
    return wide[pl.ds(y, snaps, ny), :]


def y_stencils(load, ny):
    held = {}

    def at(j):
        if j not in held:
            held[j] = load(j)
        return held[j]

    zero = jnp.zeros_like(at(0))
    for y in range(ny):
        near = (at(y + 1) if y + 1 < ny else zero) - (at(y - 1) if y >= 1 else zero)
        far = (at(y + 2) if y + 2 < ny else zero) - (at(y - 2) if y >= 2 else zero)
        held.pop(y - 2, None)
        yield y, 8.0 * near - far


def z_derivative(field, matrix, along):
    rows = field.shape[0] * field.shape[1] * field.shape[2]
    along[...] = jnp.dot(
        field.reshape(rows, field.shape[3]), matrix, preferred_element_type=jnp.float32
    ).reshape(field.shape)


def factor(metric_ref, m, layer, y):
    return metric_ref[m, layer, pl.ds(y, 1), :] * (1.0 / 12.0)


def flip(src, wide, out_ref, i):
    snaps, ny, _ = src.shape
    spread(src, wide)
    for y in range(ny):
        out_ref[i, y] = row(wide, y, snaps, ny).astype(jnp.bfloat16)


def flip_kernel(vel_ref, out_ref, buf, wide, sems):
    half = out_ref.shape[1]
    base = lax.axis_index("snap") * half
    copies = {}
    for c in range(2):
        for i in range(half):
            source = vel_ref.at[:, 1 + c, base + i]
            copies[c, i] = pltpu.make_async_copy(source, buf.at[:, c, i], sems.at[c, i])
            copies[c, i].start()
    for c in range(2):
        for i in range(half):
            copies[c, i].wait()
            flip(buf[:, c, i], wide, out_ref.at[c], i)


def omega_x_kernel(
    vel_ref, metric_ref, mine_ref, v_ref, w_ref, first_ref, ox_ref, wide, along
):
    half, ny, snaps, nz = ox_ref.shape
    group = lax.axis_index("snap")
    matrix = z_stencil(nz)
    for slot, base in ((0, (1 - group) * half), (1, group * half)):
        if slot == 0:
            for i in range(half):
                flip(vel_ref[:, 1, base + i], wide, v_ref, i)
        z_derivative(mine_ref[0] if slot else v_ref[...], matrix, along)
        for i in range(half):
            if slot == 0:
                spread(vel_ref[:, 2, base + i], wide)

            def load(j):
                if slot:
                    return mine_ref[1, i, j].astype(jnp.float32)
                value = row(wide, j, snaps, ny)
                w_ref[i, j] = value.astype(jnp.bfloat16)
                return value

            for y, across in y_stencils(load, ny):
                value = across * factor(metric_ref, 1, base + i, y)
                value = value - along[i, y] * factor(metric_ref, 2, base + i, y)
                value = value.astype(jnp.bfloat16)
                if slot:
                    ox_ref[i, y] = value
                if slot * half + i < first_ref.shape[0]:
                    first_ref[slot * half + i, y] = value


def u_kernel(half, vel_ref, metric_ref, zu_ref, yu_ref, flat, wide, along):
    snaps, _, _, ny, nz = vel_ref.shape
    matrix = z_stencil(nz)
    group = lax.axis_index("snap")
    for slot in range(2):
        base = (group if slot else 1 - group) * half
        for i in range(half):
            spread(vel_ref[:, 0, base + i], wide)

            def load(j):
                value = row(wide, j, snaps, ny)
                flat[i, j] = value.astype(jnp.bfloat16)
                return value

            for y, across in y_stencils(load, ny):
                yu_ref[slot, i, y] = across * factor(metric_ref, 1, base + i, y)
        z_derivative(flat[...], matrix, along)
        for i in range(half):
            for y in range(ny):
                zu_ref[slot, i, y] = along[i, y] * factor(metric_ref, 2, base + i, y)


def finish_curl(sign, slot, near_ref, far_ref, halo_ref, known_ref, metric_ref, out_ref):
    half, ny, _, _ = near_ref.shape
    group = lax.axis_index("snap")
    part = group if slot else 1 - group

    def run(low_ref, high_ref):
        def plane(i, y):
            if i < 0:
                ref, k = low_ref, half + i
            elif i < half:
                ref, k = near_ref, i
            else:
                ref, k = high_ref, i - half
            return ref[k, y].astype(jnp.float32)

        for y in range(ny):
            at = [plane(i, y) for i in range(-WIDTH, half + WIDTH)]
            for i in range(half):
                along = 8.0 * (at[i + 3] - at[i + 1]) - (at[i + 4] - at[i])
                along = along * factor(metric_ref, 0, part * half + i, y)
                known = known_ref[slot, i, y]
                value = along - known if sign > 0 else known - along
                out_ref[i, y] = value.astype(jnp.bfloat16)

    @pl.when(part == 0)
    def _():
        run(halo_ref, far_ref)

    @pl.when(part == 1)
    def _():
        run(far_ref, halo_ref)


def omega_yz_kernel(slot, near, far, edge, zu_ref, yu_ref, metric_ref, y_ref, z_ref):
    known = (yu_ref, zu_ref)
    for c, sign, out_ref in ((1, -1, y_ref), (0, 1, z_ref)):
        fields = near[c], far[c], edge[c], known[c]
        finish_curl(sign, slot, *fields, metric_ref, out_ref)


def omega_theirs_kernel(v_ref, w_ref, far, edge, *refs):
    far, edge, outs = [(ref.at[0], ref.at[1]) for ref in (far, edge, refs[-1])]
    omega_yz_kernel(0, (v_ref, w_ref), far, edge, *refs[:-1], *outs)


def omega_mine_kernel(*refs):
    near, far_v, far_w, edge_v, edge_w, *refs, ox_ref, out_ref = refs
    near, far = (near.at[0], near.at[1]), (far_v, far_w)
    half = ox_ref.shape[0]
    left = out_ref.shape[0] - 2 * half
    out_ref[:left] = ox_ref[half - left :]
    parts = [out_ref.at[pl.ds(left + n * half, half)] for n in range(2)]
    omega_yz_kernel(1, near, far, (edge_v, edge_w), *refs, *parts)


def gram_of(own, got, volume_ref, base):
    half, ny, _, _ = own.shape
    total = None
    for i in range(half):
        plain, heavy = [], []
        for y in range(ny):
            pair = jnp.concatenate([own[i, y], got[i, y]], axis=0)
            weight = volume_ref[base + i, pl.ds(y, 1), :]
            plain.append(pair)
            heavy.append((pair.astype(jnp.float32) * weight).astype(jnp.bfloat16))
        part = lax.dot_general(
            jnp.concatenate(heavy, axis=1),
            jnp.concatenate(plain, axis=1),
            (((1,), (1,)), ((), ())),
            preferred_element_type=jnp.float32,
        )
        total = part if total is None else total + part
    return total


def gram_kernel(parts, own_ref, got_ref, volume_ref, *refs):
    half = volume_ref.shape[0] // 2
    base = lax.axis_index("snap") * half
    total = None
    for own, got in parts:
        own, got = own_ref.at[pl.ds(own, half)], got_ref.at[pl.ds(got, half)]
        part = gram_of(own, got, volume_ref, base)
        total = part if total is None else total + part
    for earlier in refs[:-1]:
        total = total + earlier[...]
    if len(refs[-1].shape) == 3:
        count, rows, _ = refs[-1].shape
        total = jnp.concatenate(
            [total[n : n + rows] for n in range(0, total.shape[0], rows)], axis=1
        )
        for peer in range(count):
            refs[-1][peer] = total
    else:
        refs[-1][...] = total


def add_kernel(parts_ref, own_ref, other_ref):
    peers, rows, _ = parts_ref.shape
    group = lax.axis_index("snap")
    side = own_ref.shape[0]
    for out_ref, first in ((own_ref, group), (other_ref, 1 - group)):
        parts = [parts_ref[n + first] for n in range(0, peers, 2)]
        while len(parts) > 1:
            parts = [sum(parts[n : n + 2]) for n in range(0, len(parts), 2)]
        for n in range(side // rows):
            out_ref[n * rows : (n + 1) * rows] = parts[0][:, n * side : (n + 1) * side]


def coeff_kernel(coeff_ref, mine_ref, block_ref):
    snaps, count = mine_ref.shape
    rows = block_ref.shape[0]
    base = lax.axis_index("snap") * snaps

    def chosen(shape, test):
        left = lax.broadcasted_iota(jnp.int32, shape, 0)
        right = lax.broadcasted_iota(jnp.int32, shape, 1)
        return jnp.where(test(left, right), 1.0, 0.0).astype(jnp.bfloat16)

    def take(a, b, dims):
        out = lax.dot_general(a, b, (dims, ((), ())), preferred_element_type=jnp.float32)
        return out.astype(jnp.bfloat16)

    mine = chosen((snaps, count), lambda k, m: m == k + base)
    mine = take(mine, coeff_ref[...], ((1,), (1,)))
    order = chosen((count, count), lambda j, m: j == lax.rem(m + base, count))
    mine = take(mine, order, ((1,), (0,)))
    mine_ref[...] = mine.astype(jnp.float32)
    down = chosen((rows, snaps), lambda r, k: lax.rem(r, snaps) == k)
    for part in range(count // snaps):
        across = chosen((count, rows), lambda j, c: j == lax.rem(c, snaps) + part * snaps)
        wide = take(take(down, mine, ((1,), (0,))), across, ((1,), (0,)))
        same = chosen((rows, rows), lambda r, c: lax.div(r, snaps) == lax.div(c, snaps))
        block_ref[:, part * rows : (part + 1) * rows] = wide * same


def raw_blocks(own, got, block_ref, put):
    ny, snaps, nz = own.shape
    block = block_ref.shape[0] // snaps
    lanes = 2 if ny % (2 * block) == 0 else 1
    for start in range(0, ny, block * lanes):
        columns = []
        for n in range(lanes):
            at = start + n * block
            parts = [ref[at : at + block].reshape(block * snaps, nz) for ref in (own, got)]
            columns.append(jnp.concatenate(parts, axis=0))
        both = columns[0] if lanes == 1 else jnp.concatenate(columns, axis=1)
        raw = jnp.dot(block_ref[...], both, preferred_element_type=jnp.float32)
        for n in range(lanes):
            part = raw[:, n * nz : (n + 1) * nz].reshape(block, snaps, nz)
            for k in range(block):
                put(start + n * block + k, part[k])


def raw_kernel(parts, own_ref, got_ref, block_ref, *outs):
    for (own, got), out_ref in zip(parts, outs):
        _, ny, snaps, _ = own_ref.shape
        count = out_ref.shape[0] // (snaps * ny)
        for i in range(count):

            def put(y, value):
                out_ref[pl.ds(i * ny + y, snaps, count * ny), :] = value

            raw_blocks(own_ref.at[own + i], got_ref.at[got + i], block_ref, put)


def finish_kernel(
    half, scale, part_ref, other_ref, coeff_ref, block_ref,
    x_theirs, x_mine, y_mine, z_mine, own_x, own_yz, got_ref,
    out_ref, rows_ref, stage, rows_buf, factors, wide, sems,
):
    _, snaps, _, ny, nz = stage.shape
    group = lax.axis_index("snap")
    other = other_ref[...]
    other = jnp.concatenate([other[snaps:], other[:snaps]], axis=0)
    other = jnp.concatenate([other[:, snaps:], other[:, :snaps]], axis=1)
    total = (part_ref[...] + other) * scale
    coeff = coeff_ref[...]
    inner = jnp.dot(
        coeff, total, precision=lax.Precision.HIGHEST, preferred_element_type=jnp.float32
    )
    energy = jnp.sum(inner * coeff, axis=1, keepdims=True)
    factor = jnp.broadcast_to(1.0 / jnp.sqrt(energy + EPS), (snaps, nz))
    factors[...] = factor
    mine = total[:snaps]
    turned = jnp.concatenate([mine[:, snaps:], mine[:, :snaps]], axis=1)
    rows_buf[...] = jnp.where(group == 0, mine, turned)
    copies = [pltpu.make_async_copy(rows_buf, rows_ref, sems.at[6])]
    copies[0].start()
    bases = (1 - group) * half, group * half

    def send(c, slot):
        n = 2 * c + slot
        target = out_ref.at[:, c, pl.ds(bases[slot], half)]
        copies.append(pltpu.make_async_copy(stage.at[n], target, sems.at[n]))
        copies[-1].start()

    for c, raw_ref in enumerate((x_mine, y_mine, z_mine)):
        for k in range(snaps):
            value = raw_ref[k * half * ny : (k + 1) * half * ny, :] * factors[k : k + 1, :]
            stage[2 * c + 1, k] = value.astype(jnp.bfloat16).reshape(half, ny, nz)
        send(c, 1)
    early = x_theirs.shape[0] // (snaps * ny)
    for k in range(snaps):
        value = x_theirs[k * early * ny : (k + 1) * early * ny, :] * factors[k : k + 1, :]
        stage[0, k, :early] = value.astype(jnp.bfloat16).reshape(early, ny, nz)
    late = [(0, i, own_x.at[i]) for i in range(early, half)]
    late += [(c, i, own_yz.at[(c - 1) * half + i]) for c in (1, 2) for i in range(half)]
    for n, (c, i, own) in enumerate(late):
        rows = wide.at[n % wide.shape[0]]

        def put(y, value):
            rows[pl.ds(y, snaps, ny), :] = value * factor

        raw_blocks(own, got_ref.at[n], block_ref, put)
        for k in range(snaps):
            stage[2 * c, k, i] = rows[k * ny : (k + 1) * ny, :].astype(jnp.bfloat16)
        if i == half - 1:
            send(c, 0)
    for copy in copies:
        copy.wait()


def two_groups(velocity, metric, volume, coeffs):
    snaps, _, layers, ny, nz = velocity.shape
    half = layers // 2
    peers = lax.axis_size("space")
    bf16, f32 = jnp.bfloat16, jnp.float32

    def halo(first):
        pairs = []
        for s in range(peers):
            for g in range(2):
                down = (g == 0) == first
                pairs.append((s * 2 + g, ((s + (-1 if down else 1)) % peers) * 2 + g))
        return pairs

    def swap(value):
        return lax.ppermute(value, "snap", [(0, 1), (1, 0)])

    def shift(value, first):
        return lax.ppermute(value, ("space", "snap"), halo(first))

    field = jax.ShapeDtypeStruct((half, ny, snaps, nz), bf16)
    pair = jax.ShapeDtypeStruct((2, half, ny, snaps, nz), bf16)
    partial_sum = jax.ShapeDtypeStruct((2, half, ny, snaps, nz), f32)
    square = jax.ShapeDtypeStruct((2 * snaps, 2 * snaps), f32)
    cells = half * ny * snaps * nz
    wide = pltpu.VMEM((snaps * ny, nz), f32)
    along = pltpu.VMEM((half, ny, snaps, nz), f32)
    dma = pltpu.SemaphoreType.DMA

    def call(kernel, name, out_shape, args, scratch=(), in_specs=None, out_specs=None, work=5):
        return pl.pallas_call(
            kernel,
            out_shape=out_shape,
            in_specs=in_specs or [vmem()] * len(args),
            out_specs=out_specs or jax.tree.map(lambda _: vmem(), out_shape),
            scratch_shapes=list(scratch),
            compiler_params=params(),
            cost_estimate=cost(2 * work * cells, work * cells),
            name=name,
        )(*args)

    mine = call(
        flip_kernel,
        "flip_mine",
        pair,
        [pltpu.with_memory_space_constraint(velocity, pltpu.HBM)],
        [pltpu.VMEM((snaps, 2, half, ny, nz), bf16), wide, dma((2, half))],
        [hbm()],
    )
    edge_theirs = shift(mine, True)
    early = half // 2
    first = jax.ShapeDtypeStruct((half + early, ny, snaps, nz), bf16)
    last = jax.ShapeDtypeStruct((3 * half - early, ny, snaps, nz), bf16)
    *theirs, x_first, x_mine = call(
        omega_x_kernel,
        "omega_x",
        (field, field, first, field),
        [velocity, metric, mine],
        [wide, along],
    )
    got_first = swap(x_first)
    zu, yu = call(
        functools.partial(u_kernel, half),
        "u_terms",
        (partial_sum, partial_sum),
        [velocity, metric],
        [pltpu.VMEM((half, ny, snaps, nz), bf16), wide, along],
    )

    def gram_part(name, parts, shape, *args):
        return call(functools.partial(gram_kernel, parts), name, shape, args)

    def raw_modes(name, parts, counts, own, got):
        shapes = tuple(jax.ShapeDtypeStruct((snaps * n * ny, nz), f32) for n in counts)
        return call(functools.partial(raw_kernel, parts), name, shapes, [own, got, blocks])

    yz_theirs = call(
        omega_theirs_kernel,
        "omega_yz_theirs",
        pair,
        [*theirs, mine, edge_theirs, zu, yu, metric],
    )
    got_yz = swap(yz_theirs)
    *late, _ = lax.optimization_barrier((*theirs, yz_theirs))
    edge_mine = [shift(part, False) for part in late]
    coeff_rows, blocks = call(
        coeff_kernel,
        "coeff_blocks",
        (
            jax.ShapeDtypeStruct((snaps, 2 * snaps), f32),
            jax.ShapeDtypeStruct((ROWS // snaps * snaps, ROWS // snaps * 2 * snaps), bf16),
        ),
        [coeffs],
    )
    gram = gram_part("gram_x", ((0, 0),), square, x_mine, got_first, volume)
    (mine_x,) = raw_modes("raw_x_mine", ((0, 0),), (half,), x_mine, got_first)
    (theirs_x,) = raw_modes("raw_x_theirs", ((0, half),), (early,), x_first, got_first)
    *edge_mine, gram, mine_x, theirs_x = lax.optimization_barrier(
        (*edge_mine, gram, mine_x, theirs_x)
    )
    yz_mine = call(
        omega_mine_kernel,
        "omega_yz_mine",
        last,
        [mine, *theirs, *edge_mine, zu, yu, metric, x_mine],
    )
    got_last = swap(yz_mine)
    got_yz = got_yz.reshape(2 * half, ny, snaps, nz)
    left = half - early
    copies = jax.ShapeDtypeStruct((2 * peers, 4 * snaps**2 // nz, nz), f32)
    parts = ((left, 0), (left + half, half))
    grams = gram_part("gram_yz", parts, copies, yz_mine, got_yz, volume, gram)
    mine_yz = raw_modes("raw_yz_mine", parts, (half, half), yz_mine, got_yz)
    grams, *mine_yz = lax.optimization_barrier((grams, *mine_yz))
    grams = lax.all_to_all(grams, ("space", "snap"), 0, 0, tiled=True)
    gram, other = call(add_kernel, "add", (square, square), [grams])
    yz_theirs = yz_theirs.reshape(2 * half, ny, snaps, nz)
    modes, rows = call(
        functools.partial(finish_kernel, half, 1.0 / (3.0 * layers * peers * ny * nz)),
        "finish",
        (
            jax.ShapeDtypeStruct(velocity.shape, bf16),
            jax.ShapeDtypeStruct((snaps, 2 * snaps), f32),
        ),
        [
            gram, other, coeff_rows, blocks, theirs_x, mine_x, *mine_yz,
            x_first, yz_theirs, got_last,
        ],
        [
            pltpu.VMEM((6, snaps, half, ny, nz), bf16),
            pltpu.VMEM((snaps, 2 * snaps), f32),
            pltpu.VMEM((snaps, nz), f32),
            pltpu.VMEM((half, snaps * ny, nz), f32),
            dma((7,)),
        ],
        None,
        (hbm(), hbm()),
    )
    return (rows, modes)


def per_device(velocity, metric, volume, coeffs):
    peers = lax.axis_size("space")
    paired = lax.axis_size("snap") == 2 and velocity.shape[2] == 2 * WIDTH
    if paired and velocity.shape[0] % 16 == 0 and peers & (peers - 1) == 0:
        return two_groups(velocity, metric, volume, coeffs)
    return many_groups(velocity, metric, volume, coeffs)


def solution(mesh):
    placed = (
        P("snap", None, "space", None, None),
        P(None, "space", None, None),
        P("space", None, None),
        P(),
    )
    return jax.shard_map(
        per_device,
        mesh=mesh,
        in_specs=placed,
        out_specs=(P("snap", None), P("snap", None, "space", None, None)),
        check_vma=False,
    )
```

```python
import functools

import jax
import jax.numpy as jnp
from jax import lax
from jax.experimental import pallas as pl
from jax.experimental.pallas import tpu as pltpu
from jax.sharding import PartitionSpec as P

EPS = 1e-06
WIDTH = 2
ROWS = 128
LIMIT = 24 * 1024 * 1024


def with_halo(shard, sides, width):
    for axis, dim in sides:
        peers, length = (lax.axis_size(axis), shard.shape[dim])
        up = [(i, (i + 1) % peers) for i in range(peers)]
        down = [(j, i) for i, j in up]
        last = lax.slice_in_dim(shard, length - width, length, axis=dim)
        leading = lax.slice_in_dim(shard, 0, width, axis=dim)
        before = lax.ppermute(last, axis, up)
        after = lax.ppermute(leading, axis, down)
        shard = jnp.concatenate([before, shard, after], axis=dim)
    return shard


def deriv(padded, dim):
    count = padded.shape[dim] - 4

    def cut(offset):
        return lax.slice_in_dim(padded, offset, offset + count, axis=dim)

    return (8.0 * (cut(3) - cut(1)) - (cut(4) - cut(0))) / 12.0


def curl(padded_x, metric):
    inner = padded_x[:, :, 2:-2]
    padded_y = jnp.pad(inner, ((0, 0), (0, 0), (0, 0), (2, 2), (0, 0)))
    padded_z = jnp.concatenate([inner[..., -2:], inner, inner[..., :2]], axis=4)
    along_x = deriv(padded_x, 2) * metric[0]
    along_y = deriv(padded_y, 3) * metric[1]
    along_z = deriv(padded_z, 4) * metric[2]
    omega_x = along_y[:, 2] - along_z[:, 1]
    omega_y = along_z[:, 0] - along_x[:, 2]
    omega_z = along_x[:, 1] - along_y[:, 0]
    return jnp.stack([omega_x, omega_y, omega_z], axis=1).astype(jnp.bfloat16)


def many_groups(velocity, metric, volume, coeffs):
    snap_dev = velocity.shape[0]
    snaps = coeffs.shape[0]
    group = lax.axis_index("snap")
    scale = 1.0 / (
        3.0 * volume.shape[0] * lax.axis_size("space") * volume.shape[1] * volume.shape[2]
    )
    padded = with_halo(velocity, (("space", 2),), 2)
    vorticity = curl(padded.astype(jnp.float32), metric)
    coeff_f = coeffs.astype(jnp.float32)
    moved = lax.all_to_all(vorticity, "snap", split_axis=3, concat_axis=0, tiled=True)
    part_y = moved.shape[3]
    vol_part = lax.dynamic_slice_in_dim(volume, group * part_y, part_y, 1)
    weighted = (moved.astype(jnp.float32) * vol_part).astype(jnp.bfloat16).reshape(snaps, -1)
    flat = moved.reshape(snaps, -1)
    partial_value = lax.dot_general(
        weighted, flat, (((1,), (1,)), ((), ())), preferred_element_type=jnp.float32
    )
    raw = lax.dot_general(
        coeffs, flat, (((0,), (0,)), ((), ())), preferred_element_type=jnp.float32
    )
    whole = lax.psum(partial_value, ("space", "snap")) * scale
    energy = jnp.sum(coeff_f * jnp.dot(whole, coeff_f, precision=lax.Precision.HIGHEST), axis=0)
    rows = lax.dynamic_slice_in_dim(whole, group * snap_dev, snap_dev, 0)
    local_modes = (raw / jnp.sqrt(energy + EPS)[:, None]).astype(jnp.bfloat16).reshape(moved.shape)
    modes = lax.all_to_all(local_modes, "snap", split_axis=0, concat_axis=3, tiled=True)
    return (rows, modes)


def vmem():
    return pl.BlockSpec(memory_space=pltpu.VMEM)


def hbm():
    return pl.BlockSpec(memory_space=pltpu.HBM)


def params():
    return pltpu.CompilerParams(vmem_limit_bytes=LIMIT)


def cost(flops, moved):
    return pl.CostEstimate(flops=flops, bytes_accessed=moved, transcendentals=0)


def z_stencil(size):
    rows = lax.broadcasted_iota(jnp.int32, (size, size), 0)
    cols = lax.broadcasted_iota(jnp.int32, (size, size), 1)
    ahead = rows - cols
    ahead = jnp.where(ahead < 0, ahead + size, ahead)
    out = jnp.where(ahead == 1, 8.0, 0.0) - jnp.where(ahead == size - 1, 8.0, 0.0)
    out = out - jnp.where(ahead == 2, 1.0, 0.0) + jnp.where(ahead == size - 2, 1.0, 0.0)
    return out.astype(jnp.bfloat16)


def spread(src, wide):
    snaps, ny, nz = src.shape
    wide[...] = src.astype(jnp.float32).reshape(snaps * ny, nz)


def row(wide, y, snaps, ny):
    return wide[pl.ds(y, snaps, ny), :]


def y_stencils(load, ny):
    held = {}

    def at(j):
        if j not in held:
            held[j] = load(j)
        return held[j]

    zero = jnp.zeros_like(at(0))
    for y in range(ny):
        near = (at(y + 1) if y + 1 < ny else zero) - (at(y - 1) if y >= 1 else zero)
        far = (at(y + 2) if y + 2 < ny else zero) - (at(y - 2) if y >= 2 else zero)
        held.pop(y - 2, None)
        yield y, 8.0 * near - far


def z_derivative(field, matrix, along):
    rows = field.shape[0] * field.shape[1] * field.shape[2]
    along[...] = jnp.dot(
        field.reshape(rows, field.shape[3]), matrix, preferred_element_type=jnp.float32
    ).reshape(field.shape)


def factor(metric_ref, m, layer, y):
    return metric_ref[m, layer, pl.ds(y, 1), :] * (1.0 / 12.0)


def flip(src, wide, out_ref, i):
    snaps, ny, _ = src.shape
    spread(src, wide)
    for y in range(ny):
        out_ref[i, y] = row(wide, y, snaps, ny).astype(jnp.bfloat16)


def flip_kernel(vel_ref, out_ref, buf, wide, sems):
    half = out_ref.shape[1]
    base = lax.axis_index("snap") * half
    copies = {}
    for c in range(2):
        for i in range(half):
            source = vel_ref.at[:, 1 + c, base + i]
            copies[c, i] = pltpu.make_async_copy(source, buf.at[:, c, i], sems.at[c, i])
            copies[c, i].start()
    for c in range(2):
        for i in range(half):
            copies[c, i].wait()
            flip(buf[:, c, i], wide, out_ref.at[c], i)


def omega_x_kernel(
    vel_ref, metric_ref, mine_ref, v_ref, w_ref, first_ref, ox_ref, wide, along
):
    half, ny, snaps, nz = ox_ref.shape
    group = lax.axis_index("snap")
    matrix = z_stencil(nz)
    for slot, base in ((0, (1 - group) * half), (1, group * half)):
        if slot == 0:
            for i in range(half):
                flip(vel_ref[:, 1, base + i], wide, v_ref, i)
        z_derivative(mine_ref[0] if slot else v_ref[...], matrix, along)
        for i in range(half):
            if slot == 0:
                spread(vel_ref[:, 2, base + i], wide)

            def load(j):
                if slot:
                    return mine_ref[1, i, j].astype(jnp.float32)
                value = row(wide, j, snaps, ny)
                w_ref[i, j] = value.astype(jnp.bfloat16)
                return value

            for y, across in y_stencils(load, ny):
                value = across * factor(metric_ref, 1, base + i, y)
                value = value - along[i, y] * factor(metric_ref, 2, base + i, y)
                value = value.astype(jnp.bfloat16)
                if slot:
                    ox_ref[i, y] = value
                if slot * half + i < first_ref.shape[0]:
                    first_ref[slot * half + i, y] = value


def u_kernel(half, vel_ref, metric_ref, zu_ref, yu_ref, flat, wide, along):
    snaps, _, _, ny, nz = vel_ref.shape
    matrix = z_stencil(nz)
    group = lax.axis_index("snap")
    for slot in range(2):
        base = (group if slot else 1 - group) * half
        for i in range(half):
            spread(vel_ref[:, 0, base + i], wide)

            def load(j):
                value = row(wide, j, snaps, ny)
                flat[i, j] = value.astype(jnp.bfloat16)
                return value

            for y, across in y_stencils(load, ny):
                yu_ref[slot, i, y] = across * factor(metric_ref, 1, base + i, y)
        z_derivative(flat[...], matrix, along)
        for i in range(half):
            for y in range(ny):
                zu_ref[slot, i, y] = along[i, y] * factor(metric_ref, 2, base + i, y)


def finish_curl(sign, slot, near_ref, far_ref, halo_ref, known_ref, metric_ref, out_ref):
    half, ny, _, _ = near_ref.shape
    group = lax.axis_index("snap")
    part = group if slot else 1 - group

    def run(low_ref, high_ref):
        def plane(i, y):
            if i < 0:
                ref, k = low_ref, half + i
            elif i < half:
                ref, k = near_ref, i
            else:
                ref, k = high_ref, i - half
            return ref[k, y].astype(jnp.float32)

        for y in range(ny):
            at = [plane(i, y) for i in range(-WIDTH, half + WIDTH)]
            for i in range(half):
                along = 8.0 * (at[i + 3] - at[i + 1]) - (at[i + 4] - at[i])
                along = along * factor(metric_ref, 0, part * half + i, y)
                known = known_ref[slot, i, y]
                value = along - known if sign > 0 else known - along
                out_ref[i, y] = value.astype(jnp.bfloat16)

    @pl.when(part == 0)
    def _():
        run(halo_ref, far_ref)

    @pl.when(part == 1)
    def _():
        run(far_ref, halo_ref)


def omega_yz_kernel(slot, near, far, edge, zu_ref, yu_ref, metric_ref, y_ref, z_ref):
    known = (yu_ref, zu_ref)
    for c, sign, out_ref in ((1, -1, y_ref), (0, 1, z_ref)):
        fields = near[c], far[c], edge[c], known[c]
        finish_curl(sign, slot, *fields, metric_ref, out_ref)


def omega_theirs_kernel(v_ref, w_ref, far, edge, *refs):
    far, edge, outs = [(ref.at[0], ref.at[1]) for ref in (far, edge, refs[-1])]
    omega_yz_kernel(0, (v_ref, w_ref), far, edge, *refs[:-1], *outs)


def omega_mine_kernel(*refs):
    near, far_v, far_w, edge_v, edge_w, *refs, ox_ref, out_ref = refs
    near, far = (near.at[0], near.at[1]), (far_v, far_w)
    half = ox_ref.shape[0]
    left = out_ref.shape[0] - 2 * half
    out_ref[:left] = ox_ref[half - left :]
    parts = [out_ref.at[pl.ds(left + n * half, half)] for n in range(2)]
    omega_yz_kernel(1, near, far, (edge_v, edge_w), *refs, *parts)


def gram_of(own, got, volume_ref, base):
    half, ny, _, _ = own.shape
    total = None
    for i in range(half):
        plain, heavy = [], []
        for y in range(ny):
            pair = jnp.concatenate([own[i, y], got[i, y]], axis=0)
            weight = volume_ref[base + i, pl.ds(y, 1), :]
            plain.append(pair)
            heavy.append((pair.astype(jnp.float32) * weight).astype(jnp.bfloat16))
        part = lax.dot_general(
            jnp.concatenate(heavy, axis=1),
            jnp.concatenate(plain, axis=1),
            (((1,), (1,)), ((), ())),
            preferred_element_type=jnp.float32,
        )
        total = part if total is None else total + part
    return total


def gram_sum(parts, own_ref, got_ref, volume_ref, earlier):
    half = volume_ref.shape[0] // 2
    base = lax.axis_index("snap") * half
    total = None if earlier is None else earlier[...]
    for own, got in parts:
        own, got = own_ref.at[pl.ds(own, half)], got_ref.at[pl.ds(got, half)]
        part = gram_of(own, got, volume_ref, base)
        total = part if total is None else total + part
    return total


def gram_x_kernel(parts, own_ref, got_ref, volume_ref, out_ref):
    out_ref[...] = gram_sum(parts, own_ref, got_ref, volume_ref, None)


def messages_kernel(parts, scale, own_ref, got_ref, volume_ref, earlier, coeff_ref, out_ref):
    total = gram_sum(parts, own_ref, got_ref, volume_ref, earlier) * scale
    coeff = coeff_ref[...]
    inner = jnp.dot(
        total, coeff, precision=lax.Precision.HIGHEST, preferred_element_type=jnp.float32
    )
    energy = jnp.sum(inner * coeff, axis=0, keepdims=True)
    snaps = total.shape[0] // 2
    turned = jnp.concatenate([total[snaps:, snaps:], total[snaps:, :snaps]], axis=1)
    group = lax.axis_index("snap")
    spare = out_ref.shape[2] - 2 * snaps * snaps - snaps
    for other, rows in enumerate((total[:snaps], turned)):
        line = [rows[k : k + 1] for k in range(snaps)]
        line.append(energy[:, other * snaps : (other + 1) * snaps])
        line = jnp.concatenate(line + [jnp.zeros((1, spare), jnp.float32)], axis=1)
        first = 1 - group if other else group
        for n in range(0, out_ref.shape[0], 2):
            out_ref[n + first] = line


def coeff_kernel(coeff_ref, ordered_ref, block_ref):
    count, _ = coeff_ref.shape
    snaps = count // 2
    rows = block_ref.shape[0]
    base = lax.axis_index("snap") * snaps

    def chosen(shape, test):
        left = lax.broadcasted_iota(jnp.int32, shape, 0)
        right = lax.broadcasted_iota(jnp.int32, shape, 1)
        return jnp.where(test(left, right), 1.0, 0.0).astype(jnp.bfloat16)

    def take(a, b, dims):
        out = lax.dot_general(a, b, (dims, ((), ())), preferred_element_type=jnp.float32)
        return out.astype(jnp.bfloat16)

    order = chosen((count, count), lambda j, m: j == lax.rem(m + base, count))
    turned = take(take(order, coeff_ref[...], ((0,), (1,))), order, ((1,), (0,)))
    same = chosen((count, count), lambda j, m: j == m)
    ordered_ref[...] = take(same, turned, ((1,), (1,))).astype(jnp.float32)
    mine = turned[:snaps]
    down = chosen((rows, snaps), lambda r, k: lax.rem(r, snaps) == k)
    for part in range(count // snaps):
        across = chosen((count, rows), lambda j, c: j == lax.rem(c, snaps) + part * snaps)
        wide = take(take(down, mine, ((1,), (0,))), across, ((1,), (0,)))
        same = chosen((rows, rows), lambda r, c: lax.div(r, snaps) == lax.div(c, snaps))
        block_ref[:, part * rows : (part + 1) * rows] = wide * same


def raw_blocks(own, got, block_ref, put):
    ny, snaps, nz = own.shape
    block = block_ref.shape[0] // snaps
    lanes = 2 if ny % (2 * block) == 0 else 1
    for start in range(0, ny, block * lanes):
        columns = []
        for n in range(lanes):
            at = start + n * block
            parts = [ref[at : at + block].reshape(block * snaps, nz) for ref in (own, got)]
            columns.append(jnp.concatenate(parts, axis=0))
        both = columns[0] if lanes == 1 else jnp.concatenate(columns, axis=1)
        raw = jnp.dot(block_ref[...], both, preferred_element_type=jnp.float32)
        for n in range(lanes):
            part = raw[:, n * nz : (n + 1) * nz].reshape(block, snaps, nz)
            for k in range(block):
                put(start + n * block + k, part[k])


def raw_kernel(parts, own_ref, got_ref, block_ref, *outs):
    for (own, got), out_ref in zip(parts, outs):
        _, ny, snaps, _ = own_ref.shape
        count = out_ref.shape[0] // (snaps * ny)
        for i in range(count):

            def put(y, value):
                out_ref[pl.ds(i * ny + y, snaps, count * ny), :] = value

            raw_blocks(own_ref.at[own + i], got_ref.at[got + i], block_ref, put)


def finish_kernel(
    half, parts_ref, block_ref,
    x_theirs, x_mine, y_mine, z_mine, own_x, own_yz, got_ref,
    out_ref, rows_ref, stage, rows_buf, factors, wide, sems,
):
    _, snaps, _, ny, nz = stage.shape
    group = lax.axis_index("snap")
    lines = [parts_ref[n] for n in range(parts_ref.shape[0])]
    while len(lines) > 1:
        lines = [sum(lines[n : n + 2]) for n in range(0, len(lines), 2)]
    width = 2 * snaps
    line = lines[0][:, snaps * width : snaps * (width + 1)]
    down = lax.broadcasted_iota(jnp.int32, (snaps, snaps), 0)
    across = lax.broadcasted_iota(jnp.int32, (snaps, snaps), 1)
    energy = jnp.where(down == across, jnp.broadcast_to(line, (snaps, snaps)), 0.0)
    energy = jnp.sum(energy, axis=1, keepdims=True)
    factor = jnp.broadcast_to(1.0 / jnp.sqrt(energy + EPS), (snaps, nz))
    factors[...] = factor
    mine = jnp.concatenate(
        [lines[0][:, k * width : (k + 1) * width] for k in range(snaps)], axis=0
    )
    turned = jnp.concatenate([mine[:, snaps:], mine[:, :snaps]], axis=1)
    rows_buf[...] = jnp.where(group == 0, mine, turned)
    copies = [pltpu.make_async_copy(rows_buf, rows_ref, sems.at[6])]
    copies[0].start()
    bases = (1 - group) * half, group * half

    def send(c, slot):
        n = 2 * c + slot
        target = out_ref.at[:, c, pl.ds(bases[slot], half)]
        copies.append(pltpu.make_async_copy(stage.at[n], target, sems.at[n]))
        copies[-1].start()

    for c, raw_ref in enumerate((x_mine, y_mine, z_mine)):
        for k in range(snaps):
            value = raw_ref[k * half * ny : (k + 1) * half * ny, :] * factors[k : k + 1, :]
            stage[2 * c + 1, k] = value.astype(jnp.bfloat16).reshape(half, ny, nz)
        send(c, 1)
    early = x_theirs.shape[0] // (snaps * ny)
    for k in range(snaps):
        value = x_theirs[k * early * ny : (k + 1) * early * ny, :] * factors[k : k + 1, :]
        stage[0, k, :early] = value.astype(jnp.bfloat16).reshape(early, ny, nz)
    late = [(0, i, own_x.at[i]) for i in range(early, half)]
    late += [(c, i, own_yz.at[(c - 1) * half + i]) for c in (1, 2) for i in range(half)]
    for n, (c, i, own) in enumerate(late):
        rows = wide.at[n % wide.shape[0]]

        def put(y, value):
            rows[pl.ds(y, snaps, ny), :] = value * factor

        raw_blocks(own, got_ref.at[n], block_ref, put)
        for k in range(snaps):
            stage[2 * c, k, i] = rows[k * ny : (k + 1) * ny, :].astype(jnp.bfloat16)
        if i == half - 1:
            send(c, 0)
    for copy in copies:
        copy.wait()


def two_groups(velocity, metric, volume, coeffs):
    snaps, _, layers, ny, nz = velocity.shape
    half = layers // 2
    peers = lax.axis_size("space")
    bf16, f32 = jnp.bfloat16, jnp.float32

    def halo(first):
        pairs = []
        for s in range(peers):
            for g in range(2):
                down = (g == 0) == first
                pairs.append((s * 2 + g, ((s + (-1 if down else 1)) % peers) * 2 + g))
        return pairs

    def swap(value):
        return lax.ppermute(value, "snap", [(0, 1), (1, 0)])

    def shift(value, first):
        return lax.ppermute(value, ("space", "snap"), halo(first))

    field = jax.ShapeDtypeStruct((half, ny, snaps, nz), bf16)
    pair = jax.ShapeDtypeStruct((2, half, ny, snaps, nz), bf16)
    partial_sum = jax.ShapeDtypeStruct((2, half, ny, snaps, nz), f32)
    square = jax.ShapeDtypeStruct((2 * snaps, 2 * snaps), f32)
    cells = half * ny * snaps * nz
    wide = pltpu.VMEM((snaps * ny, nz), f32)
    along = pltpu.VMEM((half, ny, snaps, nz), f32)
    dma = pltpu.SemaphoreType.DMA

    def call(kernel, name, out_shape, args, scratch=(), in_specs=None, out_specs=None, work=5):
        return pl.pallas_call(
            kernel,
            out_shape=out_shape,
            in_specs=in_specs or [vmem()] * len(args),
            out_specs=out_specs or jax.tree.map(lambda _: vmem(), out_shape),
            scratch_shapes=list(scratch),
            compiler_params=params(),
            cost_estimate=cost(2 * work * cells, work * cells),
            name=name,
        )(*args)

    mine = call(
        flip_kernel,
        "flip_mine",
        pair,
        [pltpu.with_memory_space_constraint(velocity, pltpu.HBM)],
        [pltpu.VMEM((snaps, 2, half, ny, nz), bf16), wide, dma((2, half))],
        [hbm()],
    )
    edge_theirs = shift(mine, True)
    early = half // 2
    first = jax.ShapeDtypeStruct((half + early, ny, snaps, nz), bf16)
    last = jax.ShapeDtypeStruct((3 * half - early, ny, snaps, nz), bf16)
    *theirs, x_first, x_mine = call(
        omega_x_kernel,
        "omega_x",
        (field, field, first, field),
        [velocity, metric, mine],
        [wide, along],
    )
    got_first = swap(x_first)
    zu, yu = call(
        functools.partial(u_kernel, half),
        "u_terms",
        (partial_sum, partial_sum),
        [velocity, metric],
        [pltpu.VMEM((half, ny, snaps, nz), bf16), wide, along],
    )

    def raw_modes(name, parts, counts, own, got):
        shapes = tuple(jax.ShapeDtypeStruct((snaps * n * ny, nz), f32) for n in counts)
        return call(functools.partial(raw_kernel, parts), name, shapes, [own, got, blocks])

    yz_theirs = call(
        omega_theirs_kernel,
        "omega_yz_theirs",
        pair,
        [*theirs, mine, edge_theirs, zu, yu, metric],
    )
    got_yz = swap(yz_theirs)
    *late, _ = lax.optimization_barrier((*theirs, yz_theirs))
    edge_mine = [shift(part, False) for part in late]
    ordered, blocks = call(
        coeff_kernel,
        "coeff_blocks",
        (
            square,
            jax.ShapeDtypeStruct((ROWS // snaps * snaps, ROWS // snaps * 2 * snaps), bf16),
        ),
        [coeffs],
    )
    kernel = functools.partial(gram_x_kernel, ((0, 0),))
    gram = call(kernel, "gram_x", square, [x_mine, got_first, volume])
    (mine_x,) = raw_modes("raw_x_mine", ((0, 0),), (half,), x_mine, got_first)
    (theirs_x,) = raw_modes("raw_x_theirs", ((0, half),), (early,), x_first, got_first)
    *edge_mine, gram, mine_x, theirs_x = lax.optimization_barrier(
        (*edge_mine, gram, mine_x, theirs_x)
    )
    yz_mine = call(
        omega_mine_kernel,
        "omega_yz_mine",
        last,
        [mine, *theirs, *edge_mine, zu, yu, metric, x_mine],
    )
    got_last = swap(yz_mine)
    got_yz = got_yz.reshape(2 * half, ny, snaps, nz)
    left = half - early
    size = -(-snaps * (2 * snaps + 1) // nz) * nz
    messages = jax.ShapeDtypeStruct((2 * peers, 1, size), f32)
    parts = ((left, 0), (left + half, half))
    scale = 1.0 / (3.0 * layers * peers * ny * nz)
    kernel = functools.partial(messages_kernel, parts, scale)
    args = [yz_mine, got_yz, volume, gram, ordered]
    grams = call(kernel, "messages", messages, args)
    mine_yz = raw_modes("raw_yz_mine", parts, (half, half), yz_mine, got_yz)
    grams, *mine_yz = lax.optimization_barrier((grams, *mine_yz))
    grams = lax.all_to_all(grams, ("space", "snap"), 0, 0, tiled=True)
    yz_theirs = yz_theirs.reshape(2 * half, ny, snaps, nz)
    modes, rows = call(
        functools.partial(finish_kernel, half),
        "finish",
        (
            jax.ShapeDtypeStruct(velocity.shape, bf16),
            jax.ShapeDtypeStruct((snaps, 2 * snaps), f32),
        ),
        [
            grams, blocks, theirs_x, mine_x, *mine_yz,
            x_first, yz_theirs, got_last,
        ],
        [
            pltpu.VMEM((6, snaps, half, ny, nz), bf16),
            pltpu.VMEM((snaps, 2 * snaps), f32),
            pltpu.VMEM((snaps, nz), f32),
            pltpu.VMEM((half, snaps * ny, nz), f32),
            dma((7,)),
        ],
        None,
        (hbm(), hbm()),
    )
    return (rows, modes)


def per_device(velocity, metric, volume, coeffs):
    peers = lax.axis_size("space")
    paired = lax.axis_size("snap") == 2 and velocity.shape[2] == 2 * WIDTH
    if paired and velocity.shape[0] % 16 == 0 and peers & (peers - 1) == 0:
        return two_groups(velocity, metric, volume, coeffs)
    return many_groups(velocity, metric, volume, coeffs)


def solution(mesh):
    placed = (
        P("snap", None, "space", None, None),
        P(None, "space", None, None),
        P("space", None, None),
        P(),
    )
    return jax.shard_map(
        per_device,
        mesh=mesh,
        in_specs=placed,
        out_specs=(P("snap", None), P("snap", None, "space", None, None)),
        check_vma=False,
    )
```

```python
import functools

import jax
import jax.numpy as jnp
from jax import lax
from jax.experimental import pallas as pl
from jax.experimental.pallas import tpu as pltpu
from jax.sharding import PartitionSpec as P

EPS = 1e-06
WIDTH = 2
ROWS = 128
LIMIT = 24 * 1024 * 1024


def with_halo(shard, sides, width):
    for axis, dim in sides:
        peers, length = (lax.axis_size(axis), shard.shape[dim])
        up = [(i, (i + 1) % peers) for i in range(peers)]
        down = [(j, i) for i, j in up]
        last = lax.slice_in_dim(shard, length - width, length, axis=dim)
        leading = lax.slice_in_dim(shard, 0, width, axis=dim)
        before = lax.ppermute(last, axis, up)
        after = lax.ppermute(leading, axis, down)
        shard = jnp.concatenate([before, shard, after], axis=dim)
    return shard


def deriv(padded, dim):
    count = padded.shape[dim] - 4

    def cut(offset):
        return lax.slice_in_dim(padded, offset, offset + count, axis=dim)

    return (8.0 * (cut(3) - cut(1)) - (cut(4) - cut(0))) / 12.0


def curl(padded_x, metric):
    inner = padded_x[:, :, 2:-2]
    padded_y = jnp.pad(inner, ((0, 0), (0, 0), (0, 0), (2, 2), (0, 0)))
    padded_z = jnp.concatenate([inner[..., -2:], inner, inner[..., :2]], axis=4)
    along_x = deriv(padded_x, 2) * metric[0]
    along_y = deriv(padded_y, 3) * metric[1]
    along_z = deriv(padded_z, 4) * metric[2]
    omega_x = along_y[:, 2] - along_z[:, 1]
    omega_y = along_z[:, 0] - along_x[:, 2]
    omega_z = along_x[:, 1] - along_y[:, 0]
    return jnp.stack([omega_x, omega_y, omega_z], axis=1).astype(jnp.bfloat16)


def many_groups(velocity, metric, volume, coeffs):
    snap_dev = velocity.shape[0]
    snaps = coeffs.shape[0]
    group = lax.axis_index("snap")
    scale = 1.0 / (
        3.0 * volume.shape[0] * lax.axis_size("space") * volume.shape[1] * volume.shape[2]
    )
    padded = with_halo(velocity, (("space", 2),), 2)
    vorticity = curl(padded.astype(jnp.float32), metric)
    coeff_f = coeffs.astype(jnp.float32)
    moved = lax.all_to_all(vorticity, "snap", split_axis=3, concat_axis=0, tiled=True)
    part_y = moved.shape[3]
    vol_part = lax.dynamic_slice_in_dim(volume, group * part_y, part_y, 1)
    weighted = (moved.astype(jnp.float32) * vol_part).astype(jnp.bfloat16).reshape(snaps, -1)
    flat = moved.reshape(snaps, -1)
    partial_value = lax.dot_general(
        weighted, flat, (((1,), (1,)), ((), ())), preferred_element_type=jnp.float32
    )
    raw = lax.dot_general(
        coeffs, flat, (((0,), (0,)), ((), ())), preferred_element_type=jnp.float32
    )
    whole = lax.psum(partial_value, ("space", "snap")) * scale
    energy = jnp.sum(coeff_f * jnp.dot(whole, coeff_f, precision=lax.Precision.HIGHEST), axis=0)
    rows = lax.dynamic_slice_in_dim(whole, group * snap_dev, snap_dev, 0)
    local_modes = (raw / jnp.sqrt(energy + EPS)[:, None]).astype(jnp.bfloat16).reshape(moved.shape)
    modes = lax.all_to_all(local_modes, "snap", split_axis=0, concat_axis=3, tiled=True)
    return (rows, modes)


def vmem():
    return pl.BlockSpec(memory_space=pltpu.VMEM)


def hbm():
    return pl.BlockSpec(memory_space=pltpu.HBM)


def params():
    return pltpu.CompilerParams(vmem_limit_bytes=LIMIT)


def cost(flops, moved):
    return pl.CostEstimate(flops=flops, bytes_accessed=moved, transcendentals=0)


def z_stencil(size):
    rows = lax.broadcasted_iota(jnp.int32, (size, size), 0)
    cols = lax.broadcasted_iota(jnp.int32, (size, size), 1)
    ahead = rows - cols
    ahead = jnp.where(ahead < 0, ahead + size, ahead)
    out = jnp.where(ahead == 1, 8.0, 0.0) - jnp.where(ahead == size - 1, 8.0, 0.0)
    out = out - jnp.where(ahead == 2, 1.0, 0.0) + jnp.where(ahead == size - 2, 1.0, 0.0)
    return out.astype(jnp.bfloat16)


def spread(src, wide):
    snaps, ny, nz = src.shape
    wide[...] = src.astype(jnp.float32).reshape(snaps * ny, nz)


def row(wide, y, snaps, ny):
    return wide[pl.ds(y, snaps, ny), :]


def y_stencils(load, ny):
    held = {}

    def at(j):
        if j not in held:
            held[j] = load(j)
        return held[j]

    zero = jnp.zeros_like(at(0))
    for y in range(ny):
        near = (at(y + 1) if y + 1 < ny else zero) - (at(y - 1) if y >= 1 else zero)
        far = (at(y + 2) if y + 2 < ny else zero) - (at(y - 2) if y >= 2 else zero)
        held.pop(y - 2, None)
        yield y, 8.0 * near - far


def z_derivative(field, matrix, along):
    rows = field.shape[0] * field.shape[1] * field.shape[2]
    along[...] = jnp.dot(
        field.reshape(rows, field.shape[3]), matrix, preferred_element_type=jnp.float32
    ).reshape(field.shape)


def factor(metric_ref, m, layer, y):
    return metric_ref[m, layer, pl.ds(y, 1), :] * (1.0 / 12.0)


def flip(src, wide, out_ref, i):
    snaps, ny, _ = src.shape
    spread(src, wide)
    for y in range(ny):
        out_ref[i, y] = row(wide, y, snaps, ny).astype(jnp.bfloat16)


def flip_kernel(vel_ref, out_ref, buf, wide, sems):
    half = out_ref.shape[1]
    base = lax.axis_index("snap") * half
    copies = {}
    for c in range(2):
        for i in range(half):
            source = vel_ref.at[:, 1 + c, base + i]
            copies[c, i] = pltpu.make_async_copy(source, buf.at[:, c, i], sems.at[c, i])
            copies[c, i].start()
    for c in range(2):
        for i in range(half):
            copies[c, i].wait()
            flip(buf[:, c, i], wide, out_ref.at[c], i)


def omega_x_kernel(
    vel_ref, metric_ref, mine_ref, v_ref, w_ref, first_ref, ox_ref, wide, along
):
    half, ny, snaps, nz = ox_ref.shape
    group = lax.axis_index("snap")
    matrix = z_stencil(nz)
    for slot, base in ((0, (1 - group) * half), (1, group * half)):
        if slot == 0:
            for i in range(half):
                flip(vel_ref[:, 1, base + i], wide, v_ref, i)
        z_derivative(mine_ref[0] if slot else v_ref[...], matrix, along)
        for i in range(half):
            if slot == 0:
                spread(vel_ref[:, 2, base + i], wide)

            def load(j):
                if slot:
                    return mine_ref[1, i, j].astype(jnp.float32)
                value = row(wide, j, snaps, ny)
                w_ref[i, j] = value.astype(jnp.bfloat16)
                return value

            for y, across in y_stencils(load, ny):
                value = across * factor(metric_ref, 1, base + i, y)
                value = value - along[i, y] * factor(metric_ref, 2, base + i, y)
                value = value.astype(jnp.bfloat16)
                if slot:
                    ox_ref[i, y] = value
                if slot * half + i < first_ref.shape[0]:
                    first_ref[slot * half + i, y] = value


def u_kernel(half, vel_ref, metric_ref, zu_ref, yu_ref, flat, wide, along):
    snaps, _, _, ny, nz = vel_ref.shape
    matrix = z_stencil(nz)
    group = lax.axis_index("snap")
    for slot in range(2):
        base = (group if slot else 1 - group) * half
        for i in range(half):
            spread(vel_ref[:, 0, base + i], wide)

            def load(j):
                value = row(wide, j, snaps, ny)
                flat[i, j] = value.astype(jnp.bfloat16)
                return value

            for y, across in y_stencils(load, ny):
                yu_ref[slot, i, y] = across * factor(metric_ref, 1, base + i, y)
        z_derivative(flat[...], matrix, along)
        for i in range(half):
            for y in range(ny):
                zu_ref[slot, i, y] = along[i, y] * factor(metric_ref, 2, base + i, y)


def finish_curl(sign, slot, near_ref, far_ref, halo_ref, known_ref, metric_ref, out_ref):
    half, ny, _, _ = near_ref.shape
    group = lax.axis_index("snap")
    part = group if slot else 1 - group

    def run(low_ref, high_ref):
        def plane(i, y):
            if i < 0:
                ref, k = low_ref, half + i
            elif i < half:
                ref, k = near_ref, i
            else:
                ref, k = high_ref, i - half
            return ref[k, y].astype(jnp.float32)

        for y in range(ny):
            at = [plane(i, y) for i in range(-WIDTH, half + WIDTH)]
            for i in range(half):
                along = 8.0 * (at[i + 3] - at[i + 1]) - (at[i + 4] - at[i])
                along = along * factor(metric_ref, 0, part * half + i, y)
                known = known_ref[slot, i, y]
                value = along - known if sign > 0 else known - along
                out_ref[i, y] = value.astype(jnp.bfloat16)

    @pl.when(part == 0)
    def _():
        run(halo_ref, far_ref)

    @pl.when(part == 1)
    def _():
        run(far_ref, halo_ref)


def omega_yz_kernel(slot, near, far, edge, zu_ref, yu_ref, metric_ref, y_ref, z_ref):
    known = (yu_ref, zu_ref)
    for c, sign, out_ref in ((1, -1, y_ref), (0, 1, z_ref)):
        fields = near[c], far[c], edge[c], known[c]
        finish_curl(sign, slot, *fields, metric_ref, out_ref)


def omega_theirs_kernel(v_ref, w_ref, far, edge, *refs):
    far, edge, outs = [(ref.at[0], ref.at[1]) for ref in (far, edge, refs[-1])]
    omega_yz_kernel(0, (v_ref, w_ref), far, edge, *refs[:-1], *outs)


def omega_mine_kernel(*refs):
    near, far_v, far_w, edge_v, edge_w, *refs, ox_ref, out_ref = refs
    near, far = (near.at[0], near.at[1]), (far_v, far_w)
    half = ox_ref.shape[0]
    left = out_ref.shape[0] - 2 * half
    out_ref[:left] = ox_ref[half - left :]
    parts = [out_ref.at[pl.ds(left + n * half, half)] for n in range(2)]
    omega_yz_kernel(1, near, far, (edge_v, edge_w), *refs, *parts)


def gram_of(own, got, volume_ref, base):
    half, ny, _, _ = own.shape
    total = None
    for i in range(half):
        plain, heavy = [], []
        for y in range(ny):
            pair = jnp.concatenate([own[i, y], got[i, y]], axis=0)
            weight = volume_ref[base + i, pl.ds(y, 1), :]
            plain.append(pair)
            heavy.append((pair.astype(jnp.float32) * weight).astype(jnp.bfloat16))
        part = lax.dot_general(
            jnp.concatenate(heavy, axis=1),
            jnp.concatenate(plain, axis=1),
            (((1,), (1,)), ((), ())),
            preferred_element_type=jnp.float32,
        )
        total = part if total is None else total + part
    return total


def gram_sum(parts, own_ref, got_ref, volume_ref, earlier):
    half = volume_ref.shape[0] // 2
    base = lax.axis_index("snap") * half
    total = None if earlier is None else earlier[...]
    for own, got in parts:
        own, got = own_ref.at[pl.ds(own, half)], got_ref.at[pl.ds(got, half)]
        part = gram_of(own, got, volume_ref, base)
        total = part if total is None else total + part
    return total


def gram_x_kernel(parts, own_ref, got_ref, volume_ref, out_ref):
    out_ref[...] = gram_sum(parts, own_ref, got_ref, volume_ref, None)


def messages_kernel(parts, scale, own_ref, got_ref, volume_ref, earlier, coeff_ref, out_ref):
    total = gram_sum(parts, own_ref, got_ref, volume_ref, earlier) * scale
    coeff = coeff_ref[...]
    inner = jnp.dot(
        total, coeff, precision=lax.Precision.HIGHEST, preferred_element_type=jnp.float32
    )
    energy = jnp.sum(inner * coeff, axis=0, keepdims=True)
    snaps = total.shape[0] // 2
    turned = jnp.concatenate([total[snaps:, snaps:], total[snaps:, :snaps]], axis=1)
    group = lax.axis_index("snap")
    spare = out_ref.shape[2] - 2 * snaps * snaps - snaps
    for other, rows in enumerate((total[:snaps], turned)):
        line = [rows[k : k + 1] for k in range(snaps)]
        line.append(energy[:, other * snaps : (other + 1) * snaps])
        line = jnp.concatenate(line + [jnp.zeros((1, spare), jnp.float32)], axis=1)
        first = 1 - group if other else group
        for n in range(0, out_ref.shape[0], 2):
            out_ref[n + first] = line


def coeff_kernel(coeff_ref, ordered_ref, block_ref):
    count, _ = coeff_ref.shape
    snaps = count // 2
    rows = block_ref.shape[0]
    base = lax.axis_index("snap") * snaps

    def chosen(shape, test):
        left = lax.broadcasted_iota(jnp.int32, shape, 0)
        right = lax.broadcasted_iota(jnp.int32, shape, 1)
        return jnp.where(test(left, right), 1.0, 0.0).astype(jnp.bfloat16)

    def take(a, b, dims):
        out = lax.dot_general(a, b, (dims, ((), ())), preferred_element_type=jnp.float32)
        return out.astype(jnp.bfloat16)

    order = chosen((count, count), lambda j, m: j == lax.rem(m + base, count))
    turned = take(take(order, coeff_ref[...], ((0,), (1,))), order, ((1,), (0,)))
    same = chosen((count, count), lambda j, m: j == m)
    ordered_ref[...] = take(same, turned, ((1,), (1,))).astype(jnp.float32)
    mine = turned[:snaps]
    down = chosen((rows, snaps), lambda r, k: lax.rem(r, snaps) == k)
    for part in range(count // snaps):
        across = chosen((count, rows), lambda j, c: j == lax.rem(c, snaps) + part * snaps)
        wide = take(take(down, mine, ((1,), (0,))), across, ((1,), (0,)))
        same = chosen((rows, rows), lambda r, c: lax.div(r, snaps) == lax.div(c, snaps))
        block_ref[:, part * rows : (part + 1) * rows] = wide * same


def raw_blocks(own, got, block_ref, put):
    ny, snaps, nz = own.shape
    block = block_ref.shape[0] // snaps
    lanes = 2 if ny % (2 * block) == 0 else 1
    for start in range(0, ny, block * lanes):
        columns = []
        for n in range(lanes):
            at = start + n * block
            parts = [ref[at : at + block].reshape(block * snaps, nz) for ref in (own, got)]
            columns.append(jnp.concatenate(parts, axis=0))
        both = columns[0] if lanes == 1 else jnp.concatenate(columns, axis=1)
        raw = jnp.dot(block_ref[...], both, preferred_element_type=jnp.float32)
        for n in range(lanes):
            part = raw[:, n * nz : (n + 1) * nz].reshape(block, snaps, nz)
            for k in range(block):
                put(start + n * block + k, part[k])


def one_group_blocks(field, coeffs, put):
    ny, snaps, nz = field.shape
    block = coeffs.shape[0] // snaps
    lanes = 2 if ny % (2 * block) == 0 else 1
    for start in range(0, ny, block * lanes):
        columns = [
            field[at : at + block].reshape(block * snaps, nz)
            for at in range(start, start + block * lanes, block)
        ]
        both = columns[0] if lanes == 1 else jnp.concatenate(columns, axis=1)
        raw = jnp.dot(coeffs, both, preferred_element_type=jnp.float32)
        for n in range(lanes):
            part = raw[:, n * nz : (n + 1) * nz].reshape(block, snaps, nz)
            put(start + n * block, part)


def own_part_kernel(parts, block_ref, *refs):
    out_ref = refs[-1]
    coeffs = block_ref[:, : block_ref.shape[1] // 2]
    for n, (ref, layer) in enumerate(parts):

        def put(y, value):
            out_ref[n, y : y + value.shape[0]] = value

        one_group_blocks(refs[ref].at[layer], coeffs, put)


def add_other_group(known, got, block_ref, put):
    coeffs = block_ref[:, block_ref.shape[1] // 2 :]

    def put_block(y, value):
        for k in range(value.shape[0]):
            put(y + k, known[y + k] + value[k])

    one_group_blocks(got, coeffs, put_block)


def raw_from_parts_kernel(known_ref, got_ref, block_ref, *outs):
    for n, out_ref in enumerate(outs):
        _, ny, snaps, _ = known_ref.shape
        count = out_ref.shape[0] // (snaps * ny)
        for i in range(count):

            def put(y, value):
                out_ref[pl.ds(i * ny + y, snaps, count * ny), :] = value

            add_other_group(known_ref.at[n * count + i], got_ref.at[n * count + i], block_ref, put)


def raw_kernel(parts, own_ref, got_ref, block_ref, *outs):
    for (own, got), out_ref in zip(parts, outs):
        _, ny, snaps, _ = own_ref.shape
        count = out_ref.shape[0] // (snaps * ny)
        for i in range(count):

            def put(y, value):
                out_ref[pl.ds(i * ny + y, snaps, count * ny), :] = value

            raw_blocks(own_ref.at[own + i], got_ref.at[got + i], block_ref, put)


def finish_kernel(
    half, parts_ref, block_ref,
    x_theirs, x_mine, y_mine, z_mine, known_ref, got_ref,
    out_ref, rows_ref, stage, rows_buf, factors, wide, sems,
):
    _, snaps, _, ny, nz = stage.shape
    group = lax.axis_index("snap")
    lines = [parts_ref[n] for n in range(parts_ref.shape[0])]
    while len(lines) > 1:
        lines = [sum(lines[n : n + 2]) for n in range(0, len(lines), 2)]
    width = 2 * snaps
    line = lines[0][:, snaps * width : snaps * (width + 1)]
    down = lax.broadcasted_iota(jnp.int32, (snaps, snaps), 0)
    across = lax.broadcasted_iota(jnp.int32, (snaps, snaps), 1)
    energy = jnp.where(down == across, jnp.broadcast_to(line, (snaps, snaps)), 0.0)
    energy = jnp.sum(energy, axis=1, keepdims=True)
    factor = jnp.broadcast_to(1.0 / jnp.sqrt(energy + EPS), (snaps, nz))
    factors[...] = factor
    mine = jnp.concatenate(
        [lines[0][:, k * width : (k + 1) * width] for k in range(snaps)], axis=0
    )
    turned = jnp.concatenate([mine[:, snaps:], mine[:, :snaps]], axis=1)
    rows_buf[...] = jnp.where(group == 0, mine, turned)
    copies = [pltpu.make_async_copy(rows_buf, rows_ref, sems.at[6])]
    copies[0].start()
    bases = (1 - group) * half, group * half

    def send(c, slot):
        n = 2 * c + slot
        target = out_ref.at[:, c, pl.ds(bases[slot], half)]
        copies.append(pltpu.make_async_copy(stage.at[n], target, sems.at[n]))
        copies[-1].start()

    for c, raw_ref in enumerate((x_mine, y_mine, z_mine)):
        for k in range(snaps):
            value = raw_ref[k * half * ny : (k + 1) * half * ny, :] * factors[k : k + 1, :]
            stage[2 * c + 1, k] = value.astype(jnp.bfloat16).reshape(half, ny, nz)
        send(c, 1)
    early = x_theirs.shape[0] // (snaps * ny)
    for k in range(snaps):
        value = x_theirs[k * early * ny : (k + 1) * early * ny, :] * factors[k : k + 1, :]
        stage[0, k, :early] = value.astype(jnp.bfloat16).reshape(early, ny, nz)
    late = [(0, i) for i in range(early, half)]
    late += [(c, i) for c in (1, 2) for i in range(half)]
    for n, (c, i) in enumerate(late):
        rows = wide.at[n % wide.shape[0]]

        def put(y, value):
            rows[pl.ds(y, snaps, ny), :] = value * factor

        add_other_group(known_ref.at[n], got_ref.at[n], block_ref, put)
        for k in range(snaps):
            stage[2 * c, k, i] = rows[k * ny : (k + 1) * ny, :].astype(jnp.bfloat16)
        if i == half - 1:
            send(c, 0)
    for copy in copies:
        copy.wait()


def two_groups(velocity, metric, volume, coeffs):
    snaps, _, layers, ny, nz = velocity.shape
    half = layers // 2
    peers = lax.axis_size("space")
    bf16, f32 = jnp.bfloat16, jnp.float32

    def halo(first):
        pairs = []
        for s in range(peers):
            for g in range(2):
                down = (g == 0) == first
                pairs.append((s * 2 + g, ((s + (-1 if down else 1)) % peers) * 2 + g))
        return pairs

    def swap(value):
        return lax.ppermute(value, "snap", [(0, 1), (1, 0)])

    def shift(value, first):
        return lax.ppermute(value, ("space", "snap"), halo(first))

    field = jax.ShapeDtypeStruct((half, ny, snaps, nz), bf16)
    pair = jax.ShapeDtypeStruct((2, half, ny, snaps, nz), bf16)
    partial_sum = jax.ShapeDtypeStruct((2, half, ny, snaps, nz), f32)
    square = jax.ShapeDtypeStruct((2 * snaps, 2 * snaps), f32)
    cells = half * ny * snaps * nz
    wide = pltpu.VMEM((snaps * ny, nz), f32)
    along = pltpu.VMEM((half, ny, snaps, nz), f32)
    dma = pltpu.SemaphoreType.DMA

    def call(kernel, name, out_shape, args, scratch=(), in_specs=None, out_specs=None, work=5):
        return pl.pallas_call(
            kernel,
            out_shape=out_shape,
            in_specs=in_specs or [vmem()] * len(args),
            out_specs=out_specs or jax.tree.map(lambda _: vmem(), out_shape),
            scratch_shapes=list(scratch),
            compiler_params=params(),
            cost_estimate=cost(2 * work * cells, work * cells),
            name=name,
        )(*args)

    mine = call(
        flip_kernel,
        "flip_mine",
        pair,
        [pltpu.with_memory_space_constraint(velocity, pltpu.HBM)],
        [pltpu.VMEM((snaps, 2, half, ny, nz), bf16), wide, dma((2, half))],
        [hbm()],
    )
    edge_theirs = shift(mine, True)
    early = half // 2
    first = jax.ShapeDtypeStruct((half + early, ny, snaps, nz), bf16)
    last = jax.ShapeDtypeStruct((3 * half - early, ny, snaps, nz), bf16)
    *theirs, x_first, x_mine = call(
        omega_x_kernel,
        "omega_x",
        (field, field, first, field),
        [velocity, metric, mine],
        [wide, along],
    )
    got_first = swap(x_first)
    zu, yu = call(
        functools.partial(u_kernel, half),
        "u_terms",
        (partial_sum, partial_sum),
        [velocity, metric],
        [pltpu.VMEM((half, ny, snaps, nz), bf16), wide, along],
    )

    def own_part(name, parts, *fields):
        shape = jax.ShapeDtypeStruct((len(parts), ny, snaps, nz), f32)
        return call(functools.partial(own_part_kernel, parts), name, shape, [blocks, *fields])

    def raw_modes(name, parts, counts, own, got):
        shapes = tuple(jax.ShapeDtypeStruct((snaps * n * ny, nz), f32) for n in counts)
        return call(functools.partial(raw_kernel, parts), name, shapes, [own, got, blocks])

    yz_theirs = call(
        omega_theirs_kernel,
        "omega_yz_theirs",
        pair,
        [*theirs, mine, edge_theirs, zu, yu, metric],
    )
    got_yz = swap(yz_theirs)
    *late, _ = lax.optimization_barrier((*theirs, yz_theirs))
    edge_mine = [shift(part, False) for part in late]
    ordered, blocks = call(
        coeff_kernel,
        "coeff_blocks",
        (
            square,
            jax.ShapeDtypeStruct((ROWS // snaps * snaps, ROWS // snaps * 2 * snaps), bf16),
        ),
        [coeffs],
    )
    kernel = functools.partial(gram_x_kernel, ((0, 0),))
    gram = call(kernel, "gram_x", square, [x_mine, got_first, volume])
    (mine_x,) = raw_modes("raw_x_mine", ((0, 0),), (half,), x_mine, got_first)
    (theirs_x,) = raw_modes("raw_x_theirs", ((0, half),), (early,), x_first, got_first)
    *edge_mine, gram, mine_x, theirs_x = lax.optimization_barrier(
        (*edge_mine, gram, mine_x, theirs_x)
    )
    yz_mine = call(
        omega_mine_kernel,
        "omega_yz_mine",
        last,
        [mine, *theirs, *edge_mine, zu, yu, metric, x_mine],
    )
    got_last = swap(yz_mine)
    got_yz = got_yz.reshape(2 * half, ny, snaps, nz)
    left = half - early
    size = -(-snaps * (2 * snaps + 1) // nz) * nz
    messages = jax.ShapeDtypeStruct((2 * peers, 1, size), f32)
    parts = ((left, 0), (left + half, half))
    yz_theirs = yz_theirs.reshape(2 * half, ny, snaps, nz)
    known_mine = own_part("own_mine", [(0, left + n) for n in range(2 * half)], yz_mine)
    known_theirs = own_part(
        "own_theirs",
        [(0, n) for n in range(early, half)] + [(1, n) for n in range(2 * half)],
        x_first,
        yz_theirs,
    )
    got_yz, known_mine, known_theirs = lax.optimization_barrier(
        (got_yz, known_mine, known_theirs)
    )
    scale = 1.0 / (3.0 * layers * peers * ny * nz)
    kernel = functools.partial(messages_kernel, parts, scale)
    args = [yz_mine, got_yz, volume, gram, ordered]
    grams = call(kernel, "messages", messages, args)
    fields = jax.ShapeDtypeStruct((snaps * half * ny, nz), f32)
    mine_yz = call(
        raw_from_parts_kernel, "raw_yz_mine", (fields, fields), [known_mine, got_yz, blocks]
    )
    grams, *mine_yz = lax.optimization_barrier((grams, *mine_yz))
    grams = lax.all_to_all(grams, ("space", "snap"), 0, 0, tiled=True)
    modes, rows = call(
        functools.partial(finish_kernel, half),
        "finish",
        (
            jax.ShapeDtypeStruct(velocity.shape, bf16),
            jax.ShapeDtypeStruct((snaps, 2 * snaps), f32),
        ),
        [
            grams, blocks, theirs_x, mine_x, *mine_yz,
            known_theirs, got_last,
        ],
        [
            pltpu.VMEM((6, snaps, half, ny, nz), bf16),
            pltpu.VMEM((snaps, 2 * snaps), f32),
            pltpu.VMEM((snaps, nz), f32),
            pltpu.VMEM((half, snaps * ny, nz), f32),
            dma((7,)),
        ],
        None,
        (hbm(), hbm()),
    )
    return (rows, modes)


def per_device(velocity, metric, volume, coeffs):
    peers = lax.axis_size("space")
    paired = lax.axis_size("snap") == 2 and velocity.shape[2] == 2 * WIDTH
    if paired and velocity.shape[0] % 16 == 0 and peers & (peers - 1) == 0:
        return two_groups(velocity, metric, volume, coeffs)
    return many_groups(velocity, metric, volume, coeffs)


def solution(mesh):
    placed = (
        P("snap", None, "space", None, None),
        P(None, "space", None, None),
        P("space", None, None),
        P(),
    )
    return jax.shard_map(
        per_device,
        mesh=mesh,
        in_specs=placed,
        out_specs=(P("snap", None), P("snap", None, "space", None, None)),
        check_vma=False,
    )
```

```python
import functools

import jax
import jax.numpy as jnp
from jax import lax
from jax.experimental import pallas as pl
from jax.experimental.pallas import tpu as pltpu
from jax.sharding import PartitionSpec as P

EPS = 1e-06
WIDTH = 2
ROWS = 128
LIMIT = 24 * 1024 * 1024


def with_halo(shard, sides, width):
    for axis, dim in sides:
        peers, length = (lax.axis_size(axis), shard.shape[dim])
        up = [(i, (i + 1) % peers) for i in range(peers)]
        down = [(j, i) for i, j in up]
        last = lax.slice_in_dim(shard, length - width, length, axis=dim)
        leading = lax.slice_in_dim(shard, 0, width, axis=dim)
        before = lax.ppermute(last, axis, up)
        after = lax.ppermute(leading, axis, down)
        shard = jnp.concatenate([before, shard, after], axis=dim)
    return shard


def deriv(padded, dim):
    count = padded.shape[dim] - 4

    def cut(offset):
        return lax.slice_in_dim(padded, offset, offset + count, axis=dim)

    return (8.0 * (cut(3) - cut(1)) - (cut(4) - cut(0))) / 12.0


def curl(padded_x, metric):
    inner = padded_x[:, :, 2:-2]
    padded_y = jnp.pad(inner, ((0, 0), (0, 0), (0, 0), (2, 2), (0, 0)))
    padded_z = jnp.concatenate([inner[..., -2:], inner, inner[..., :2]], axis=4)
    along_x = deriv(padded_x, 2) * metric[0]
    along_y = deriv(padded_y, 3) * metric[1]
    along_z = deriv(padded_z, 4) * metric[2]
    omega_x = along_y[:, 2] - along_z[:, 1]
    omega_y = along_z[:, 0] - along_x[:, 2]
    omega_z = along_x[:, 1] - along_y[:, 0]
    return jnp.stack([omega_x, omega_y, omega_z], axis=1).astype(jnp.bfloat16)


def many_groups(velocity, metric, volume, coeffs):
    snap_dev = velocity.shape[0]
    snaps = coeffs.shape[0]
    group = lax.axis_index("snap")
    scale = 1.0 / (
        3.0 * volume.shape[0] * lax.axis_size("space") * volume.shape[1] * volume.shape[2]
    )
    padded = with_halo(velocity, (("space", 2),), 2)
    vorticity = curl(padded.astype(jnp.float32), metric)
    coeff_f = coeffs.astype(jnp.float32)
    moved = lax.all_to_all(vorticity, "snap", split_axis=3, concat_axis=0, tiled=True)
    part_y = moved.shape[3]
    vol_part = lax.dynamic_slice_in_dim(volume, group * part_y, part_y, 1)
    weighted = (moved.astype(jnp.float32) * vol_part).astype(jnp.bfloat16).reshape(snaps, -1)
    flat = moved.reshape(snaps, -1)
    partial_value = lax.dot_general(
        weighted, flat, (((1,), (1,)), ((), ())), preferred_element_type=jnp.float32
    )
    raw = lax.dot_general(
        coeffs, flat, (((0,), (0,)), ((), ())), preferred_element_type=jnp.float32
    )
    whole = lax.psum(partial_value, ("space", "snap")) * scale
    energy = jnp.sum(coeff_f * jnp.dot(whole, coeff_f, precision=lax.Precision.HIGHEST), axis=0)
    rows = lax.dynamic_slice_in_dim(whole, group * snap_dev, snap_dev, 0)
    local_modes = (raw / jnp.sqrt(energy + EPS)[:, None]).astype(jnp.bfloat16).reshape(moved.shape)
    modes = lax.all_to_all(local_modes, "snap", split_axis=0, concat_axis=3, tiled=True)
    return (rows, modes)


def vmem():
    return pl.BlockSpec(memory_space=pltpu.VMEM)


def hbm():
    return pl.BlockSpec(memory_space=pltpu.HBM)


def params():
    return pltpu.CompilerParams(vmem_limit_bytes=LIMIT)


def cost(flops, moved):
    return pl.CostEstimate(flops=flops, bytes_accessed=moved, transcendentals=0)


def z_stencil(size):
    rows = lax.broadcasted_iota(jnp.int32, (size, size), 0)
    cols = lax.broadcasted_iota(jnp.int32, (size, size), 1)
    ahead = rows - cols
    ahead = jnp.where(ahead < 0, ahead + size, ahead)
    out = jnp.where(ahead == 1, 8.0, 0.0) - jnp.where(ahead == size - 1, 8.0, 0.0)
    out = out - jnp.where(ahead == 2, 1.0, 0.0) + jnp.where(ahead == size - 2, 1.0, 0.0)
    return out.astype(jnp.bfloat16)


def spread(src, wide):
    snaps, ny, _ = src.shape
    for s in range(snaps):
        wide[s * (ny + 1) : s * (ny + 1) + ny, :] = src[s].astype(jnp.float32)


def row(wide, y, snaps, ny):
    return wide[pl.ds(y, snaps, ny + 1), :]


def y_stencils(load, ny):
    held = {}

    def at(j):
        if j not in held:
            held[j] = load(j)
        return held[j]

    zero = jnp.zeros_like(at(0))
    for y in range(ny):
        near = (at(y + 1) if y + 1 < ny else zero) - (at(y - 1) if y >= 1 else zero)
        far = (at(y + 2) if y + 2 < ny else zero) - (at(y - 2) if y >= 2 else zero)
        held.pop(y - 2, None)
        yield y, 8.0 * near - far


def z_derivative(field, matrix, along):
    rows = field.shape[0] * field.shape[1] * field.shape[2]
    along[...] = jnp.dot(
        field.reshape(rows, field.shape[3]), matrix, preferred_element_type=jnp.float32
    ).reshape(field.shape)


def factor(metric_ref, m, layer, y):
    return metric_ref[m, layer, pl.ds(y, 1), :] * (1.0 / 12.0)


def flip(src, wide, out_ref, i):
    snaps, ny, _ = src.shape
    spread(src, wide)
    for y in range(ny):
        out_ref[i, y] = row(wide, y, snaps, ny).astype(jnp.bfloat16)


def flip_kernel(vel_ref, out_ref, buf, wide, sems):
    half = out_ref.shape[1]
    base = lax.axis_index("snap") * half
    copies = {}
    for c in range(2):
        for i in range(half):
            source = vel_ref.at[:, 1 + c, base + i]
            copies[c, i] = pltpu.make_async_copy(source, buf.at[:, c, i], sems.at[c, i])
            copies[c, i].start()
    for c in range(2):
        for i in range(half):
            copies[c, i].wait()
            flip(buf[:, c, i], wide, out_ref.at[c], i)


def omega_x_kernel(
    vel_ref, metric_ref, mine_ref, v_ref, w_ref, first_ref, ox_ref, wide, along
):
    half, ny, snaps, nz = ox_ref.shape
    group = lax.axis_index("snap")
    matrix = z_stencil(nz)
    for slot, base in ((0, (1 - group) * half), (1, group * half)):
        if slot == 0:
            for i in range(half):
                flip(vel_ref[:, 1, base + i], wide, v_ref, i)
        z_derivative(mine_ref[0] if slot else v_ref[...], matrix, along)
        for i in range(half):
            if slot == 0:
                spread(vel_ref[:, 2, base + i], wide)

            def load(j):
                if slot:
                    return mine_ref[1, i, j].astype(jnp.float32)
                value = row(wide, j, snaps, ny)
                w_ref[i, j] = value.astype(jnp.bfloat16)
                return value

            for y, across in y_stencils(load, ny):
                value = across * factor(metric_ref, 1, base + i, y)
                value = value - along[i, y] * factor(metric_ref, 2, base + i, y)
                value = value.astype(jnp.bfloat16)
                if slot:
                    ox_ref[i, y] = value
                if slot * half + i < first_ref.shape[0]:
                    first_ref[slot * half + i, y] = value


def u_kernel(half, vel_ref, metric_ref, zu_ref, yu_ref, flat, wide, along):
    snaps, _, _, ny, nz = vel_ref.shape
    matrix = z_stencil(nz)
    group = lax.axis_index("snap")
    for slot in range(2):
        base = (group if slot else 1 - group) * half
        for i in range(half):
            spread(vel_ref[:, 0, base + i], wide)

            def load(j):
                value = row(wide, j, snaps, ny)
                flat[i, j] = value.astype(jnp.bfloat16)
                return value

            for y, across in y_stencils(load, ny):
                yu_ref[slot, i, y] = across * factor(metric_ref, 1, base + i, y)
        z_derivative(flat[...], matrix, along)
        for i in range(half):
            for y in range(ny):
                zu_ref[slot, i, y] = along[i, y] * factor(metric_ref, 2, base + i, y)


def finish_curl(sign, slot, near_ref, far_ref, halo_ref, known_ref, metric_ref, out_ref):
    half, ny, _, _ = near_ref.shape
    group = lax.axis_index("snap")
    part = group if slot else 1 - group

    def run(low_ref, high_ref):
        def plane(i, y):
            if i < 0:
                ref, k = low_ref, half + i
            elif i < half:
                ref, k = near_ref, i
            else:
                ref, k = high_ref, i - half
            return ref[k, y].astype(jnp.float32)

        for y in range(ny):
            at = [plane(i, y) for i in range(-WIDTH, half + WIDTH)]
            for i in range(half):
                along = 8.0 * (at[i + 3] - at[i + 1]) - (at[i + 4] - at[i])
                along = along * factor(metric_ref, 0, part * half + i, y)
                known = known_ref[slot, i, y]
                value = along - known if sign > 0 else known - along
                out_ref[i, y] = value.astype(jnp.bfloat16)

    @pl.when(part == 0)
    def _():
        run(halo_ref, far_ref)

    @pl.when(part == 1)
    def _():
        run(far_ref, halo_ref)


def omega_yz_kernel(slot, near, far, edge, zu_ref, yu_ref, metric_ref, y_ref, z_ref):
    known = (yu_ref, zu_ref)
    for c, sign, out_ref in ((1, -1, y_ref), (0, 1, z_ref)):
        fields = near[c], far[c], edge[c], known[c]
        finish_curl(sign, slot, *fields, metric_ref, out_ref)


def omega_theirs_kernel(v_ref, w_ref, far, edge, *refs):
    far, edge, outs = [(ref.at[0], ref.at[1]) for ref in (far, edge, refs[-1])]
    omega_yz_kernel(0, (v_ref, w_ref), far, edge, *refs[:-1], *outs)


def omega_mine_kernel(*refs):
    near, far_v, far_w, edge_v, edge_w, *refs, ox_ref, out_ref = refs
    near, far = (near.at[0], near.at[1]), (far_v, far_w)
    half = ox_ref.shape[0]
    left = out_ref.shape[0] - 2 * half
    out_ref[:left] = ox_ref[half - left :]
    parts = [out_ref.at[pl.ds(left + n * half, half)] for n in range(2)]
    omega_yz_kernel(1, near, far, (edge_v, edge_w), *refs, *parts)


def gram_of(own, got, volume_ref, base):
    half, ny, _, _ = own.shape
    total = None
    for i in range(half):
        plain, heavy = [], []
        for y in range(ny):
            pair = jnp.concatenate([own[i, y], got[i, y]], axis=0)
            weight = volume_ref[base + i, pl.ds(y, 1), :]
            plain.append(pair)
            heavy.append((pair.astype(jnp.float32) * weight).astype(jnp.bfloat16))
        part = lax.dot_general(
            jnp.concatenate(heavy, axis=1),
            jnp.concatenate(plain, axis=1),
            (((1,), (1,)), ((), ())),
            preferred_element_type=jnp.float32,
        )
        total = part if total is None else total + part
    return total


def gram_sum(parts, own_ref, got_ref, volume_ref, earlier):
    half = volume_ref.shape[0] // 2
    base = lax.axis_index("snap") * half
    total = None if earlier is None else earlier[...]
    for own, got in parts:
        own, got = own_ref.at[pl.ds(own, half)], got_ref.at[pl.ds(got, half)]
        part = gram_of(own, got, volume_ref, base)
        total = part if total is None else total + part
    return total


def gram_x_kernel(parts, own_ref, got_ref, volume_ref, out_ref):
    out_ref[...] = gram_sum(parts, own_ref, got_ref, volume_ref, None)


def messages_kernel(parts, scale, own_ref, got_ref, volume_ref, earlier, coeff_ref, out_ref):
    total = gram_sum(parts, own_ref, got_ref, volume_ref, earlier) * scale
    coeff = coeff_ref[...]
    inner = jnp.dot(
        total, coeff, precision=lax.Precision.HIGHEST, preferred_element_type=jnp.float32
    )
    energy = jnp.sum(inner * coeff, axis=0, keepdims=True)
    snaps = total.shape[0] // 2
    turned = jnp.concatenate([total[snaps:, snaps:], total[snaps:, :snaps]], axis=1)
    group = lax.axis_index("snap")
    spare = out_ref.shape[2] - 2 * snaps * snaps - snaps
    for other, rows in enumerate((total[:snaps], turned)):
        line = [rows[k : k + 1] for k in range(snaps)]
        line.append(energy[:, other * snaps : (other + 1) * snaps])
        line = jnp.concatenate(line + [jnp.zeros((1, spare), jnp.float32)], axis=1)
        first = 1 - group if other else group
        for n in range(0, out_ref.shape[0], 2):
            out_ref[n + first] = line


def coeff_kernel(coeff_ref, ordered_ref, block_ref):
    count, _ = coeff_ref.shape
    snaps = count // 2
    rows = block_ref.shape[0]
    base = lax.axis_index("snap") * snaps

    def chosen(shape, test):
        left = lax.broadcasted_iota(jnp.int32, shape, 0)
        right = lax.broadcasted_iota(jnp.int32, shape, 1)
        return jnp.where(test(left, right), 1.0, 0.0).astype(jnp.bfloat16)

    def take(a, b, dims):
        out = lax.dot_general(a, b, (dims, ((), ())), preferred_element_type=jnp.float32)
        return out.astype(jnp.bfloat16)

    order = chosen((count, count), lambda j, m: j == lax.rem(m + base, count))
    turned = take(take(order, coeff_ref[...], ((0,), (1,))), order, ((1,), (0,)))
    same = chosen((count, count), lambda j, m: j == m)
    ordered_ref[...] = take(same, turned, ((1,), (1,))).astype(jnp.float32)
    mine = turned[:snaps]
    down = chosen((rows, snaps), lambda r, k: lax.rem(r, snaps) == k)
    for part in range(count // snaps):
        across = chosen((count, rows), lambda j, c: j == lax.rem(c, snaps) + part * snaps)
        wide = take(take(down, mine, ((1,), (0,))), across, ((1,), (0,)))
        same = chosen((rows, rows), lambda r, c: lax.div(r, snaps) == lax.div(c, snaps))
        block_ref[:, part * rows : (part + 1) * rows] = wide * same


def raw_blocks(own, got, block_ref, put):
    ny, snaps, nz = own.shape
    block = block_ref.shape[0] // snaps
    lanes = 2 if ny % (2 * block) == 0 else 1
    for start in range(0, ny, block * lanes):
        columns = []
        for n in range(lanes):
            at = start + n * block
            parts = [ref[at : at + block].reshape(block * snaps, nz) for ref in (own, got)]
            columns.append(jnp.concatenate(parts, axis=0))
        both = columns[0] if lanes == 1 else jnp.concatenate(columns, axis=1)
        raw = jnp.dot(block_ref[...], both, preferred_element_type=jnp.float32)
        for n in range(lanes):
            part = raw[:, n * nz : (n + 1) * nz].reshape(block, snaps, nz)
            for k in range(block):
                put(start + n * block + k, part[k])


def one_group_blocks(field, coeffs, put):
    ny, snaps, nz = field.shape
    block = coeffs.shape[0] // snaps
    lanes = 2 if ny % (2 * block) == 0 else 1
    for start in range(0, ny, block * lanes):
        columns = [
            field[at : at + block].reshape(block * snaps, nz)
            for at in range(start, start + block * lanes, block)
        ]
        both = columns[0] if lanes == 1 else jnp.concatenate(columns, axis=1)
        raw = jnp.dot(coeffs, both, preferred_element_type=jnp.float32)
        for n in range(lanes):
            part = raw[:, n * nz : (n + 1) * nz].reshape(block, snaps, nz)
            put(start + n * block, part)


def own_part_kernel(parts, block_ref, *refs):
    out_ref = refs[-1]
    coeffs = block_ref[:, : block_ref.shape[1] // 2]
    for n, (ref, layer) in enumerate(parts):

        def put(y, value):
            out_ref[n, y : y + value.shape[0]] = value

        one_group_blocks(refs[ref].at[layer], coeffs, put)


def add_other_group(known, got, block_ref, put):
    coeffs = block_ref[:, block_ref.shape[1] // 2 :]

    def put_block(y, value):
        for k in range(value.shape[0]):
            put(y + k, known[y + k] + value[k])

    one_group_blocks(got, coeffs, put_block)


def raw_from_parts_kernel(known_ref, got_ref, block_ref, *outs):
    for n, out_ref in enumerate(outs):
        _, ny, snaps, _ = known_ref.shape
        stride = out_ref.shape[0] // snaps
        count = stride // ny
        for i in range(count):

            def put(y, value):
                out_ref[pl.ds(i * ny + y, snaps, stride), :] = value

            add_other_group(known_ref.at[n * count + i], got_ref.at[n * count + i], block_ref, put)


def raw_kernel(parts, own_ref, got_ref, block_ref, *outs):
    for (own, got), out_ref in zip(parts, outs):
        _, ny, snaps, _ = own_ref.shape
        stride = out_ref.shape[0] // snaps
        count = stride // ny
        for i in range(count):

            def put(y, value):
                out_ref[pl.ds(i * ny + y, snaps, stride), :] = value

            raw_blocks(own_ref.at[own + i], got_ref.at[got + i], block_ref, put)


def finish_kernel(
    half, parts_ref, block_ref,
    x_theirs, x_mine, y_mine, z_mine, known_ref, got_ref,
    out_ref, rows_ref, stage, rows_buf, factors, wide, sems,
):
    _, snaps, _, ny, nz = stage.shape
    group = lax.axis_index("snap")
    lines = [parts_ref[n] for n in range(parts_ref.shape[0])]
    while len(lines) > 1:
        lines = [sum(lines[n : n + 2]) for n in range(0, len(lines), 2)]
    width = 2 * snaps
    line = lines[0][:, snaps * width : snaps * (width + 1)]
    down = lax.broadcasted_iota(jnp.int32, (snaps, snaps), 0)
    across = lax.broadcasted_iota(jnp.int32, (snaps, snaps), 1)
    energy = jnp.where(down == across, jnp.broadcast_to(line, (snaps, snaps)), 0.0)
    energy = jnp.sum(energy, axis=1, keepdims=True)
    factor = jnp.broadcast_to(1.0 / jnp.sqrt(energy + EPS), (snaps, nz))
    factors[...] = factor
    mine = jnp.concatenate(
        [lines[0][:, k * width : (k + 1) * width] for k in range(snaps)], axis=0
    )
    turned = jnp.concatenate([mine[:, snaps:], mine[:, :snaps]], axis=1)
    rows_buf[...] = jnp.where(group == 0, mine, turned)
    copies = [pltpu.make_async_copy(rows_buf, rows_ref, sems.at[6])]
    copies[0].start()
    bases = (1 - group) * half, group * half

    def send(c, slot):
        n = 2 * c + slot
        target = out_ref.at[:, c, pl.ds(bases[slot], half)]
        copies.append(pltpu.make_async_copy(stage.at[n], target, sems.at[n]))
        copies[-1].start()

    for c, raw_ref in enumerate((x_mine, y_mine, z_mine)):
        for k in range(snaps):
            at = k * (half * ny + 1)
            value = raw_ref[at : at + half * ny, :] * factors[k : k + 1, :]
            stage[2 * c + 1, k] = value.astype(jnp.bfloat16).reshape(half, ny, nz)
        send(c, 1)
    early = x_theirs.shape[0] // snaps // ny
    for k in range(snaps):
        at = k * (early * ny + 1)
        value = x_theirs[at : at + early * ny, :] * factors[k : k + 1, :]
        stage[0, k, :early] = value.astype(jnp.bfloat16).reshape(early, ny, nz)
    late = [(0, i) for i in range(early, half)]
    late += [(c, i) for c in (1, 2) for i in range(half)]
    for n, (c, i) in enumerate(late):
        rows = wide.at[n % wide.shape[0]]

        def put(y, value):
            rows[pl.ds(y, snaps, ny + 1), :] = value * factor

        add_other_group(known_ref.at[n], got_ref.at[n], block_ref, put)
        for k in range(snaps):
            at = k * (ny + 1)
            stage[2 * c, k, i] = rows[at : at + ny, :].astype(jnp.bfloat16)
        if i == half - 1:
            send(c, 0)
    for copy in copies:
        copy.wait()


def two_groups(velocity, metric, volume, coeffs):
    snaps, _, layers, ny, nz = velocity.shape
    half = layers // 2
    peers = lax.axis_size("space")
    bf16, f32 = jnp.bfloat16, jnp.float32

    def halo(first):
        pairs = []
        for s in range(peers):
            for g in range(2):
                down = (g == 0) == first
                pairs.append((s * 2 + g, ((s + (-1 if down else 1)) % peers) * 2 + g))
        return pairs

    def swap(value):
        return lax.ppermute(value, "snap", [(0, 1), (1, 0)])

    def shift(value, first):
        return lax.ppermute(value, ("space", "snap"), halo(first))

    field = jax.ShapeDtypeStruct((half, ny, snaps, nz), bf16)
    pair = jax.ShapeDtypeStruct((2, half, ny, snaps, nz), bf16)
    partial_sum = jax.ShapeDtypeStruct((2, half, ny, snaps, nz), f32)
    square = jax.ShapeDtypeStruct((2 * snaps, 2 * snaps), f32)
    cells = half * ny * snaps * nz
    wide = pltpu.VMEM((snaps * (ny + 1), nz), f32)
    along = pltpu.VMEM((half, ny, snaps, nz), f32)
    dma = pltpu.SemaphoreType.DMA

    def call(kernel, name, out_shape, args, scratch=(), in_specs=None, out_specs=None, work=5):
        return pl.pallas_call(
            kernel,
            out_shape=out_shape,
            in_specs=in_specs or [vmem()] * len(args),
            out_specs=out_specs or jax.tree.map(lambda _: vmem(), out_shape),
            scratch_shapes=list(scratch),
            compiler_params=params(),
            cost_estimate=cost(2 * work * cells, work * cells),
            name=name,
        )(*args)

    mine = call(
        flip_kernel,
        "flip_mine",
        pair,
        [pltpu.with_memory_space_constraint(velocity, pltpu.HBM)],
        [pltpu.VMEM((snaps, 2, half, ny, nz), bf16), wide, dma((2, half))],
        [hbm()],
    )
    edge_theirs = shift(mine, True)
    early = half // 2
    first = jax.ShapeDtypeStruct((half + early, ny, snaps, nz), bf16)
    last = jax.ShapeDtypeStruct((3 * half - early, ny, snaps, nz), bf16)
    *theirs, x_first, x_mine = call(
        omega_x_kernel,
        "omega_x",
        (field, field, first, field),
        [velocity, metric, mine],
        [wide, along],
    )
    got_first = swap(x_first)
    zu, yu = call(
        functools.partial(u_kernel, half),
        "u_terms",
        (partial_sum, partial_sum),
        [velocity, metric],
        [pltpu.VMEM((half, ny, snaps, nz), bf16), wide, along],
    )

    def own_part(name, parts, *fields):
        shape = jax.ShapeDtypeStruct((len(parts), ny, snaps, nz), f32)
        return call(functools.partial(own_part_kernel, parts), name, shape, [blocks, *fields])

    def raw_modes(name, parts, counts, own, got):
        shapes = tuple(jax.ShapeDtypeStruct((snaps * (n * ny + 1), nz), f32) for n in counts)
        return call(functools.partial(raw_kernel, parts), name, shapes, [own, got, blocks])

    yz_theirs = call(
        omega_theirs_kernel,
        "omega_yz_theirs",
        pair,
        [*theirs, mine, edge_theirs, zu, yu, metric],
    )
    got_yz = swap(yz_theirs)
    *late, _ = lax.optimization_barrier((*theirs, yz_theirs))
    edge_mine = [shift(part, False) for part in late]
    ordered, blocks = call(
        coeff_kernel,
        "coeff_blocks",
        (
            square,
            jax.ShapeDtypeStruct((ROWS // snaps * snaps, ROWS // snaps * 2 * snaps), bf16),
        ),
        [coeffs],
    )
    kernel = functools.partial(gram_x_kernel, ((0, 0),))
    gram = call(kernel, "gram_x", square, [x_mine, got_first, volume])
    (mine_x,) = raw_modes("raw_x_mine", ((0, 0),), (half,), x_mine, got_first)
    (theirs_x,) = raw_modes("raw_x_theirs", ((0, half),), (early,), x_first, got_first)
    *edge_mine, gram, mine_x, theirs_x = lax.optimization_barrier(
        (*edge_mine, gram, mine_x, theirs_x)
    )
    yz_mine = call(
        omega_mine_kernel,
        "omega_yz_mine",
        last,
        [mine, *theirs, *edge_mine, zu, yu, metric, x_mine],
    )
    got_last = swap(yz_mine)
    got_yz = got_yz.reshape(2 * half, ny, snaps, nz)
    left = half - early
    size = -(-snaps * (2 * snaps + 1) // nz) * nz
    messages = jax.ShapeDtypeStruct((2 * peers, 1, size), f32)
    parts = ((left, 0), (left + half, half))
    yz_theirs = yz_theirs.reshape(2 * half, ny, snaps, nz)
    known_mine = own_part("own_mine", [(0, left + n) for n in range(2 * half)], yz_mine)
    known_theirs = own_part(
        "own_theirs",
        [(0, n) for n in range(early, half)] + [(1, n) for n in range(2 * half)],
        x_first,
        yz_theirs,
    )
    got_yz, known_mine, known_theirs = lax.optimization_barrier(
        (got_yz, known_mine, known_theirs)
    )
    scale = 1.0 / (3.0 * layers * peers * ny * nz)
    kernel = functools.partial(messages_kernel, parts, scale)
    args = [yz_mine, got_yz, volume, gram, ordered]
    grams = call(kernel, "messages", messages, args)
    fields = jax.ShapeDtypeStruct((snaps * (half * ny + 1), nz), f32)
    mine_yz = call(
        raw_from_parts_kernel, "raw_yz_mine", (fields, fields), [known_mine, got_yz, blocks]
    )
    grams, *mine_yz = lax.optimization_barrier((grams, *mine_yz))
    grams = lax.all_to_all(grams, ("space", "snap"), 0, 0, tiled=True)
    modes, rows = call(
        functools.partial(finish_kernel, half),
        "finish",
        (
            jax.ShapeDtypeStruct(velocity.shape, bf16),
            jax.ShapeDtypeStruct((snaps, 2 * snaps), f32),
        ),
        [
            grams, blocks, theirs_x, mine_x, *mine_yz,
            known_theirs, got_last,
        ],
        [
            pltpu.VMEM((6, snaps, half, ny, nz), bf16),
            pltpu.VMEM((snaps, 2 * snaps), f32),
            pltpu.VMEM((snaps, nz), f32),
            pltpu.VMEM((half, snaps * (ny + 1), nz), f32),
            dma((7,)),
        ],
        None,
        (hbm(), hbm()),
    )
    return (rows, modes)


def per_device(velocity, metric, volume, coeffs):
    peers = lax.axis_size("space")
    paired = lax.axis_size("snap") == 2 and velocity.shape[2] == 2 * WIDTH
    if paired and velocity.shape[0] % 16 == 0 and peers & (peers - 1) == 0:
        return two_groups(velocity, metric, volume, coeffs)
    return many_groups(velocity, metric, volume, coeffs)


def solution(mesh):
    placed = (
        P("snap", None, "space", None, None),
        P(None, "space", None, None),
        P("space", None, None),
        P(),
    )
    return jax.shard_map(
        per_device,
        mesh=mesh,
        in_specs=placed,
        out_specs=(P("snap", None), P("snap", None, "space", None, None)),
        check_vma=False,
    )
```

```python
import functools

import jax
import jax.numpy as jnp
from jax import lax
from jax.experimental import pallas as pl
from jax.experimental.pallas import tpu as pltpu
from jax.sharding import PartitionSpec as P

EPS = 1e-06
WIDTH = 2
ROWS = 128
LIMIT = 24 * 1024 * 1024


def with_halo(shard, sides, width):
    for axis, dim in sides:
        peers, length = (lax.axis_size(axis), shard.shape[dim])
        up = [(i, (i + 1) % peers) for i in range(peers)]
        down = [(j, i) for i, j in up]
        last = lax.slice_in_dim(shard, length - width, length, axis=dim)
        leading = lax.slice_in_dim(shard, 0, width, axis=dim)
        before = lax.ppermute(last, axis, up)
        after = lax.ppermute(leading, axis, down)
        shard = jnp.concatenate([before, shard, after], axis=dim)
    return shard


def deriv(padded, dim):
    count = padded.shape[dim] - 4

    def cut(offset):
        return lax.slice_in_dim(padded, offset, offset + count, axis=dim)

    return (8.0 * (cut(3) - cut(1)) - (cut(4) - cut(0))) / 12.0


def curl(padded_x, metric):
    inner = padded_x[:, :, 2:-2]
    padded_y = jnp.pad(inner, ((0, 0), (0, 0), (0, 0), (2, 2), (0, 0)))
    padded_z = jnp.concatenate([inner[..., -2:], inner, inner[..., :2]], axis=4)
    along_x = deriv(padded_x, 2) * metric[0]
    along_y = deriv(padded_y, 3) * metric[1]
    along_z = deriv(padded_z, 4) * metric[2]
    omega_x = along_y[:, 2] - along_z[:, 1]
    omega_y = along_z[:, 0] - along_x[:, 2]
    omega_z = along_x[:, 1] - along_y[:, 0]
    return jnp.stack([omega_x, omega_y, omega_z], axis=1).astype(jnp.bfloat16)


def many_groups(velocity, metric, volume, coeffs):
    snap_dev = velocity.shape[0]
    snaps = coeffs.shape[0]
    group = lax.axis_index("snap")
    scale = 1.0 / (
        3.0 * volume.shape[0] * lax.axis_size("space") * volume.shape[1] * volume.shape[2]
    )
    padded = with_halo(velocity, (("space", 2),), 2)
    vorticity = curl(padded.astype(jnp.float32), metric)
    coeff_f = coeffs.astype(jnp.float32)
    moved = lax.all_to_all(vorticity, "snap", split_axis=3, concat_axis=0, tiled=True)
    part_y = moved.shape[3]
    vol_part = lax.dynamic_slice_in_dim(volume, group * part_y, part_y, 1)
    weighted = (moved.astype(jnp.float32) * vol_part).astype(jnp.bfloat16).reshape(snaps, -1)
    flat = moved.reshape(snaps, -1)
    partial_value = lax.dot_general(
        weighted, flat, (((1,), (1,)), ((), ())), preferred_element_type=jnp.float32
    )
    raw = lax.dot_general(
        coeffs, flat, (((0,), (0,)), ((), ())), preferred_element_type=jnp.float32
    )
    whole = lax.psum(partial_value, ("space", "snap")) * scale
    energy = jnp.sum(coeff_f * jnp.dot(whole, coeff_f, precision=lax.Precision.HIGHEST), axis=0)
    rows = lax.dynamic_slice_in_dim(whole, group * snap_dev, snap_dev, 0)
    local_modes = (raw / jnp.sqrt(energy + EPS)[:, None]).astype(jnp.bfloat16).reshape(moved.shape)
    modes = lax.all_to_all(local_modes, "snap", split_axis=0, concat_axis=3, tiled=True)
    return (rows, modes)


def vmem():
    return pl.BlockSpec(memory_space=pltpu.VMEM)


def hbm():
    return pl.BlockSpec(memory_space=pltpu.HBM)


def params():
    return pltpu.CompilerParams(vmem_limit_bytes=LIMIT)


def cost(flops, moved):
    return pl.CostEstimate(flops=flops, bytes_accessed=moved, transcendentals=0)


def z_stencil(size):
    rows = lax.broadcasted_iota(jnp.int32, (size, size), 0)
    cols = lax.broadcasted_iota(jnp.int32, (size, size), 1)
    ahead = rows - cols
    ahead = jnp.where(ahead < 0, ahead + size, ahead)
    out = jnp.where(ahead == 1, 8.0, 0.0) - jnp.where(ahead == size - 1, 8.0, 0.0)
    out = out - jnp.where(ahead == 2, 1.0, 0.0) + jnp.where(ahead == size - 2, 1.0, 0.0)
    return out.astype(jnp.bfloat16)


def spread(src, wide):
    snaps, ny, _ = src.shape
    for s in range(snaps):
        wide[s * (ny + 1) : s * (ny + 1) + ny, :] = src[s].astype(jnp.float32)


def row(wide, y, snaps, ny):
    return wide[pl.ds(y, snaps, ny + 1), :]


def y_stencils(load, ny):
    held = {}

    def at(j):
        if j not in held:
            held[j] = load(j)
        return held[j]

    zero = jnp.zeros_like(at(0))
    for y in range(ny):
        near = (at(y + 1) if y + 1 < ny else zero) - (at(y - 1) if y >= 1 else zero)
        far = (at(y + 2) if y + 2 < ny else zero) - (at(y - 2) if y >= 2 else zero)
        held.pop(y - 2, None)
        yield y, 8.0 * near - far


def z_derivative(field, matrix, along):
    rows = field.shape[0] * field.shape[1] * field.shape[2]
    along[...] = jnp.dot(
        field.reshape(rows, field.shape[3]), matrix, preferred_element_type=jnp.float32
    ).reshape(field.shape)


def factor(metric_ref, m, layer, y):
    return metric_ref[m, layer, pl.ds(y, 1), :] * (1.0 / 12.0)


def flip(src, wide, out_ref, i):
    snaps, ny, _ = src.shape
    spread(src, wide)
    for y in range(ny):
        out_ref[i, y] = row(wide, y, snaps, ny).astype(jnp.bfloat16)


def flip_kernel(vel_ref, out_ref, buf, wide, sems):
    half = out_ref.shape[1]
    base = lax.axis_index("snap") * half
    copies = {}
    for c in range(2):
        for i in range(half):
            source = vel_ref.at[:, 1 + c, base + i]
            copies[c, i] = pltpu.make_async_copy(source, buf.at[:, c, i], sems.at[c, i])
            copies[c, i].start()
    for c in range(2):
        for i in range(half):
            copies[c, i].wait()
            flip(buf[:, c, i], wide, out_ref.at[c], i)


def omega_x_kernel(
    vel_ref, metric_ref, mine_ref, vw_ref, first_ref, ox_ref, wide, along
):
    half, ny, snaps, nz = ox_ref.shape
    v_ref, w_ref = vw_ref.at[0], vw_ref.at[1]
    group = lax.axis_index("snap")
    matrix = z_stencil(nz)
    for slot, base in ((0, (1 - group) * half), (1, group * half)):
        if slot == 0:
            for i in range(half):
                flip(vel_ref[:, 1, base + i], wide, v_ref, i)
        z_derivative(mine_ref[0] if slot else v_ref[...], matrix, along)
        for i in range(half):
            if slot == 0:
                spread(vel_ref[:, 2, base + i], wide)

            def load(j):
                if slot:
                    return mine_ref[1, i, j].astype(jnp.float32)
                value = row(wide, j, snaps, ny)
                w_ref[i, j] = value.astype(jnp.bfloat16)
                return value

            for y, across in y_stencils(load, ny):
                value = across * factor(metric_ref, 1, base + i, y)
                value = value - along[i, y] * factor(metric_ref, 2, base + i, y)
                value = value.astype(jnp.bfloat16)
                if slot:
                    ox_ref[i, y] = value
                if slot * half + i < first_ref.shape[0]:
                    first_ref[slot * half + i, y] = value


def u_kernel(half, vel_ref, metric_ref, zu_ref, yu_ref, flat, wide, along):
    snaps, _, _, ny, nz = vel_ref.shape
    matrix = z_stencil(nz)
    group = lax.axis_index("snap")
    for slot in range(2):
        base = (group if slot else 1 - group) * half
        for i in range(half):
            spread(vel_ref[:, 0, base + i], wide)

            def load(j):
                value = row(wide, j, snaps, ny)
                flat[i, j] = value.astype(jnp.bfloat16)
                return value

            for y, across in y_stencils(load, ny):
                yu_ref[slot, i, y] = across * factor(metric_ref, 1, base + i, y)
        z_derivative(flat[...], matrix, along)
        for i in range(half):
            for y in range(ny):
                zu_ref[slot, i, y] = along[i, y] * factor(metric_ref, 2, base + i, y)


def finish_curl(sign, slot, near_ref, far_ref, halo_ref, known_ref, metric_ref, out_ref):
    half, ny, _, _ = near_ref.shape
    group = lax.axis_index("snap")
    part = group if slot else 1 - group

    def run(low_ref, high_ref):
        def plane(i, y):
            if i < 0:
                ref, k = low_ref, half + i
            elif i < half:
                ref, k = near_ref, i
            else:
                ref, k = high_ref, i - half
            return ref[k, y].astype(jnp.float32)

        for y in range(ny):
            at = [plane(i, y) for i in range(-WIDTH, half + WIDTH)]
            for i in range(half):
                along = 8.0 * (at[i + 3] - at[i + 1]) - (at[i + 4] - at[i])
                along = along * factor(metric_ref, 0, part * half + i, y)
                known = known_ref[slot, i, y]
                value = along - known if sign > 0 else known - along
                out_ref[i, y] = value.astype(jnp.bfloat16)

    @pl.when(part == 0)
    def _():
        run(halo_ref, far_ref)

    @pl.when(part == 1)
    def _():
        run(far_ref, halo_ref)


def omega_yz_kernel(slot, near, far, edge, zu_ref, yu_ref, metric_ref, y_ref, z_ref):
    known = (yu_ref, zu_ref)
    for c, sign, out_ref in ((1, -1, y_ref), (0, 1, z_ref)):
        fields = near[c], far[c], edge[c], known[c]
        finish_curl(sign, slot, *fields, metric_ref, out_ref)


def omega_theirs_kernel(near, far, edge, *refs):
    near, far, edge, outs = [(ref.at[0], ref.at[1]) for ref in (near, far, edge, refs[-1])]
    omega_yz_kernel(0, near, far, edge, *refs[:-1], *outs)


def omega_mine_kernel(*refs):
    near, far, edge, *refs, ox_ref, out_ref = refs
    near, far, edge = [(ref.at[0], ref.at[1]) for ref in (near, far, edge)]
    half = ox_ref.shape[0]
    left = out_ref.shape[0] - 2 * half
    if left:
        out_ref[:left] = ox_ref[half - left :]
    parts = [out_ref.at[pl.ds(left + n * half, half)] for n in range(2)]
    omega_yz_kernel(1, near, far, edge, *refs, *parts)


def gram_of(own, got, volume_ref, base):
    half, ny, _, _ = own.shape
    total = None
    for i in range(half):
        plain, heavy = [], []
        for y in range(ny):
            pair = jnp.concatenate([own[i, y], got[i, y]], axis=0)
            weight = volume_ref[base + i, pl.ds(y, 1), :]
            plain.append(pair)
            heavy.append((pair.astype(jnp.float32) * weight).astype(jnp.bfloat16))
        part = lax.dot_general(
            jnp.concatenate(heavy, axis=1),
            jnp.concatenate(plain, axis=1),
            (((1,), (1,)), ((), ())),
            preferred_element_type=jnp.float32,
        )
        total = part if total is None else total + part
    return total


def gram_sum(parts, own_ref, got_ref, volume_ref, earlier):
    half = volume_ref.shape[0] // 2
    base = lax.axis_index("snap") * half
    total = None if earlier is None else earlier[...]
    for own, got in parts:
        own, got = own_ref.at[pl.ds(own, half)], got_ref.at[pl.ds(got, half)]
        part = gram_of(own, got, volume_ref, base)
        total = part if total is None else total + part
    return total


def gram_x_kernel(parts, own_ref, got_ref, volume_ref, out_ref):
    out_ref[...] = gram_sum(parts, own_ref, got_ref, volume_ref, None)


def messages_kernel(parts, scale, own_ref, got_ref, volume_ref, earlier, coeff_ref, out_ref):
    total = gram_sum(parts, own_ref, got_ref, volume_ref, earlier) * scale
    coeff = coeff_ref[...]
    inner = jnp.dot(
        total, coeff, precision=lax.Precision.HIGHEST, preferred_element_type=jnp.float32
    )
    energy = jnp.sum(inner * coeff, axis=0, keepdims=True)
    snaps = total.shape[0] // 2
    turned = jnp.concatenate([total[snaps:, snaps:], total[snaps:, :snaps]], axis=1)
    group = lax.axis_index("snap")
    spare = out_ref.shape[2] - 2 * snaps * snaps - snaps
    for other, rows in enumerate((total[:snaps], turned)):
        line = [rows[k : k + 1] for k in range(snaps)]
        line.append(energy[:, other * snaps : (other + 1) * snaps])
        line = jnp.concatenate(line + [jnp.zeros((1, spare), jnp.float32)], axis=1)
        first = 1 - group if other else group
        for n in range(0, out_ref.shape[0], 2):
            out_ref[n + first] = line


def coeff_kernel(coeff_ref, ordered_ref, block_ref):
    count, _ = coeff_ref.shape
    snaps = count // 2
    rows = block_ref.shape[0]
    base = lax.axis_index("snap") * snaps

    def chosen(shape, test):
        left = lax.broadcasted_iota(jnp.int32, shape, 0)
        right = lax.broadcasted_iota(jnp.int32, shape, 1)
        return jnp.where(test(left, right), 1.0, 0.0).astype(jnp.bfloat16)

    def take(a, b, dims):
        out = lax.dot_general(a, b, (dims, ((), ())), preferred_element_type=jnp.float32)
        return out.astype(jnp.bfloat16)

    order = chosen((count, count), lambda j, m: j == lax.rem(m + base, count))
    turned = take(take(order, coeff_ref[...], ((0,), (1,))), order, ((1,), (0,)))
    same = chosen((count, count), lambda j, m: j == m)
    ordered_ref[...] = take(same, turned, ((1,), (1,))).astype(jnp.float32)
    mine = turned[:snaps]
    down = chosen((rows, snaps), lambda r, k: lax.rem(r, snaps) == k)
    for part in range(count // snaps):
        across = chosen((count, rows), lambda j, c: j == lax.rem(c, snaps) + part * snaps)
        wide = take(take(down, mine, ((1,), (0,))), across, ((1,), (0,)))
        same = chosen((rows, rows), lambda r, c: lax.div(r, snaps) == lax.div(c, snaps))
        block_ref[:, part * rows : (part + 1) * rows] = wide * same


def raw_blocks(own, got, block_ref, put):
    ny, snaps, nz = own.shape
    block = block_ref.shape[0] // snaps
    lanes = 2 if ny % (2 * block) == 0 else 1
    for start in range(0, ny, block * lanes):
        columns = []
        for n in range(lanes):
            at = start + n * block
            parts = [ref[at : at + block].reshape(block * snaps, nz) for ref in (own, got)]
            columns.append(jnp.concatenate(parts, axis=0))
        both = columns[0] if lanes == 1 else jnp.concatenate(columns, axis=1)
        raw = jnp.dot(block_ref[...], both, preferred_element_type=jnp.float32)
        for n in range(lanes):
            part = raw[:, n * nz : (n + 1) * nz].reshape(block, snaps, nz)
            for k in range(block):
                put(start + n * block + k, part[k])


def one_group_blocks(field, coeffs, put):
    ny, snaps, nz = field.shape
    block = coeffs.shape[0] // snaps
    lanes = 2 if ny % (2 * block) == 0 else 1
    for start in range(0, ny, block * lanes):
        columns = [
            field[at : at + block].reshape(block * snaps, nz)
            for at in range(start, start + block * lanes, block)
        ]
        both = columns[0] if lanes == 1 else jnp.concatenate(columns, axis=1)
        raw = jnp.dot(coeffs, both, preferred_element_type=jnp.float32)
        for n in range(lanes):
            part = raw[:, n * nz : (n + 1) * nz].reshape(block, snaps, nz)
            put(start + n * block, part)


def own_part_kernel(parts, block_ref, *refs):
    out_ref = refs[-1]
    coeffs = block_ref[:, : block_ref.shape[1] // 2]
    for n, (ref, layer) in enumerate(parts):

        def put(y, value):
            out_ref[n, y : y + value.shape[0]] = value

        one_group_blocks(refs[ref].at[layer], coeffs, put)


def add_other_group(known, got, block_ref, put):
    coeffs = block_ref[:, block_ref.shape[1] // 2 :]

    def put_block(y, value):
        for k in range(value.shape[0]):
            put(y + k, known[y + k] + value[k])

    one_group_blocks(got, coeffs, put_block)


def raw_from_parts_kernel(known_ref, got_ref, block_ref, *outs):
    for n, out_ref in enumerate(outs):
        _, ny, snaps, _ = known_ref.shape
        stride = out_ref.shape[0] // snaps
        count = stride // ny
        for i in range(count):

            def put(y, value):
                out_ref[pl.ds(i * ny + y, snaps, stride), :] = value

            add_other_group(known_ref.at[n * count + i], got_ref.at[n * count + i], block_ref, put)


def raw_kernel(parts, own_ref, got_ref, block_ref, *outs):
    for (own, got), out_ref in zip(parts, outs):
        _, ny, snaps, _ = own_ref.shape
        stride = out_ref.shape[0] // snaps
        count = stride // ny
        for i in range(count):

            def put(y, value):
                out_ref[pl.ds(i * ny + y, snaps, stride), :] = value

            raw_blocks(own_ref.at[own + i], got_ref.at[got + i], block_ref, put)


def finish_kernel(
    half, parts_ref, block_ref,
    x_theirs, x_mine, y_mine, z_mine, known_ref, got_ref,
    out_ref, rows_ref, stage, rows_buf, factors, wide, sems,
):
    _, snaps, _, ny, nz = stage.shape
    group = lax.axis_index("snap")
    lines = [parts_ref[n] for n in range(parts_ref.shape[0])]
    while len(lines) > 1:
        lines = [sum(lines[n : n + 2]) for n in range(0, len(lines), 2)]
    width = 2 * snaps
    line = lines[0][:, snaps * width : snaps * (width + 1)]
    down = lax.broadcasted_iota(jnp.int32, (snaps, snaps), 0)
    across = lax.broadcasted_iota(jnp.int32, (snaps, snaps), 1)
    energy = jnp.where(down == across, jnp.broadcast_to(line, (snaps, snaps)), 0.0)
    energy = jnp.sum(energy, axis=1, keepdims=True)
    factor = jnp.broadcast_to(1.0 / jnp.sqrt(energy + EPS), (snaps, nz))
    factors[...] = factor
    mine = jnp.concatenate(
        [lines[0][:, k * width : (k + 1) * width] for k in range(snaps)], axis=0
    )
    turned = jnp.concatenate([mine[:, snaps:], mine[:, :snaps]], axis=1)
    rows_buf[...] = jnp.where(group == 0, mine, turned)
    copies = [pltpu.make_async_copy(rows_buf, rows_ref, sems.at[6])]
    copies[0].start()
    bases = (1 - group) * half, group * half

    def send(c, slot):
        n = 2 * c + slot
        target = out_ref.at[:, c, pl.ds(bases[slot], half)]
        copies.append(pltpu.make_async_copy(stage.at[n], target, sems.at[n]))
        copies[-1].start()

    for c, raw_ref in enumerate((x_mine, y_mine, z_mine)):
        for k in range(snaps):
            at = k * (half * ny + 1)
            value = raw_ref[at : at + half * ny, :] * factors[k : k + 1, :]
            stage[2 * c + 1, k] = value.astype(jnp.bfloat16).reshape(half, ny, nz)
        send(c, 1)
    early = x_theirs.shape[0] // snaps // ny
    for k in range(snaps):
        at = k * (early * ny + 1)
        value = x_theirs[at : at + early * ny, :] * factors[k : k + 1, :]
        stage[0, k, :early] = value.astype(jnp.bfloat16).reshape(early, ny, nz)
    if early == half:
        send(0, 0)
    late = [(0, i) for i in range(early, half)]
    late += [(c, i) for c in (1, 2) for i in range(half)]
    for n, (c, i) in enumerate(late):
        rows = wide.at[n % wide.shape[0]]

        def put(y, value):
            rows[pl.ds(y, snaps, ny + 1), :] = value * factor

        add_other_group(known_ref.at[n], got_ref.at[n], block_ref, put)
        for k in range(snaps):
            at = k * (ny + 1)
            stage[2 * c, k, i] = rows[at : at + ny, :].astype(jnp.bfloat16)
        if i == half - 1:
            send(c, 0)
    for copy in copies:
        copy.wait()


def two_groups(velocity, metric, volume, coeffs):
    snaps, _, layers, ny, nz = velocity.shape
    half = layers // 2
    peers = lax.axis_size("space")
    bf16, f32 = jnp.bfloat16, jnp.float32

    def halo(first):
        pairs = []
        for s in range(peers):
            for g in range(2):
                down = (g == 0) == first
                pairs.append((s * 2 + g, ((s + (-1 if down else 1)) % peers) * 2 + g))
        return pairs

    def swap(value):
        return lax.ppermute(value, "snap", [(0, 1), (1, 0)])

    def shift(value, first):
        return lax.ppermute(value, ("space", "snap"), halo(first))

    field = jax.ShapeDtypeStruct((half, ny, snaps, nz), bf16)
    pair = jax.ShapeDtypeStruct((2, half, ny, snaps, nz), bf16)
    partial_sum = jax.ShapeDtypeStruct((2, half, ny, snaps, nz), f32)
    square = jax.ShapeDtypeStruct((2 * snaps, 2 * snaps), f32)
    cells = half * ny * snaps * nz
    wide = pltpu.VMEM((snaps * (ny + 1), nz), f32)
    along = pltpu.VMEM((half, ny, snaps, nz), f32)
    dma = pltpu.SemaphoreType.DMA

    def call(kernel, name, out_shape, args, scratch=(), in_specs=None, out_specs=None, work=5):
        return pl.pallas_call(
            kernel,
            out_shape=out_shape,
            in_specs=in_specs or [vmem()] * len(args),
            out_specs=out_specs or jax.tree.map(lambda _: vmem(), out_shape),
            scratch_shapes=list(scratch),
            compiler_params=params(),
            cost_estimate=cost(2 * work * cells, work * cells),
            name=name,
        )(*args)

    mine = call(
        flip_kernel,
        "flip_mine",
        pair,
        [pltpu.with_memory_space_constraint(velocity, pltpu.HBM)],
        [pltpu.VMEM((snaps, 2, half, ny, nz), bf16), wide, dma((2, half))],
        [hbm()],
    )
    edge_theirs = shift(mine, True)
    early = half
    first = jax.ShapeDtypeStruct((half + early, ny, snaps, nz), bf16)
    last = jax.ShapeDtypeStruct((3 * half - early, ny, snaps, nz), bf16)
    theirs, x_first, x_mine = call(
        omega_x_kernel,
        "omega_x",
        (pair, first, field),
        [velocity, metric, mine],
        [wide, along],
    )
    got_first = swap(x_first)
    zu, yu = call(
        functools.partial(u_kernel, half),
        "u_terms",
        (partial_sum, partial_sum),
        [velocity, metric],
        [pltpu.VMEM((half, ny, snaps, nz), bf16), wide, along],
    )

    def own_part(name, parts, *fields):
        shape = jax.ShapeDtypeStruct((len(parts), ny, snaps, nz), f32)
        return call(functools.partial(own_part_kernel, parts), name, shape, [blocks, *fields])

    def raw_modes(name, parts, counts, own, got):
        shapes = tuple(jax.ShapeDtypeStruct((snaps * (n * ny + 1), nz), f32) for n in counts)
        return call(functools.partial(raw_kernel, parts), name, shapes, [own, got, blocks])

    yz_theirs = call(
        omega_theirs_kernel,
        "omega_yz_theirs",
        pair,
        [theirs, mine, edge_theirs, zu, yu, metric],
    )
    got_yz = swap(yz_theirs)
    late, _ = lax.optimization_barrier((theirs, yz_theirs))
    edge_mine = shift(late, False)
    ordered, blocks = call(
        coeff_kernel,
        "coeff_blocks",
        (
            square,
            jax.ShapeDtypeStruct((ROWS // snaps * snaps, ROWS // snaps * 2 * snaps), bf16),
        ),
        [coeffs],
    )
    kernel = functools.partial(gram_x_kernel, ((0, 0),))
    gram = call(kernel, "gram_x", square, [x_mine, got_first, volume])
    (mine_x,) = raw_modes("raw_x_mine", ((0, 0),), (half,), x_mine, got_first)
    (theirs_x,) = raw_modes("raw_x_theirs", ((0, half),), (early,), x_first, got_first)
    edge_mine, gram, mine_x, theirs_x = lax.optimization_barrier(
        (edge_mine, gram, mine_x, theirs_x)
    )
    yz_mine = call(
        omega_mine_kernel,
        "omega_yz_mine",
        last,
        [mine, theirs, edge_mine, zu, yu, metric, x_mine],
    )
    got_last = swap(yz_mine)
    got_yz = got_yz.reshape(2 * half, ny, snaps, nz)
    left = half - early
    size = -(-snaps * (2 * snaps + 1) // nz) * nz
    messages = jax.ShapeDtypeStruct((2 * peers, 1, size), f32)
    parts = ((left, 0), (left + half, half))
    yz_theirs = yz_theirs.reshape(2 * half, ny, snaps, nz)
    known_mine = own_part("own_mine", [(0, left + n) for n in range(2 * half)], yz_mine)
    known_theirs = own_part(
        "own_theirs",
        [(0, n) for n in range(early, half)] + [(1, n) for n in range(2 * half)],
        x_first,
        yz_theirs,
    )
    got_yz, known_mine, known_theirs = lax.optimization_barrier(
        (got_yz, known_mine, known_theirs)
    )
    scale = 1.0 / (3.0 * layers * peers * ny * nz)
    kernel = functools.partial(messages_kernel, parts, scale)
    args = [yz_mine, got_yz, volume, gram, ordered]
    grams = call(kernel, "messages", messages, args)
    fields = jax.ShapeDtypeStruct((snaps * (half * ny + 1), nz), f32)
    mine_yz = call(
        raw_from_parts_kernel, "raw_yz_mine", (fields, fields), [known_mine, got_yz, blocks]
    )
    grams, *mine_yz = lax.optimization_barrier((grams, *mine_yz))
    grams = lax.all_to_all(grams, ("space", "snap"), 0, 0, tiled=True)
    modes, rows = call(
        functools.partial(finish_kernel, half),
        "finish",
        (
            jax.ShapeDtypeStruct(velocity.shape, bf16),
            jax.ShapeDtypeStruct((snaps, 2 * snaps), f32),
        ),
        [
            grams, blocks, theirs_x, mine_x, *mine_yz,
            known_theirs, got_last,
        ],
        [
            pltpu.VMEM((6, snaps, half, ny, nz), bf16),
            pltpu.VMEM((snaps, 2 * snaps), f32),
            pltpu.VMEM((snaps, nz), f32),
            pltpu.VMEM((half, snaps * (ny + 1), nz), f32),
            dma((7,)),
        ],
        None,
        (hbm(), hbm()),
    )
    return (rows, modes)


def per_device(velocity, metric, volume, coeffs):
    peers = lax.axis_size("space")
    paired = lax.axis_size("snap") == 2 and velocity.shape[2] == 2 * WIDTH
    if paired and velocity.shape[0] % 16 == 0 and peers & (peers - 1) == 0:
        return two_groups(velocity, metric, volume, coeffs)
    return many_groups(velocity, metric, volume, coeffs)


def solution(mesh):
    placed = (
        P("snap", None, "space", None, None),
        P(None, "space", None, None),
        P("space", None, None),
        P(),
    )
    return jax.shard_map(
        per_device,
        mesh=mesh,
        in_specs=placed,
        out_specs=(P("snap", None), P("snap", None, "space", None, None)),
        check_vma=False,
    )
```

```python
import functools

import jax
import jax.numpy as jnp
from jax import lax
from jax.experimental import pallas as pl
from jax.experimental.pallas import tpu as pltpu
from jax.sharding import PartitionSpec as P

EPS = 1e-06
WIDTH = 2
ROWS = 128
LIMIT = 24 * 1024 * 1024


def with_halo(shard, sides, width):
    for axis, dim in sides:
        peers, length = (lax.axis_size(axis), shard.shape[dim])
        up = [(i, (i + 1) % peers) for i in range(peers)]
        down = [(j, i) for i, j in up]
        last = lax.slice_in_dim(shard, length - width, length, axis=dim)
        leading = lax.slice_in_dim(shard, 0, width, axis=dim)
        before = lax.ppermute(last, axis, up)
        after = lax.ppermute(leading, axis, down)
        shard = jnp.concatenate([before, shard, after], axis=dim)
    return shard


def deriv(padded, dim):
    count = padded.shape[dim] - 4

    def cut(offset):
        return lax.slice_in_dim(padded, offset, offset + count, axis=dim)

    return (8.0 * (cut(3) - cut(1)) - (cut(4) - cut(0))) / 12.0


def curl(padded_x, metric):
    inner = padded_x[:, :, 2:-2]
    padded_y = jnp.pad(inner, ((0, 0), (0, 0), (0, 0), (2, 2), (0, 0)))
    padded_z = jnp.concatenate([inner[..., -2:], inner, inner[..., :2]], axis=4)
    along_x = deriv(padded_x, 2) * metric[0]
    along_y = deriv(padded_y, 3) * metric[1]
    along_z = deriv(padded_z, 4) * metric[2]
    omega_x = along_y[:, 2] - along_z[:, 1]
    omega_y = along_z[:, 0] - along_x[:, 2]
    omega_z = along_x[:, 1] - along_y[:, 0]
    return jnp.stack([omega_x, omega_y, omega_z], axis=1).astype(jnp.bfloat16)


def many_groups(velocity, metric, volume, coeffs):
    snap_dev = velocity.shape[0]
    snaps = coeffs.shape[0]
    group = lax.axis_index("snap")
    scale = 1.0 / (
        3.0 * volume.shape[0] * lax.axis_size("space") * volume.shape[1] * volume.shape[2]
    )
    padded = with_halo(velocity, (("space", 2),), 2)
    vorticity = curl(padded.astype(jnp.float32), metric)
    coeff_f = coeffs.astype(jnp.float32)
    moved = lax.all_to_all(vorticity, "snap", split_axis=3, concat_axis=0, tiled=True)
    part_y = moved.shape[3]
    vol_part = lax.dynamic_slice_in_dim(volume, group * part_y, part_y, 1)
    weighted = (moved.astype(jnp.float32) * vol_part).astype(jnp.bfloat16).reshape(snaps, -1)
    flat = moved.reshape(snaps, -1)
    partial_value = lax.dot_general(
        weighted, flat, (((1,), (1,)), ((), ())), preferred_element_type=jnp.float32
    )
    raw = lax.dot_general(
        coeffs, flat, (((0,), (0,)), ((), ())), preferred_element_type=jnp.float32
    )
    whole = lax.psum(partial_value, ("space", "snap")) * scale
    energy = jnp.sum(coeff_f * jnp.dot(whole, coeff_f, precision=lax.Precision.HIGHEST), axis=0)
    rows = lax.dynamic_slice_in_dim(whole, group * snap_dev, snap_dev, 0)
    local_modes = (raw / jnp.sqrt(energy + EPS)[:, None]).astype(jnp.bfloat16).reshape(moved.shape)
    modes = lax.all_to_all(local_modes, "snap", split_axis=0, concat_axis=3, tiled=True)
    return (rows, modes)


def vmem():
    return pl.BlockSpec(memory_space=pltpu.VMEM)


def hbm():
    return pl.BlockSpec(memory_space=pltpu.HBM)


def params():
    return pltpu.CompilerParams(vmem_limit_bytes=LIMIT)


def cost(flops, moved):
    return pl.CostEstimate(flops=flops, bytes_accessed=moved, transcendentals=0)


def z_stencil(size):
    rows = lax.broadcasted_iota(jnp.int32, (size, size), 0)
    cols = lax.broadcasted_iota(jnp.int32, (size, size), 1)
    ahead = rows - cols
    ahead = jnp.where(ahead < 0, ahead + size, ahead)
    out = jnp.where(ahead == 1, 8.0, 0.0) - jnp.where(ahead == size - 1, 8.0, 0.0)
    out = out - jnp.where(ahead == 2, 1.0, 0.0) + jnp.where(ahead == size - 2, 1.0, 0.0)
    return out.astype(jnp.bfloat16)


def spread(src, wide):
    snaps, ny, _ = src.shape
    for s in range(snaps):
        wide[s * (ny + 1) : s * (ny + 1) + ny, :] = src[s].astype(jnp.float32)


def row(wide, y, snaps, ny):
    return wide[pl.ds(y, snaps, ny + 1), :]


def y_stencils(load, ny):
    held = {}

    def at(j):
        if j not in held:
            held[j] = load(j)
        return held[j]

    zero = jnp.zeros_like(at(0))
    for y in range(ny):
        near = (at(y + 1) if y + 1 < ny else zero) - (at(y - 1) if y >= 1 else zero)
        far = (at(y + 2) if y + 2 < ny else zero) - (at(y - 2) if y >= 2 else zero)
        held.pop(y - 2, None)
        yield y, 8.0 * near - far


def z_derivative(field, matrix, along):
    rows = field.shape[0] * field.shape[1] * field.shape[2]
    along[...] = jnp.dot(
        field.reshape(rows, field.shape[3]), matrix, preferred_element_type=jnp.float32
    ).reshape(field.shape)


def factor(metric_ref, m, layer, y):
    return metric_ref[m, layer, pl.ds(y, 1), :] * (1.0 / 12.0)


def flip(src, wide, out_ref, i):
    snaps, ny, _ = src.shape
    spread(src, wide)
    for y in range(ny):
        out_ref[i, y] = row(wide, y, snaps, ny).astype(jnp.bfloat16)


def flip_kernel(vel_ref, out_ref, buf, wide, sems):
    half = out_ref.shape[1]
    base = lax.axis_index("snap") * half
    copies = {}
    for c in range(2):
        for i in range(half):
            source = vel_ref.at[:, 1 + c, base + i]
            copies[c, i] = pltpu.make_async_copy(source, buf.at[:, c, i], sems.at[c, i])
            copies[c, i].start()
    for c in range(2):
        for i in range(half):
            copies[c, i].wait()
            flip(buf[:, c, i], wide, out_ref.at[c], i)


def omega_x_kernel(
    vel_ref, metric_ref, mine_ref, v_ref, w_ref, first_ref, ox_ref, wide, along
):
    half, ny, snaps, nz = ox_ref.shape
    group = lax.axis_index("snap")
    matrix = z_stencil(nz)
    for slot, base in ((0, (1 - group) * half), (1, group * half)):
        if slot == 0:
            for i in range(half):
                flip(vel_ref[:, 1, base + i], wide, v_ref, i)
        z_derivative(mine_ref[0] if slot else v_ref[...], matrix, along)
        for i in range(half):
            if slot == 0:
                spread(vel_ref[:, 2, base + i], wide)

            def load(j):
                if slot:
                    return mine_ref[1, i, j].astype(jnp.float32)
                value = row(wide, j, snaps, ny)
                w_ref[i, j] = value.astype(jnp.bfloat16)
                return value

            for y, across in y_stencils(load, ny):
                value = across * factor(metric_ref, 1, base + i, y)
                value = value - along[i, y] * factor(metric_ref, 2, base + i, y)
                value = value.astype(jnp.bfloat16)
                if slot:
                    ox_ref[i, y] = value
                unit, at = divmod((slot * half + i) * ny + y, first_ref.shape[1])
                if unit < first_ref.shape[0]:
                    first_ref[unit, at] = value


def u_kernel(half, vel_ref, metric_ref, zu_ref, yu_ref, flat, wide, along):
    snaps, _, _, ny, nz = vel_ref.shape
    matrix = z_stencil(nz)
    group = lax.axis_index("snap")
    for slot in range(2):
        base = (group if slot else 1 - group) * half
        for i in range(half):
            spread(vel_ref[:, 0, base + i], wide)

            def load(j):
                value = row(wide, j, snaps, ny)
                flat[i, j] = value.astype(jnp.bfloat16)
                return value

            for y, across in y_stencils(load, ny):
                yu_ref[slot, i, y] = across * factor(metric_ref, 1, base + i, y)
        z_derivative(flat[...], matrix, along)
        for i in range(half):
            for y in range(ny):
                zu_ref[slot, i, y] = along[i, y] * factor(metric_ref, 2, base + i, y)


def finish_curl(sign, slot, near_ref, far_ref, halo_ref, known_ref, metric_ref, put):
    half, ny, _, _ = near_ref.shape
    group = lax.axis_index("snap")
    part = group if slot else 1 - group

    def run(low_ref, high_ref):
        def plane(i, y):
            if i < 0:
                ref, k = low_ref, half + i
            elif i < half:
                ref, k = near_ref, i
            else:
                ref, k = high_ref, i - half
            return ref[k, y].astype(jnp.float32)

        for y in range(ny):
            at = [plane(i, y) for i in range(-WIDTH, half + WIDTH)]
            for i in range(half):
                along = 8.0 * (at[i + 3] - at[i + 1]) - (at[i + 4] - at[i])
                along = along * factor(metric_ref, 0, part * half + i, y)
                known = known_ref[slot, i, y]
                value = along - known if sign > 0 else known - along
                put(i, y, value.astype(jnp.bfloat16))

    @pl.when(part == 0)
    def _():
        run(halo_ref, far_ref)

    @pl.when(part == 1)
    def _():
        run(far_ref, halo_ref)


def omega_yz_kernel(slot, near, far, edge, zu_ref, yu_ref, metric_ref, y_ref, z_ref):
    known = (yu_ref, zu_ref)
    for c, sign, out_ref in ((1, -1, y_ref), (0, 1, z_ref)):
        fields = near[c], far[c], edge[c], known[c]
        finish_curl(sign, slot, *fields, metric_ref, out_ref)


def into(ref, start=0):
    def put(i, y, value):
        unit, at = divmod(i * ny_of[0] + y, ref.shape[1])
        ref[start + unit, at] = value

    ny_of = [ref.shape[1]]
    return put, ny_of


def omega_theirs_kernel(v_ref, w_ref, far, edge, *refs):
    far, edge = [(ref.at[0], ref.at[1]) for ref in (far, edge)]
    puts = [into(refs[-1].at[n])[0] for n in range(2)]
    omega_yz_kernel(0, (v_ref, w_ref), far, edge, *refs[:-1], *puts)


def omega_mine_kernel(*refs):
    near, far_v, far_w, edge_v, edge_w, *refs, ox_ref, out_ref = refs
    near, far = (near.at[0], near.at[1]), (far_v, far_w)
    _, ny, _, _ = far_v.shape
    whole = ox_ref.shape[0]
    left = out_ref.shape[0] - 2 * whole
    out_ref[:left] = ox_ref[whole - left :]
    puts = []
    for n in range(2):
        put, rows = into(out_ref, left + n * whole)
        rows[0] = ny
        puts.append(put)
    omega_yz_kernel(1, near, far, (edge_v, edge_w), *refs, *puts)


def gram_of(own, got, volume_ref, base):
    half, ny, _, _ = own.shape
    total = None
    for i in range(half):
        plain, heavy = [], []
        for y in range(ny):
            pair = jnp.concatenate([own[i, y], got[i, y]], axis=0)
            layer, at = divmod(i * ny + y, volume_ref.shape[1])
            weight = volume_ref[base + layer, pl.ds(at, 1), :]
            plain.append(pair)
            heavy.append((pair.astype(jnp.float32) * weight).astype(jnp.bfloat16))
        part = lax.dot_general(
            jnp.concatenate(heavy, axis=1),
            jnp.concatenate(plain, axis=1),
            (((1,), (1,)), ((), ())),
            preferred_element_type=jnp.float32,
        )
        total = part if total is None else total + part
    return total


def gram_sum(parts, own_ref, got_ref, volume_ref, earlier):
    half = volume_ref.shape[0] // 2
    base = lax.axis_index("snap") * half
    units = half * volume_ref.shape[1] // own_ref.shape[1]
    total = None if earlier is None else earlier[...]
    for own, got in parts:
        own, got = own_ref.at[pl.ds(own, units)], got_ref.at[pl.ds(got, units)]
        part = gram_of(own, got, volume_ref, base)
        total = part if total is None else total + part
    return total


def gram_x_kernel(parts, own_ref, got_ref, volume_ref, out_ref):
    out_ref[...] = gram_sum(parts, own_ref, got_ref, volume_ref, None)


def messages_kernel(parts, scale, own_ref, got_ref, volume_ref, earlier, coeff_ref, out_ref):
    total = gram_sum(parts, own_ref, got_ref, volume_ref, earlier) * scale
    coeff = coeff_ref[...]
    inner = jnp.dot(
        total, coeff, precision=lax.Precision.HIGHEST, preferred_element_type=jnp.float32
    )
    energy = jnp.sum(inner * coeff, axis=0, keepdims=True)
    snaps = total.shape[0] // 2
    turned = jnp.concatenate([total[snaps:, snaps:], total[snaps:, :snaps]], axis=1)
    group = lax.axis_index("snap")
    spare = out_ref.shape[2] - 2 * snaps * snaps - snaps
    for other, rows in enumerate((total[:snaps], turned)):
        line = [rows[k : k + 1] for k in range(snaps)]
        line.append(energy[:, other * snaps : (other + 1) * snaps])
        line = jnp.concatenate(line + [jnp.zeros((1, spare), jnp.float32)], axis=1)
        first = 1 - group if other else group
        for n in range(0, out_ref.shape[0], 2):
            out_ref[n + first] = line


def coeff_kernel(coeff_ref, ordered_ref, block_ref):
    count, _ = coeff_ref.shape
    snaps = count // 2
    rows = block_ref.shape[0]
    base = lax.axis_index("snap") * snaps

    def chosen(shape, test):
        left = lax.broadcasted_iota(jnp.int32, shape, 0)
        right = lax.broadcasted_iota(jnp.int32, shape, 1)
        return jnp.where(test(left, right), 1.0, 0.0).astype(jnp.bfloat16)

    def take(a, b, dims):
        out = lax.dot_general(a, b, (dims, ((), ())), preferred_element_type=jnp.float32)
        return out.astype(jnp.bfloat16)

    order = chosen((count, count), lambda j, m: j == lax.rem(m + base, count))
    turned = take(take(order, coeff_ref[...], ((0,), (1,))), order, ((1,), (0,)))
    same = chosen((count, count), lambda j, m: j == m)
    ordered_ref[...] = take(same, turned, ((1,), (1,))).astype(jnp.float32)
    mine = turned[:snaps]
    down = chosen((rows, snaps), lambda r, k: lax.rem(r, snaps) == k)
    for part in range(count // snaps):
        across = chosen((count, rows), lambda j, c: j == lax.rem(c, snaps) + part * snaps)
        wide = take(take(down, mine, ((1,), (0,))), across, ((1,), (0,)))
        same = chosen((rows, rows), lambda r, c: lax.div(r, snaps) == lax.div(c, snaps))
        block_ref[:, part * rows : (part + 1) * rows] = wide * same


def raw_blocks(own, got, block_ref, put):
    ny, snaps, nz = own.shape
    block = block_ref.shape[0] // snaps
    lanes = 2 if ny % (2 * block) == 0 else 1
    for start in range(0, ny, block * lanes):
        columns = []
        for n in range(lanes):
            at = start + n * block
            parts = [ref[at : at + block].reshape(block * snaps, nz) for ref in (own, got)]
            columns.append(jnp.concatenate(parts, axis=0))
        both = columns[0] if lanes == 1 else jnp.concatenate(columns, axis=1)
        raw = jnp.dot(block_ref[...], both, preferred_element_type=jnp.float32)
        for n in range(lanes):
            part = raw[:, n * nz : (n + 1) * nz].reshape(block, snaps, nz)
            for k in range(block):
                put(start + n * block + k, part[k])


def one_group_blocks(field, coeffs, put):
    ny, snaps, nz = field.shape
    block = coeffs.shape[0] // snaps
    lanes = 2 if ny % (2 * block) == 0 else 1
    for start in range(0, ny, block * lanes):
        columns = [
            field[at : at + block].reshape(block * snaps, nz)
            for at in range(start, start + block * lanes, block)
        ]
        both = columns[0] if lanes == 1 else jnp.concatenate(columns, axis=1)
        raw = jnp.dot(coeffs, both, preferred_element_type=jnp.float32)
        for n in range(lanes):
            part = raw[:, n * nz : (n + 1) * nz].reshape(block, snaps, nz)
            put(start + n * block, part)


def own_part_kernel(parts, block_ref, *refs):
    out_ref = refs[-1]
    coeffs = block_ref[:, : block_ref.shape[1] // 2]
    for n, (ref, layer) in enumerate(parts):

        def put(y, value):
            out_ref[n, y : y + value.shape[0]] = value

        one_group_blocks(refs[ref].at[layer], coeffs, put)


def add_other_group(known, got, block_ref, put):
    coeffs = block_ref[:, block_ref.shape[1] // 2 :]

    def put_block(y, value):
        for k in range(value.shape[0]):
            put(y + k, known[y + k] + value[k])

    one_group_blocks(got, coeffs, put_block)


def raw_from_parts_kernel(known_ref, got_ref, block_ref, *outs):
    for n, out_ref in enumerate(outs):
        _, ny, snaps, _ = known_ref.shape
        stride = out_ref.shape[0] // snaps
        count = stride // ny
        for i in range(count):

            def put(y, value):
                out_ref[pl.ds(i * ny + y, snaps, stride), :] = value

            add_other_group(known_ref.at[n * count + i], got_ref.at[n * count + i], block_ref, put)


def raw_kernel(parts, own_ref, got_ref, block_ref, *outs):
    for (own, got), out_ref in zip(parts, outs):
        _, ny, snaps, _ = own_ref.shape
        stride = out_ref.shape[0] // snaps
        count = stride // ny
        for i in range(count):

            def put(y, value):
                out_ref[pl.ds(i * ny + y, snaps, stride), :] = value

            raw_blocks(own_ref.at[own + i], got_ref.at[got + i], block_ref, put)


def finish_kernel(
    half, parts_ref, block_ref,
    x_theirs, x_mine, y_mine, z_mine, known_ref, got_ref,
    out_ref, rows_ref, stage, rows_buf, factors, wide, sems,
):
    _, snaps, _, ny, nz = stage.shape
    group = lax.axis_index("snap")
    lines = [parts_ref[n] for n in range(parts_ref.shape[0])]
    while len(lines) > 1:
        lines = [sum(lines[n : n + 2]) for n in range(0, len(lines), 2)]
    width = 2 * snaps
    line = lines[0][:, snaps * width : snaps * (width + 1)]
    down = lax.broadcasted_iota(jnp.int32, (snaps, snaps), 0)
    across = lax.broadcasted_iota(jnp.int32, (snaps, snaps), 1)
    energy = jnp.where(down == across, jnp.broadcast_to(line, (snaps, snaps)), 0.0)
    energy = jnp.sum(energy, axis=1, keepdims=True)
    factor = jnp.broadcast_to(1.0 / jnp.sqrt(energy + EPS), (snaps, nz))
    factors[...] = factor
    mine = jnp.concatenate(
        [lines[0][:, k * width : (k + 1) * width] for k in range(snaps)], axis=0
    )
    turned = jnp.concatenate([mine[:, snaps:], mine[:, :snaps]], axis=1)
    rows_buf[...] = jnp.where(group == 0, mine, turned)
    copies = [pltpu.make_async_copy(rows_buf, rows_ref, sems.at[6])]
    copies[0].start()
    bases = (1 - group) * half, group * half

    def send(c, slot):
        n = 2 * c + slot
        target = out_ref.at[:, c, pl.ds(bases[slot], half)]
        copies.append(pltpu.make_async_copy(stage.at[n], target, sems.at[n]))
        copies[-1].start()

    for c, raw_ref in enumerate((x_mine, y_mine, z_mine)):
        for k in range(snaps):
            at = k * (half * ny + 1)
            value = raw_ref[at : at + half * ny, :] * factors[k : k + 1, :]
            stage[2 * c + 1, k] = value.astype(jnp.bfloat16).reshape(half, ny, nz)
        send(c, 1)
    part = got_ref.shape[1]
    early = x_theirs.shape[0] // snaps // part
    for k in range(snaps):
        for n in range(early):
            at = k * (early * part + 1) + n * part
            value = x_theirs[at : at + part, :] * factors[k : k + 1, :]
            i, y = divmod(n * part, ny)
            stage[0, k, i, y : y + part] = value.astype(jnp.bfloat16)
    units = half * ny // part
    late = [(0, n) for n in range(early, units)]
    late += [(c, n) for c in (1, 2) for n in range(units)]
    for n, (c, unit) in enumerate(late):
        rows = wide.at[n % wide.shape[0]]

        def put(y, value):
            rows[pl.ds(y, snaps, part + 1), :] = value * factor

        add_other_group(known_ref.at[n], got_ref.at[n], block_ref, put)
        i, y = divmod(unit * part, ny)
        for k in range(snaps):
            at = k * (part + 1)
            stage[2 * c, k, i, y : y + part] = rows[at : at + part, :].astype(jnp.bfloat16)
        if unit == units - 1:
            send(c, 0)
    for copy in copies:
        copy.wait()


def two_groups(velocity, metric, volume, coeffs):
    snaps, _, layers, ny, nz = velocity.shape
    half = layers // 2
    peers = lax.axis_size("space")
    bf16, f32 = jnp.bfloat16, jnp.float32

    def halo(first):
        pairs = []
        for s in range(peers):
            for g in range(2):
                down = (g == 0) == first
                pairs.append((s * 2 + g, ((s + (-1 if down else 1)) % peers) * 2 + g))
        return pairs

    def swap(value):
        return lax.ppermute(value, "snap", [(0, 1), (1, 0)])

    def shift(value, first):
        return lax.ppermute(value, ("space", "snap"), halo(first))

    field = jax.ShapeDtypeStruct((half, ny, snaps, nz), bf16)
    pair = jax.ShapeDtypeStruct((2, half, ny, snaps, nz), bf16)
    partial_sum = jax.ShapeDtypeStruct((2, half, ny, snaps, nz), f32)
    square = jax.ShapeDtypeStruct((2 * snaps, 2 * snaps), f32)
    cells = half * ny * snaps * nz
    wide = pltpu.VMEM((snaps * (ny + 1), nz), f32)
    along = pltpu.VMEM((half, ny, snaps, nz), f32)
    dma = pltpu.SemaphoreType.DMA

    def call(kernel, name, out_shape, args, scratch=(), in_specs=None, out_specs=None, work=5):
        return pl.pallas_call(
            kernel,
            out_shape=out_shape,
            in_specs=in_specs or [vmem()] * len(args),
            out_specs=out_specs or jax.tree.map(lambda _: vmem(), out_shape),
            scratch_shapes=list(scratch),
            compiler_params=params(),
            cost_estimate=cost(2 * work * cells, work * cells),
            name=name,
        )(*args)

    mine = call(
        flip_kernel,
        "flip_mine",
        pair,
        [pltpu.with_memory_space_constraint(velocity, pltpu.HBM)],
        [pltpu.VMEM((snaps, 2, half, ny, nz), bf16), wide, dma((2, half))],
        [hbm()],
    )
    edge_theirs = shift(mine, True)
    part = ny // 2
    units = half * ny // part
    early = units - 1
    first = jax.ShapeDtypeStruct((units + early, part, snaps, nz), bf16)
    last = jax.ShapeDtypeStruct((3 * units - early, part, snaps, nz), bf16)
    *theirs, x_first, x_mine = call(
        omega_x_kernel,
        "omega_x",
        (field, field, first, field),
        [velocity, metric, mine],
        [wide, along],
    )
    got_first = swap(x_first)
    x_mine = x_mine.reshape(units, part, snaps, nz)
    zu, yu = call(
        functools.partial(u_kernel, half),
        "u_terms",
        (partial_sum, partial_sum),
        [velocity, metric],
        [pltpu.VMEM((half, ny, snaps, nz), bf16), wide, along],
    )

    def own_part(name, parts, *fields):
        shape = jax.ShapeDtypeStruct((len(parts), part, snaps, nz), f32)
        return call(functools.partial(own_part_kernel, parts), name, shape, [blocks, *fields])

    def raw_modes(name, parts, counts, own, got):
        shapes = tuple(jax.ShapeDtypeStruct((snaps * (n * part + 1), nz), f32) for n in counts)
        return call(functools.partial(raw_kernel, parts), name, shapes, [own, got, blocks])

    yz_theirs = call(
        omega_theirs_kernel,
        "omega_yz_theirs",
        pair,
        [*theirs, mine, edge_theirs, zu, yu, metric],
    )
    got_yz = swap(yz_theirs)
    *late, _ = lax.optimization_barrier((*theirs, yz_theirs))
    edge_mine = [shift(part, False) for part in late]
    ordered, blocks = call(
        coeff_kernel,
        "coeff_blocks",
        (
            square,
            jax.ShapeDtypeStruct((ROWS // snaps * snaps, ROWS // snaps * 2 * snaps), bf16),
        ),
        [coeffs],
    )
    kernel = functools.partial(gram_x_kernel, ((0, 0),))
    gram = call(kernel, "gram_x", square, [x_mine, got_first, volume])
    (mine_x,) = raw_modes("raw_x_mine", ((0, 0),), (units,), x_mine, got_first)
    (theirs_x,) = raw_modes("raw_x_theirs", ((0, units),), (early,), x_first, got_first)
    *edge_mine, gram, mine_x, theirs_x = lax.optimization_barrier(
        (*edge_mine, gram, mine_x, theirs_x)
    )
    yz_mine = call(
        omega_mine_kernel,
        "omega_yz_mine",
        last,
        [mine, *theirs, *edge_mine, zu, yu, metric, x_mine],
    )
    got_last = swap(yz_mine)
    got_yz = got_yz.reshape(2 * units, part, snaps, nz)
    left = units - early
    size = -(-snaps * (2 * snaps + 1) // nz) * nz
    messages = jax.ShapeDtypeStruct((2 * peers, 1, size), f32)
    parts = ((left, 0), (left + units, units))
    yz_theirs = yz_theirs.reshape(2 * units, part, snaps, nz)
    known_mine = own_part("own_mine", [(0, left + n) for n in range(2 * units)], yz_mine)
    known_theirs = own_part(
        "own_theirs",
        [(0, n) for n in range(early, units)] + [(1, n) for n in range(2 * units)],
        x_first,
        yz_theirs,
    )
    got_yz, known_mine, known_theirs = lax.optimization_barrier(
        (got_yz, known_mine, known_theirs)
    )
    scale = 1.0 / (3.0 * layers * peers * ny * nz)
    kernel = functools.partial(messages_kernel, parts, scale)
    args = [yz_mine, got_yz, volume, gram, ordered]
    grams = call(kernel, "messages", messages, args)
    fields = jax.ShapeDtypeStruct((snaps * (half * ny + 1), nz), f32)
    mine_yz = call(
        raw_from_parts_kernel, "raw_yz_mine", (fields, fields), [known_mine, got_yz, blocks]
    )
    grams, *mine_yz = lax.optimization_barrier((grams, *mine_yz))
    grams = lax.all_to_all(grams, ("space", "snap"), 0, 0, tiled=True)
    modes, rows = call(
        functools.partial(finish_kernel, half),
        "finish",
        (
            jax.ShapeDtypeStruct(velocity.shape, bf16),
            jax.ShapeDtypeStruct((snaps, 2 * snaps), f32),
        ),
        [
            grams, blocks, theirs_x, mine_x, *mine_yz,
            known_theirs, got_last,
        ],
        [
            pltpu.VMEM((6, snaps, half, ny, nz), bf16),
            pltpu.VMEM((snaps, 2 * snaps), f32),
            pltpu.VMEM((snaps, nz), f32),
            pltpu.VMEM((half, snaps * (part + 1), nz), f32),
            dma((7,)),
        ],
        None,
        (hbm(), hbm()),
    )
    return (rows, modes)


def per_device(velocity, metric, volume, coeffs):
    peers = lax.axis_size("space")
    paired = lax.axis_size("snap") == 2 and velocity.shape[2] == 2 * WIDTH
    if paired and velocity.shape[0] % 16 == 0 and peers & (peers - 1) == 0:
        return two_groups(velocity, metric, volume, coeffs)
    return many_groups(velocity, metric, volume, coeffs)


def solution(mesh):
    placed = (
        P("snap", None, "space", None, None),
        P(None, "space", None, None),
        P("space", None, None),
        P(),
    )
    return jax.shard_map(
        per_device,
        mesh=mesh,
        in_specs=placed,
        out_specs=(P("snap", None), P("snap", None, "space", None, None)),
        check_vma=False,
    )
```

```python
import functools

import jax
import jax.numpy as jnp
from jax import lax
from jax.experimental import pallas as pl
from jax.experimental.pallas import tpu as pltpu
from jax.sharding import PartitionSpec as P

EPS = 1e-06
WIDTH = 2
ROWS = 128
LIMIT = 24 * 1024 * 1024


def with_halo(shard, sides, width):
    for axis, dim in sides:
        peers, length = (lax.axis_size(axis), shard.shape[dim])
        up = [(i, (i + 1) % peers) for i in range(peers)]
        down = [(j, i) for i, j in up]
        last = lax.slice_in_dim(shard, length - width, length, axis=dim)
        leading = lax.slice_in_dim(shard, 0, width, axis=dim)
        before = lax.ppermute(last, axis, up)
        after = lax.ppermute(leading, axis, down)
        shard = jnp.concatenate([before, shard, after], axis=dim)
    return shard


def deriv(padded, dim):
    count = padded.shape[dim] - 4

    def cut(offset):
        return lax.slice_in_dim(padded, offset, offset + count, axis=dim)

    return (8.0 * (cut(3) - cut(1)) - (cut(4) - cut(0))) / 12.0


def curl(padded_x, metric):
    inner = padded_x[:, :, 2:-2]
    padded_y = jnp.pad(inner, ((0, 0), (0, 0), (0, 0), (2, 2), (0, 0)))
    padded_z = jnp.concatenate([inner[..., -2:], inner, inner[..., :2]], axis=4)
    along_x = deriv(padded_x, 2) * metric[0]
    along_y = deriv(padded_y, 3) * metric[1]
    along_z = deriv(padded_z, 4) * metric[2]
    omega_x = along_y[:, 2] - along_z[:, 1]
    omega_y = along_z[:, 0] - along_x[:, 2]
    omega_z = along_x[:, 1] - along_y[:, 0]
    return jnp.stack([omega_x, omega_y, omega_z], axis=1).astype(jnp.bfloat16)


def many_groups(velocity, metric, volume, coeffs):
    snap_dev = velocity.shape[0]
    snaps = coeffs.shape[0]
    group = lax.axis_index("snap")
    scale = 1.0 / (
        3.0 * volume.shape[0] * lax.axis_size("space") * volume.shape[1] * volume.shape[2]
    )
    padded = with_halo(velocity, (("space", 2),), 2)
    vorticity = curl(padded.astype(jnp.float32), metric)
    coeff_f = coeffs.astype(jnp.float32)
    moved = lax.all_to_all(vorticity, "snap", split_axis=3, concat_axis=0, tiled=True)
    part_y = moved.shape[3]
    vol_part = lax.dynamic_slice_in_dim(volume, group * part_y, part_y, 1)
    weighted = (moved.astype(jnp.float32) * vol_part).astype(jnp.bfloat16).reshape(snaps, -1)
    flat = moved.reshape(snaps, -1)
    partial_value = lax.dot_general(
        weighted, flat, (((1,), (1,)), ((), ())), preferred_element_type=jnp.float32
    )
    raw = lax.dot_general(
        coeffs, flat, (((0,), (0,)), ((), ())), preferred_element_type=jnp.float32
    )
    whole = lax.psum(partial_value, ("space", "snap")) * scale
    energy = jnp.sum(coeff_f * jnp.dot(whole, coeff_f, precision=lax.Precision.HIGHEST), axis=0)
    rows = lax.dynamic_slice_in_dim(whole, group * snap_dev, snap_dev, 0)
    local_modes = (raw / jnp.sqrt(energy + EPS)[:, None]).astype(jnp.bfloat16).reshape(moved.shape)
    modes = lax.all_to_all(local_modes, "snap", split_axis=0, concat_axis=3, tiled=True)
    return (rows, modes)


def vmem():
    return pl.BlockSpec(memory_space=pltpu.VMEM)


def hbm():
    return pl.BlockSpec(memory_space=pltpu.HBM)


def params():
    return pltpu.CompilerParams(vmem_limit_bytes=LIMIT)


def cost(flops, moved):
    return pl.CostEstimate(flops=flops, bytes_accessed=moved, transcendentals=0)


def z_stencil(size):
    rows = lax.broadcasted_iota(jnp.int32, (size, size), 0)
    cols = lax.broadcasted_iota(jnp.int32, (size, size), 1)
    ahead = rows - cols
    ahead = jnp.where(ahead < 0, ahead + size, ahead)
    out = jnp.where(ahead == 1, 8.0, 0.0) - jnp.where(ahead == size - 1, 8.0, 0.0)
    out = out - jnp.where(ahead == 2, 1.0, 0.0) + jnp.where(ahead == size - 2, 1.0, 0.0)
    return out.astype(jnp.bfloat16)


def spread(src, wide):
    snaps, ny, _ = src.shape
    for s in range(snaps):
        wide[s * (ny + 1) : s * (ny + 1) + ny, :] = src[s].astype(jnp.float32)


def row(wide, y, snaps, ny):
    return wide[pl.ds(y, snaps, ny + 1), :]


def y_stencils(load, ny):
    held = {}

    def at(j):
        if j not in held:
            held[j] = load(j)
        return held[j]

    zero = jnp.zeros_like(at(0))
    for y in range(ny):
        near = (at(y + 1) if y + 1 < ny else zero) - (at(y - 1) if y >= 1 else zero)
        far = (at(y + 2) if y + 2 < ny else zero) - (at(y - 2) if y >= 2 else zero)
        held.pop(y - 2, None)
        yield y, 8.0 * near - far


def z_derivative(field, matrix, along):
    rows = field.shape[0] * field.shape[1] * field.shape[2]
    along[...] = jnp.dot(
        field.reshape(rows, field.shape[3]), matrix, preferred_element_type=jnp.float32
    ).reshape(field.shape)


def factor(metric_ref, m, layer, y):
    return metric_ref[m, layer, pl.ds(y, 1), :] * (1.0 / 12.0)


def flip(src, wide, out_ref, i):
    snaps, ny, _ = src.shape
    spread(src, wide)
    for y in range(ny):
        out_ref[i, y] = row(wide, y, snaps, ny).astype(jnp.bfloat16)


def flip_kernel(vel_ref, out_ref, buf, wide, sems):
    half = out_ref.shape[1]
    base = lax.axis_index("snap") * half
    copies = {}
    for c in range(2):
        for i in range(half):
            source = vel_ref.at[:, 1 + c, base + i]
            copies[c, i] = pltpu.make_async_copy(source, buf.at[:, c, i], sems.at[c, i])
            copies[c, i].start()
    for c in range(2):
        for i in range(half):
            copies[c, i].wait()
            flip(buf[:, c, i], wide, out_ref.at[c], i)


def omega_x_kernel(
    vel_ref, metric_ref, mine_ref, v_ref, w_ref, first_ref, ox_ref, wide, along
):
    half, ny, snaps, nz = ox_ref.shape
    group = lax.axis_index("snap")
    matrix = z_stencil(nz)
    for slot, base in ((0, (1 - group) * half), (1, group * half)):
        if slot == 0:
            for i in range(half):
                flip(vel_ref[:, 1, base + i], wide, v_ref, i)
        z_derivative(mine_ref[0] if slot else v_ref[...], matrix, along)
        for i in range(half):
            if slot == 0:
                spread(vel_ref[:, 2, base + i], wide)

            def load(j):
                if slot:
                    return mine_ref[1, i, j].astype(jnp.float32)
                value = row(wide, j, snaps, ny)
                w_ref[i, j] = value.astype(jnp.bfloat16)
                return value

            for y, across in y_stencils(load, ny):
                value = across * factor(metric_ref, 1, base + i, y)
                value = value - along[i, y] * factor(metric_ref, 2, base + i, y)
                value = value.astype(jnp.bfloat16)
                if slot:
                    ox_ref[i, y] = value
                unit, at = divmod((slot * half + i) * ny + y, first_ref.shape[1])
                if unit < first_ref.shape[0]:
                    first_ref[unit, at] = value


def u_kernel(half, vel_ref, metric_ref, zu_ref, yu_ref, flat, wide, along):
    snaps, _, _, ny, nz = vel_ref.shape
    matrix = z_stencil(nz)
    group = lax.axis_index("snap")
    for slot in range(2):
        base = (group if slot else 1 - group) * half
        for i in range(half):
            spread(vel_ref[:, 0, base + i], wide)

            def load(j):
                value = row(wide, j, snaps, ny)
                flat[i, j] = value.astype(jnp.bfloat16)
                return value

            for y, across in y_stencils(load, ny):
                yu_ref[slot, i, y] = across * factor(metric_ref, 1, base + i, y)
        z_derivative(flat[...], matrix, along)
        for i in range(half):
            for y in range(ny):
                zu_ref[slot, i, y] = along[i, y] * factor(metric_ref, 2, base + i, y)


def finish_curl(sign, slot, near_ref, far_ref, halo_ref, known_ref, metric_ref, put):
    half, ny, _, _ = near_ref.shape
    group = lax.axis_index("snap")
    part = group if slot else 1 - group

    def run(low_ref, high_ref):
        def plane(i, y):
            if i < 0:
                ref, k = low_ref, half + i
            elif i < half:
                ref, k = near_ref, i
            else:
                ref, k = high_ref, i - half
            return ref[k, y].astype(jnp.float32)

        for y in range(ny):
            at = [plane(i, y) for i in range(-WIDTH, half + WIDTH)]
            for i in range(half):
                along = 8.0 * (at[i + 3] - at[i + 1]) - (at[i + 4] - at[i])
                along = along * factor(metric_ref, 0, part * half + i, y)
                known = known_ref[slot, i, y]
                value = along - known if sign > 0 else known - along
                put(i, y, value.astype(jnp.bfloat16))

    @pl.when(part == 0)
    def _():
        run(halo_ref, far_ref)

    @pl.when(part == 1)
    def _():
        run(far_ref, halo_ref)


def omega_yz_kernel(slot, near, far, edge, zu_ref, yu_ref, metric_ref, y_ref, z_ref):
    known = (yu_ref, zu_ref)
    for c, sign, out_ref in ((1, -1, y_ref), (0, 1, z_ref)):
        fields = near[c], far[c], edge[c], known[c]
        finish_curl(sign, slot, *fields, metric_ref, out_ref)


def into(ref, start=0):
    def put(i, y, value):
        unit, at = divmod(i * ny_of[0] + y, ref.shape[1])
        ref[start + unit, at] = value

    ny_of = [ref.shape[1]]
    return put, ny_of


def omega_theirs_kernel(v_ref, w_ref, far, edge, *refs):
    far, edge = [(ref.at[0], ref.at[1]) for ref in (far, edge)]
    puts = [into(refs[-1].at[n])[0] for n in range(2)]
    omega_yz_kernel(0, (v_ref, w_ref), far, edge, *refs[:-1], *puts)


def omega_mine_kernel(*refs):
    near, far_v, far_w, edge_v, edge_w, *refs, ox_ref, out_ref = refs
    near, far = (near.at[0], near.at[1]), (far_v, far_w)
    _, ny, _, _ = far_v.shape
    whole = ox_ref.shape[0]
    left = out_ref.shape[0] - 2 * whole
    out_ref[:left] = ox_ref[whole - left :]
    puts = []
    for n in range(2):
        put, rows = into(out_ref, left + n * whole)
        rows[0] = ny
        puts.append(put)
    omega_yz_kernel(1, near, far, (edge_v, edge_w), *refs, *puts)


def gram_of(own, got, volume_ref, base):
    half, ny, _, _ = own.shape
    total = None
    for i in range(half):
        plain, heavy = [], []
        for y in range(ny):
            pair = jnp.concatenate([own[i, y], got[i, y]], axis=0)
            layer, at = divmod(i * ny + y, volume_ref.shape[1])
            weight = volume_ref[base + layer, pl.ds(at, 1), :]
            plain.append(pair)
            heavy.append((pair.astype(jnp.float32) * weight).astype(jnp.bfloat16))
        part = lax.dot_general(
            jnp.concatenate(heavy, axis=1),
            jnp.concatenate(plain, axis=1),
            (((1,), (1,)), ((), ())),
            preferred_element_type=jnp.float32,
        )
        total = part if total is None else total + part
    return total


def gram_sum(parts, own_ref, got_ref, volume_ref, earlier):
    half = volume_ref.shape[0] // 2
    base = lax.axis_index("snap") * half
    units = half * volume_ref.shape[1] // own_ref.shape[1]
    total = None if earlier is None else earlier[...]
    for own, got in parts:
        own, got = own_ref.at[pl.ds(own, units)], got_ref.at[pl.ds(got, units)]
        part = gram_of(own, got, volume_ref, base)
        total = part if total is None else total + part
    return total


def gram_x_kernel(parts, own_ref, got_ref, volume_ref, out_ref):
    out_ref[...] = gram_sum(parts, own_ref, got_ref, volume_ref, None)


def messages_kernel(parts, scale, own_ref, got_ref, volume_ref, earlier, coeff_ref, out_ref):
    total = gram_sum(parts, own_ref, got_ref, volume_ref, earlier) * scale
    coeff = coeff_ref[...]
    inner = jnp.dot(
        total, coeff, precision=lax.Precision.HIGHEST, preferred_element_type=jnp.float32
    )
    energy = jnp.sum(inner * coeff, axis=0, keepdims=True)
    snaps = total.shape[0] // 2
    turned = jnp.concatenate([total[snaps:, snaps:], total[snaps:, :snaps]], axis=1)
    group = lax.axis_index("snap")
    spare = out_ref.shape[2] - 2 * snaps * snaps - snaps
    for other, rows in enumerate((total[:snaps], turned)):
        line = [rows[k : k + 1] for k in range(snaps)]
        line.append(energy[:, other * snaps : (other + 1) * snaps])
        line = jnp.concatenate(line + [jnp.zeros((1, spare), jnp.float32)], axis=1)
        first = 1 - group if other else group
        for n in range(0, out_ref.shape[0], 2):
            out_ref[n + first] = line


def coeff_kernel(coeff_ref, ordered_ref, block_ref):
    count, _ = coeff_ref.shape
    snaps = count // 2
    rows = block_ref.shape[0]
    base = lax.axis_index("snap") * snaps

    def chosen(shape, test):
        left = lax.broadcasted_iota(jnp.int32, shape, 0)
        right = lax.broadcasted_iota(jnp.int32, shape, 1)
        return jnp.where(test(left, right), 1.0, 0.0).astype(jnp.bfloat16)

    def take(a, b, dims):
        out = lax.dot_general(a, b, (dims, ((), ())), preferred_element_type=jnp.float32)
        return out.astype(jnp.bfloat16)

    order = chosen((count, count), lambda j, m: j == lax.rem(m + base, count))
    turned = take(take(order, coeff_ref[...], ((0,), (1,))), order, ((1,), (0,)))
    same = chosen((count, count), lambda j, m: j == m)
    ordered_ref[...] = take(same, turned, ((1,), (1,))).astype(jnp.float32)
    mine = turned[:snaps]
    down = chosen((rows, snaps), lambda r, k: lax.rem(r, snaps) == k)
    for part in range(count // snaps):
        across = chosen((count, rows), lambda j, c: j == lax.rem(c, snaps) + part * snaps)
        wide = take(take(down, mine, ((1,), (0,))), across, ((1,), (0,)))
        same = chosen((rows, rows), lambda r, c: lax.div(r, snaps) == lax.div(c, snaps))
        block_ref[:, part * rows : (part + 1) * rows] = wide * same


def raw_blocks(own, got, block_ref, put):
    ny, snaps, nz = own.shape
    block = block_ref.shape[0] // snaps
    lanes = 2 if ny % (2 * block) == 0 else 1
    for start in range(0, ny, block * lanes):
        columns = []
        for n in range(lanes):
            at = start + n * block
            parts = [ref[at : at + block].reshape(block * snaps, nz) for ref in (own, got)]
            columns.append(jnp.concatenate(parts, axis=0))
        both = columns[0] if lanes == 1 else jnp.concatenate(columns, axis=1)
        raw = jnp.dot(block_ref[...], both, preferred_element_type=jnp.float32)
        for n in range(lanes):
            part = raw[:, n * nz : (n + 1) * nz].reshape(block, snaps, nz)
            for k in range(block):
                put(start + n * block + k, part[k])


def one_group_blocks(field, coeffs, put):
    ny, snaps, nz = field.shape
    block = coeffs.shape[0] // snaps
    lanes = 2 if ny % (2 * block) == 0 else 1
    for start in range(0, ny, block * lanes):
        columns = [
            field[at : at + block].reshape(block * snaps, nz)
            for at in range(start, start + block * lanes, block)
        ]
        both = columns[0] if lanes == 1 else jnp.concatenate(columns, axis=1)
        raw = jnp.dot(coeffs, both, preferred_element_type=jnp.float32)
        for n in range(lanes):
            part = raw[:, n * nz : (n + 1) * nz].reshape(block, snaps, nz)
            put(start + n * block, part)


def own_part_kernel(parts, block_ref, *refs):
    out_ref = refs[-1]
    coeffs = block_ref[:, : block_ref.shape[1] // 2]
    for n, (ref, layer) in enumerate(parts):

        def put(y, value):
            out_ref[n, y : y + value.shape[0]] = value

        one_group_blocks(refs[ref].at[layer], coeffs, put)


def add_other_group(known, got, block_ref, put):
    coeffs = block_ref[:, block_ref.shape[1] // 2 :]

    def put_block(y, value):
        for k in range(value.shape[0]):
            put(y + k, known[y + k] + value[k])

    one_group_blocks(got, coeffs, put_block)


def raw_kernel(parts, own_ref, got_ref, block_ref, *outs):
    for (own, got), out_ref in zip(parts, outs):
        _, ny, snaps, _ = own_ref.shape
        stride = out_ref.shape[0] // snaps
        count = stride // ny
        for i in range(count):

            def put(y, value):
                out_ref[pl.ds(i * ny + y, snaps, stride), :] = value

            raw_blocks(own_ref.at[own + i], got_ref.at[got + i], block_ref, put)


def finish_kernel(
    half, parts_ref, block_ref,
    x_theirs, x_mine, known_mine, got_mine, known_ref, got_ref,
    out_ref, rows_ref, stage, rows_buf, factors, wide, sems,
):
    _, snaps, _, ny, nz = stage.shape
    group = lax.axis_index("snap")
    lines = [parts_ref[n] for n in range(parts_ref.shape[0])]
    while len(lines) > 1:
        lines = [sum(lines[n : n + 2]) for n in range(0, len(lines), 2)]
    width = 2 * snaps
    line = lines[0][:, snaps * width : snaps * (width + 1)]
    down = lax.broadcasted_iota(jnp.int32, (snaps, snaps), 0)
    across = lax.broadcasted_iota(jnp.int32, (snaps, snaps), 1)
    energy = jnp.where(down == across, jnp.broadcast_to(line, (snaps, snaps)), 0.0)
    energy = jnp.sum(energy, axis=1, keepdims=True)
    factor = jnp.broadcast_to(1.0 / jnp.sqrt(energy + EPS), (snaps, nz))
    factors[...] = factor
    mine = jnp.concatenate(
        [lines[0][:, k * width : (k + 1) * width] for k in range(snaps)], axis=0
    )
    turned = jnp.concatenate([mine[:, snaps:], mine[:, :snaps]], axis=1)
    rows_buf[...] = jnp.where(group == 0, mine, turned)
    copies = [pltpu.make_async_copy(rows_buf, rows_ref, sems.at[6])]
    copies[0].start()
    bases = (1 - group) * half, group * half

    def send(c, slot):
        n = 2 * c + slot
        target = out_ref.at[:, c, pl.ds(bases[slot], half)]
        copies.append(pltpu.make_async_copy(stage.at[n], target, sems.at[n]))
        copies[-1].start()

    for k in range(snaps):
        at = k * (half * ny + 1)
        value = x_mine[at : at + half * ny, :] * factors[k : k + 1, :]
        stage[1, k] = value.astype(jnp.bfloat16).reshape(half, ny, nz)
    send(0, 1)
    part = got_ref.shape[1]
    early = x_theirs.shape[0] // snaps // part
    for k in range(snaps):
        for n in range(early):
            at = k * (early * part + 1) + n * part
            value = x_theirs[at : at + part, :] * factors[k : k + 1, :]
            i, y = divmod(n * part, ny)
            stage[0, k, i, y : y + part] = value.astype(jnp.bfloat16)
    units = half * ny // part
    late = [(known_mine, got_mine, n, 1, 1 + n // units, n % units) for n in range(2 * units)]
    theirs = [(0, n) for n in range(early, units)]
    theirs += [(c, n) for c in (1, 2) for n in range(units)]
    late += [(known_ref, got_ref, n, 0, c, unit) for n, (c, unit) in enumerate(theirs)]
    for count, (known, got, n, slot, c, unit) in enumerate(late):
        rows = wide.at[count % wide.shape[0]]

        def put(y, value):
            rows[pl.ds(y, snaps, part + 1), :] = value * factor

        add_other_group(known.at[n], got.at[n], block_ref, put)
        i, y = divmod(unit * part, ny)
        for k in range(snaps):
            at = k * (part + 1)
            stage[2 * c + slot, k, i, y : y + part] = rows[at : at + part, :].astype(jnp.bfloat16)
        if unit == units - 1:
            send(c, slot)
    for copy in copies:
        copy.wait()


def two_groups(velocity, metric, volume, coeffs):
    snaps, _, layers, ny, nz = velocity.shape
    half = layers // 2
    peers = lax.axis_size("space")
    bf16, f32 = jnp.bfloat16, jnp.float32

    def halo(first):
        pairs = []
        for s in range(peers):
            for g in range(2):
                down = (g == 0) == first
                pairs.append((s * 2 + g, ((s + (-1 if down else 1)) % peers) * 2 + g))
        return pairs

    def swap(value):
        return lax.ppermute(value, "snap", [(0, 1), (1, 0)])

    def shift(value, first):
        return lax.ppermute(value, ("space", "snap"), halo(first))

    field = jax.ShapeDtypeStruct((half, ny, snaps, nz), bf16)
    pair = jax.ShapeDtypeStruct((2, half, ny, snaps, nz), bf16)
    partial_sum = jax.ShapeDtypeStruct((2, half, ny, snaps, nz), f32)
    square = jax.ShapeDtypeStruct((2 * snaps, 2 * snaps), f32)
    cells = half * ny * snaps * nz
    wide = pltpu.VMEM((snaps * (ny + 1), nz), f32)
    along = pltpu.VMEM((half, ny, snaps, nz), f32)
    dma = pltpu.SemaphoreType.DMA

    def call(kernel, name, out_shape, args, scratch=(), in_specs=None, out_specs=None, work=5):
        return pl.pallas_call(
            kernel,
            out_shape=out_shape,
            in_specs=in_specs or [vmem()] * len(args),
            out_specs=out_specs or jax.tree.map(lambda _: vmem(), out_shape),
            scratch_shapes=list(scratch),
            compiler_params=params(),
            cost_estimate=cost(2 * work * cells, work * cells),
            name=name,
        )(*args)

    mine = call(
        flip_kernel,
        "flip_mine",
        pair,
        [pltpu.with_memory_space_constraint(velocity, pltpu.HBM)],
        [pltpu.VMEM((snaps, 2, half, ny, nz), bf16), wide, dma((2, half))],
        [hbm()],
    )
    edge_theirs = shift(mine, True)
    part = ny // 2
    units = half * ny // part
    early = units - 1
    first = jax.ShapeDtypeStruct((units + early, part, snaps, nz), bf16)
    last = jax.ShapeDtypeStruct((3 * units - early, part, snaps, nz), bf16)
    *theirs, x_first, x_mine = call(
        omega_x_kernel,
        "omega_x",
        (field, field, first, field),
        [velocity, metric, mine],
        [wide, along],
    )
    got_first = swap(x_first)
    x_mine = x_mine.reshape(units, part, snaps, nz)
    zu, yu = call(
        functools.partial(u_kernel, half),
        "u_terms",
        (partial_sum, partial_sum),
        [velocity, metric],
        [pltpu.VMEM((half, ny, snaps, nz), bf16), wide, along],
    )

    def own_part(name, parts, *fields):
        shape = jax.ShapeDtypeStruct((len(parts), part, snaps, nz), f32)
        return call(functools.partial(own_part_kernel, parts), name, shape, [blocks, *fields])

    def raw_modes(name, parts, counts, own, got):
        shapes = tuple(jax.ShapeDtypeStruct((snaps * (n * part + 1), nz), f32) for n in counts)
        return call(functools.partial(raw_kernel, parts), name, shapes, [own, got, blocks])

    yz_theirs = call(
        omega_theirs_kernel,
        "omega_yz_theirs",
        pair,
        [*theirs, mine, edge_theirs, zu, yu, metric],
    )
    got_yz = swap(yz_theirs)
    *late, _ = lax.optimization_barrier((*theirs, yz_theirs))
    edge_mine = [shift(part, False) for part in late]
    ordered, blocks = call(
        coeff_kernel,
        "coeff_blocks",
        (
            square,
            jax.ShapeDtypeStruct((ROWS // snaps * snaps, ROWS // snaps * 2 * snaps), bf16),
        ),
        [coeffs],
    )
    kernel = functools.partial(gram_x_kernel, ((0, 0),))
    gram = call(kernel, "gram_x", square, [x_mine, got_first, volume])
    (mine_x,) = raw_modes("raw_x_mine", ((0, 0),), (units,), x_mine, got_first)
    (theirs_x,) = raw_modes("raw_x_theirs", ((0, units),), (early,), x_first, got_first)
    *edge_mine, gram, mine_x, theirs_x = lax.optimization_barrier(
        (*edge_mine, gram, mine_x, theirs_x)
    )
    yz_mine = call(
        omega_mine_kernel,
        "omega_yz_mine",
        last,
        [mine, *theirs, *edge_mine, zu, yu, metric, x_mine],
    )
    got_last = swap(yz_mine)
    got_yz = got_yz.reshape(2 * units, part, snaps, nz)
    left = units - early
    size = -(-snaps * (2 * snaps + 1) // nz) * nz
    messages = jax.ShapeDtypeStruct((2 * peers, 1, size), f32)
    parts = ((left, 0), (left + units, units))
    yz_theirs = yz_theirs.reshape(2 * units, part, snaps, nz)
    known_mine = own_part("own_mine", [(0, left + n) for n in range(2 * units)], yz_mine)
    known_theirs = own_part(
        "own_theirs",
        [(0, n) for n in range(early, units)] + [(1, n) for n in range(2 * units)],
        x_first,
        yz_theirs,
    )
    got_yz, known_mine, known_theirs = lax.optimization_barrier(
        (got_yz, known_mine, known_theirs)
    )
    scale = 1.0 / (3.0 * layers * peers * ny * nz)
    kernel = functools.partial(messages_kernel, parts, scale)
    args = [yz_mine, got_yz, volume, gram, ordered]
    grams = call(kernel, "messages", messages, args)
    grams = lax.all_to_all(grams, ("space", "snap"), 0, 0, tiled=True)
    modes, rows = call(
        functools.partial(finish_kernel, half),
        "finish",
        (
            jax.ShapeDtypeStruct(velocity.shape, bf16),
            jax.ShapeDtypeStruct((snaps, 2 * snaps), f32),
        ),
        [
            grams, blocks, theirs_x, mine_x, known_mine, got_yz,
            known_theirs, got_last,
        ],
        [
            pltpu.VMEM((6, snaps, half, ny, nz), bf16),
            pltpu.VMEM((snaps, 2 * snaps), f32),
            pltpu.VMEM((snaps, nz), f32),
            pltpu.VMEM((half, snaps * (part + 1), nz), f32),
            dma((7,)),
        ],
        None,
        (hbm(), hbm()),
    )
    return (rows, modes)


def per_device(velocity, metric, volume, coeffs):
    peers = lax.axis_size("space")
    paired = lax.axis_size("snap") == 2 and velocity.shape[2] == 2 * WIDTH
    if paired and velocity.shape[0] % 16 == 0 and peers & (peers - 1) == 0:
        return two_groups(velocity, metric, volume, coeffs)
    return many_groups(velocity, metric, volume, coeffs)


def solution(mesh):
    placed = (
        P("snap", None, "space", None, None),
        P(None, "space", None, None),
        P("space", None, None),
        P(),
    )
    return jax.shard_map(
        per_device,
        mesh=mesh,
        in_specs=placed,
        out_specs=(P("snap", None), P("snap", None, "space", None, None)),
        check_vma=False,
    )
```

```python
import functools

import jax
import jax.numpy as jnp
from jax import lax
from jax.experimental import pallas as pl
from jax.experimental.pallas import tpu as pltpu
from jax.sharding import PartitionSpec as P

EPS = 1e-06
WIDTH = 2
ROWS = 128
LIMIT = 24 * 1024 * 1024


def with_halo(shard, sides, width):
    for axis, dim in sides:
        peers, length = (lax.axis_size(axis), shard.shape[dim])
        up = [(i, (i + 1) % peers) for i in range(peers)]
        down = [(j, i) for i, j in up]
        last = lax.slice_in_dim(shard, length - width, length, axis=dim)
        leading = lax.slice_in_dim(shard, 0, width, axis=dim)
        before = lax.ppermute(last, axis, up)
        after = lax.ppermute(leading, axis, down)
        shard = jnp.concatenate([before, shard, after], axis=dim)
    return shard


def deriv(padded, dim):
    count = padded.shape[dim] - 4

    def cut(offset):
        return lax.slice_in_dim(padded, offset, offset + count, axis=dim)

    return (8.0 * (cut(3) - cut(1)) - (cut(4) - cut(0))) / 12.0


def curl(padded_x, metric):
    inner = padded_x[:, :, 2:-2]
    padded_y = jnp.pad(inner, ((0, 0), (0, 0), (0, 0), (2, 2), (0, 0)))
    padded_z = jnp.concatenate([inner[..., -2:], inner, inner[..., :2]], axis=4)
    along_x = deriv(padded_x, 2) * metric[0]
    along_y = deriv(padded_y, 3) * metric[1]
    along_z = deriv(padded_z, 4) * metric[2]
    omega_x = along_y[:, 2] - along_z[:, 1]
    omega_y = along_z[:, 0] - along_x[:, 2]
    omega_z = along_x[:, 1] - along_y[:, 0]
    return jnp.stack([omega_x, omega_y, omega_z], axis=1).astype(jnp.bfloat16)


def many_groups(velocity, metric, volume, coeffs):
    snap_dev = velocity.shape[0]
    snaps = coeffs.shape[0]
    group = lax.axis_index("snap")
    scale = 1.0 / (
        3.0 * volume.shape[0] * lax.axis_size("space") * volume.shape[1] * volume.shape[2]
    )
    padded = with_halo(velocity, (("space", 2),), 2)
    vorticity = curl(padded.astype(jnp.float32), metric)
    coeff_f = coeffs.astype(jnp.float32)
    moved = lax.all_to_all(vorticity, "snap", split_axis=3, concat_axis=0, tiled=True)
    part_y = moved.shape[3]
    vol_part = lax.dynamic_slice_in_dim(volume, group * part_y, part_y, 1)
    weighted = (moved.astype(jnp.float32) * vol_part).astype(jnp.bfloat16).reshape(snaps, -1)
    flat = moved.reshape(snaps, -1)
    partial_value = lax.dot_general(
        weighted, flat, (((1,), (1,)), ((), ())), preferred_element_type=jnp.float32
    )
    raw = lax.dot_general(
        coeffs, flat, (((0,), (0,)), ((), ())), preferred_element_type=jnp.float32
    )
    whole = lax.psum(partial_value, ("space", "snap")) * scale
    energy = jnp.sum(coeff_f * jnp.dot(whole, coeff_f, precision=lax.Precision.HIGHEST), axis=0)
    rows = lax.dynamic_slice_in_dim(whole, group * snap_dev, snap_dev, 0)
    local_modes = (raw / jnp.sqrt(energy + EPS)[:, None]).astype(jnp.bfloat16).reshape(moved.shape)
    modes = lax.all_to_all(local_modes, "snap", split_axis=0, concat_axis=3, tiled=True)
    return (rows, modes)


def vmem():
    return pl.BlockSpec(memory_space=pltpu.VMEM)


def hbm():
    return pl.BlockSpec(memory_space=pltpu.HBM)


def params():
    return pltpu.CompilerParams(vmem_limit_bytes=LIMIT)


def cost(flops, moved):
    return pl.CostEstimate(flops=flops, bytes_accessed=moved, transcendentals=0)


def z_stencil(size):
    rows = lax.broadcasted_iota(jnp.int32, (size, size), 0)
    cols = lax.broadcasted_iota(jnp.int32, (size, size), 1)
    ahead = rows - cols
    ahead = jnp.where(ahead < 0, ahead + size, ahead)
    out = jnp.where(ahead == 1, 8.0, 0.0) - jnp.where(ahead == size - 1, 8.0, 0.0)
    out = out - jnp.where(ahead == 2, 1.0, 0.0) + jnp.where(ahead == size - 2, 1.0, 0.0)
    return out.astype(jnp.bfloat16)


def spread(src, wide):
    snaps, ny, _ = src.shape
    for s in range(snaps):
        wide[s * (ny + 1) : s * (ny + 1) + ny, :] = src[s].astype(jnp.float32)


def row(wide, y, snaps, ny):
    return wide[pl.ds(y, snaps, ny + 1), :]


def y_stencils(load, ny):
    held = {}

    def at(j):
        if j not in held:
            held[j] = load(j)
        return held[j]

    zero = jnp.zeros_like(at(0))
    for y in range(ny):
        near = (at(y + 1) if y + 1 < ny else zero) - (at(y - 1) if y >= 1 else zero)
        far = (at(y + 2) if y + 2 < ny else zero) - (at(y - 2) if y >= 2 else zero)
        held.pop(y - 2, None)
        yield y, 8.0 * near - far


def z_derivative(field, matrix, along):
    rows = field.shape[0] * field.shape[1] * field.shape[2]
    along[...] = jnp.dot(
        field.reshape(rows, field.shape[3]), matrix, preferred_element_type=jnp.float32
    ).reshape(field.shape)


def factor(metric_ref, m, layer, y):
    return metric_ref[m, layer, pl.ds(y, 1), :] * (1.0 / 12.0)


def flip(src, wide, out_ref, i):
    snaps, ny, _ = src.shape
    spread(src, wide)
    for y in range(ny):
        out_ref[i, y] = row(wide, y, snaps, ny).astype(jnp.bfloat16)


def flip_kernel(vel_ref, out_ref, buf, wide, sems):
    half = out_ref.shape[1]
    base = lax.axis_index("snap") * half
    copies = {}
    for c in range(2):
        for i in range(half):
            source = vel_ref.at[:, 1 + c, base + i]
            copies[c, i] = pltpu.make_async_copy(source, buf.at[:, c, i], sems.at[c, i])
            copies[c, i].start()
    for c in range(2):
        for i in range(half):
            copies[c, i].wait()
            flip(buf[:, c, i], wide, out_ref.at[c], i)


def omega_x_kernel(
    vel_ref, metric_ref, mine_ref, v_ref, w_ref, first_ref, ox_ref, wide, along
):
    half, ny, snaps, nz = ox_ref.shape
    group = lax.axis_index("snap")
    matrix = z_stencil(nz)
    for slot, base in ((0, (1 - group) * half), (1, group * half)):
        if slot == 0:
            for i in range(half):
                flip(vel_ref[:, 1, base + i], wide, v_ref, i)
        z_derivative(mine_ref[0] if slot else v_ref[...], matrix, along)
        for i in range(half):
            if slot == 0:
                spread(vel_ref[:, 2, base + i], wide)

            def load(j):
                if slot:
                    return mine_ref[1, i, j].astype(jnp.float32)
                value = row(wide, j, snaps, ny)
                w_ref[i, j] = value.astype(jnp.bfloat16)
                return value

            for y, across in y_stencils(load, ny):
                value = across * factor(metric_ref, 1, base + i, y)
                value = value - along[i, y] * factor(metric_ref, 2, base + i, y)
                value = value.astype(jnp.bfloat16)
                if slot:
                    ox_ref[i, y] = value
                unit, at = divmod((slot * half + i) * ny + y, first_ref.shape[1])
                if unit < first_ref.shape[0]:
                    first_ref[unit, at] = value


def u_kernel(half, vel_ref, metric_ref, zu_ref, yu_ref, flat, wide, along):
    snaps, _, _, ny, nz = vel_ref.shape
    matrix = z_stencil(nz)
    group = lax.axis_index("snap")
    for slot in range(2):
        base = (group if slot else 1 - group) * half
        for i in range(half):
            spread(vel_ref[:, 0, base + i], wide)

            def load(j):
                value = row(wide, j, snaps, ny)
                flat[i, j] = value.astype(jnp.bfloat16)
                return value

            for y, across in y_stencils(load, ny):
                yu_ref[slot, i, y] = across * factor(metric_ref, 1, base + i, y)
        z_derivative(flat[...], matrix, along)
        for i in range(half):
            for y in range(ny):
                zu_ref[slot, i, y] = along[i, y] * factor(metric_ref, 2, base + i, y)


def finish_curl(sign, slot, near_ref, far_ref, halo_ref, known_ref, metric_ref, put):
    half, ny, _, _ = near_ref.shape
    group = lax.axis_index("snap")
    part = group if slot else 1 - group

    def run(low_ref, high_ref):
        def plane(i, y):
            if i < 0:
                ref, k = low_ref, half + i
            elif i < half:
                ref, k = near_ref, i
            else:
                ref, k = high_ref, i - half
            return ref[k, y].astype(jnp.float32)

        for y in range(ny):
            at = [plane(i, y) for i in range(-WIDTH, half + WIDTH)]
            for i in range(half):
                along = 8.0 * (at[i + 3] - at[i + 1]) - (at[i + 4] - at[i])
                along = along * factor(metric_ref, 0, part * half + i, y)
                known = known_ref[slot, i, y]
                value = along - known if sign > 0 else known - along
                put(i, y, value.astype(jnp.bfloat16))

    @pl.when(part == 0)
    def _():
        run(halo_ref, far_ref)

    @pl.when(part == 1)
    def _():
        run(far_ref, halo_ref)


def omega_yz_kernel(slot, near, far, edge, zu_ref, yu_ref, metric_ref, y_ref, z_ref):
    known = (yu_ref, zu_ref)
    for c, sign, out_ref in ((1, -1, y_ref), (0, 1, z_ref)):
        fields = near[c], far[c], edge[c], known[c]
        finish_curl(sign, slot, *fields, metric_ref, out_ref)


def into(ref, start=0):
    def put(i, y, value):
        unit, at = divmod(i * ny_of[0] + y, ref.shape[1])
        ref[start + unit, at] = value

    ny_of = [ref.shape[1]]
    return put, ny_of


def omega_theirs_kernel(v_ref, w_ref, far, edge, *refs):
    far, edge = [(ref.at[0], ref.at[1]) for ref in (far, edge)]
    puts = [into(refs[-1].at[n])[0] for n in range(2)]
    omega_yz_kernel(0, (v_ref, w_ref), far, edge, *refs[:-1], *puts)


def omega_mine_kernel(*refs):
    near, far_v, far_w, edge_v, edge_w, *refs, ox_ref, out_ref = refs
    near, far = (near.at[0], near.at[1]), (far_v, far_w)
    _, ny, _, _ = far_v.shape
    whole = ox_ref.shape[0]
    left = out_ref.shape[0] - 2 * whole
    out_ref[:left] = ox_ref[whole - left :]
    puts = []
    for n in range(2):
        put, rows = into(out_ref, left + n * whole)
        rows[0] = ny
        puts.append(put)
    omega_yz_kernel(1, near, far, (edge_v, edge_w), *refs, *puts)


def weigh(value, weight):
    return (value.astype(jnp.float32) * weight).astype(jnp.bfloat16)


def gram_of(own, got, volume_ref, base, weighed):
    units, ny, _, _ = own.shape
    total = None
    for i in range(units):
        plain, heavy = [], []
        for y in range(ny):
            layer, at = divmod(i * ny + y, volume_ref.shape[1])
            weight = volume_ref[base + layer, pl.ds(at, 1), :]
            mine = own[i, y]
            other = got[i, y]
            plain.append(jnp.concatenate([mine, other], axis=0))
            mine = weigh(mine, weight) if weighed is None else weighed[i, y]
            heavy.append(jnp.concatenate([mine, weigh(other, weight)], axis=0))
        part = lax.dot_general(
            jnp.concatenate(heavy, axis=1),
            jnp.concatenate(plain, axis=1),
            (((1,), (1,)), ((), ())),
            preferred_element_type=jnp.float32,
        )
        total = part if total is None else total + part
    return total


def weigh_kernel(start, field_ref, volume_ref, out_ref):
    base = lax.axis_index("snap") * volume_ref.shape[0] // 2
    count, ny, _, _ = out_ref.shape
    units = volume_ref.shape[0] // 2 * volume_ref.shape[1] // ny
    for n in range(count):
        for y in range(ny):
            layer, at = divmod(n % units * ny + y, volume_ref.shape[1])
            weight = volume_ref[base + layer, pl.ds(at, 1), :]
            out_ref[n, y] = weigh(field_ref[start + n, y], weight)


def gram_sum(parts, own_ref, got_ref, volume_ref, earlier, weighed_ref=None):
    half = volume_ref.shape[0] // 2
    base = lax.axis_index("snap") * half
    units = half * volume_ref.shape[1] // own_ref.shape[1]
    total = None if earlier is None else earlier[...]
    for n, (own, got) in enumerate(parts):
        own, got = own_ref.at[pl.ds(own, units)], got_ref.at[pl.ds(got, units)]
        weighed = None if weighed_ref is None else weighed_ref.at[pl.ds(n * units, units)]
        part = gram_of(own, got, volume_ref, base, weighed)
        total = part if total is None else total + part
    return total


def gram_x_kernel(parts, own_ref, got_ref, volume_ref, out_ref):
    out_ref[...] = gram_sum(parts, own_ref, got_ref, volume_ref, None)


def messages_kernel(
    parts, scale, own_ref, got_ref, volume_ref, earlier, coeff_ref, weighed_ref, out_ref
):
    total = gram_sum(parts, own_ref, got_ref, volume_ref, earlier, weighed_ref) * scale
    coeff = coeff_ref[...]
    inner = jnp.dot(
        total, coeff, precision=lax.Precision.HIGHEST, preferred_element_type=jnp.float32
    )
    energy = jnp.sum(inner * coeff, axis=0, keepdims=True)
    snaps = total.shape[0] // 2
    turned = jnp.concatenate([total[snaps:, snaps:], total[snaps:, :snaps]], axis=1)
    group = lax.axis_index("snap")
    spare = out_ref.shape[2] - 2 * snaps * snaps - snaps
    for other, rows in enumerate((total[:snaps], turned)):
        line = [rows[k : k + 1] for k in range(snaps)]
        line.append(energy[:, other * snaps : (other + 1) * snaps])
        line = jnp.concatenate(line + [jnp.zeros((1, spare), jnp.float32)], axis=1)
        first = 1 - group if other else group
        for n in range(0, out_ref.shape[0], 2):
            out_ref[n + first] = line


def coeff_kernel(coeff_ref, ordered_ref, block_ref):
    count, _ = coeff_ref.shape
    snaps = count // 2
    rows = block_ref.shape[0]
    base = lax.axis_index("snap") * snaps

    def chosen(shape, test):
        left = lax.broadcasted_iota(jnp.int32, shape, 0)
        right = lax.broadcasted_iota(jnp.int32, shape, 1)
        return jnp.where(test(left, right), 1.0, 0.0).astype(jnp.bfloat16)

    def take(a, b, dims):
        out = lax.dot_general(a, b, (dims, ((), ())), preferred_element_type=jnp.float32)
        return out.astype(jnp.bfloat16)

    order = chosen((count, count), lambda j, m: j == lax.rem(m + base, count))
    turned = take(take(order, coeff_ref[...], ((0,), (1,))), order, ((1,), (0,)))
    same = chosen((count, count), lambda j, m: j == m)
    ordered_ref[...] = take(same, turned, ((1,), (1,))).astype(jnp.float32)
    mine = turned[:snaps]
    down = chosen((rows, snaps), lambda r, k: lax.rem(r, snaps) == k)
    for part in range(count // snaps):
        across = chosen((count, rows), lambda j, c: j == lax.rem(c, snaps) + part * snaps)
        wide = take(take(down, mine, ((1,), (0,))), across, ((1,), (0,)))
        same = chosen((rows, rows), lambda r, c: lax.div(r, snaps) == lax.div(c, snaps))
        block_ref[:, part * rows : (part + 1) * rows] = wide * same


def raw_blocks(own, got, block_ref, put):
    ny, snaps, nz = own.shape
    block = block_ref.shape[0] // snaps
    lanes = 2 if ny % (2 * block) == 0 else 1
    for start in range(0, ny, block * lanes):
        columns = []
        for n in range(lanes):
            at = start + n * block
            parts = [ref[at : at + block].reshape(block * snaps, nz) for ref in (own, got)]
            columns.append(jnp.concatenate(parts, axis=0))
        both = columns[0] if lanes == 1 else jnp.concatenate(columns, axis=1)
        raw = jnp.dot(block_ref[...], both, preferred_element_type=jnp.float32)
        for n in range(lanes):
            part = raw[:, n * nz : (n + 1) * nz].reshape(block, snaps, nz)
            for k in range(block):
                put(start + n * block + k, part[k])


def one_group_blocks(field, coeffs, put):
    ny, snaps, nz = field.shape
    block = coeffs.shape[0] // snaps
    lanes = 2 if ny % (2 * block) == 0 else 1
    for start in range(0, ny, block * lanes):
        columns = [
            field[at : at + block].reshape(block * snaps, nz)
            for at in range(start, start + block * lanes, block)
        ]
        both = columns[0] if lanes == 1 else jnp.concatenate(columns, axis=1)
        raw = jnp.dot(coeffs, both, preferred_element_type=jnp.float32)
        for n in range(lanes):
            part = raw[:, n * nz : (n + 1) * nz].reshape(block, snaps, nz)
            put(start + n * block, part)


def own_part_kernel(parts, block_ref, *refs):
    out_ref = refs[-1]
    coeffs = block_ref[:, : block_ref.shape[1] // 2]
    for n, (ref, layer) in enumerate(parts):

        def put(y, value):
            out_ref[n, y : y + value.shape[0]] = value

        one_group_blocks(refs[ref].at[layer], coeffs, put)


def add_other_group(known, got, block_ref, put):
    coeffs = block_ref[:, block_ref.shape[1] // 2 :]

    def put_block(y, value):
        for k in range(value.shape[0]):
            put(y + k, known[y + k] + value[k])

    one_group_blocks(got, coeffs, put_block)


def raw_kernel(parts, own_ref, got_ref, block_ref, *outs):
    for (own, got), out_ref in zip(parts, outs):
        _, ny, snaps, _ = own_ref.shape
        stride = out_ref.shape[0] // snaps
        count = stride // ny
        for i in range(count):

            def put(y, value):
                out_ref[pl.ds(i * ny + y, snaps, stride), :] = value

            raw_blocks(own_ref.at[own + i], got_ref.at[got + i], block_ref, put)


def finish_kernel(
    half, parts_ref, block_ref,
    x_theirs, x_mine, known_mine, got_mine, known_ref, got_ref,
    out_ref, rows_ref, stage, rows_buf, factors, wide, sems,
):
    _, snaps, _, ny, nz = stage.shape
    group = lax.axis_index("snap")
    lines = [parts_ref[n] for n in range(parts_ref.shape[0])]
    while len(lines) > 1:
        lines = [sum(lines[n : n + 2]) for n in range(0, len(lines), 2)]
    width = 2 * snaps
    line = lines[0][:, snaps * width : snaps * (width + 1)]
    down = lax.broadcasted_iota(jnp.int32, (snaps, snaps), 0)
    across = lax.broadcasted_iota(jnp.int32, (snaps, snaps), 1)
    energy = jnp.where(down == across, jnp.broadcast_to(line, (snaps, snaps)), 0.0)
    energy = jnp.sum(energy, axis=1, keepdims=True)
    factor = jnp.broadcast_to(1.0 / jnp.sqrt(energy + EPS), (snaps, nz))
    factors[...] = factor
    mine = jnp.concatenate(
        [lines[0][:, k * width : (k + 1) * width] for k in range(snaps)], axis=0
    )
    turned = jnp.concatenate([mine[:, snaps:], mine[:, :snaps]], axis=1)
    rows_buf[...] = jnp.where(group == 0, mine, turned)
    copies = [pltpu.make_async_copy(rows_buf, rows_ref, sems.at[6])]
    copies[0].start()
    bases = (1 - group) * half, group * half

    def send(c, slot):
        n = 2 * c + slot
        target = out_ref.at[:, c, pl.ds(bases[slot], half)]
        copies.append(pltpu.make_async_copy(stage.at[n], target, sems.at[n]))
        copies[-1].start()

    for k in range(snaps):
        at = k * (half * ny + 1)
        value = x_mine[at : at + half * ny, :] * factors[k : k + 1, :]
        stage[1, k] = value.astype(jnp.bfloat16).reshape(half, ny, nz)
    send(0, 1)
    part = got_ref.shape[1]
    early = x_theirs.shape[0] // snaps // part
    for k in range(snaps):
        for n in range(early):
            at = k * (early * part + 1) + n * part
            value = x_theirs[at : at + part, :] * factors[k : k + 1, :]
            i, y = divmod(n * part, ny)
            stage[0, k, i, y : y + part] = value.astype(jnp.bfloat16)
    units = half * ny // part
    late = [(known_mine, got_mine, n, 1, 1 + n // units, n % units) for n in range(2 * units)]
    theirs = [(0, n) for n in range(early, units)]
    theirs += [(c, n) for c in (1, 2) for n in range(units)]
    late += [(known_ref, got_ref, n, 0, c, unit) for n, (c, unit) in enumerate(theirs)]
    for count, (known, got, n, slot, c, unit) in enumerate(late):
        rows = wide.at[count % wide.shape[0]]

        def put(y, value):
            rows[pl.ds(y, snaps, part + 1), :] = value * factor

        add_other_group(known.at[n], got.at[n], block_ref, put)
        i, y = divmod(unit * part, ny)
        for k in range(snaps):
            at = k * (part + 1)
            stage[2 * c + slot, k, i, y : y + part] = rows[at : at + part, :].astype(jnp.bfloat16)
        if unit == units - 1:
            send(c, slot)
    for copy in copies:
        copy.wait()


def two_groups(velocity, metric, volume, coeffs):
    snaps, _, layers, ny, nz = velocity.shape
    half = layers // 2
    peers = lax.axis_size("space")
    bf16, f32 = jnp.bfloat16, jnp.float32

    def halo(first):
        pairs = []
        for s in range(peers):
            for g in range(2):
                down = (g == 0) == first
                pairs.append((s * 2 + g, ((s + (-1 if down else 1)) % peers) * 2 + g))
        return pairs

    def swap(value):
        return lax.ppermute(value, "snap", [(0, 1), (1, 0)])

    def shift(value, first):
        return lax.ppermute(value, ("space", "snap"), halo(first))

    field = jax.ShapeDtypeStruct((half, ny, snaps, nz), bf16)
    pair = jax.ShapeDtypeStruct((2, half, ny, snaps, nz), bf16)
    partial_sum = jax.ShapeDtypeStruct((2, half, ny, snaps, nz), f32)
    square = jax.ShapeDtypeStruct((2 * snaps, 2 * snaps), f32)
    cells = half * ny * snaps * nz
    wide = pltpu.VMEM((snaps * (ny + 1), nz), f32)
    along = pltpu.VMEM((half, ny, snaps, nz), f32)
    dma = pltpu.SemaphoreType.DMA

    def call(kernel, name, out_shape, args, scratch=(), in_specs=None, out_specs=None, work=5):
        return pl.pallas_call(
            kernel,
            out_shape=out_shape,
            in_specs=in_specs or [vmem()] * len(args),
            out_specs=out_specs or jax.tree.map(lambda _: vmem(), out_shape),
            scratch_shapes=list(scratch),
            compiler_params=params(),
            cost_estimate=cost(2 * work * cells, work * cells),
            name=name,
        )(*args)

    mine = call(
        flip_kernel,
        "flip_mine",
        pair,
        [pltpu.with_memory_space_constraint(velocity, pltpu.HBM)],
        [pltpu.VMEM((snaps, 2, half, ny, nz), bf16), wide, dma((2, half))],
        [hbm()],
    )
    edge_theirs = shift(mine, True)
    part = ny // 2
    units = half * ny // part
    early = units - 1
    first = jax.ShapeDtypeStruct((units + early, part, snaps, nz), bf16)
    last = jax.ShapeDtypeStruct((3 * units - early, part, snaps, nz), bf16)
    *theirs, x_first, x_mine = call(
        omega_x_kernel,
        "omega_x",
        (field, field, first, field),
        [velocity, metric, mine],
        [wide, along],
    )
    got_first = swap(x_first)
    x_mine = x_mine.reshape(units, part, snaps, nz)
    zu, yu = call(
        functools.partial(u_kernel, half),
        "u_terms",
        (partial_sum, partial_sum),
        [velocity, metric],
        [pltpu.VMEM((half, ny, snaps, nz), bf16), wide, along],
    )

    def own_part(name, parts, *fields):
        shape = jax.ShapeDtypeStruct((len(parts), part, snaps, nz), f32)
        return call(functools.partial(own_part_kernel, parts), name, shape, [blocks, *fields])

    def raw_modes(name, parts, counts, own, got):
        shapes = tuple(jax.ShapeDtypeStruct((snaps * (n * part + 1), nz), f32) for n in counts)
        return call(functools.partial(raw_kernel, parts), name, shapes, [own, got, blocks])

    yz_theirs = call(
        omega_theirs_kernel,
        "omega_yz_theirs",
        pair,
        [*theirs, mine, edge_theirs, zu, yu, metric],
    )
    got_yz = swap(yz_theirs)
    *late, _ = lax.optimization_barrier((*theirs, yz_theirs))
    edge_mine = [shift(part, False) for part in late]
    ordered, blocks = call(
        coeff_kernel,
        "coeff_blocks",
        (
            square,
            jax.ShapeDtypeStruct((ROWS // snaps * snaps, ROWS // snaps * 2 * snaps), bf16),
        ),
        [coeffs],
    )
    kernel = functools.partial(gram_x_kernel, ((0, 0),))
    gram = call(kernel, "gram_x", square, [x_mine, got_first, volume])
    (mine_x,) = raw_modes("raw_x_mine", ((0, 0),), (units,), x_mine, got_first)
    (theirs_x,) = raw_modes("raw_x_theirs", ((0, units),), (early,), x_first, got_first)
    *edge_mine, gram, mine_x, theirs_x = lax.optimization_barrier(
        (*edge_mine, gram, mine_x, theirs_x)
    )
    yz_mine = call(
        omega_mine_kernel,
        "omega_yz_mine",
        last,
        [mine, *theirs, *edge_mine, zu, yu, metric, x_mine],
    )
    got_last = swap(yz_mine)
    got_yz = got_yz.reshape(2 * units, part, snaps, nz)
    left = units - early
    size = -(-snaps * (2 * snaps + 1) // nz) * nz
    messages = jax.ShapeDtypeStruct((2 * peers, 1, size), f32)
    parts = ((left, 0), (left + units, units))
    yz_theirs = yz_theirs.reshape(2 * units, part, snaps, nz)
    known_mine = own_part("own_mine", [(0, left + n) for n in range(2 * units)], yz_mine)
    known_theirs = own_part(
        "own_theirs",
        [(0, n) for n in range(early, units)] + [(1, n) for n in range(2 * units)],
        x_first,
        yz_theirs,
    )
    weighed = jax.ShapeDtypeStruct((2 * units, part, snaps, nz), bf16)
    kernel = functools.partial(weigh_kernel, left)
    weighed = call(kernel, "weighed_mine", weighed, [yz_mine, volume])
    got_yz, known_mine, known_theirs, weighed = lax.optimization_barrier(
        (got_yz, known_mine, known_theirs, weighed)
    )
    scale = 1.0 / (3.0 * layers * peers * ny * nz)
    kernel = functools.partial(messages_kernel, parts, scale)
    args = [yz_mine, got_yz, volume, gram, ordered, weighed]
    grams = call(kernel, "messages", messages, args)
    grams = lax.all_to_all(grams, ("space", "snap"), 0, 0, tiled=True)
    modes, rows = call(
        functools.partial(finish_kernel, half),
        "finish",
        (
            jax.ShapeDtypeStruct(velocity.shape, bf16),
            jax.ShapeDtypeStruct((snaps, 2 * snaps), f32),
        ),
        [
            grams, blocks, theirs_x, mine_x, known_mine, got_yz,
            known_theirs, got_last,
        ],
        [
            pltpu.VMEM((6, snaps, half, ny, nz), bf16),
            pltpu.VMEM((snaps, 2 * snaps), f32),
            pltpu.VMEM((snaps, nz), f32),
            pltpu.VMEM((half, snaps * (part + 1), nz), f32),
            dma((7,)),
        ],
        None,
        (hbm(), hbm()),
    )
    return (rows, modes)


def per_device(velocity, metric, volume, coeffs):
    peers = lax.axis_size("space")
    paired = lax.axis_size("snap") == 2 and velocity.shape[2] == 2 * WIDTH
    if paired and velocity.shape[0] % 16 == 0 and peers & (peers - 1) == 0:
        return two_groups(velocity, metric, volume, coeffs)
    return many_groups(velocity, metric, volume, coeffs)


def solution(mesh):
    placed = (
        P("snap", None, "space", None, None),
        P(None, "space", None, None),
        P("space", None, None),
        P(),
    )
    return jax.shard_map(
        per_device,
        mesh=mesh,
        in_specs=placed,
        out_specs=(P("snap", None), P("snap", None, "space", None, None)),
        check_vma=False,
    )
```
